32 devices in a mesh: comp: 2 (over x), tx: 4 (over z), ty: 4 (over y, core).
Axes of the slice: x: 2, y: 2, z: 4, core: 2. Of those that a mesh axis runs over, the one named last changes fastest.
Arguments:
- state: float32 [2, 16, 512, 2048], P('comp', None, 'tx', 'ty'), may hold values from -6 to 6
- coefs: float32 [2, 3, 512, 2048], P('comp', None, 'tx', 'ty'), may hold values from -0.2 to 0.2
- land_sea: int32 [512, 2048], P('tx', 'ty'), may hold values 0 or 1
- gamma: float32 [2, 8], P('comp'), may hold values from 0.1 to 0.4
- pair_src: int32 [2, 8192], P('comp', ('tx', 'ty')), may hold values from 0 to 511
- pair_dev: int32 [2, 8192, 1], P('comp', ('tx', 'ty')), may hold values from 0 to 15; in each aligned block of 512 rows (0 to 511, 512 to 1023, ..., all dimensions but the last counted through in order) at most 64 rows name the same one
- pair_blk: int32 [2, 8192], P('comp', ('tx', 'ty')), may hold values from 0 to 511
- weights: bfloat16 [2, 8192, 128, 128], P('comp', ('tx', 'ty')), may hold values from -0.375 to 0.375
Outputs:
- new_state: float32 [2, 16, 512, 2048], P('comp', None, 'tx', 'ty')
- remapped: float32 [2, 8, 512, 2048], P('comp', None, 'tx', 'ty')
The draws below stay inside these ranges and needn't reach their ends.
Inputs may be any that keep to these rules, and one draw needn't show every extreme that they name: `pair_dev`: among the 512 weight blocks of one tile of one component, at most 64 name the same target tile, a bound that some block reaches.
All inputs are finite; a program needn't handle non-finite values. No bound on the sum of `land_sea` on one device may be relied on, other than what follows from the above.
Results may differ from the reference program's by a relative error of at most 0.0029.
Values sent between devices are 32-bit elements; how exact they have to be, the bound alone decides.
No kernel may reach another device: no remote copies, remote signals or barrier semaphores. Data moves between devices by JAX's collectives and lax.ppermute only.
A program may use at most 128 MiB of HBM per device.

```python
import math
import jax
import jax.numpy as jnp
import numpy as np
from jax import lax

NF = 16
CH = 8
BLK = 128
CX = 128
CY = 512
PAIRS = 512
TILES = 16
NB = 512
CAP = 64
NX = 512
NY = 2048
N_TX = 4
N_TY = 4


def with_ends(entries, own_key, low, high):
    index_at = [jax.random.randint(jax.random.fold_in(own_key, axis), (), 0, length) for axis, length in enumerate(entries.shape)]
    widest = entries.shape.index(max(entries.shape))
    neighbour = index_at[:widest] + [(index_at[widest] + 1) % entries.shape[widest]] + index_at[widest + 1:]
    return entries.at[tuple(index_at)].set(low).at[tuple(neighbour)].set(high)


def block_scale(rng, dims, shards, low, largest):
    def one(dim, shards_of):
        draws = jax.random.uniform(jax.random.fold_in(jax.random.fold_in(rng, 6), dim), (shards_of,), jnp.float32, low / len(shards), largest / len(shards))
        return jnp.repeat(jnp.exp(draws), dims[dim] // shards_of).reshape((-1,) + (1,) * (len(dims) - dim - 1))

    factor_of = one(*shards[0])
    for cut in shards[1:]:
        factor_of = factor_of * one(*cut)
    return factor_of


def deal_out(stream_key, own, number, rows, number_of, top, reach, skew):
    order = jax.random.permutation(stream_key, number_of)
    crowded, common = shares(number_of, rows * top, reach, skew, True), shares(number_of, rows * top, reach, skew, False)
    places = jnp.arange(number_of)

    def named(tallies, offset_by):
        used = int((tallies > 0).sum())
        fixed = max(1, used // 4)
        moved = fixed + (places - fixed + offset_by * (used - fixed)) % max(1, number_of - fixed)
        return jnp.zeros((number_of,), jnp.int32).at[order[jnp.where(places < fixed, places, moved)]].set(jnp.asarray(tallies, jnp.int32))

    tallies = jnp.where(number % 4 == 0, named(crowded, number // 4), named(common, number - number // 4 - 1))
    mixed = jax.random.permutation(jax.random.fold_in(own, 3), number_of)
    source_of, taker = mixed[0:number_of // 2 * 2:2], mixed[1:number_of // 2 * 2:2]
    margin = jnp.minimum(tallies[source_of] - 1, reach - tallies[taker]) // 2
    margin = jnp.where((source_of == order[0]) | (taker == order[0]) | (tallies[taker] == 0), 0, jnp.maximum(margin, 0))
    moved = jax.random.randint(jax.random.fold_in(own, 4), (number_of // 2,), 0, 1 << 20) % (margin + 1)
    tallies = tallies.at[source_of].add(-moved).at[taker].add(moved)
    items = jnp.searchsorted(jnp.cumsum(tallies), jnp.arange(rows * top), side="right").astype(jnp.int32)
    table = items.reshape(top, rows).T
    table = table[jax.random.permutation(jax.random.fold_in(own, 1), rows)]
    offset_by = jax.random.randint(jax.random.fold_in(own, 2), (rows, 1), 0, top)
    return jnp.take_along_axis(table, (jnp.arange(top)[None, :] + offset_by) % top, axis=1)


def shares(count, total, reach, slope, full):
    portions = [(1 << 20) // math.isqrt(rank ** slope) + 1 for rank in range(1, count + 1)]
    largest = reach if full else min(reach, max(-(-total // count), total * portions[0] // sum(portions)))
    least = 1 if total - largest >= count - 1 else 0
    given, rest = [largest] + [least] * (count - 1), total - largest - least * (count - 1)
    while rest > 0:
        candidates = [i for i in range(1, count) if given[i] < largest] or [i for i in range(1, count) if given[i] < reach]
        mass, budget = sum([portions[i] for i in candidates]), rest
        for i in candidates:
            addition = min(reach - given[i], max(1, budget * portions[i] // mass), rest)
            given[i] = given[i] + addition
            rest = rest - addition
    return np.array(given)


def noise(own_key, shape, spread, most, cuts=(), held_as=jnp.bfloat16):
    array = jax.random.normal(own_key, shape, jnp.float32) * spread
    if len(cuts) > 0:
        array = block_scale(own_key, shape, cuts, -0.22, 0.18) * array
    return jnp.clip(array, min=-most, max=most).astype(held_as)


def setup_inputs(seed: int = 0) -> dict:
    key_of = jax.random.split(jax.random.key(seed), 9)
    state = noise(key_of[0], (2, NF, NX, NY), 1.0, 6.0, ((0, 2), (2, 4), (3, 4)), jnp.float32)
    coefs = jnp.clip(jax.random.uniform(key_of[1], (2, 3, NX, NY), jnp.float32, -0.2, 0.2) * block_scale(key_of[1], (2, 3, NX, NY), ((0, 2), (2, 4), (3, 4)), -0.4, 0.0), -0.2, 0.2)
    land_sea = with_ends((jax.random.randint(key_of[2], (NX, NY), 0, 10) < 7).astype(jnp.int32), jax.random.fold_in(key_of[2], 1), 0, 1)
    gamma = jnp.clip(jnp.exp(math.log(0.4) - 1.3862944 * jax.random.uniform(key_of[3], (2, CH), jnp.float32) ** block_scale(key_of[3], (2, CH), ((0, 2),), -0.2, 0.2)), 0.1, 0.4)
    pair_src = with_ends(jax.random.randint(key_of[4], (2, TILES * PAIRS), 0, NB), jax.random.fold_in(key_of[4], 1), 0, NB - 1).astype(jnp.int32)
    pair_dev_keys = jax.random.split(jax.random.fold_in(key_of[5], 1), 2 * (TILES * PAIRS) // PAIRS)
    pair_dev_turns = jax.random.permutation(jax.random.fold_in(key_of[5], 3), 2 * (TILES * PAIRS) // PAIRS)
    pair_dev = jax.vmap(lambda own, number: deal_out(jax.random.fold_in(key_of[5], 2), own, number, PAIRS, TILES, 1, CAP, 2))(pair_dev_keys, pair_dev_turns).reshape((2, TILES * PAIRS, 1))
    pair_blk = with_ends(jax.random.randint(key_of[6], (2, TILES * PAIRS), 0, NB), jax.random.fold_in(key_of[6], 1), 0, NB - 1).astype(jnp.int32)
    weights = noise(key_of[7], (2, TILES * PAIRS, BLK, BLK), (2 * BLK) ** -0.5, 0.375, ((0, 2), (1, 16)))
    return dict(state=state, coefs=coefs, land_sea=land_sea, gamma=gamma, pair_src=pair_src, pair_dev=pair_dev, pair_blk=pair_blk, weights=weights)


def tendency(padded, coefs, recv, gamma, keep):
    center = padded[:, 1:-1, 1:-1]
    xminus = padded[:, :-2, 1:-1]
    xplus = padded[:, 2:, 1:-1]
    yminus = padded[:, 1:-1, :-2]
    yplus = padded[:, 1:-1, 2:]
    speed_x = coefs[0]
    speed_y = coefs[1]
    kappa = coefs[2]
    advect = -(jnp.maximum(speed_x, 0.0) * (center - xminus) + jnp.minimum(speed_x, 0.0) * (xplus - center))
    advect = advect - (jnp.maximum(speed_y, 0.0) * (center - yminus) + jnp.minimum(speed_y, 0.0) * (yplus - center))
    diffuse = kappa * (xplus + xminus + yplus + yminus - 4.0 * center)
    chan = recv.shape[0]
    couple = gamma[:, None, None] * (recv - center[:chan])
    couple = jnp.concatenate([couple, jnp.zeros_like(center[chan:])], axis=0)
    return keep * (advect + diffuse + couple)


def to_blocks(field):
    two, chan = field.shape[0], field.shape[1]
    tiled = field.reshape(two, chan, N_TX, CX, N_TY, CY).transpose(0, 1, 2, 4, 3, 5)
    return tiled.reshape(two, chan, N_TX * N_TY * (CX * CY // BLK), BLK)


def from_blocks(blocks):
    two, chan = blocks.shape[0], blocks.shape[1]
    tiled = blocks.reshape(two, chan, N_TX, N_TY, CX, CY).transpose(0, 1, 2, 4, 3, 5)
    return tiled.reshape(two, chan, N_TX * CX, N_TY * CY)


def reference(state, coefs, land_sea, gamma, pair_src, pair_dev, pair_blk, weights):
    tiles = N_TX * N_TY
    nblock = CX * CY // BLK
    surface = to_blocks(state[:, :CH]).astype(jnp.bfloat16)
    owner = jnp.arange(tiles * PAIRS, dtype=jnp.int32) // PAIRS
    received = []
    for comp in range(2):
        source = (owner * nblock + pair_src[comp]).astype(jnp.int32)
        picked = jnp.take(surface[comp], source, axis=1)
        picked = picked.transpose(1, 0, 2).reshape(tiles, PAIRS, CH, BLK)
        blocks = weights[comp].reshape(tiles, PAIRS, BLK, BLK)

        def apply_tile(pieces):
            return jnp.einsum("pts,pcs->pct", pieces[0].astype(jnp.float32), pieces[1].astype(jnp.float32))

        contrib = lax.map(apply_tile, (blocks, picked)).reshape(tiles * PAIRS, CH, BLK)
        target = (pair_dev[comp, :, 0] * nblock + pair_blk[comp]).astype(jnp.int32)
        summed = jax.ops.segment_sum(contrib, target, num_segments=tiles * nblock)
        received.append(summed.transpose(1, 0, 2))
    remapped = from_blocks(jnp.stack([received[1], received[0]]))
    results = []
    for comp in range(2):
        if comp == 0:
            keep = jnp.ones(land_sea.shape, jnp.float32)
            mix_a, mix_b = 0.0, 1.0
        else:
            keep = land_sea.astype(jnp.float32)
            mix_a, mix_b = 0.5, 0.5
        start = state[comp]
        first = tendency(jnp.pad(start, ((0, 0), (1, 1), (1, 1))), coefs[comp], remapped[comp], gamma[comp], keep)
        section = start + first
        second = tendency(jnp.pad(section, ((0, 0), (1, 1), (1, 1))), coefs[comp], remapped[comp], gamma[comp], keep)
        results.append(mix_a * start + (1.0 - mix_a) * section + mix_b * second)
    return jnp.stack(results), remapped
```

```python
import functools

import jax
import jax.numpy as jnp
from jax import lax
from jax.experimental import pallas as pl
from jax.experimental.pallas import tpu as pltpu
from jax.sharding import PartitionSpec as P

LANES = 128
STEP_PAIRS = 64
NT = (((1,), (1,)), ((), ()))


def shift_pairs(count, by):
    return [(i, i + by) for i in range(count) if 0 <= i + by < count]


def crossed(axis, by):
    count = lax.axis_size(axis)
    return [
        (c * count + i, (1 - c) * count + j) for c in range(2) for i, j in shift_pairs(count, by)
    ]


def contribution_kernel(dims, src_ref, dev_ref, blk_ref, state_ref, weights_ref, *rest):
    tiles, capacity, pairs, fields, cells_x, cells_y, width, chunks = dims
    outs = rest[: len(chunks)]
    cells, left_ref, product, w_ref, place_v, place_s = rest[len(chunks) : len(chunks) + 6]
    field_sems, weight_sems, place_sem = rest[len(chunks) + 6 :]
    parts = cells_y // width
    steps = pairs // STEP_PAIRS

    field_copies = [
        pltpu.make_async_copy(
            state_ref.at[0, f, :, pl.ds(q * width, width)],
            cells.at[pl.ds((q * fields + f) * cells_x, cells_x), :],
            field_sems.at[f * parts + q],
        )
        for f in range(fields)
        for q in range(parts)
    ]

    def weight_copy(step):
        some = pl.ds(step * STEP_PAIRS, STEP_PAIRS)
        return pltpu.make_async_copy(
            weights_ref.at[0, some], w_ref.at[some], weight_sems.at[step]
        )

    for copy in field_copies:
        copy.start()
    for step in range(steps):
        weight_copy(step).start()

    dev = dev_ref[...]
    tile_of = lax.broadcasted_iota(jnp.int32, (tiles, pairs), 0)
    lane_of = lax.broadcasted_iota(jnp.int32, (tiles, pairs), 1)
    member = (tile_of == dev).astype(jnp.float32)
    total = member
    shift = 1
    while shift < pairs:
        total = total + jnp.where(lane_of >= shift, pltpu.roll(total, shift, 1), 0.0)
        shift *= 2
    rank = (jnp.sum(member * total, axis=0, keepdims=True) - 1.0).astype(jnp.int32)
    src = src_ref[...]
    place_v[0:1, :] = dev * (capacity + 1) + rank
    place_v[1:2, :] = (src % parts) * (fields * cells_x) + src // parts
    to_scalars = pltpu.make_async_copy(place_v, place_s, place_sem)
    to_scalars.start()

    for out in outs:
        out[...] = jnp.zeros_like(out)
    slot_of = lax.broadcasted_iota(jnp.int32, (LANES, pairs), 0) % capacity
    chosen = (slot_of == rank).astype(jnp.bfloat16)
    blk = blk_ref[...]

    def spread(values):
        return lax.dot_general(
            (member * values).astype(jnp.bfloat16), chosen, NT, preferred_element_type=jnp.float32
        )

    ids = spread((blk // 256).astype(jnp.float32)) * 256.0
    ids = ids + spread((blk % 256).astype(jnp.float32))
    ids = jnp.where(spread(jnp.ones(dev.shape, jnp.float32)) > 0.5, ids, -1.0)
    for t in range(tiles):
        row = jnp.broadcast_to(ids[t : t + 1, :], (fields, LANES))
        for out in outs:
            out[t * (capacity + 1) + capacity] = row[: out.shape[1]]
    to_scalars.wait()
    for copy in field_copies:
        copy.wait()

    zeros = jnp.zeros((fields, width), jnp.float32)

    def cells_of(p):
        return cells[pl.ds(place_s[1, p], fields, stride=cells_x), :]

    def gather(step, carry):
        for i in range(0, STEP_PAIRS, 2):
            p = step * STEP_PAIRS + i
            one = jnp.concatenate([cells_of(p), zeros], axis=1)
            two = jnp.concatenate([zeros, cells_of(p + 1)], axis=1)
            rows = pl.ds(pl.multiple_of(p * fields, 2 * fields), 2 * fields)
            left_ref[rows, :] = jnp.concatenate([one, two], axis=0).astype(jnp.bfloat16)
        return carry

    def multiply(step, carry):
        weight_copy(step).wait()
        for i in range(0, STEP_PAIRS, 4):
            p = step * STEP_PAIRS + i
            rows = pl.ds(pl.multiple_of(p * fields, 4 * fields), 4 * fields)
            w = [w_ref[p + j] for j in range(4)]
            right = jnp.concatenate(
                [jnp.concatenate(w[0:2], axis=1), jnp.concatenate(w[2:4], axis=1)], axis=0
            )
            four = lax.dot_general(
                left_ref[rows, :], right, NT, preferred_element_type=jnp.float32
            )
            low = pl.ds(pl.multiple_of(p * fields, 2 * fields), 2 * fields)
            high = pl.ds(pl.multiple_of((p + 2) * fields, 2 * fields), 2 * fields)
            product[low, :] = four[: 2 * fields, :width]
            product[high, :] = four[2 * fields :, width:]
        return carry

    def scatter(step, carry):
        for i in range(STEP_PAIRS):
            p = step * STEP_PAIRS + i
            slot = place_s[0, p]
            one = product[pl.ds(pl.multiple_of(p * fields, fields), fields), :]
            for out, (first, last) in zip(outs, chunks):
                out[slot] = one[first:last]
        return carry

    lax.fori_loop(0, steps, gather, 0)
    lax.fori_loop(0, steps, multiply, 0)
    lax.fori_loop(0, steps, scatter, 0)


def contributions(state, pair_src, pair_dev, pair_blk, weights, tiles, capacity, chunks):
    _, _, cells_x, cells_y = state.shape
    fields = chunks[-1][1]
    pairs, width = weights.shape[1], weights.shape[2]
    rows = tiles * (capacity + 1)
    dims = (tiles, capacity, pairs, fields, cells_x, cells_y, width, chunks)
    parts = cells_y // width
    shapes = [(rows, last - first, width) for first, last in chunks]
    return pl.pallas_call(
        functools.partial(contribution_kernel, dims),
        in_specs=[pl.BlockSpec(memory_space=pltpu.VMEM)] * 3
        + [pl.BlockSpec(memory_space=pltpu.HBM)] * 2,
        out_specs=[pl.BlockSpec(memory_space=pltpu.VMEM) for _ in shapes],
        out_shape=[jax.ShapeDtypeStruct(shape, jnp.float32) for shape in shapes],
        scratch_shapes=[
            pltpu.VMEM((parts * fields * cells_x, width), jnp.float32),
            pltpu.VMEM((pairs * fields, 2 * width), jnp.bfloat16),
            pltpu.VMEM((pairs * fields, width), jnp.float32),
            pltpu.VMEM((pairs, width, width), jnp.bfloat16),
            pltpu.VMEM((8, pairs), jnp.int32),
            pltpu.SMEM((8, pairs), jnp.int32),
            pltpu.SemaphoreType.DMA((parts * fields,)),
            pltpu.SemaphoreType.DMA((pairs // STEP_PAIRS,)),
            pltpu.SemaphoreType.DMA,
        ],
        compiler_params=pltpu.CompilerParams(vmem_limit_bytes=56 * 1024 * 1024),
        cost_estimate=pl.CostEstimate(
            flops=2 * pairs * fields * width * width,
            bytes_accessed=2 * pairs * width * width + 8 * rows * fields * width,
            transcendentals=0,
        ),
        name="contributions",
    )(pair_src, pair_dev.reshape(1, pairs), pair_blk, state, weights)


def sum_kernel(dims, in_ref, out_ref, top_ref, bottom_ref, left_ref, right_ref, pick, high, low):
    tiles, capacity, fields, cells_x, cells_y, width = dims
    parts = cells_y // width
    group = LANES // capacity
    stride = (capacity + 1) * fields
    block_of = lax.broadcasted_iota(jnp.int32, (cells_x * parts, LANES), 0)
    block_of = (block_of % cells_x) * parts + block_of // cells_x
    block_of = block_of.astype(jnp.float32)
    lane = lax.broadcasted_iota(jnp.int32, (1, LANES), 1)
    for k in range(tiles // group):
        columns = pl.ds(k * LANES, LANES)
        ids = None
        for i in range(group):
            source = k * group + i
            row = in_ref[pl.ds(source * stride + capacity * fields, 1), :]
            ids = row if ids is None else jnp.where(lane // capacity == i, row, ids)
            for f in range(fields):
                x = in_ref[pl.ds(source * stride + f, capacity, stride=fields), :]
                rounded = x.astype(jnp.bfloat16)
                place = (
                    pl.ds(source * capacity, capacity),
                    pl.ds(f * width, width),
                )
                high[place] = rounded
                low[place] = (x - rounded.astype(jnp.float32)).astype(jnp.bfloat16)
        pick[:, columns] = (block_of == ids).astype(jnp.bfloat16)
    for q in range(parts):
        chosen = pick[pl.ds(q * cells_x, cells_x), :]
        total = jnp.dot(chosen, high[...], preferred_element_type=jnp.float32)
        total = total + jnp.dot(chosen, low[...], preferred_element_type=jnp.float32)
        for f in range(fields):
            tile = total[:, f * width : (f + 1) * width]
            out_ref[f, :, pl.ds(q * width, width)] = tile
            top_ref[pl.ds(f, 1), pl.ds(q * width, width)] = tile[:1]
            bottom_ref[pl.ds(f, 1), pl.ds(q * width, width)] = tile[cells_x - 1 :]
            if q == 0:
                left_ref[pl.ds(f, 1), :] = tile.T[:1]
            if q == parts - 1:
                right_ref[pl.ds(f, 1), :] = tile.T[width - 1 :]


def summed(rows, tiles, capacity, fields, cells_x, cells_y, width):
    dims = (tiles, capacity, fields, cells_x, cells_y, width)
    slots = tiles * capacity
    blocks = cells_x * cells_y // width
    shapes = [
        (fields, cells_x, cells_y),
        (fields, cells_y),
        (fields, cells_y),
        (fields, cells_x),
        (fields, cells_x),
    ]
    return pl.pallas_call(
        functools.partial(sum_kernel, dims),
        out_shape=[jax.ShapeDtypeStruct(shape, jnp.float32) for shape in shapes],
        scratch_shapes=[
            pltpu.VMEM((blocks, slots), jnp.bfloat16),
            pltpu.VMEM((slots, fields * width), jnp.bfloat16),
            pltpu.VMEM((slots, fields * width), jnp.bfloat16),
        ],
        compiler_params=pltpu.CompilerParams(vmem_limit_bytes=40 * 1024 * 1024),
        cost_estimate=pl.CostEstimate(
            flops=4 * blocks * slots * fields * width,
            bytes_accessed=4 * fields * width * (slots + blocks),
            transcendentals=0,
        ),
        name="sum_by_block",
    )(rows.reshape(tiles * (capacity + 1) * fields, width))


def stencil_factors(coefs, keep):
    u, v, kappa = coefs
    return [
        keep,
        keep * (jnp.maximum(u, 0.0) + kappa),
        keep * (kappa - jnp.minimum(u, 0.0)),
        keep * (jnp.maximum(v, 0.0) + kappa),
        keep * (kappa - jnp.minimum(v, 0.0)),
        -keep * (jnp.abs(u) + jnp.abs(v) + 4.0 * kappa),
    ]


def tendency(s, rate, factors, top, bottom, left, right):
    cells_x, cells_y = s.shape
    x_of = lax.broadcasted_iota(jnp.int32, s.shape, 0)
    y_of = lax.broadcasted_iota(jnp.int32, s.shape, 1)
    out = (factors[5] - rate * factors[0]) * s
    out += factors[1] * jnp.where(x_of == 0, top, pltpu.roll(s, 1, 0))
    out += factors[2] * jnp.where(x_of == cells_x - 1, bottom, pltpu.roll(s, cells_x - 1, 0))
    out += factors[3] * jnp.where(y_of == 0, left, pltpu.roll(s, 1, 1))
    out += factors[4] * jnp.where(y_of == cells_y - 1, right, pltpu.roll(s, cells_y - 1, 1))
    return out


def columns_of(rows):
    spare = 8 - rows.shape[0]
    if spare:
        rows = jnp.concatenate([rows, jnp.zeros((spare, rows.shape[1]), rows.dtype)], axis=0)
    return rows.T


def line_count(nfield):
    return 2 * nfield + 8


def edge_kernel(mix_ref, state_tops, state_ends, state_lefts, state_rights, coefs_tops, coefs_ends,
                coefs_lefts, coefs_rights, land_tops, land_ends, land_lefts, land_rights,
                x_low, x_high, y_low, y_high):
    nfield = state_tops.shape[1]
    last_row, last_lane = state_tops.shape[2] - 1, state_lefts.shape[3] - 1
    atmos = mix_ref[0, 1] == 1.0

    def kept(land):
        return jnp.where(atmos, 1.0, land.astype(jnp.float32))

    for out, state, coefs, land, lines in (
        (x_low, state_tops, coefs_tops, land_tops, (0, 1)),
        (x_high, state_ends, coefs_ends, land_ends, (last_row - 1, last_row)),
    ):
        outer = lines[0] if lines[0] == 0 else lines[1]
        out[2 * nfield :, :] = jnp.zeros((8, out.shape[1]), jnp.float32)
        for j, line in enumerate(lines):
            for f in range(nfield):
                out[j * nfield + f : j * nfield + f + 1, :] = state[0, f, line : line + 1, :]
        for c in range(3):
            out[2 * nfield + c : 2 * nfield + c + 1, :] = coefs[0, c, outer : outer + 1, :]
        out[2 * nfield + 3 : 2 * nfield + 4, :] = kept(land[outer : outer + 1, :])

    for out, state, coefs, land, lines in (
        (y_low, state_lefts, coefs_lefts, land_lefts, (0, 1)),
        (y_high, state_rights, coefs_rights, land_rights, (last_lane - 1, last_lane)),
    ):
        outer = lines[0] if lines[0] == 0 else lines[1]
        lane = lax.broadcasted_iota(jnp.int32, land.shape, 1)
        packed = jnp.zeros(land.shape, jnp.float32)

        def put(packed, tile, at, to):
            moved = (to - at) % LANES
            tile = pltpu.roll(tile, moved, 1) if moved else tile
            return jnp.where(lane == to, tile, packed)

        for j, line in enumerate(lines):
            for f in range(nfield):
                packed = put(packed, state[0, f], line, j * nfield + f)
        for c in range(3):
            packed = put(packed, coefs[0, c], outer, 2 * nfield + c)
        packed = put(packed, kept(land[...]), outer, 2 * nfield + 3)
        out[...] = packed.T[: out.shape[0]]


def edges_of(state, coefs, land_sea, mix):
    _, nfield, cells_x, cells_y = state.shape
    lines = line_count(nfield)
    ends = [
        ((8, cells_y), (0, 0)),
        ((8, cells_y), (cells_x // 8 - 1, 0)),
        ((cells_x, LANES), (0, 0)),
        ((cells_x, LANES), (0, cells_y // LANES - 1)),
    ]
    at = lambda lead, place: lambda i: (0,) * len(lead) + place
    specs = [pl.BlockSpec(memory_space=pltpu.SMEM)]
    for lead in ((1, nfield), (1, 3), ()):
        specs += [pl.BlockSpec(lead + shape, at(lead, place)) for shape, place in ends]
    shapes = [(lines, cells_y)] * 2 + [(lines, cells_x)] * 2
    return pl.pallas_call(
        edge_kernel,
        grid=(1,),
        in_specs=specs,
        out_specs=[pl.BlockSpec(shape, lambda i: (0, 0)) for shape in shapes],
        out_shape=[jax.ShapeDtypeStruct(shape, jnp.float32) for shape in shapes],
        compiler_params=pltpu.CompilerParams(vmem_limit_bytes=40 * 1024 * 1024),
        cost_estimate=pl.CostEstimate(
            flops=state.size, bytes_accessed=4 * 1024 * 1024, transcendentals=0
        ),
        name="edges",
    )(mix, *[state] * 4, *[coefs] * 4, *[land_sea] * 4)


def outer_section(center, across, along, factors, rate):
    lane = lax.broadcasted_iota(jnp.int32, center.shape, 1)
    count = center.shape[1]
    before = jnp.where(lane == 0, along[0], pltpu.roll(center, 1, 1))
    after = jnp.where(lane == count - 1, along[1], pltpu.roll(center, count - 1, 1))
    keep, low, high, back, ahead, middle = factors
    out = center + low * across[0] + high * across[1] + back * before + ahead * after
    return out + (middle - rate * keep) * center


def base_kernel(rate_ref, mix_ref, rates_ref, coefs_ref, land_ref, x_low, x_high, y_low, y_high,
                above, below, left, right, corners_left, corners_right, state_ref,
                out_ref, factors, rows, cols):
    f = pl.program_id(0)
    nfield = rates_ref.shape[0]
    lines = line_count(nfield)

    @pl.when(f == 0)
    def _():
        keep = jnp.where(mix_ref[0, 1] == 1.0, 1.0, land_ref[...].astype(jnp.float32))
        for i, factor in enumerate(stencil_factors([coefs_ref[0, c] for c in range(3)], keep)):
            factors[i] = factor
        rate = rates_ref[:, 0:1]
        near, far = pl.ds(0, nfield), pl.ds(nfield, nfield)
        last = corners_left.shape[1] - 1
        corner = (
            (corners_left[nfield : 2 * nfield, last:], corners_left[lines : lines + nfield, last:]),
            (corners_right[nfield : 2 * nfield, 0:1], corners_right[lines : lines + nfield, 0:1]),
        )
        for i, (ref, center, across, along, is_column) in enumerate(
            (
                (above, above[far, :], (above[near, :], x_low[near, :]), (corner[0][0], corner[1][0]), False),
                (below, below[near, :], (x_high[far, :], below[far, :]), (corner[0][1], corner[1][1]), False),
                (left, left[far, :], (left[near, :], y_low[near, :]), corner[0], True),
                (right, right[near, :], (y_high[far, :], right[far, :]), corner[1], True),
            )
        ):
            first = 2 * nfield
            of_line = stencil_factors(
                [ref[first + c : first + c + 1, :] for c in range(3)],
                ref[first + 3 : first + 4, :],
            )
            if is_column:
                of_line = [of_line[j] for j in (0, 3, 4, 1, 2, 5)]
            section = outer_section(center, across, along, of_line, rate)
            kept = cols if is_column else rows
            kept[pl.ds(i % 2 * nfield, nfield), :] = center
            kept[pl.ds((2 + i % 2) * nfield, nfield), :] = section

    rate = rate_ref[0, f]
    mix_a, mix_b = mix_ref[0, 0], mix_ref[0, 1]
    s = state_ref[0, 0]
    row = [rows[pl.ds(i * nfield + f, 1), :] for i in range(4)]
    col = columns_of(
        jnp.concatenate([cols[pl.ds(i * nfield + f, 1), :] for i in range(4)], axis=0)
    )
    s1 = s + tendency(s, rate, factors, row[0], row[1], col[:, 0:1], col[:, 1:2])
    more = tendency(s1, rate, factors, row[2], row[3], col[:, 2:3], col[:, 3:4])
    out_ref[0, 0] = mix_a * s + (1.0 - mix_a) * s1 + mix_b * more


def base_of(state, coefs, land_sea, rates, mix, edges, received, corners):
    _, nfield, cells_x, cells_y = state.shape
    field = pl.BlockSpec((1, 1, cells_x, cells_y), lambda f: (0, f, 0, 0))
    whole = lambda a: pl.BlockSpec(a.shape, lambda f: (0,) * a.ndim)
    rates_wide = jnp.broadcast_to(rates.T, (nfield, LANES))
    operands = [rates_wide, coefs, land_sea, *edges, *received, *corners]
    return pl.pallas_call(
        base_kernel,
        grid=(nfield,),
        in_specs=[
            pl.BlockSpec(memory_space=pltpu.SMEM),
            pl.BlockSpec(memory_space=pltpu.SMEM),
            *[whole(a) for a in operands],
            field,
        ],
        out_specs=[field, pl.BlockSpec((6, cells_x, cells_y), lambda f: (0, 0, 0))],
        out_shape=[
            jax.ShapeDtypeStruct(state.shape, jnp.float32),
            jax.ShapeDtypeStruct((6, cells_x, cells_y), jnp.float32),
        ],
        scratch_shapes=[
            pltpu.VMEM((4 * nfield, cells_y), jnp.float32),
            pltpu.VMEM((4 * nfield, cells_x), jnp.float32),
        ],
        compiler_params=pltpu.CompilerParams(vmem_limit_bytes=40 * 1024 * 1024),
        cost_estimate=pl.CostEstimate(
            flops=40 * state.size, bytes_accessed=8 * state.size, transcendentals=0
        ),
        name="base",
    )(rates, mix, *operands, state)


def finish_kernel(
    first, gamma_ref, mix_ref, factors, above, below, before, after, base_ref, recv_ref,
    top_ref, bottom_ref, left_ref, right_ref, *rest
):
    new_ref, out_ref = rest[-2:]
    f = pl.program_id(0)
    rate = gamma_ref[0, first + f]
    mix_b = mix_ref[0, 1]
    recv = recv_ref[0]
    g = factors[0] * recv * rate
    row = pl.ds(f, 1)
    keep_row = above.shape[0] - 5
    keep = slice(keep_row, keep_row + 1)
    top = above[keep, :] * top_ref[row, :] * rate
    bottom = below[keep, :] * bottom_ref[row, :] * rate
    left = before[keep, :] * left_ref[row, :] * rate
    right = after[keep, :] * right_ref[row, :] * rate
    cols = columns_of(jnp.concatenate([left, right], axis=0))
    more = tendency(g, rate, factors, top, bottom, cols[:, 0:1], cols[:, 1:2])
    new_ref[0, 0] = base_ref[0, 0] + mix_b * (2.0 * g + more)
    out_ref[0, 0] = recv


def finished(first, new_state, remapped, recv, rims, gamma, mix, factors, received):
    fields, cells_x, cells_y = recv.shape
    chan = gamma.shape[1]
    whole = lambda a: pl.BlockSpec(a.shape, lambda f: (0,) * a.ndim)
    field = pl.BlockSpec((1, 1, cells_x, cells_y), lambda f: (0, first + f, 0, 0))
    operands = [gamma, mix, factors, *received, new_state, recv, *rims]
    specs = [
        pl.BlockSpec(memory_space=pltpu.SMEM),
        pl.BlockSpec(memory_space=pltpu.SMEM),
        whole(factors),
        *[whole(lines) for lines in received],
        field,
        pl.BlockSpec((1, cells_x, cells_y), lambda f: (f, 0, 0)),
        *[whole(rim) for rim in rims],
    ]
    aliases = {7: 0}
    if remapped is not None:
        aliases[len(operands)] = 1
        operands.append(remapped)
        specs.append(pl.BlockSpec(memory_space=pl.ANY))
    return pl.pallas_call(
        functools.partial(finish_kernel, first),
        grid=(fields,),
        in_specs=specs,
        out_specs=[field, field],
        out_shape=[
            jax.ShapeDtypeStruct(new_state.shape, jnp.float32),
            jax.ShapeDtypeStruct((1, chan, cells_x, cells_y), jnp.float32),
        ],
        input_output_aliases=aliases,
        compiler_params=pltpu.CompilerParams(vmem_limit_bytes=40 * 1024 * 1024),
        cost_estimate=pl.CostEstimate(
            flops=20 * recv.size, bytes_accessed=20 * recv.size, transcendentals=0
        ),
        name="finish",
    )(*operands)


def body(state, coefs, land_sea, gamma, pair_src, pair_dev, pair_blk, weights):
    tx, ty = lax.axis_size("tx"), lax.axis_size("ty")
    tiles = tx * ty
    nfield, cells_x, cells_y = state.shape[1:]
    chan = gamma.shape[1]
    pairs, width = weights.shape[1], weights.shape[2]
    capacity = max(2, 2 * pairs // tiles)
    half = chan // 2
    chunks = ((0, half), (half, chan))
    early, late = contributions(
        state, pair_src, pair_dev, pair_blk, weights, tiles, capacity, chunks
    )
    swap = [(0, 1), (1, 0)]

    def exchanged(rows):
        rows = rows.reshape(tiles, capacity + 1, rows.shape[1], width)
        return lax.all_to_all(rows, ("tx", "ty"), split_axis=0, concat_axis=0, tiled=True)

    def add_up(rows):
        return summed(rows, tiles, capacity, half, cells_x, cells_y, width)

    late_in = exchanged(late)
    early_in = lax.ppermute(early, "comp", swap)

    land_after, _ = lax.optimization_barrier((land_sea, late))
    is_atmos = lax.axis_index("comp") == 0
    mix = jnp.where(is_atmos, jnp.array([[0.0, 1.0]]), jnp.array([[0.5, 0.5]]))
    mix = mix.astype(jnp.float32)
    rates = jnp.concatenate([gamma, jnp.zeros((1, nfield - chan), jnp.float32)], axis=1)
    x_low, x_high, y_low, y_high = edges_of(state, coefs, land_after, mix)
    left = lax.ppermute(y_high, "ty", shift_pairs(ty, 1))
    right = lax.ppermute(y_low, "ty", shift_pairs(ty, -1))
    above = lax.ppermute(x_high, "tx", shift_pairs(tx, 1))
    below = lax.ppermute(x_low, "tx", shift_pairs(tx, -1))
    received = (above, below, left, right)

    early_in = exchanged(early_in)

    ends = jnp.concatenate([above[:, cells_y - LANES :], below[:, cells_y - LANES :]], axis=0)
    starts = jnp.concatenate([above[:, :LANES], below[:, :LANES]], axis=0)
    corners_left = lax.ppermute(ends, "ty", shift_pairs(ty, 1))
    corners_right = lax.ppermute(starts, "ty", shift_pairs(ty, -1))
    base, factors = base_of(
        state, coefs, land_after, rates, mix, (x_low, x_high, y_low, y_high), received,
        (corners_left, corners_right),
    )

    recv_late, top, bottom, left, right = add_up(late_in)
    recv_late = lax.ppermute(recv_late, "comp", swap)
    rims_late = (
        lax.ppermute(bottom, ("comp", "tx"), crossed("tx", 1)),
        lax.ppermute(top, ("comp", "tx"), crossed("tx", -1)),
        lax.ppermute(right, ("comp", "ty"), crossed("ty", 1)),
        lax.ppermute(left, ("comp", "ty"), crossed("ty", -1)),
    )
    recv_early, top, bottom, left, right = add_up(early_in)
    rims_early = (
        lax.ppermute(bottom, "tx", shift_pairs(tx, 1)),
        lax.ppermute(top, "tx", shift_pairs(tx, -1)),
        lax.ppermute(right, "ty", shift_pairs(ty, 1)),
        lax.ppermute(left, "ty", shift_pairs(ty, -1)),
    )
    rest = (gamma, mix, factors, received)
    new_state, remapped = finished(half, base, None, recv_late, rims_late, *rest)
    new_state, remapped = finished(0, new_state, remapped, recv_early, rims_early, *rest)
    return new_state, remapped


def solution(mesh):
    placed = (
        P("comp", None, "tx", "ty"),
        P("comp", None, "tx", "ty"),
        P("tx", "ty"),
        P("comp", None),
        P("comp", ("tx", "ty")),
        P("comp", ("tx", "ty"), None),
        P("comp", ("tx", "ty")),
        P("comp", ("tx", "ty"), None, None),
    )
    return jax.shard_map(
        body,
        mesh=mesh,
        in_specs=placed,
        out_specs=(P("comp", None, "tx", "ty"), P("comp", None, "tx", "ty")),
        check_vma=False,
    )
```

```python
import functools

import jax
import jax.numpy as jnp
from jax import lax
from jax.experimental import pallas as pl
from jax.experimental.pallas import tpu as pltpu
from jax.sharding import PartitionSpec as P

LANES = 128
STEP_PAIRS = 64
NT = (((1,), (1,)), ((), ()))


def shift_pairs(count, by):
    return [(i, i + by) for i in range(count) if 0 <= i + by < count]


def crossed(axis, by):
    count = lax.axis_size(axis)
    return [
        (c * count + i, (1 - c) * count + j) for c in range(2) for i, j in shift_pairs(count, by)
    ]


def contribution_kernel(dims, src_ref, dev_ref, blk_ref, state_ref, weights_ref, *rest):
    tiles, capacity, pairs, fields, cells_x, cells_y, width, chunks = dims
    outs = rest[: len(chunks)]
    cells, left_ref, w_ref, pair_v, place_v, place_s = rest[len(chunks) : len(chunks) + 6]
    field_sems, weight_sems, pair_sems, place_sem = rest[len(chunks) + 6 :]
    parts = cells_y // width
    steps = pairs // STEP_PAIRS

    field_copies = [
        pltpu.make_async_copy(
            state_ref.at[0, f, :, pl.ds(q * width, width)],
            cells.at[pl.ds((q * fields + f) * cells_x, cells_x), :],
            field_sems.at[f * parts + q],
        )
        for f in range(fields)
        for q in range(parts)
    ]

    def weight_copy(step):
        some = pl.ds(step * STEP_PAIRS, STEP_PAIRS)
        return pltpu.make_async_copy(
            weights_ref.at[0, some], w_ref.at[some], weight_sems.at[step]
        )

    pair_copies = [
        pltpu.make_async_copy(ref, pair_v.at[i], pair_sems.at[i])
        for i, ref in enumerate((src_ref, dev_ref, blk_ref))
    ]
    for copy in pair_copies + field_copies:
        copy.start()
    for step in range(steps):
        weight_copy(step).start()
    for copy in pair_copies:
        copy.wait()

    src, dev, blk = pair_v[0], pair_v[1], pair_v[2]
    tile_of = lax.broadcasted_iota(jnp.int32, (tiles, pairs), 0)
    lane_of = lax.broadcasted_iota(jnp.int32, (tiles, pairs), 1)
    member = (tile_of == dev).astype(jnp.float32)
    total = member
    shift = 1
    while shift < pairs:
        total = total + jnp.where(lane_of >= shift, pltpu.roll(total, shift, 1), 0.0)
        shift *= 2
    rank = (jnp.sum(member * total, axis=0, keepdims=True) - 1.0).astype(jnp.int32)
    place_v[0:1, :] = dev * (capacity + 1) + rank
    place_v[1:2, :] = (src % parts) * (fields * cells_x) + src // parts
    to_scalars = pltpu.make_async_copy(place_v, place_s, place_sem)
    to_scalars.start()

    for out in outs:
        out[...] = jnp.zeros_like(out)
    slot_of = lax.broadcasted_iota(jnp.int32, (LANES, pairs), 0) % capacity
    chosen = (slot_of == rank).astype(jnp.bfloat16)

    def spread(values):
        return lax.dot_general(
            (member * values).astype(jnp.bfloat16), chosen, NT, preferred_element_type=jnp.float32
        )

    ids = spread((blk // 256).astype(jnp.float32)) * 256.0
    ids = ids + spread((blk % 256).astype(jnp.float32))
    ids = jnp.where(spread(jnp.ones(dev.shape, jnp.float32)) > 0.5, ids, -1.0)
    for t in range(tiles):
        row = jnp.broadcast_to(ids[t : t + 1, :], (fields, LANES))
        for out in outs:
            out[t * (capacity + 1) + capacity] = row[: out.shape[1]]
    to_scalars.wait()
    for copy in field_copies:
        copy.wait()

    group = LANES // fields
    lane = lax.broadcasted_iota(jnp.int32, (width, LANES), 1) // fields

    def gather(step, carry):
        for i in range(STEP_PAIRS):
            p = step * STEP_PAIRS + i
            rows = pl.ds(pl.multiple_of(p * fields, fields), fields)
            left_ref[rows, :] = cells[pl.ds(place_s[1, p], fields, stride=cells_x), :]
        return carry

    def multiply(step, carry):
        weight_copy(step).wait()
        for first_pair in range(0, STEP_PAIRS, group):
            p = step * STEP_PAIRS + first_pair
            rows = pl.ds(pl.multiple_of(p * fields, LANES), LANES)
            right = left_ref[rows, :].T.astype(jnp.bfloat16)
            kept = None
            for j in range(group):
                one = jnp.dot(w_ref[p + j], right, preferred_element_type=jnp.float32)
                kept = one if kept is None else jnp.where(lane == j, one, kept)
            kept = kept.T
            for j in range(group):
                slot = place_s[0, p + j]
                for out, (first, last) in zip(outs, chunks):
                    out[slot] = kept[j * fields + first : j * fields + last]
        return carry

    lax.fori_loop(0, steps, gather, 0)
    lax.fori_loop(0, steps, multiply, 0)


def contributions(state, pair_src, pair_dev, pair_blk, weights, tiles, capacity, chunks):
    _, _, cells_x, cells_y = state.shape
    fields = chunks[-1][1]
    pairs, width = weights.shape[1], weights.shape[2]
    rows = tiles * (capacity + 1)
    dims = (tiles, capacity, pairs, fields, cells_x, cells_y, width, chunks)
    parts = cells_y // width
    shapes = [(rows, last - first, width) for first, last in chunks]
    return pl.pallas_call(
        functools.partial(contribution_kernel, dims),
        in_specs=[pl.BlockSpec(memory_space=pltpu.HBM)] * 5,
        out_specs=[pl.BlockSpec(memory_space=pltpu.VMEM) for _ in shapes],
        out_shape=[jax.ShapeDtypeStruct(shape, jnp.float32) for shape in shapes],
        scratch_shapes=[
            pltpu.VMEM((parts * fields * cells_x, width), jnp.float32),
            pltpu.VMEM((pairs * fields, width), jnp.float32),
            pltpu.VMEM((pairs, width, width), jnp.bfloat16),
            pltpu.VMEM((3, 1, pairs), jnp.int32),
            pltpu.VMEM((8, pairs), jnp.int32),
            pltpu.SMEM((8, pairs), jnp.int32),
            pltpu.SemaphoreType.DMA((parts * fields,)),
            pltpu.SemaphoreType.DMA((pairs // STEP_PAIRS,)),
            pltpu.SemaphoreType.DMA((3,)),
            pltpu.SemaphoreType.DMA,
        ],
        compiler_params=pltpu.CompilerParams(vmem_limit_bytes=56 * 1024 * 1024),
        cost_estimate=pl.CostEstimate(
            flops=2 * pairs * fields * width * width,
            bytes_accessed=2 * pairs * width * width + 8 * rows * fields * width,
            transcendentals=0,
        ),
        name="contributions",
    )(pair_src, pair_dev.reshape(1, pairs), pair_blk, state, weights)


def sum_kernel(dims, in_ref, out_ref, top_ref, bottom_ref, left_ref, right_ref, pick, high, low):
    tiles, capacity, fields, cells_x, cells_y, width = dims
    parts = cells_y // width
    group = LANES // capacity
    stride = (capacity + 1) * fields
    block_of = lax.broadcasted_iota(jnp.int32, (cells_x * parts, LANES), 0)
    block_of = (block_of % cells_x) * parts + block_of // cells_x
    block_of = block_of.astype(jnp.float32)
    lane = lax.broadcasted_iota(jnp.int32, (1, LANES), 1)
    for k in range(tiles // group):
        columns = pl.ds(k * LANES, LANES)
        ids = None
        for i in range(group):
            source = k * group + i
            row = in_ref[pl.ds(source * stride + capacity * fields, 1), :]
            ids = row if ids is None else jnp.where(lane // capacity == i, row, ids)
            for f in range(fields):
                x = in_ref[pl.ds(source * stride + f, capacity, stride=fields), :]
                rounded = x.astype(jnp.bfloat16)
                place = (
                    pl.ds(source * capacity, capacity),
                    pl.ds(f * width, width),
                )
                high[place] = rounded
                low[place] = (x - rounded.astype(jnp.float32)).astype(jnp.bfloat16)
        pick[:, columns] = (block_of == ids).astype(jnp.bfloat16)
    for q in range(parts):
        chosen = pick[pl.ds(q * cells_x, cells_x), :]
        total = jnp.dot(chosen, high[...], preferred_element_type=jnp.float32)
        total = total + jnp.dot(chosen, low[...], preferred_element_type=jnp.float32)
        for f in range(fields):
            tile = total[:, f * width : (f + 1) * width]
            out_ref[f, :, pl.ds(q * width, width)] = tile
            top_ref[pl.ds(f, 1), pl.ds(q * width, width)] = tile[:1]
            bottom_ref[pl.ds(f, 1), pl.ds(q * width, width)] = tile[cells_x - 1 :]
            if q == 0:
                left_ref[pl.ds(f, 1), :] = tile.T[:1]
            if q == parts - 1:
                right_ref[pl.ds(f, 1), :] = tile.T[width - 1 :]


def summed(rows, tiles, capacity, fields, cells_x, cells_y, width):
    dims = (tiles, capacity, fields, cells_x, cells_y, width)
    slots = tiles * capacity
    blocks = cells_x * cells_y // width
    shapes = [
        (fields, cells_x, cells_y),
        (fields, cells_y),
        (fields, cells_y),
        (fields, cells_x),
        (fields, cells_x),
    ]
    return pl.pallas_call(
        functools.partial(sum_kernel, dims),
        out_shape=[jax.ShapeDtypeStruct(shape, jnp.float32) for shape in shapes],
        scratch_shapes=[
            pltpu.VMEM((blocks, slots), jnp.bfloat16),
            pltpu.VMEM((slots, fields * width), jnp.bfloat16),
            pltpu.VMEM((slots, fields * width), jnp.bfloat16),
        ],
        compiler_params=pltpu.CompilerParams(vmem_limit_bytes=40 * 1024 * 1024),
        cost_estimate=pl.CostEstimate(
            flops=4 * blocks * slots * fields * width,
            bytes_accessed=4 * fields * width * (slots + blocks),
            transcendentals=0,
        ),
        name="sum_by_block",
    )(rows.reshape(tiles * (capacity + 1) * fields, width))


def stencil_factors(coefs, keep):
    u, v, kappa = coefs
    return [
        keep,
        keep * (jnp.maximum(u, 0.0) + kappa),
        keep * (kappa - jnp.minimum(u, 0.0)),
        keep * (jnp.maximum(v, 0.0) + kappa),
        keep * (kappa - jnp.minimum(v, 0.0)),
        -keep * (jnp.abs(u) + jnp.abs(v) + 4.0 * kappa),
    ]


def tendency(s, rate, factors, top, bottom, left, right):
    cells_x, cells_y = s.shape
    x_of = lax.broadcasted_iota(jnp.int32, s.shape, 0)
    y_of = lax.broadcasted_iota(jnp.int32, s.shape, 1)
    out = (factors[5] - rate * factors[0]) * s
    out += factors[1] * jnp.where(x_of == 0, top, pltpu.roll(s, 1, 0))
    out += factors[2] * jnp.where(x_of == cells_x - 1, bottom, pltpu.roll(s, cells_x - 1, 0))
    out += factors[3] * jnp.where(y_of == 0, left, pltpu.roll(s, 1, 1))
    out += factors[4] * jnp.where(y_of == cells_y - 1, right, pltpu.roll(s, cells_y - 1, 1))
    return out


def columns_of(rows):
    spare = 8 - rows.shape[0]
    if spare:
        rows = jnp.concatenate([rows, jnp.zeros((spare, rows.shape[1]), rows.dtype)], axis=0)
    return rows.T


def line_count(nfield):
    return 2 * nfield + 8


def edge_kernel(mix_ref, state_tops, state_ends, state_lefts, state_rights, coefs_tops, coefs_ends,
                coefs_lefts, coefs_rights, land_tops, land_ends, land_lefts, land_rights,
                x_low, x_high, y_low, y_high):
    nfield = state_tops.shape[1]
    last_row, last_lane = state_tops.shape[2] - 1, state_lefts.shape[3] - 1
    atmos = mix_ref[0, 1] == 1.0

    def kept(land):
        return jnp.where(atmos, 1.0, land.astype(jnp.float32))

    for out, state, coefs, land, lines in (
        (x_low, state_tops, coefs_tops, land_tops, (0, 1)),
        (x_high, state_ends, coefs_ends, land_ends, (last_row - 1, last_row)),
    ):
        outer = lines[0] if lines[0] == 0 else lines[1]
        out[2 * nfield :, :] = jnp.zeros((8, out.shape[1]), jnp.float32)
        for j, line in enumerate(lines):
            for f in range(nfield):
                out[j * nfield + f : j * nfield + f + 1, :] = state[0, f, line : line + 1, :]
        for c in range(3):
            out[2 * nfield + c : 2 * nfield + c + 1, :] = coefs[0, c, outer : outer + 1, :]
        out[2 * nfield + 3 : 2 * nfield + 4, :] = kept(land[outer : outer + 1, :])

    for out, state, coefs, land, lines in (
        (y_low, state_lefts, coefs_lefts, land_lefts, (0, 1)),
        (y_high, state_rights, coefs_rights, land_rights, (last_lane - 1, last_lane)),
    ):
        outer = lines[0] if lines[0] == 0 else lines[1]
        lane = lax.broadcasted_iota(jnp.int32, land.shape, 1)
        packed = jnp.zeros(land.shape, jnp.float32)

        def put(packed, tile, at, to):
            moved = (to - at) % LANES
            tile = pltpu.roll(tile, moved, 1) if moved else tile
            return jnp.where(lane == to, tile, packed)

        for j, line in enumerate(lines):
            for f in range(nfield):
                packed = put(packed, state[0, f], line, j * nfield + f)
        for c in range(3):
            packed = put(packed, coefs[0, c], outer, 2 * nfield + c)
        packed = put(packed, kept(land[...]), outer, 2 * nfield + 3)
        out[...] = packed.T[: out.shape[0]]


def edges_of(state, coefs, land_sea, mix):
    _, nfield, cells_x, cells_y = state.shape
    lines = line_count(nfield)
    ends = [
        ((8, cells_y), (0, 0)),
        ((8, cells_y), (cells_x // 8 - 1, 0)),
        ((cells_x, LANES), (0, 0)),
        ((cells_x, LANES), (0, cells_y // LANES - 1)),
    ]
    at = lambda lead, place: lambda i: (0,) * len(lead) + place
    specs = [pl.BlockSpec(memory_space=pltpu.SMEM)]
    for lead in ((1, nfield), (1, 3), ()):
        specs += [pl.BlockSpec(lead + shape, at(lead, place)) for shape, place in ends]
    shapes = [(lines, cells_y)] * 2 + [(lines, cells_x)] * 2
    return pl.pallas_call(
        edge_kernel,
        grid=(1,),
        in_specs=specs,
        out_specs=[pl.BlockSpec(shape, lambda i: (0, 0)) for shape in shapes],
        out_shape=[jax.ShapeDtypeStruct(shape, jnp.float32) for shape in shapes],
        compiler_params=pltpu.CompilerParams(vmem_limit_bytes=40 * 1024 * 1024),
        cost_estimate=pl.CostEstimate(
            flops=state.size, bytes_accessed=4 * 1024 * 1024, transcendentals=0
        ),
        name="edges",
    )(mix, *[state] * 4, *[coefs] * 4, *[land_sea] * 4)


def outer_section(center, across, along, factors, rate):
    lane = lax.broadcasted_iota(jnp.int32, center.shape, 1)
    count = center.shape[1]
    before = jnp.where(lane == 0, along[0], pltpu.roll(center, 1, 1))
    after = jnp.where(lane == count - 1, along[1], pltpu.roll(center, count - 1, 1))
    keep, low, high, back, ahead, middle = factors
    out = center + low * across[0] + high * across[1] + back * before + ahead * after
    return out + (middle - rate * keep) * center


def base_kernel(rate_ref, mix_ref, rates_ref, coefs_ref, land_ref, x_low, x_high, y_low, y_high,
                above, below, left, right, corners_left, corners_right, state_ref,
                out_ref, factors, rows, cols):
    f = pl.program_id(0)
    nfield = rates_ref.shape[0]
    lines = line_count(nfield)

    @pl.when(f == 0)
    def _():
        keep = jnp.where(mix_ref[0, 1] == 1.0, 1.0, land_ref[...].astype(jnp.float32))
        for i, factor in enumerate(stencil_factors([coefs_ref[0, c] for c in range(3)], keep)):
            factors[i] = factor
        rate = rates_ref[:, 0:1]
        near, far = pl.ds(0, nfield), pl.ds(nfield, nfield)
        last = corners_left.shape[1] - 1
        corner = (
            (corners_left[nfield : 2 * nfield, last:], corners_left[lines : lines + nfield, last:]),
            (corners_right[nfield : 2 * nfield, 0:1], corners_right[lines : lines + nfield, 0:1]),
        )
        for i, (ref, center, across, along, is_column) in enumerate(
            (
                (above, above[far, :], (above[near, :], x_low[near, :]), (corner[0][0], corner[1][0]), False),
                (below, below[near, :], (x_high[far, :], below[far, :]), (corner[0][1], corner[1][1]), False),
                (left, left[far, :], (left[near, :], y_low[near, :]), corner[0], True),
                (right, right[near, :], (y_high[far, :], right[far, :]), corner[1], True),
            )
        ):
            first = 2 * nfield
            of_line = stencil_factors(
                [ref[first + c : first + c + 1, :] for c in range(3)],
                ref[first + 3 : first + 4, :],
            )
            if is_column:
                of_line = [of_line[j] for j in (0, 3, 4, 1, 2, 5)]
            section = outer_section(center, across, along, of_line, rate)
            kept = cols if is_column else rows
            kept[pl.ds(i % 2 * nfield, nfield), :] = center
            kept[pl.ds((2 + i % 2) * nfield, nfield), :] = section

    rate = rate_ref[0, f]
    mix_a, mix_b = mix_ref[0, 0], mix_ref[0, 1]
    s = state_ref[0, 0]
    row = [rows[pl.ds(i * nfield + f, 1), :] for i in range(4)]
    col = columns_of(
        jnp.concatenate([cols[pl.ds(i * nfield + f, 1), :] for i in range(4)], axis=0)
    )
    s1 = s + tendency(s, rate, factors, row[0], row[1], col[:, 0:1], col[:, 1:2])
    more = tendency(s1, rate, factors, row[2], row[3], col[:, 2:3], col[:, 3:4])
    out_ref[0, 0] = mix_a * s + (1.0 - mix_a) * s1 + mix_b * more


def base_of(state, coefs, land_sea, rates, mix, edges, received, corners):
    _, nfield, cells_x, cells_y = state.shape
    field = pl.BlockSpec((1, 1, cells_x, cells_y), lambda f: (0, f, 0, 0))
    whole = lambda a: pl.BlockSpec(a.shape, lambda f: (0,) * a.ndim)
    rates_wide = jnp.broadcast_to(rates.T, (nfield, LANES))
    operands = [rates_wide, coefs, land_sea, *edges, *received, *corners]
    return pl.pallas_call(
        base_kernel,
        grid=(nfield,),
        in_specs=[
            pl.BlockSpec(memory_space=pltpu.SMEM),
            pl.BlockSpec(memory_space=pltpu.SMEM),
            *[whole(a) for a in operands],
            field,
        ],
        out_specs=[field, pl.BlockSpec((6, cells_x, cells_y), lambda f: (0, 0, 0))],
        out_shape=[
            jax.ShapeDtypeStruct(state.shape, jnp.float32),
            jax.ShapeDtypeStruct((6, cells_x, cells_y), jnp.float32),
        ],
        scratch_shapes=[
            pltpu.VMEM((4 * nfield, cells_y), jnp.float32),
            pltpu.VMEM((4 * nfield, cells_x), jnp.float32),
        ],
        compiler_params=pltpu.CompilerParams(vmem_limit_bytes=40 * 1024 * 1024),
        cost_estimate=pl.CostEstimate(
            flops=40 * state.size, bytes_accessed=8 * state.size, transcendentals=0
        ),
        name="base",
    )(rates, mix, *operands, state)


def finish_kernel(
    first, gamma_ref, mix_ref, factors, above, below, before, after, base_ref, recv_ref,
    top_ref, bottom_ref, left_ref, right_ref, *rest
):
    new_ref, out_ref = rest[-2:]
    f = pl.program_id(0)
    rate = gamma_ref[0, first + f]
    mix_b = mix_ref[0, 1]
    recv = recv_ref[0]
    g = factors[0] * recv * rate
    row = pl.ds(f, 1)
    keep_row = above.shape[0] - 5
    keep = slice(keep_row, keep_row + 1)
    top = above[keep, :] * top_ref[row, :] * rate
    bottom = below[keep, :] * bottom_ref[row, :] * rate
    left = before[keep, :] * left_ref[row, :] * rate
    right = after[keep, :] * right_ref[row, :] * rate
    cols = columns_of(jnp.concatenate([left, right], axis=0))
    more = tendency(g, rate, factors, top, bottom, cols[:, 0:1], cols[:, 1:2])
    new_ref[0, 0] = base_ref[0, 0] + mix_b * (2.0 * g + more)
    out_ref[0, 0] = recv


def finished(first, new_state, remapped, recv, rims, gamma, mix, factors, received):
    fields, cells_x, cells_y = recv.shape
    chan = gamma.shape[1]
    whole = lambda a: pl.BlockSpec(a.shape, lambda f: (0,) * a.ndim)
    field = pl.BlockSpec((1, 1, cells_x, cells_y), lambda f: (0, first + f, 0, 0))
    operands = [gamma, mix, factors, *received, new_state, recv, *rims]
    specs = [
        pl.BlockSpec(memory_space=pltpu.SMEM),
        pl.BlockSpec(memory_space=pltpu.SMEM),
        whole(factors),
        *[whole(lines) for lines in received],
        field,
        pl.BlockSpec((1, cells_x, cells_y), lambda f: (f, 0, 0)),
        *[whole(rim) for rim in rims],
    ]
    aliases = {7: 0}
    if remapped is not None:
        aliases[len(operands)] = 1
        operands.append(remapped)
        specs.append(pl.BlockSpec(memory_space=pl.ANY))
    return pl.pallas_call(
        functools.partial(finish_kernel, first),
        grid=(fields,),
        in_specs=specs,
        out_specs=[field, field],
        out_shape=[
            jax.ShapeDtypeStruct(new_state.shape, jnp.float32),
            jax.ShapeDtypeStruct((1, chan, cells_x, cells_y), jnp.float32),
        ],
        input_output_aliases=aliases,
        compiler_params=pltpu.CompilerParams(vmem_limit_bytes=40 * 1024 * 1024),
        cost_estimate=pl.CostEstimate(
            flops=20 * recv.size, bytes_accessed=20 * recv.size, transcendentals=0
        ),
        name="finish",
    )(*operands)


def body(state, coefs, land_sea, gamma, pair_src, pair_dev, pair_blk, weights):
    tx, ty = lax.axis_size("tx"), lax.axis_size("ty")
    tiles = tx * ty
    nfield, cells_x, cells_y = state.shape[1:]
    chan = gamma.shape[1]
    pairs, width = weights.shape[1], weights.shape[2]
    capacity = max(2, 2 * pairs // tiles)
    half = chan // 2
    chunks = ((0, half), (half, chan))
    early, late = contributions(
        state, pair_src, pair_dev, pair_blk, weights, tiles, capacity, chunks
    )
    swap = [(0, 1), (1, 0)]

    def exchanged(rows):
        rows = rows.reshape(tiles, capacity + 1, rows.shape[1], width)
        return lax.all_to_all(rows, ("tx", "ty"), split_axis=0, concat_axis=0, tiled=True)

    def add_up(rows):
        return summed(rows, tiles, capacity, half, cells_x, cells_y, width)

    late_in = exchanged(late)
    early_in = lax.ppermute(early, "comp", swap)

    land_after, _ = lax.optimization_barrier((land_sea, late))
    is_atmos = lax.axis_index("comp") == 0
    mix = jnp.where(is_atmos, jnp.array([[0.0, 1.0]]), jnp.array([[0.5, 0.5]]))
    mix = mix.astype(jnp.float32)
    rates = jnp.concatenate([gamma, jnp.zeros((1, nfield - chan), jnp.float32)], axis=1)
    x_low, x_high, y_low, y_high = edges_of(state, coefs, land_after, mix)
    left = lax.ppermute(y_high, "ty", shift_pairs(ty, 1))
    right = lax.ppermute(y_low, "ty", shift_pairs(ty, -1))
    above = lax.ppermute(x_high, "tx", shift_pairs(tx, 1))
    below = lax.ppermute(x_low, "tx", shift_pairs(tx, -1))
    early_in, above, below, left, right = lax.optimization_barrier(
        (early_in, above, below, left, right)
    )
    received = (above, below, left, right)
    early_in = exchanged(early_in)

    ends = jnp.concatenate([above[:, cells_y - LANES :], below[:, cells_y - LANES :]], axis=0)
    starts = jnp.concatenate([above[:, :LANES], below[:, :LANES]], axis=0)
    corners_left = lax.ppermute(ends, "ty", shift_pairs(ty, 1))
    corners_right = lax.ppermute(starts, "ty", shift_pairs(ty, -1))
    base, factors = base_of(
        state, coefs, land_after, rates, mix, (x_low, x_high, y_low, y_high), received,
        (corners_left, corners_right),
    )

    recv_late, top, bottom, left, right = add_up(late_in)
    recv_late = lax.ppermute(recv_late, "comp", swap)
    rims_late = (
        lax.ppermute(bottom, ("comp", "tx"), crossed("tx", 1)),
        lax.ppermute(top, ("comp", "tx"), crossed("tx", -1)),
        lax.ppermute(right, ("comp", "ty"), crossed("ty", 1)),
        lax.ppermute(left, ("comp", "ty"), crossed("ty", -1)),
    )
    early_in, factors = lax.optimization_barrier((early_in, factors))
    recv_early, top, bottom, left, right = add_up(early_in)
    rims_early = (
        lax.ppermute(bottom, "tx", shift_pairs(tx, 1)),
        lax.ppermute(top, "tx", shift_pairs(tx, -1)),
        lax.ppermute(right, "ty", shift_pairs(ty, 1)),
        lax.ppermute(left, "ty", shift_pairs(ty, -1)),
    )
    rest = (gamma, mix, factors, received)
    new_state, remapped = finished(half, base, None, recv_late, rims_late, *rest)
    new_state, remapped = finished(0, new_state, remapped, recv_early, rims_early, *rest)
    return new_state, remapped


def solution(mesh):
    placed = (
        P("comp", None, "tx", "ty"),
        P("comp", None, "tx", "ty"),
        P("tx", "ty"),
        P("comp", None),
        P("comp", ("tx", "ty")),
        P("comp", ("tx", "ty"), None),
        P("comp", ("tx", "ty")),
        P("comp", ("tx", "ty"), None, None),
    )
    return jax.shard_map(
        body,
        mesh=mesh,
        in_specs=placed,
        out_specs=(P("comp", None, "tx", "ty"), P("comp", None, "tx", "ty")),
        check_vma=False,
    )
```

```python
import functools

import jax
import jax.numpy as jnp
from jax import lax
from jax.experimental import pallas as pl
from jax.experimental.pallas import tpu as pltpu
from jax.sharding import PartitionSpec as P

LANES = 128
STEP_PAIRS = 64
STRIP = 8
NT = (((1,), (1,)), ((), ()))


def shift_pairs(count, by):
    return [(i, i + by) for i in range(count) if 0 <= i + by < count]


def crossed(axis, by):
    count = lax.axis_size(axis)
    return [
        (c * count + i, (1 - c) * count + j) for c in range(2) for i, j in shift_pairs(count, by)
    ]


def split(value, parts):
    if parts & (parts - 1) == 0:
        return lax.shift_right_logical(value, parts.bit_length() - 1), value & (parts - 1)
    return lax.div(value, parts), lax.rem(value, parts)


def contribution_kernel(dims, src_ref, dev_ref, blk_ref, state_ref, weights_ref, *rest):
    tiles, capacity, pairs, fields, cells_x, cells_y, width, chunks = dims
    outs = rest[: len(chunks)]
    cells, w_ref, pair_v, pair_s, taken = rest[len(chunks) : len(chunks) + 5]
    field_sems, weight_sems, pair_sems = rest[len(chunks) + 5 :]
    parts = cells_y // width
    steps = pairs // STEP_PAIRS

    scalar_copies = [
        pltpu.make_async_copy(ref, pair_s.at[pl.ds(i, 1), :], pair_sems.at[i])
        for i, ref in enumerate((src_ref, dev_ref))
    ]
    vector_copies = [
        pltpu.make_async_copy(ref, pair_v.at[i], pair_sems.at[2 + i])
        for i, ref in enumerate((dev_ref, blk_ref))
    ]
    field_copies = [
        pltpu.make_async_copy(
            state_ref.at[0, f, :, pl.ds(q * width, width)],
            cells.at[pl.ds((q * fields + f) * cells_x, cells_x), :],
            field_sems.at[f * parts + q],
        )
        for f in range(fields)
        for q in range(parts)
    ]

    def weight_copy(step):
        some = pl.ds(step * STEP_PAIRS, STEP_PAIRS)
        return pltpu.make_async_copy(
            weights_ref.at[0, some], w_ref.at[some], weight_sems.at[step]
        )

    for copy in scalar_copies + vector_copies + field_copies:
        copy.start()
    for step in range(steps):
        weight_copy(step).start()
    for out in outs:
        out[...] = jnp.zeros_like(out)
    for t in range(tiles):
        taken[t] = t * (capacity + 1)

    for copy in vector_copies:
        copy.wait()
    dev, blk = pair_v[0], pair_v[1]
    tile_of = lax.broadcasted_iota(jnp.int32, (tiles, pairs), 0)
    lane_of = lax.broadcasted_iota(jnp.int32, (tiles, pairs), 1)
    member = (tile_of == dev).astype(jnp.float32)
    total = member
    shift = 1
    while shift < pairs:
        total = total + jnp.where(lane_of >= shift, pltpu.roll(total, shift, 1), 0.0)
        shift *= 2
    rank = (jnp.sum(member * total, axis=0, keepdims=True) - 1.0).astype(jnp.int32)
    slot_of = lax.broadcasted_iota(jnp.int32, (LANES, pairs), 0) % capacity
    chosen = (slot_of == rank).astype(jnp.bfloat16)

    def spread(values):
        return lax.dot_general(
            (member * values).astype(jnp.bfloat16), chosen, NT, preferred_element_type=jnp.float32
        )

    high, low = split(blk, 256)
    ids = spread(high.astype(jnp.float32)) * 256.0 + spread(low.astype(jnp.float32))
    ids = jnp.where(spread(jnp.ones(dev.shape, jnp.float32)) > 0.5, ids, -1.0)
    for t in range(tiles):
        row = jnp.broadcast_to(ids[t : t + 1, :], (fields, LANES))
        for out in outs:
            out[t * (capacity + 1) + capacity] = row[: out.shape[1]]
    for copy in scalar_copies + field_copies:
        copy.wait()

    def cells_of(p):
        x, part = split(pair_s[0, p], parts)
        return cells[pl.ds(part * (fields * cells_x) + x, fields, stride=cells_x), :]

    def some_pairs(step, carry):
        weight_copy(step).wait()
        for i in range(0, STEP_PAIRS, 2):
            p = step * STEP_PAIRS + i
            left = jnp.concatenate([cells_of(p), cells_of(p + 1)], axis=0).astype(jnp.bfloat16)
            right = w_ref[pl.ds(p, 2)].reshape(2 * width, width)
            both = lax.dot_general(left, right, NT, preferred_element_type=jnp.float32)
            for j in range(2):
                tile = pair_s[1, p + j]
                slot = taken[tile]
                taken[tile] = slot + 1
                one = both[j * fields : (j + 1) * fields, j * width : (j + 1) * width]
                for out, (first, last) in zip(outs, chunks):
                    out[slot] = one[first:last]
        return carry

    lax.fori_loop(0, steps, some_pairs, 0)


def contributions(state, pair_src, pair_dev, pair_blk, weights, tiles, capacity, chunks):
    _, _, cells_x, cells_y = state.shape
    fields = chunks[-1][1]
    pairs, width = weights.shape[1], weights.shape[2]
    rows = tiles * (capacity + 1)
    dims = (tiles, capacity, pairs, fields, cells_x, cells_y, width, chunks)
    parts = cells_y // width
    shapes = [(rows, last - first, width) for first, last in chunks]
    return pl.pallas_call(
        functools.partial(contribution_kernel, dims),
        in_specs=[pl.BlockSpec(memory_space=pltpu.HBM)] * 5,
        out_specs=[pl.BlockSpec(memory_space=pltpu.VMEM) for _ in shapes],
        out_shape=[jax.ShapeDtypeStruct(shape, jnp.float32) for shape in shapes],
        scratch_shapes=[
            pltpu.VMEM((parts * fields * cells_x, width), jnp.float32),
            pltpu.VMEM((pairs, width, width), jnp.bfloat16),
            pltpu.VMEM((2, 1, pairs), jnp.int32),
            pltpu.SMEM((2, pairs), jnp.int32),
            pltpu.SMEM((tiles,), jnp.int32),
            pltpu.SemaphoreType.DMA((parts * fields,)),
            pltpu.SemaphoreType.DMA((pairs // STEP_PAIRS,)),
            pltpu.SemaphoreType.DMA((4,)),
        ],
        compiler_params=pltpu.CompilerParams(vmem_limit_bytes=47 * 1024 * 1024),
        cost_estimate=pl.CostEstimate(
            flops=2 * pairs * fields * width * width,
            bytes_accessed=2 * pairs * width * width + 8 * rows * fields * width,
            transcendentals=0,
        ),
        name="contributions",
    )(pair_src, pair_dev.reshape(1, pairs), pair_blk, state, weights)


def sum_kernel(dims, in_ref, out_ref, top_ref, bottom_ref, left_ref, right_ref, pick, high, low):
    tiles, capacity, fields, cells_x, cells_y, width = dims
    parts = cells_y // width
    group = LANES // capacity
    stride = (capacity + 1) * fields
    block_of = lax.broadcasted_iota(jnp.int32, (cells_x * parts, LANES), 0)
    block_of = (block_of % cells_x) * parts + block_of // cells_x
    block_of = block_of.astype(jnp.float32)
    lane = lax.broadcasted_iota(jnp.int32, (1, LANES), 1)
    for k in range(tiles // group):
        columns = pl.ds(k * LANES, LANES)
        ids = None
        for i in range(group):
            source = k * group + i
            row = in_ref[pl.ds(source * stride + capacity * fields, 1), :]
            ids = row if ids is None else jnp.where(lane // capacity == i, row, ids)
            for f in range(fields):
                x = in_ref[pl.ds(source * stride + f, capacity, stride=fields), :]
                rounded = x.astype(jnp.bfloat16)
                place = (
                    pl.ds(source * capacity, capacity),
                    pl.ds(f * width, width),
                )
                high[place] = rounded
                low[place] = (x - rounded.astype(jnp.float32)).astype(jnp.bfloat16)
        pick[:, columns] = (block_of == ids).astype(jnp.bfloat16)
    for q in range(parts):
        chosen = pick[pl.ds(q * cells_x, cells_x), :]
        total = jnp.dot(chosen, high[...], preferred_element_type=jnp.float32)
        total = total + jnp.dot(chosen, low[...], preferred_element_type=jnp.float32)
        for f in range(fields):
            tile = total[:, f * width : (f + 1) * width]
            out_ref[f, :, pl.ds(q * width, width)] = tile
            top_ref[pl.ds(f, 1), pl.ds(q * width, width)] = tile[:1]
            bottom_ref[pl.ds(f, 1), pl.ds(q * width, width)] = tile[cells_x - 1 :]
            if q == 0:
                left_ref[pl.ds(f, 1), :] = tile.T[:1]
            if q == parts - 1:
                right_ref[pl.ds(f, 1), :] = tile.T[width - 1 :]


def summed(rows, tiles, capacity, fields, cells_x, cells_y, width):
    dims = (tiles, capacity, fields, cells_x, cells_y, width)
    slots = tiles * capacity
    blocks = cells_x * cells_y // width
    shapes = [
        (fields, cells_x, cells_y),
        (fields, cells_y),
        (fields, cells_y),
        (fields, cells_x),
        (fields, cells_x),
    ]
    return pl.pallas_call(
        functools.partial(sum_kernel, dims),
        out_shape=[jax.ShapeDtypeStruct(shape, jnp.float32) for shape in shapes],
        scratch_shapes=[
            pltpu.VMEM((blocks, slots), jnp.bfloat16),
            pltpu.VMEM((slots, fields * width), jnp.bfloat16),
            pltpu.VMEM((slots, fields * width), jnp.bfloat16),
        ],
        compiler_params=pltpu.CompilerParams(vmem_limit_bytes=40 * 1024 * 1024),
        cost_estimate=pl.CostEstimate(
            flops=4 * blocks * slots * fields * width,
            bytes_accessed=4 * fields * width * (slots + blocks),
            transcendentals=0,
        ),
        name="sum_by_block",
    )(rows.reshape(tiles * (capacity + 1) * fields, width))


def stencil_factors(coefs, keep):
    u, v, kappa = coefs
    return [
        keep,
        keep * (jnp.maximum(u, 0.0) + kappa),
        keep * (kappa - jnp.minimum(u, 0.0)),
        keep * (jnp.maximum(v, 0.0) + kappa),
        keep * (kappa - jnp.minimum(v, 0.0)),
        -keep * (jnp.abs(u) + jnp.abs(v) + 4.0 * kappa),
    ]


def tendency(s, rate, factors, top, bottom, left, right):
    cells_x, cells_y = s.shape
    x_of = lax.broadcasted_iota(jnp.int32, s.shape, 0)
    y_of = lax.broadcasted_iota(jnp.int32, s.shape, 1)
    out = (factors[5] - rate * factors[0]) * s
    out += factors[1] * jnp.where(x_of == 0, top, pltpu.roll(s, 1, 0))
    out += factors[2] * jnp.where(x_of == cells_x - 1, bottom, pltpu.roll(s, cells_x - 1, 0))
    out += factors[3] * jnp.where(y_of == 0, left, pltpu.roll(s, 1, 1))
    out += factors[4] * jnp.where(y_of == cells_y - 1, right, pltpu.roll(s, cells_y - 1, 1))
    return out


def columns_of(rows):
    spare = 8 - rows.shape[0]
    if spare:
        rows = jnp.concatenate([rows, jnp.zeros((spare, rows.shape[1]), rows.dtype)], axis=0)
    return rows.T


def line_count(nfield):
    return 2 * nfield + 8


def edge_kernel(mix_ref, state_tops, state_ends, state_lefts, state_rights, coefs_tops, coefs_ends,
                coefs_lefts, coefs_rights, land_tops, land_ends, land_lefts, land_rights,
                x_low, x_high, y_low, y_high):
    nfield = state_tops.shape[1]
    last_row, last_lane = state_tops.shape[2] - 1, state_lefts.shape[3] - 1
    atmos = mix_ref[0, 1] == 1.0

    def kept(land):
        return jnp.where(atmos, 1.0, land.astype(jnp.float32))

    for out, state, coefs, land, lines in (
        (x_low, state_tops, coefs_tops, land_tops, (0, 1)),
        (x_high, state_ends, coefs_ends, land_ends, (last_row - 1, last_row)),
    ):
        outer = lines[0] if lines[0] == 0 else lines[1]
        out[2 * nfield :, :] = jnp.zeros((8, out.shape[1]), jnp.float32)
        for j, line in enumerate(lines):
            for f in range(nfield):
                out[j * nfield + f : j * nfield + f + 1, :] = state[0, f, line : line + 1, :]
        for c in range(3):
            out[2 * nfield + c : 2 * nfield + c + 1, :] = coefs[0, c, outer : outer + 1, :]
        out[2 * nfield + 3 : 2 * nfield + 4, :] = kept(land[outer : outer + 1, :])

    for out, state, coefs, land, lines in (
        (y_low, state_lefts, coefs_lefts, land_lefts, (0, 1)),
        (y_high, state_rights, coefs_rights, land_rights, (last_lane - 1, last_lane)),
    ):
        outer = lines[0] if lines[0] == 0 else lines[1]
        lane = lax.broadcasted_iota(jnp.int32, land.shape, 1)
        packed = jnp.zeros(land.shape, jnp.float32)

        def put(packed, tile, at, to):
            moved = (to - at) % LANES
            tile = pltpu.roll(tile, moved, 1) if moved else tile
            return jnp.where(lane == to, tile, packed)

        for j, line in enumerate(lines):
            for f in range(nfield):
                packed = put(packed, state[0, f], line, j * nfield + f)
        for c in range(3):
            packed = put(packed, coefs[0, c], outer, 2 * nfield + c)
        packed = put(packed, kept(land[...]), outer, 2 * nfield + 3)
        out[...] = packed.T[: out.shape[0]]


def edges_of(state, coefs, land_sea, mix):
    _, nfield, cells_x, cells_y = state.shape
    lines = line_count(nfield)
    ends = [
        ((8, cells_y), (0, 0)),
        ((8, cells_y), (cells_x // 8 - 1, 0)),
        ((cells_x, LANES), (0, 0)),
        ((cells_x, LANES), (0, cells_y // LANES - 1)),
    ]
    at = lambda lead, place: lambda i: (0,) * len(lead) + place
    specs = [pl.BlockSpec(memory_space=pltpu.SMEM)]
    for lead in ((1, nfield), (1, 3), ()):
        specs += [pl.BlockSpec(lead + shape, at(lead, place)) for shape, place in ends]
    shapes = [(lines, cells_y)] * 2 + [(lines, cells_x)] * 2
    return pl.pallas_call(
        edge_kernel,
        grid=(1,),
        in_specs=specs,
        out_specs=[pl.BlockSpec(shape, lambda i: (0, 0)) for shape in shapes],
        out_shape=[jax.ShapeDtypeStruct(shape, jnp.float32) for shape in shapes],
        compiler_params=pltpu.CompilerParams(vmem_limit_bytes=56 * 1024 * 1024),
        cost_estimate=pl.CostEstimate(
            flops=state.size, bytes_accessed=4 * 1024 * 1024, transcendentals=0
        ),
        name="edges",
    )(mix, *[state] * 4, *[coefs] * 4, *[land_sea] * 4)


def outer_section(center, across, along, factors, rate):
    lane = lax.broadcasted_iota(jnp.int32, center.shape, 1)
    count = center.shape[1]
    before = jnp.where(lane == 0, along[0], pltpu.roll(center, 1, 1))
    after = jnp.where(lane == count - 1, along[1], pltpu.roll(center, count - 1, 1))
    keep, low, high, back, ahead, middle = factors
    out = center + low * across[0] + high * across[1] + back * before + ahead * after
    return out + (middle - rate * keep) * center


def base_kernel(rate_ref, mix_ref, rates_ref, coefs_ref, land_ref, x_low, x_high, y_low, y_high,
                above, below, left, right, corners_left, corners_right, state_ref,
                out_ref, factors, rows, cols):
    f = pl.program_id(0)
    nfield = rates_ref.shape[0]
    lines = line_count(nfield)

    @pl.when(f == 0)
    def _():
        keep = jnp.where(mix_ref[0, 1] == 1.0, 1.0, land_ref[...].astype(jnp.float32))
        for i, factor in enumerate(stencil_factors([coefs_ref[0, c] for c in range(3)], keep)):
            factors[i] = factor
        rate = rates_ref[:, 0:1]
        near, far = pl.ds(0, nfield), pl.ds(nfield, nfield)
        last = corners_left.shape[1] - 1
        corner = (
            (corners_left[nfield : 2 * nfield, last:], corners_left[lines : lines + nfield, last:]),
            (corners_right[nfield : 2 * nfield, 0:1], corners_right[lines : lines + nfield, 0:1]),
        )
        for i, (ref, center, across, along, is_column) in enumerate(
            (
                (above, above[far, :], (above[near, :], x_low[near, :]), (corner[0][0], corner[1][0]), False),
                (below, below[near, :], (x_high[far, :], below[far, :]), (corner[0][1], corner[1][1]), False),
                (left, left[far, :], (left[near, :], y_low[near, :]), corner[0], True),
                (right, right[near, :], (y_high[far, :], right[far, :]), corner[1], True),
            )
        ):
            first = 2 * nfield
            of_line = stencil_factors(
                [ref[first + c : first + c + 1, :] for c in range(3)],
                ref[first + 3 : first + 4, :],
            )
            if is_column:
                of_line = [of_line[j] for j in (0, 3, 4, 1, 2, 5)]
            section = outer_section(center, across, along, of_line, rate)
            kept = cols if is_column else rows
            kept[pl.ds(i % 2 * nfield, nfield), :] = center
            kept[pl.ds((2 + i % 2) * nfield, nfield), :] = section

    rate = rate_ref[0, f]
    mix_a, mix_b = mix_ref[0, 0], mix_ref[0, 1]
    s = state_ref[0, 0]
    row = [rows[pl.ds(i * nfield + f, 1), :] for i in range(4)]
    col = columns_of(
        jnp.concatenate([cols[pl.ds(i * nfield + f, 1), :] for i in range(4)], axis=0)
    )
    s1 = s + tendency(s, rate, factors, row[0], row[1], col[:, 0:1], col[:, 1:2])
    more = tendency(s1, rate, factors, row[2], row[3], col[:, 2:3], col[:, 3:4])
    out_ref[0, 0] = mix_a * s + (1.0 - mix_a) * s1 + mix_b * more


def base_of(state, coefs, land_sea, rates, mix, edges, received, corners):
    _, nfield, cells_x, cells_y = state.shape
    field = pl.BlockSpec((1, 1, cells_x, cells_y), lambda f: (0, f, 0, 0))
    whole = lambda a: pl.BlockSpec(a.shape, lambda f: (0,) * a.ndim)
    rates_wide = jnp.broadcast_to(rates.T, (nfield, LANES))
    operands = [rates_wide, coefs, land_sea, *edges, *received, *corners]
    return pl.pallas_call(
        base_kernel,
        grid=(nfield,),
        in_specs=[
            pl.BlockSpec(memory_space=pltpu.SMEM),
            pl.BlockSpec(memory_space=pltpu.SMEM),
            *[whole(a) for a in operands],
            field,
        ],
        out_specs=[field, pl.BlockSpec((6, cells_x, cells_y), lambda f: (0, 0, 0))],
        out_shape=[
            jax.ShapeDtypeStruct(state.shape, jnp.float32),
            jax.ShapeDtypeStruct((6, cells_x, cells_y), jnp.float32),
        ],
        scratch_shapes=[
            pltpu.VMEM((4 * nfield, cells_y), jnp.float32),
            pltpu.VMEM((4 * nfield, cells_x), jnp.float32),
        ],
        compiler_params=pltpu.CompilerParams(vmem_limit_bytes=40 * 1024 * 1024),
        cost_estimate=pl.CostEstimate(
            flops=40 * state.size, bytes_accessed=8 * state.size, transcendentals=0
        ),
        name="base",
    )(rates, mix, *operands, state)


def finish_kernel(
    first, gamma_ref, mix_ref, factors, above, below, before, after, base_ref, recv_ref,
    top_ref, bottom_ref, left_ref, right_ref, *rest
):
    new_ref, out_ref, wide = rest[-3:]
    f = pl.program_id(0)
    rate = gamma_ref[0, first + f]
    mix_b = mix_ref[0, 1]
    recv = recv_ref[0]
    g = factors[0] * recv * rate
    row = pl.ds(f, 1)
    keep_row = above.shape[0] - 5
    keep = slice(keep_row, keep_row + 1)
    cells_x, cells_y = recv.shape
    left = before[keep, :] * left_ref[row, :] * rate
    right = after[keep, :] * right_ref[row, :] * rate
    cols = columns_of(jnp.concatenate([left, right], axis=0))
    wide[STRIP - 1 : STRIP, :] = above[keep, :] * top_ref[row, :] * rate
    wide[STRIP + cells_x : STRIP + cells_x + 1, :] = below[keep, :] * bottom_ref[row, :] * rate
    wide[STRIP : STRIP + cells_x, :] = g
    out_ref[0, 0] = recv
    lane = lax.broadcasted_iota(jnp.int32, (STRIP, cells_y), 1)
    for i in range(0, cells_x, STRIP):
        rows = slice(i, i + STRIP)
        mid = wide[STRIP + i : 2 * STRIP + i, :]
        more = (factors[5, rows, :] - rate * factors[0, rows, :]) * mid
        more += factors[1, rows, :] * wide[STRIP + i - 1 : 2 * STRIP + i - 1, :]
        more += factors[2, rows, :] * wide[STRIP + i + 1 : 2 * STRIP + i + 1, :]
        prior = jnp.where(lane == 0, cols[rows, 0:1], pltpu.roll(mid, 1, 1))
        later = jnp.where(lane == cells_y - 1, cols[rows, 1:2], pltpu.roll(mid, cells_y - 1, 1))
        more += factors[3, rows, :] * prior + factors[4, rows, :] * later
        new_ref[0, 0, rows, :] = base_ref[0, 0, rows, :] + mix_b * (2.0 * mid + more)


def finished(first, new_state, remapped, recv, rims, gamma, mix, factors, received):
    fields, cells_x, cells_y = recv.shape
    chan = gamma.shape[1]
    whole = lambda a: pl.BlockSpec(a.shape, lambda f: (0,) * a.ndim)
    field = pl.BlockSpec((1, 1, cells_x, cells_y), lambda f: (0, first + f, 0, 0))
    operands = [gamma, mix, factors, *received, new_state, recv, *rims]
    specs = [
        pl.BlockSpec(memory_space=pltpu.SMEM),
        pl.BlockSpec(memory_space=pltpu.SMEM),
        whole(factors),
        *[whole(lines) for lines in received],
        field,
        pl.BlockSpec((1, cells_x, cells_y), lambda f: (f, 0, 0)),
        *[whole(rim) for rim in rims],
    ]
    aliases = {7: 0}
    if remapped is not None:
        aliases[len(operands)] = 1
        operands.append(remapped)
        specs.append(pl.BlockSpec(memory_space=pl.ANY))
    return pl.pallas_call(
        functools.partial(finish_kernel, first),
        grid=(fields,),
        in_specs=specs,
        out_specs=[field, field],
        out_shape=[
            jax.ShapeDtypeStruct(new_state.shape, jnp.float32),
            jax.ShapeDtypeStruct((1, chan, cells_x, cells_y), jnp.float32),
        ],
        input_output_aliases=aliases,
        scratch_shapes=[pltpu.VMEM((cells_x + 2 * STRIP, cells_y), jnp.float32)],
        compiler_params=pltpu.CompilerParams(vmem_limit_bytes=40 * 1024 * 1024),
        cost_estimate=pl.CostEstimate(
            flops=20 * recv.size, bytes_accessed=20 * recv.size, transcendentals=0
        ),
        name="finish",
    )(*operands)


def body(state, coefs, land_sea, gamma, pair_src, pair_dev, pair_blk, weights):
    tx, ty = lax.axis_size("tx"), lax.axis_size("ty")
    tiles = tx * ty
    nfield, cells_x, cells_y = state.shape[1:]
    chan = gamma.shape[1]
    pairs, width = weights.shape[1], weights.shape[2]
    capacity = max(2, 2 * pairs // tiles)
    half = chan // 2
    chunks = ((0, half), (half, chan))
    early, late = contributions(
        state, pair_src, pair_dev, pair_blk, weights, tiles, capacity, chunks
    )
    swap = [(0, 1), (1, 0)]

    def exchanged(rows):
        rows = rows.reshape(tiles, capacity + 1, rows.shape[1], width)
        return lax.all_to_all(rows, ("tx", "ty"), split_axis=0, concat_axis=0, tiled=True)

    def add_up(rows):
        return summed(rows, tiles, capacity, half, cells_x, cells_y, width)

    late_in = exchanged(late)
    early_in = lax.ppermute(early, "comp", swap)

    land_after, _ = lax.optimization_barrier((land_sea, late))
    is_atmos = lax.axis_index("comp") == 0
    mix = jnp.where(is_atmos, jnp.array([[0.0, 1.0]]), jnp.array([[0.5, 0.5]]))
    mix = mix.astype(jnp.float32)
    rates = jnp.concatenate([gamma, jnp.zeros((1, nfield - chan), jnp.float32)], axis=1)
    x_low, x_high, y_low, y_high = edges_of(state, coefs, land_after, mix)
    left = lax.ppermute(y_high, "ty", shift_pairs(ty, 1))
    right = lax.ppermute(y_low, "ty", shift_pairs(ty, -1))
    above = lax.ppermute(x_high, "tx", shift_pairs(tx, 1))
    below = lax.ppermute(x_low, "tx", shift_pairs(tx, -1))
    early_in, above, below, left, right = lax.optimization_barrier(
        (early_in, above, below, left, right)
    )
    received = (above, below, left, right)
    early_in = exchanged(early_in)

    ends = jnp.concatenate([above[:, cells_y - LANES :], below[:, cells_y - LANES :]], axis=0)
    starts = jnp.concatenate([above[:, :LANES], below[:, :LANES]], axis=0)
    corners_left = lax.ppermute(ends, "ty", shift_pairs(ty, 1))
    corners_right = lax.ppermute(starts, "ty", shift_pairs(ty, -1))
    base, factors = base_of(
        state, coefs, land_after, rates, mix, (x_low, x_high, y_low, y_high), received,
        (corners_left, corners_right),
    )

    recv_late, top, bottom, left, right = add_up(late_in)
    recv_late = lax.ppermute(recv_late, "comp", swap)
    rims_late = (
        lax.ppermute(bottom, ("comp", "tx"), crossed("tx", 1)),
        lax.ppermute(top, ("comp", "tx"), crossed("tx", -1)),
        lax.ppermute(right, ("comp", "ty"), crossed("ty", 1)),
        lax.ppermute(left, ("comp", "ty"), crossed("ty", -1)),
    )
    early_in, factors = lax.optimization_barrier((early_in, factors))
    recv_early, top, bottom, left, right = add_up(early_in)
    rims_early = (
        lax.ppermute(bottom, "tx", shift_pairs(tx, 1)),
        lax.ppermute(top, "tx", shift_pairs(tx, -1)),
        lax.ppermute(right, "ty", shift_pairs(ty, 1)),
        lax.ppermute(left, "ty", shift_pairs(ty, -1)),
    )
    rest = (gamma, mix, factors, received)
    new_state, remapped = finished(half, base, None, recv_late, rims_late, *rest)
    new_state, remapped = finished(0, new_state, remapped, recv_early, rims_early, *rest)
    return new_state, remapped


def solution(mesh):
    placed = (
        P("comp", None, "tx", "ty"),
        P("comp", None, "tx", "ty"),
        P("tx", "ty"),
        P("comp", None),
        P("comp", ("tx", "ty")),
        P("comp", ("tx", "ty"), None),
        P("comp", ("tx", "ty")),
        P("comp", ("tx", "ty"), None, None),
    )
    return jax.shard_map(
        body,
        mesh=mesh,
        in_specs=placed,
        out_specs=(P("comp", None, "tx", "ty"), P("comp", None, "tx", "ty")),
        check_vma=False,
    )
```

```python
import functools

import jax
import jax.numpy as jnp
from jax import lax
from jax.experimental import pallas as pl
from jax.experimental.pallas import tpu as pltpu
from jax.sharding import PartitionSpec as P

LANES = 128
STEP_PAIRS = 64
STRIP = 8
NT = (((1,), (1,)), ((), ()))


def shift_pairs(count, by):
    return [(i, i + by) for i in range(count) if 0 <= i + by < count]


def crossed(axis, by):
    count = lax.axis_size(axis)
    return [
        (c * count + i, (1 - c) * count + j) for c in range(2) for i, j in shift_pairs(count, by)
    ]


def split(value, parts):
    if parts & (parts - 1) == 0:
        return lax.shift_right_logical(value, parts.bit_length() - 1), value & (parts - 1)
    return lax.div(value, parts), lax.rem(value, parts)


def slot_table(dev, blk, tiles, capacity):
    pairs = dev.shape[1]
    tile_of = lax.broadcasted_iota(jnp.int32, (tiles, pairs), 0)
    lane_of = lax.broadcasted_iota(jnp.int32, (tiles, pairs), 1)
    member = (tile_of == dev).astype(jnp.float32)
    total = member
    shift = 1
    while shift < pairs:
        total = total + jnp.where(lane_of >= shift, pltpu.roll(total, shift, 1), 0.0)
        shift *= 2
    rank = (jnp.sum(member * total, axis=0, keepdims=True) - 1.0).astype(jnp.int32)
    slot_of = lax.broadcasted_iota(jnp.int32, (LANES, pairs), 0) % capacity
    chosen = (slot_of == rank).astype(jnp.bfloat16)

    def spread(values):
        return lax.dot_general(
            (member * values).astype(jnp.bfloat16), chosen, NT, preferred_element_type=jnp.float32
        )

    high, low = split(blk, 256)
    ids = spread(high.astype(jnp.float32)) * 256.0 + spread(low.astype(jnp.float32))
    return rank, jnp.where(spread(jnp.ones(dev.shape, jnp.float32)) > 0.5, ids, -1.0)


def put_ids(out, ids, tiles, capacity):
    for t in range(tiles):
        out[t * (capacity + 1) + capacity] = jnp.broadcast_to(ids[t : t + 1, :], out.shape[1:])


def contribution_kernel(
    dims, src_ref, dev_ref, blk_ref, state_ref, weights_ref, early_ref, late_ref,
    cells, w_ref, pair_v, pair_s, taken, field_sems, weight_sems, pair_sems,
):
    tiles, capacity, pairs, fields, cells_x, cells_y, width = dims
    half = fields // 2
    parts = cells_y // width
    steps = pairs // STEP_PAIRS

    scalar_copies = [
        pltpu.make_async_copy(ref, pair_s.at[pl.ds(i, 1), :], pair_sems.at[i])
        for i, ref in enumerate((src_ref, dev_ref))
    ]
    vector_copies = [
        pltpu.make_async_copy(ref, pair_v.at[i], pair_sems.at[2 + i])
        for i, ref in enumerate((dev_ref, blk_ref))
    ]
    field_copies = [
        pltpu.make_async_copy(
            state_ref.at[0, f, :, pl.ds(q * width, width)],
            cells.at[pl.ds((q * fields + f) * cells_x, cells_x), :],
            field_sems.at[f * parts + q],
        )
        for f in range(fields)
        for q in range(parts)
    ]

    def weight_copy(step):
        some = pl.ds(step * STEP_PAIRS, STEP_PAIRS)
        return pltpu.make_async_copy(
            weights_ref.at[0, some], w_ref.at[some], weight_sems.at[step]
        )

    for copy in scalar_copies + vector_copies + field_copies:
        copy.start()
    for step in range(steps):
        weight_copy(step).start()
    late_ref[...] = jnp.zeros_like(late_ref)
    for t in range(tiles):
        taken[t] = t * (capacity + 1)

    for copy in vector_copies:
        copy.wait()
    dev, blk = pair_v[0], pair_v[1]
    _, ids = slot_table(dev, blk, tiles, capacity)
    put_ids(late_ref, ids, tiles, capacity)
    code = (dev * (cells_x * parts) + blk).astype(jnp.float32)
    for i in range(pairs // width):
        place = (pairs + i // half, slice(i % half, i % half + 1), slice(None))
        early_ref[place] = code[:, i * width : (i + 1) * width]
    for copy in scalar_copies + field_copies:
        copy.wait()

    def cells_of(p):
        x, part = split(pair_s[0, p], parts)
        return cells[pl.ds(part * (fields * cells_x) + x, fields, stride=cells_x), :]

    def some_pairs(step, carry):
        weight_copy(step).wait()
        for i in range(0, STEP_PAIRS, 2):
            p = step * STEP_PAIRS + i
            left = jnp.concatenate([cells_of(p), cells_of(p + 1)], axis=0).astype(jnp.bfloat16)
            right = w_ref[pl.ds(p, 2)].reshape(2 * width, width)
            both = lax.dot_general(left, right, NT, preferred_element_type=jnp.float32)
            for j in range(2):
                tile = pair_s[1, p + j]
                slot = taken[tile]
                taken[tile] = slot + 1
                one = both[j * fields : (j + 1) * fields, j * width : (j + 1) * width]
                early_ref[p + j] = one[:half]
                late_ref[slot] = one[half:]
        return carry

    lax.fori_loop(0, steps, some_pairs, 0)


def contributions(state, pair_src, pair_dev, pair_blk, weights, tiles, capacity, fields):
    _, _, cells_x, cells_y = state.shape
    half = fields // 2
    pairs, width = weights.shape[1], weights.shape[2]
    rows = tiles * (capacity + 1)
    dims = (tiles, capacity, pairs, fields, cells_x, cells_y, width)
    parts = cells_y // width
    shapes = [(pairs + -(-pairs // (half * width)), half, width), (rows, half, width)]
    return pl.pallas_call(
        functools.partial(contribution_kernel, dims),
        in_specs=[pl.BlockSpec(memory_space=pltpu.HBM)] * 5,
        out_specs=[pl.BlockSpec(memory_space=pltpu.VMEM) for _ in shapes],
        out_shape=[jax.ShapeDtypeStruct(shape, jnp.float32) for shape in shapes],
        scratch_shapes=[
            pltpu.VMEM((parts * fields * cells_x, width), jnp.float32),
            pltpu.VMEM((pairs, width, width), jnp.bfloat16),
            pltpu.VMEM((2, 1, pairs), jnp.int32),
            pltpu.SMEM((2, pairs), jnp.int32),
            pltpu.SMEM((tiles,), jnp.int32),
            pltpu.SemaphoreType.DMA((parts * fields,)),
            pltpu.SemaphoreType.DMA((pairs // STEP_PAIRS,)),
            pltpu.SemaphoreType.DMA((4,)),
        ],
        compiler_params=pltpu.CompilerParams(vmem_limit_bytes=56 * 1024 * 1024),
        cost_estimate=pl.CostEstimate(
            flops=2 * pairs * fields * width * width,
            bytes_accessed=2 * pairs * width * width + 8 * rows * fields * width,
            transcendentals=0,
        ),
        name="contributions",
    )(pair_src, pair_dev.reshape(1, pairs), pair_blk, state, weights)


def place_kernel(dims, in_ref, out_ref, place_v, place_s, place_sem):
    tiles, capacity, pairs, blocks = dims
    half, width = in_ref.shape[1:]
    code = jnp.concatenate(
        [in_ref[pairs + i // half][i % half : i % half + 1] for i in range(pairs // width)], axis=1
    ).astype(jnp.int32)
    dev, blk = split(code, blocks)
    rank, ids = slot_table(dev, blk, tiles, capacity)
    place_v[...] = jnp.broadcast_to(dev * (capacity + 1) + rank, place_v.shape)
    copy = pltpu.make_async_copy(place_v, place_s, place_sem)
    copy.start()
    out_ref[...] = jnp.zeros_like(out_ref)
    put_ids(out_ref, ids, tiles, capacity)
    copy.wait()

    def some_rows(step, carry):
        for i in range(STEP_PAIRS):
            p = step * STEP_PAIRS + i
            out_ref[place_s[0, p]] = in_ref[p]
        return carry

    lax.fori_loop(0, pairs // STEP_PAIRS, some_rows, 0)


def placed_rows(rows, tiles, capacity, pairs, blocks):
    half, width = rows.shape[1:]
    shape = (tiles * (capacity + 1), half, width)
    return pl.pallas_call(
        functools.partial(place_kernel, (tiles, capacity, pairs, blocks)),
        out_shape=jax.ShapeDtypeStruct(shape, jnp.float32),
        scratch_shapes=[
            pltpu.VMEM((8, pairs), jnp.int32),
            pltpu.SMEM((8, pairs), jnp.int32),
            pltpu.SemaphoreType.DMA,
        ],
        compiler_params=pltpu.CompilerParams(vmem_limit_bytes=40 * 1024 * 1024),
        cost_estimate=pl.CostEstimate(
            flops=4 * rows.size, bytes_accessed=12 * rows.size, transcendentals=0
        ),
        name="place_in_slots",
    )(rows)


def sum_kernel(dims, in_ref, out_ref, top_ref, bottom_ref, left_ref, right_ref, pick, high, low):
    tiles, capacity, fields, cells_x, cells_y, width = dims
    parts = cells_y // width
    group = LANES // capacity
    stride = (capacity + 1) * fields
    block_of = lax.broadcasted_iota(jnp.int32, (cells_x * parts, LANES), 0)
    block_of = (block_of % cells_x) * parts + block_of // cells_x
    block_of = block_of.astype(jnp.float32)
    lane = lax.broadcasted_iota(jnp.int32, (1, LANES), 1)
    for k in range(tiles // group):
        columns = pl.ds(k * LANES, LANES)
        ids = None
        for i in range(group):
            source = k * group + i
            row = in_ref[pl.ds(source * stride + capacity * fields, 1), :]
            ids = row if ids is None else jnp.where(lane // capacity == i, row, ids)
            for f in range(fields):
                x = in_ref[pl.ds(source * stride + f, capacity, stride=fields), :]
                rounded = x.astype(jnp.bfloat16)
                place = (
                    pl.ds(source * capacity, capacity),
                    pl.ds(f * width, width),
                )
                high[place] = rounded
                low[place] = (x - rounded.astype(jnp.float32)).astype(jnp.bfloat16)
        pick[:, columns] = (block_of == ids).astype(jnp.bfloat16)
    for q in range(parts):
        chosen = pick[pl.ds(q * cells_x, cells_x), :]
        total = jnp.dot(chosen, high[...], preferred_element_type=jnp.float32)
        total = total + jnp.dot(chosen, low[...], preferred_element_type=jnp.float32)
        for f in range(fields):
            tile = total[:, f * width : (f + 1) * width]
            out_ref[f, :, pl.ds(q * width, width)] = tile
            top_ref[pl.ds(f, 1), pl.ds(q * width, width)] = tile[:1]
            bottom_ref[pl.ds(f, 1), pl.ds(q * width, width)] = tile[cells_x - 1 :]
            if q == 0:
                left_ref[pl.ds(f, 1), :] = tile.T[:1]
            if q == parts - 1:
                right_ref[pl.ds(f, 1), :] = tile.T[width - 1 :]


def summed(rows, tiles, capacity, fields, cells_x, cells_y, width):
    dims = (tiles, capacity, fields, cells_x, cells_y, width)
    slots = tiles * capacity
    blocks = cells_x * cells_y // width
    shapes = [
        (fields, cells_x, cells_y),
        (fields, cells_y),
        (fields, cells_y),
        (fields, cells_x),
        (fields, cells_x),
    ]
    return pl.pallas_call(
        functools.partial(sum_kernel, dims),
        out_shape=[jax.ShapeDtypeStruct(shape, jnp.float32) for shape in shapes],
        scratch_shapes=[
            pltpu.VMEM((blocks, slots), jnp.bfloat16),
            pltpu.VMEM((slots, fields * width), jnp.bfloat16),
            pltpu.VMEM((slots, fields * width), jnp.bfloat16),
        ],
        compiler_params=pltpu.CompilerParams(vmem_limit_bytes=40 * 1024 * 1024),
        cost_estimate=pl.CostEstimate(
            flops=4 * blocks * slots * fields * width,
            bytes_accessed=4 * fields * width * (slots + blocks),
            transcendentals=0,
        ),
        name="sum_by_block",
    )(rows.reshape(tiles * (capacity + 1) * fields, width))


def stencil_factors(coefs, keep):
    u, v, kappa = coefs
    return [
        keep,
        keep * (jnp.maximum(u, 0.0) + kappa),
        keep * (kappa - jnp.minimum(u, 0.0)),
        keep * (jnp.maximum(v, 0.0) + kappa),
        keep * (kappa - jnp.minimum(v, 0.0)),
        -keep * (jnp.abs(u) + jnp.abs(v) + 4.0 * kappa),
    ]


def tendency(s, rate, factors, top, bottom, left, right):
    cells_x, cells_y = s.shape
    x_of = lax.broadcasted_iota(jnp.int32, s.shape, 0)
    y_of = lax.broadcasted_iota(jnp.int32, s.shape, 1)
    out = (factors[5] - rate * factors[0]) * s
    out += factors[1] * jnp.where(x_of == 0, top, pltpu.roll(s, 1, 0))
    out += factors[2] * jnp.where(x_of == cells_x - 1, bottom, pltpu.roll(s, cells_x - 1, 0))
    out += factors[3] * jnp.where(y_of == 0, left, pltpu.roll(s, 1, 1))
    out += factors[4] * jnp.where(y_of == cells_y - 1, right, pltpu.roll(s, cells_y - 1, 1))
    return out


def columns_of(rows):
    spare = 8 - rows.shape[0]
    if spare:
        rows = jnp.concatenate([rows, jnp.zeros((spare, rows.shape[1]), rows.dtype)], axis=0)
    return rows.T


def line_count(nfield):
    return 2 * nfield + 8


def edge_kernel(mix_ref, state_tops, state_ends, state_lefts, state_rights, coefs_tops, coefs_ends,
                coefs_lefts, coefs_rights, land_tops, land_ends, land_lefts, land_rights,
                x_low, x_high, y_low, y_high):
    nfield = state_tops.shape[1]
    last_row, last_lane = state_tops.shape[2] - 1, state_lefts.shape[3] - 1
    atmos = mix_ref[0, 1] == 1.0

    def kept(land):
        return jnp.where(atmos, 1.0, land.astype(jnp.float32))

    for out, state, coefs, land, lines in (
        (x_low, state_tops, coefs_tops, land_tops, (0, 1)),
        (x_high, state_ends, coefs_ends, land_ends, (last_row - 1, last_row)),
    ):
        outer = lines[0] if lines[0] == 0 else lines[1]
        out[2 * nfield :, :] = jnp.zeros((8, out.shape[1]), jnp.float32)
        for j, line in enumerate(lines):
            for f in range(nfield):
                out[j * nfield + f : j * nfield + f + 1, :] = state[0, f, line : line + 1, :]
        for c in range(3):
            out[2 * nfield + c : 2 * nfield + c + 1, :] = coefs[0, c, outer : outer + 1, :]
        out[2 * nfield + 3 : 2 * nfield + 4, :] = kept(land[outer : outer + 1, :])

    for out, state, coefs, land, lines in (
        (y_low, state_lefts, coefs_lefts, land_lefts, (0, 1)),
        (y_high, state_rights, coefs_rights, land_rights, (last_lane - 1, last_lane)),
    ):
        outer = lines[0] if lines[0] == 0 else lines[1]
        lane = lax.broadcasted_iota(jnp.int32, land.shape, 1)
        packed = jnp.zeros(land.shape, jnp.float32)

        def put(packed, tile, at, to):
            moved = (to - at) % LANES
            tile = pltpu.roll(tile, moved, 1) if moved else tile
            return jnp.where(lane == to, tile, packed)

        for j, line in enumerate(lines):
            for f in range(nfield):
                packed = put(packed, state[0, f], line, j * nfield + f)
        for c in range(3):
            packed = put(packed, coefs[0, c], outer, 2 * nfield + c)
        packed = put(packed, kept(land[...]), outer, 2 * nfield + 3)
        out[...] = packed.T[: out.shape[0]]


def edges_of(state, coefs, land_sea, mix):
    _, nfield, cells_x, cells_y = state.shape
    lines = line_count(nfield)
    ends = [
        ((8, cells_y), (0, 0)),
        ((8, cells_y), (cells_x // 8 - 1, 0)),
        ((cells_x, LANES), (0, 0)),
        ((cells_x, LANES), (0, cells_y // LANES - 1)),
    ]
    at = lambda lead, place: lambda i: (0,) * len(lead) + place
    specs = [pl.BlockSpec(memory_space=pltpu.SMEM)]
    for lead in ((1, nfield), (1, 3), ()):
        specs += [pl.BlockSpec(lead + shape, at(lead, place)) for shape, place in ends]
    shapes = [(lines, cells_y)] * 2 + [(lines, cells_x)] * 2
    return pl.pallas_call(
        edge_kernel,
        grid=(1,),
        in_specs=specs,
        out_specs=[pl.BlockSpec(shape, lambda i: (0, 0)) for shape in shapes],
        out_shape=[jax.ShapeDtypeStruct(shape, jnp.float32) for shape in shapes],
        compiler_params=pltpu.CompilerParams(vmem_limit_bytes=40 * 1024 * 1024),
        cost_estimate=pl.CostEstimate(
            flops=state.size, bytes_accessed=4 * 1024 * 1024, transcendentals=0
        ),
        name="edges",
    )(mix, *[state] * 4, *[coefs] * 4, *[land_sea] * 4)


def outer_section(center, across, along, factors, rate):
    lane = lax.broadcasted_iota(jnp.int32, center.shape, 1)
    count = center.shape[1]
    before = jnp.where(lane == 0, along[0], pltpu.roll(center, 1, 1))
    after = jnp.where(lane == count - 1, along[1], pltpu.roll(center, count - 1, 1))
    keep, low, high, back, ahead, middle = factors
    out = center + low * across[0] + high * across[1] + back * before + ahead * after
    return out + (middle - rate * keep) * center


def base_kernel(rate_ref, mix_ref, rates_ref, coefs_ref, land_ref, x_low, x_high, y_low, y_high,
                above, below, left, right, corners_left, corners_right, state_ref,
                out_ref, factors, rows, cols):
    f = pl.program_id(0)
    nfield = rates_ref.shape[0]
    lines = line_count(nfield)

    @pl.when(f == 0)
    def _():
        keep = jnp.where(mix_ref[0, 1] == 1.0, 1.0, land_ref[...].astype(jnp.float32))
        for i, factor in enumerate(stencil_factors([coefs_ref[0, c] for c in range(3)], keep)):
            factors[i] = factor
        rate = rates_ref[:, 0:1]
        near, far = pl.ds(0, nfield), pl.ds(nfield, nfield)
        last = corners_left.shape[1] - 1
        corner = (
            (corners_left[nfield : 2 * nfield, last:], corners_left[lines : lines + nfield, last:]),
            (corners_right[nfield : 2 * nfield, 0:1], corners_right[lines : lines + nfield, 0:1]),
        )
        for i, (ref, center, across, along, is_column) in enumerate(
            (
                (above, above[far, :], (above[near, :], x_low[near, :]), (corner[0][0], corner[1][0]), False),
                (below, below[near, :], (x_high[far, :], below[far, :]), (corner[0][1], corner[1][1]), False),
                (left, left[far, :], (left[near, :], y_low[near, :]), corner[0], True),
                (right, right[near, :], (y_high[far, :], right[far, :]), corner[1], True),
            )
        ):
            first = 2 * nfield
            of_line = stencil_factors(
                [ref[first + c : first + c + 1, :] for c in range(3)],
                ref[first + 3 : first + 4, :],
            )
            if is_column:
                of_line = [of_line[j] for j in (0, 3, 4, 1, 2, 5)]
            section = outer_section(center, across, along, of_line, rate)
            kept = cols if is_column else rows
            kept[pl.ds(i % 2 * nfield, nfield), :] = center
            kept[pl.ds((2 + i % 2) * nfield, nfield), :] = section

    rate = rate_ref[0, f]
    mix_a, mix_b = mix_ref[0, 0], mix_ref[0, 1]
    s = state_ref[0, 0]
    row = [rows[pl.ds(i * nfield + f, 1), :] for i in range(4)]
    col = columns_of(
        jnp.concatenate([cols[pl.ds(i * nfield + f, 1), :] for i in range(4)], axis=0)
    )
    s1 = s + tendency(s, rate, factors, row[0], row[1], col[:, 0:1], col[:, 1:2])
    more = tendency(s1, rate, factors, row[2], row[3], col[:, 2:3], col[:, 3:4])
    out_ref[0, 0] = mix_a * s + (1.0 - mix_a) * s1 + mix_b * more


def base_of(state, coefs, land_sea, rates, mix, edges, received, corners):
    _, nfield, cells_x, cells_y = state.shape
    field = pl.BlockSpec((1, 1, cells_x, cells_y), lambda f: (0, f, 0, 0))
    whole = lambda a: pl.BlockSpec(a.shape, lambda f: (0,) * a.ndim)
    rates_wide = jnp.broadcast_to(rates.T, (nfield, LANES))
    operands = [rates_wide, coefs, land_sea, *edges, *received, *corners]
    return pl.pallas_call(
        base_kernel,
        grid=(nfield,),
        in_specs=[
            pl.BlockSpec(memory_space=pltpu.SMEM),
            pl.BlockSpec(memory_space=pltpu.SMEM),
            *[whole(a) for a in operands],
            field,
        ],
        out_specs=[field, pl.BlockSpec((6, cells_x, cells_y), lambda f: (0, 0, 0))],
        out_shape=[
            jax.ShapeDtypeStruct(state.shape, jnp.float32),
            jax.ShapeDtypeStruct((6, cells_x, cells_y), jnp.float32),
        ],
        scratch_shapes=[
            pltpu.VMEM((4 * nfield, cells_y), jnp.float32),
            pltpu.VMEM((4 * nfield, cells_x), jnp.float32),
        ],
        compiler_params=pltpu.CompilerParams(vmem_limit_bytes=40 * 1024 * 1024),
        cost_estimate=pl.CostEstimate(
            flops=40 * state.size, bytes_accessed=8 * state.size, transcendentals=0
        ),
        name="base",
    )(rates, mix, *operands, state)


def finish_kernel(
    half, gamma_ref, mix_ref, factors, above, below, before, after, base_ref, early_ref, late_ref, *rest
):
    early_rims, late_rims = rest[:4], rest[4:8]
    new_ref, out_ref, wide, cols = rest[8:]
    f = pl.program_id(0)
    rate = gamma_ref[0, f]
    mix_b = mix_ref[0, 1]
    cells_x, cells_y = base_ref.shape[2:]
    keep_row = above.shape[0] - 5
    keep = slice(keep_row, keep_row + 1)

    def widen(recv_ref, rims, f):
        top, bottom, left, right = (rim[pl.ds(f, 1), :] for rim in rims)
        wide[STRIP - 1 : STRIP, :] = above[keep, :] * top * rate
        wide[STRIP + cells_x : STRIP + cells_x + 1, :] = below[keep, :] * bottom * rate
        sides = [before[keep, :] * left * rate, after[keep, :] * right * rate]
        cols[...] = columns_of(jnp.concatenate(sides, axis=0))
        for i in range(0, cells_x, STRIP):
            recv = recv_ref[0, i : i + STRIP, :]
            out_ref[0, 0, i : i + STRIP, :] = recv
            wide[STRIP + i : 2 * STRIP + i, :] = factors[0, i : i + STRIP, :] * recv * rate

    @pl.when(f < half)
    def _():
        widen(early_ref, early_rims, f)

    @pl.when(f >= half)
    def _():
        widen(late_ref, late_rims, f - half)

    lane = lax.broadcasted_iota(jnp.int32, (STRIP, cells_y), 1)
    for i in range(0, cells_x, STRIP):
        rows = slice(i, i + STRIP)
        mid = wide[STRIP + i : 2 * STRIP + i, :]
        more = (factors[5, rows, :] - rate * factors[0, rows, :]) * mid
        more += factors[1, rows, :] * wide[STRIP + i - 1 : 2 * STRIP + i - 1, :]
        more += factors[2, rows, :] * wide[STRIP + i + 1 : 2 * STRIP + i + 1, :]
        prior = jnp.where(lane == 0, cols[rows, 0:1], pltpu.roll(mid, 1, 1))
        later = jnp.where(lane == cells_y - 1, cols[rows, 1:2], pltpu.roll(mid, cells_y - 1, 1))
        more += factors[3, rows, :] * prior + factors[4, rows, :] * later
        new_ref[0, 0, rows, :] = base_ref[0, 0, rows, :] + mix_b * (2.0 * mid + more)


def finished(base, early, early_rims, late, late_rims, gamma, mix, factors, received):
    half, cells_x, cells_y = early.shape
    whole = lambda a: pl.BlockSpec(a.shape, lambda f: (0,) * a.ndim)
    field = pl.BlockSpec((1, 1, cells_x, cells_y), lambda f: (0, f, 0, 0))
    recv = lambda at: pl.BlockSpec((1, cells_x, cells_y), lambda f: (at(f), 0, 0))
    return pl.pallas_call(
        functools.partial(finish_kernel, half),
        grid=(2 * half,),
        in_specs=[
            pl.BlockSpec(memory_space=pltpu.SMEM),
            pl.BlockSpec(memory_space=pltpu.SMEM),
            whole(factors),
            *[whole(lines) for lines in received],
            field,
            recv(lambda f: jnp.minimum(f, half - 1)),
            recv(lambda f: jnp.maximum(f - half, 0)),
            *[whole(rim) for rim in (*early_rims, *late_rims)],
        ],
        out_specs=[field, field],
        out_shape=[
            jax.ShapeDtypeStruct(base.shape, jnp.float32),
            jax.ShapeDtypeStruct((1, 2 * half, cells_x, cells_y), jnp.float32),
        ],
        input_output_aliases={7: 0},
        scratch_shapes=[
            pltpu.VMEM((cells_x + 2 * STRIP, cells_y), jnp.float32),
            pltpu.VMEM((cells_x, 8), jnp.float32),
        ],
        compiler_params=pltpu.CompilerParams(vmem_limit_bytes=40 * 1024 * 1024),
        cost_estimate=pl.CostEstimate(
            flops=40 * early.size, bytes_accessed=40 * early.size, transcendentals=0
        ),
        name="finish",
    )(gamma, mix, factors, *received, base, early, late, *early_rims, *late_rims)


def body(state, coefs, land_sea, gamma, pair_src, pair_dev, pair_blk, weights):
    tx, ty = lax.axis_size("tx"), lax.axis_size("ty")
    tiles = tx * ty
    nfield, cells_x, cells_y = state.shape[1:]
    chan = gamma.shape[1]
    pairs, width = weights.shape[1], weights.shape[2]
    capacity = max(2, 2 * pairs // tiles)
    half = chan // 2
    early, late = contributions(
        state, pair_src, pair_dev, pair_blk, weights, tiles, capacity, chan
    )
    swap = [(0, 1), (1, 0)]

    def exchanged(rows):
        rows = rows.reshape(tiles, capacity + 1, rows.shape[1], width)
        return lax.all_to_all(rows, ("tx", "ty"), split_axis=0, concat_axis=0, tiled=True)

    def add_up(rows):
        return summed(rows, tiles, capacity, half, cells_x, cells_y, width)

    late_in = exchanged(late)
    early = lax.ppermute(early, "comp", swap)
    early_in = placed_rows(early, tiles, capacity, pairs, cells_x * cells_y // width)

    land_after, _ = lax.optimization_barrier((land_sea, late))
    is_atmos = lax.axis_index("comp") == 0
    mix = jnp.where(is_atmos, jnp.array([[0.0, 1.0]]), jnp.array([[0.5, 0.5]]))
    mix = mix.astype(jnp.float32)
    rates = jnp.concatenate([gamma, jnp.zeros((1, nfield - chan), jnp.float32)], axis=1)
    x_low, x_high, y_low, y_high = edges_of(state, coefs, land_after, mix)
    left = lax.ppermute(y_high, "ty", shift_pairs(ty, 1))
    right = lax.ppermute(y_low, "ty", shift_pairs(ty, -1))
    above = lax.ppermute(x_high, "tx", shift_pairs(tx, 1))
    below = lax.ppermute(x_low, "tx", shift_pairs(tx, -1))
    early_in, above, below, left, right = lax.optimization_barrier(
        (early_in, above, below, left, right)
    )
    received = (above, below, left, right)
    early_in = exchanged(early_in)

    ends = jnp.concatenate([above[:, cells_y - LANES :], below[:, cells_y - LANES :]], axis=0)
    starts = jnp.concatenate([above[:, :LANES], below[:, :LANES]], axis=0)
    corners_left = lax.ppermute(ends, "ty", shift_pairs(ty, 1))
    corners_right = lax.ppermute(starts, "ty", shift_pairs(ty, -1))
    base, factors = base_of(
        state, coefs, land_after, rates, mix, (x_low, x_high, y_low, y_high), received,
        (corners_left, corners_right),
    )

    recv_late, top, bottom, left, right = add_up(late_in)
    recv_late = lax.ppermute(recv_late, "comp", swap)
    rims_late = (
        lax.ppermute(bottom, ("comp", "tx"), crossed("tx", 1)),
        lax.ppermute(top, ("comp", "tx"), crossed("tx", -1)),
        lax.ppermute(right, ("comp", "ty"), crossed("ty", 1)),
        lax.ppermute(left, ("comp", "ty"), crossed("ty", -1)),
    )
    early_in, factors = lax.optimization_barrier((early_in, factors))
    recv_early, top, bottom, left, right = add_up(early_in)
    rims_early = (
        lax.ppermute(bottom, "tx", shift_pairs(tx, 1)),
        lax.ppermute(top, "tx", shift_pairs(tx, -1)),
        lax.ppermute(right, "ty", shift_pairs(ty, 1)),
        lax.ppermute(left, "ty", shift_pairs(ty, -1)),
    )
    return finished(
        base, recv_early, rims_early, recv_late, rims_late, gamma, mix, factors, received
    )


def solution(mesh):
    placed = (
        P("comp", None, "tx", "ty"),
        P("comp", None, "tx", "ty"),
        P("tx", "ty"),
        P("comp", None),
        P("comp", ("tx", "ty")),
        P("comp", ("tx", "ty"), None),
        P("comp", ("tx", "ty")),
        P("comp", ("tx", "ty"), None, None),
    )
    return jax.shard_map(
        body,
        mesh=mesh,
        in_specs=placed,
        out_specs=(P("comp", None, "tx", "ty"), P("comp", None, "tx", "ty")),
        check_vma=False,
    )
```

```python
import functools

import jax
import jax.numpy as jnp
from jax import lax
from jax.experimental import pallas as pl
from jax.experimental.pallas import tpu as pltpu
from jax.sharding import PartitionSpec as P

LANES = 128
STEP_PAIRS = 64
STRIP = 8
NT = (((1,), (1,)), ((), ()))


def shift_pairs(count, by):
    return [(i, i + by) for i in range(count) if 0 <= i + by < count]


def crossed(axis, by):
    count = lax.axis_size(axis)
    return [
        (c * count + i, (1 - c) * count + j) for c in range(2) for i, j in shift_pairs(count, by)
    ]


def split(value, parts):
    if parts & (parts - 1) == 0:
        return lax.shift_right_logical(value, parts.bit_length() - 1), value & (parts - 1)
    return lax.div(value, parts), lax.rem(value, parts)


def slot_table(dev, blk, tiles, capacity):
    pairs = dev.shape[1]
    tile_of = lax.broadcasted_iota(jnp.int32, (tiles, pairs), 0)
    lane_of = lax.broadcasted_iota(jnp.int32, (tiles, pairs), 1)
    member = (tile_of == dev).astype(jnp.float32)
    total = member
    shift = 1
    while shift < pairs:
        total = total + jnp.where(lane_of >= shift, pltpu.roll(total, shift, 1), 0.0)
        shift *= 2
    rank = (jnp.sum(member * total, axis=0, keepdims=True) - 1.0).astype(jnp.int32)
    slot_of = lax.broadcasted_iota(jnp.int32, (LANES, pairs), 0) % capacity
    chosen = (slot_of == rank).astype(jnp.bfloat16)

    def spread(values):
        return lax.dot_general(
            (member * values).astype(jnp.bfloat16), chosen, NT, preferred_element_type=jnp.float32
        )

    high, low = split(blk, 256)
    ids = spread(high.astype(jnp.float32)) * 256.0 + spread(low.astype(jnp.float32))
    return rank, jnp.where(spread(jnp.ones(dev.shape, jnp.float32)) > 0.5, ids, -1.0)


def put_ids(out, ids, tiles, capacity):
    for t in range(tiles):
        out[t * (capacity + 1) + capacity] = jnp.broadcast_to(ids[t : t + 1, :], out.shape[1:])


def contribution_kernel(
    dims, src_ref, dev_ref, blk_ref, state_ref, weights_ref, early_ref, late_ref,
    cells, w_ref, pair_v, pair_s, taken, field_sems, weight_sems, pair_sems,
):
    tiles, capacity, pairs, fields, cells_x, cells_y, width = dims
    half = fields // 2
    parts = cells_y // width
    steps = pairs // STEP_PAIRS

    scalar_copies = [
        pltpu.make_async_copy(ref, pair_s.at[pl.ds(i, 1), :], pair_sems.at[i])
        for i, ref in enumerate((src_ref, dev_ref))
    ]
    vector_copies = [
        pltpu.make_async_copy(ref, pair_v.at[i], pair_sems.at[2 + i])
        for i, ref in enumerate((dev_ref, blk_ref))
    ]
    field_copies = [
        pltpu.make_async_copy(
            state_ref.at[0, f, :, pl.ds(q * width, width)],
            cells.at[q, :, f, :],
            field_sems.at[f * parts + q],
        )
        for f in range(fields)
        for q in range(parts)
    ]

    def weight_copy(step):
        some = pl.ds(step * STEP_PAIRS, STEP_PAIRS)
        return pltpu.make_async_copy(
            weights_ref.at[0, some], w_ref.at[some], weight_sems.at[step]
        )

    for copy in scalar_copies + vector_copies + field_copies:
        copy.start()
    for step in range(steps):
        weight_copy(step).start()
    late_ref[...] = jnp.zeros_like(late_ref)
    for t in range(tiles):
        taken[t] = t * (capacity + 1)

    for copy in vector_copies:
        copy.wait()
    dev, blk = pair_v[0], pair_v[1]
    _, ids = slot_table(dev, blk, tiles, capacity)
    put_ids(late_ref, ids, tiles, capacity)
    code = (dev * (cells_x * parts) + blk).astype(jnp.float32)
    for i in range(pairs // width):
        place = (pairs + i // half, slice(i % half, i % half + 1), slice(None))
        early_ref[place] = code[:, i * width : (i + 1) * width]
    for copy in scalar_copies + field_copies:
        copy.wait()

    def cells_of(p):
        x, part = split(pair_s[0, p], parts)
        return cells[part, x]

    zeros = jnp.zeros((fields, width), jnp.float32)

    def some_pairs(step, carry):
        weight_copy(step).wait()
        for i in range(0, STEP_PAIRS, 4):
            p = step * STEP_PAIRS + i
            left = [
                jnp.concatenate([cells_of(p + j), zeros][:: 1 - j % 2 * 2], axis=1) for j in range(4)
            ]
            left = jnp.concatenate(left, axis=0).astype(jnp.bfloat16)
            w = [w_ref[p + j] for j in range(4)]
            right = jnp.concatenate(
                [jnp.concatenate(w[:2], axis=1), jnp.concatenate(w[2:], axis=1)], axis=0
            )
            four = lax.dot_general(left, right, NT, preferred_element_type=jnp.float32)
            for j in range(4):
                tile = pair_s[1, p + j]
                slot = taken[tile]
                taken[tile] = slot + 1
                at = j // 2 * width
                one = four[j * fields : (j + 1) * fields, at : at + width]
                early_ref[p + j] = one[:half]
                late_ref[slot] = one[half:]
        return carry

    lax.fori_loop(0, steps, some_pairs, 0)


def contributions(state, pair_src, pair_dev, pair_blk, weights, tiles, capacity, fields):
    _, _, cells_x, cells_y = state.shape
    half = fields // 2
    pairs, width = weights.shape[1], weights.shape[2]
    rows = tiles * (capacity + 1)
    dims = (tiles, capacity, pairs, fields, cells_x, cells_y, width)
    parts = cells_y // width
    shapes = [(pairs + -(-pairs // (half * width)), half, width), (rows, half, width)]
    return pl.pallas_call(
        functools.partial(contribution_kernel, dims),
        in_specs=[pl.BlockSpec(memory_space=pltpu.HBM)] * 5,
        out_specs=[pl.BlockSpec(memory_space=pltpu.VMEM) for _ in shapes],
        out_shape=[jax.ShapeDtypeStruct(shape, jnp.float32) for shape in shapes],
        scratch_shapes=[
            pltpu.VMEM((parts, cells_x, fields, width), jnp.float32),
            pltpu.VMEM((pairs, width, width), jnp.bfloat16),
            pltpu.VMEM((2, 1, pairs), jnp.int32),
            pltpu.SMEM((2, pairs), jnp.int32),
            pltpu.SMEM((tiles,), jnp.int32),
            pltpu.SemaphoreType.DMA((parts * fields,)),
            pltpu.SemaphoreType.DMA((pairs // STEP_PAIRS,)),
            pltpu.SemaphoreType.DMA((4,)),
        ],
        compiler_params=pltpu.CompilerParams(vmem_limit_bytes=56 * 1024 * 1024),
        cost_estimate=pl.CostEstimate(
            flops=2 * pairs * fields * width * width,
            bytes_accessed=2 * pairs * width * width + 8 * rows * fields * width,
            transcendentals=0,
        ),
        name="contributions",
    )(pair_src, pair_dev.reshape(1, pairs), pair_blk, state, weights)


def place_kernel(dims, in_ref, out_ref, place_v, place_s, place_sem):
    tiles, capacity, pairs, blocks = dims
    half, width = in_ref.shape[1:]
    code = jnp.concatenate(
        [in_ref[pairs + i // half][i % half : i % half + 1] for i in range(pairs // width)], axis=1
    ).astype(jnp.int32)
    dev, blk = split(code, blocks)
    rank, ids = slot_table(dev, blk, tiles, capacity)
    place_v[...] = jnp.broadcast_to(dev * (capacity + 1) + rank, place_v.shape)
    copy = pltpu.make_async_copy(place_v, place_s, place_sem)
    copy.start()
    out_ref[...] = jnp.zeros_like(out_ref)
    put_ids(out_ref, ids, tiles, capacity)
    copy.wait()

    def some_rows(step, carry):
        for i in range(STEP_PAIRS):
            p = step * STEP_PAIRS + i
            out_ref[place_s[0, p]] = in_ref[p]
        return carry

    lax.fori_loop(0, pairs // STEP_PAIRS, some_rows, 0)


def placed_rows(rows, tiles, capacity, pairs, blocks):
    half, width = rows.shape[1:]
    shape = (tiles * (capacity + 1), half, width)
    return pl.pallas_call(
        functools.partial(place_kernel, (tiles, capacity, pairs, blocks)),
        out_shape=jax.ShapeDtypeStruct(shape, jnp.float32),
        scratch_shapes=[
            pltpu.VMEM((8, pairs), jnp.int32),
            pltpu.SMEM((8, pairs), jnp.int32),
            pltpu.SemaphoreType.DMA,
        ],
        compiler_params=pltpu.CompilerParams(vmem_limit_bytes=16 * 1024 * 1024),
        cost_estimate=pl.CostEstimate(
            flops=4 * rows.size, bytes_accessed=12 * rows.size, transcendentals=0
        ),
        name="place_in_slots",
    )(rows)


def sum_kernel(dims, in_ref, out_ref, top_ref, bottom_ref, left_ref, right_ref, pick, high, low):
    tiles, capacity, fields, cells_x, cells_y, width = dims
    parts = cells_y // width
    group = LANES // capacity
    stride = (capacity + 1) * fields
    block_of = lax.broadcasted_iota(jnp.int32, (cells_x * parts, LANES), 0)
    block_of = (block_of % cells_x) * parts + block_of // cells_x
    block_of = block_of.astype(jnp.float32)
    lane = lax.broadcasted_iota(jnp.int32, (1, LANES), 1)
    for k in range(tiles // group):
        columns = pl.ds(k * LANES, LANES)
        ids = None
        for i in range(group):
            source = k * group + i
            row = in_ref[pl.ds(source * stride + capacity * fields, 1), :]
            ids = row if ids is None else jnp.where(lane // capacity == i, row, ids)
            for f in range(fields):
                x = in_ref[pl.ds(source * stride + f, capacity, stride=fields), :]
                rounded = x.astype(jnp.bfloat16)
                place = (
                    pl.ds(source * capacity, capacity),
                    pl.ds(f * width, width),
                )
                high[place] = rounded
                low[place] = (x - rounded.astype(jnp.float32)).astype(jnp.bfloat16)
        pick[:, columns] = (block_of == ids).astype(jnp.bfloat16)
    for q in range(parts):
        chosen = pick[pl.ds(q * cells_x, cells_x), :]
        total = jnp.dot(chosen, high[...], preferred_element_type=jnp.float32)
        total = total + jnp.dot(chosen, low[...], preferred_element_type=jnp.float32)
        for f in range(fields):
            tile = total[:, f * width : (f + 1) * width]
            out_ref[f, :, pl.ds(q * width, width)] = tile
            top_ref[pl.ds(f, 1), pl.ds(q * width, width)] = tile[:1]
            bottom_ref[pl.ds(f, 1), pl.ds(q * width, width)] = tile[cells_x - 1 :]
            if q == 0:
                left_ref[pl.ds(f, 1), :] = tile.T[:1]
            if q == parts - 1:
                right_ref[pl.ds(f, 1), :] = tile.T[width - 1 :]


def summed(rows, tiles, capacity, fields, cells_x, cells_y, width, grant):
    dims = (tiles, capacity, fields, cells_x, cells_y, width)
    slots = tiles * capacity
    blocks = cells_x * cells_y // width
    shapes = [
        (fields, cells_x, cells_y),
        (fields, cells_y),
        (fields, cells_y),
        (fields, cells_x),
        (fields, cells_x),
    ]
    return pl.pallas_call(
        functools.partial(sum_kernel, dims),
        out_shape=[jax.ShapeDtypeStruct(shape, jnp.float32) for shape in shapes],
        scratch_shapes=[
            pltpu.VMEM((blocks, slots), jnp.bfloat16),
            pltpu.VMEM((slots, fields * width), jnp.bfloat16),
            pltpu.VMEM((slots, fields * width), jnp.bfloat16),
        ],
        compiler_params=pltpu.CompilerParams(vmem_limit_bytes=grant * 1024 * 1024),
        cost_estimate=pl.CostEstimate(
            flops=4 * blocks * slots * fields * width,
            bytes_accessed=4 * fields * width * (slots + blocks),
            transcendentals=0,
        ),
        name="sum_by_block",
    )(rows.reshape(tiles * (capacity + 1) * fields, width))


def stencil_factors(coefs, keep):
    u, v, kappa = coefs
    return [
        keep,
        keep * (jnp.maximum(u, 0.0) + kappa),
        keep * (kappa - jnp.minimum(u, 0.0)),
        keep * (jnp.maximum(v, 0.0) + kappa),
        keep * (kappa - jnp.minimum(v, 0.0)),
        -keep * (jnp.abs(u) + jnp.abs(v) + 4.0 * kappa),
    ]


def tendency(s, rate, factors, top, bottom, left, right):
    cells_x, cells_y = s.shape
    x_of = lax.broadcasted_iota(jnp.int32, s.shape, 0)
    y_of = lax.broadcasted_iota(jnp.int32, s.shape, 1)
    out = (factors[5] - rate * factors[0]) * s
    out += factors[1] * jnp.where(x_of == 0, top, pltpu.roll(s, 1, 0))
    out += factors[2] * jnp.where(x_of == cells_x - 1, bottom, pltpu.roll(s, cells_x - 1, 0))
    out += factors[3] * jnp.where(y_of == 0, left, pltpu.roll(s, 1, 1))
    out += factors[4] * jnp.where(y_of == cells_y - 1, right, pltpu.roll(s, cells_y - 1, 1))
    return out


def columns_of(rows):
    spare = 8 - rows.shape[0]
    if spare:
        rows = jnp.concatenate([rows, jnp.zeros((spare, rows.shape[1]), rows.dtype)], axis=0)
    return rows.T


def line_count(nfield):
    return 2 * nfield + 8


def edge_kernel(mix_ref, state_tops, state_ends, state_lefts, state_rights, coefs_tops, coefs_ends,
                coefs_lefts, coefs_rights, land_tops, land_ends, land_lefts, land_rights,
                x_low, x_high, y_low, y_high):
    nfield = state_tops.shape[1]
    last_row, last_lane = state_tops.shape[2] - 1, state_lefts.shape[3] - 1
    atmos = mix_ref[0, 1] == 1.0

    def kept(land):
        return jnp.where(atmos, 1.0, land.astype(jnp.float32))

    for out, state, coefs, land, lines in (
        (x_low, state_tops, coefs_tops, land_tops, (0, 1)),
        (x_high, state_ends, coefs_ends, land_ends, (last_row - 1, last_row)),
    ):
        outer = lines[0] if lines[0] == 0 else lines[1]
        out[2 * nfield :, :] = jnp.zeros((8, out.shape[1]), jnp.float32)
        for j, line in enumerate(lines):
            for f in range(nfield):
                out[j * nfield + f : j * nfield + f + 1, :] = state[0, f, line : line + 1, :]
        for c in range(3):
            out[2 * nfield + c : 2 * nfield + c + 1, :] = coefs[0, c, outer : outer + 1, :]
        out[2 * nfield + 3 : 2 * nfield + 4, :] = kept(land[outer : outer + 1, :])

    for out, state, coefs, land, lines in (
        (y_low, state_lefts, coefs_lefts, land_lefts, (0, 1)),
        (y_high, state_rights, coefs_rights, land_rights, (last_lane - 1, last_lane)),
    ):
        outer = lines[0] if lines[0] == 0 else lines[1]
        lane = lax.broadcasted_iota(jnp.int32, land.shape, 1)
        packed = jnp.zeros(land.shape, jnp.float32)

        def put(packed, tile, at, to):
            moved = (to - at) % LANES
            tile = pltpu.roll(tile, moved, 1) if moved else tile
            return jnp.where(lane == to, tile, packed)

        for j, line in enumerate(lines):
            for f in range(nfield):
                packed = put(packed, state[0, f], line, j * nfield + f)
        for c in range(3):
            packed = put(packed, coefs[0, c], outer, 2 * nfield + c)
        packed = put(packed, kept(land[...]), outer, 2 * nfield + 3)
        out[...] = packed.T[: out.shape[0]]


def edges_of(state, coefs, land_sea, mix):
    _, nfield, cells_x, cells_y = state.shape
    lines = line_count(nfield)
    ends = [
        ((8, cells_y), (0, 0)),
        ((8, cells_y), (cells_x // 8 - 1, 0)),
        ((cells_x, LANES), (0, 0)),
        ((cells_x, LANES), (0, cells_y // LANES - 1)),
    ]
    at = lambda lead, place: lambda i: (0,) * len(lead) + place
    specs = [pl.BlockSpec(memory_space=pltpu.SMEM)]
    for lead in ((1, nfield), (1, 3), ()):
        specs += [pl.BlockSpec(lead + shape, at(lead, place)) for shape, place in ends]
    shapes = [(lines, cells_y)] * 2 + [(lines, cells_x)] * 2
    return pl.pallas_call(
        edge_kernel,
        grid=(1,),
        in_specs=specs,
        out_specs=[pl.BlockSpec(shape, lambda i: (0, 0)) for shape in shapes],
        out_shape=[jax.ShapeDtypeStruct(shape, jnp.float32) for shape in shapes],
        compiler_params=pltpu.CompilerParams(vmem_limit_bytes=40 * 1024 * 1024),
        cost_estimate=pl.CostEstimate(
            flops=state.size, bytes_accessed=4 * 1024 * 1024, transcendentals=0
        ),
        name="edges",
    )(mix, *[state] * 4, *[coefs] * 4, *[land_sea] * 4)


def outer_section(center, across, along, factors, rate):
    lane = lax.broadcasted_iota(jnp.int32, center.shape, 1)
    count = center.shape[1]
    before = jnp.where(lane == 0, along[0], pltpu.roll(center, 1, 1))
    after = jnp.where(lane == count - 1, along[1], pltpu.roll(center, count - 1, 1))
    keep, low, high, back, ahead, middle = factors
    out = center + low * across[0] + high * across[1] + back * before + ahead * after
    return out + (middle - rate * keep) * center


def base_kernel(rate_ref, mix_ref, rates_ref, coefs_ref, land_ref, x_low, x_high, y_low, y_high,
                above, below, left, right, corners_left, corners_right, state_ref,
                out_ref, factors, rows, cols):
    f = pl.program_id(0)
    nfield = rates_ref.shape[0]
    lines = line_count(nfield)

    @pl.when(f == 0)
    def _():
        keep = jnp.where(mix_ref[0, 1] == 1.0, 1.0, land_ref[...].astype(jnp.float32))
        for i, factor in enumerate(stencil_factors([coefs_ref[0, c] for c in range(3)], keep)):
            factors[i] = factor
        rate = rates_ref[:, 0:1]
        near, far = pl.ds(0, nfield), pl.ds(nfield, nfield)
        last = corners_left.shape[1] - 1
        corner = (
            (corners_left[nfield : 2 * nfield, last:], corners_left[lines : lines + nfield, last:]),
            (corners_right[nfield : 2 * nfield, 0:1], corners_right[lines : lines + nfield, 0:1]),
        )
        for i, (ref, center, across, along, is_column) in enumerate(
            (
                (above, above[far, :], (above[near, :], x_low[near, :]), (corner[0][0], corner[1][0]), False),
                (below, below[near, :], (x_high[far, :], below[far, :]), (corner[0][1], corner[1][1]), False),
                (left, left[far, :], (left[near, :], y_low[near, :]), corner[0], True),
                (right, right[near, :], (y_high[far, :], right[far, :]), corner[1], True),
            )
        ):
            first = 2 * nfield
            of_line = stencil_factors(
                [ref[first + c : first + c + 1, :] for c in range(3)],
                ref[first + 3 : first + 4, :],
            )
            if is_column:
                of_line = [of_line[j] for j in (0, 3, 4, 1, 2, 5)]
            section = outer_section(center, across, along, of_line, rate)
            kept = cols if is_column else rows
            kept[pl.ds(i % 2 * nfield, nfield), :] = center
            kept[pl.ds((2 + i % 2) * nfield, nfield), :] = section

    rate = rate_ref[0, f]
    mix_a, mix_b = mix_ref[0, 0], mix_ref[0, 1]
    s = state_ref[0, 0]
    row = [rows[pl.ds(i * nfield + f, 1), :] for i in range(4)]
    col = columns_of(
        jnp.concatenate([cols[pl.ds(i * nfield + f, 1), :] for i in range(4)], axis=0)
    )
    s1 = s + tendency(s, rate, factors, row[0], row[1], col[:, 0:1], col[:, 1:2])
    more = tendency(s1, rate, factors, row[2], row[3], col[:, 2:3], col[:, 3:4])
    out_ref[0, 0] = mix_a * s + (1.0 - mix_a) * s1 + mix_b * more


def base_of(state, coefs, land_sea, rates, mix, edges, received, corners):
    _, nfield, cells_x, cells_y = state.shape
    field = pl.BlockSpec((1, 1, cells_x, cells_y), lambda f: (0, f, 0, 0))
    whole = lambda a: pl.BlockSpec(a.shape, lambda f: (0,) * a.ndim)
    rates_wide = jnp.broadcast_to(rates.T, (nfield, LANES))
    operands = [rates_wide, coefs, land_sea, *edges, *received, *corners]
    return pl.pallas_call(
        base_kernel,
        grid=(nfield,),
        in_specs=[
            pl.BlockSpec(memory_space=pltpu.SMEM),
            pl.BlockSpec(memory_space=pltpu.SMEM),
            *[whole(a) for a in operands],
            field,
        ],
        out_specs=[field, pl.BlockSpec((6, cells_x, cells_y), lambda f: (0, 0, 0))],
        out_shape=[
            jax.ShapeDtypeStruct(state.shape, jnp.float32),
            jax.ShapeDtypeStruct((6, cells_x, cells_y), jnp.float32),
        ],
        scratch_shapes=[
            pltpu.VMEM((4 * nfield, cells_y), jnp.float32),
            pltpu.VMEM((4 * nfield, cells_x), jnp.float32),
        ],
        compiler_params=pltpu.CompilerParams(vmem_limit_bytes=24 * 1024 * 1024),
        cost_estimate=pl.CostEstimate(
            flops=40 * state.size, bytes_accessed=8 * state.size, transcendentals=0
        ),
        name="base",
    )(rates, mix, *operands, state)


def finish_kernel(
    first, gamma_ref, mix_ref, above, below, before, after, top, bottom, left, right,
    factors_ref, base_ref, recv_ref, *rest
):
    new_ref, out_ref = rest[-11:-9]
    factors, base, recv, wide, lines, sides, factor_sem, in_sems, out_sems = rest[-9:]
    count, cells_x, cells_y = base.shape
    mix_b = mix_ref[0, 1]
    keep_row = above.shape[0] - 5
    keep = slice(keep_row, keep_row + 1)

    def in_copies(f):
        return (
            pltpu.make_async_copy(recv_ref.at[f], recv.at[f], in_sems.at[0, f]),
            pltpu.make_async_copy(base_ref.at[0, first + f], base.at[f], in_sems.at[1, f]),
        )

    def out_copies(f):
        return (
            pltpu.make_async_copy(recv.at[f], out_ref.at[0, first + f], out_sems.at[0, f]),
            pltpu.make_async_copy(base.at[f], new_ref.at[0, first + f], out_sems.at[1, f]),
        )

    copy_factors = pltpu.make_async_copy(factors_ref, factors, factor_sem)
    copy_factors.start()
    for f in range(count):
        for copy in in_copies(f):
            copy.start()
    lines[:count, :] = top[...] * above[keep, :]
    lines[count:, :] = bottom[...] * below[keep, :]
    sides[:count, :] = left[...] * before[keep, :]
    sides[count:, :] = right[...] * after[keep, :]
    copy_factors.wait()
    lane = lax.broadcasted_iota(jnp.int32, (STRIP, cells_y), 1)

    def one_field(f, carry):
        rate = gamma_ref[0, first + f]
        both = [sides[pl.ds(f, 1), :] * rate, sides[pl.ds(count + f, 1), :] * rate]
        cols = columns_of(jnp.concatenate(both, axis=0))
        wide[STRIP - 1 : STRIP, :] = lines[pl.ds(f, 1), :] * rate
        wide[STRIP + cells_x : STRIP + cells_x + 1, :] = lines[pl.ds(count + f, 1), :] * rate
        recv_in, base_in = in_copies(f)
        recv_out, base_out = out_copies(f)
        recv_in.wait()
        recv_out.start()
        for i in range(0, cells_x, STRIP):
            rows = slice(i, i + STRIP)
            wide[STRIP + i : 2 * STRIP + i, :] = factors[0, rows, :] * recv[f, rows, :] * rate
        base_in.wait()
        for i in range(0, cells_x, STRIP):
            rows = slice(i, i + STRIP)
            mid = wide[STRIP + i : 2 * STRIP + i, :]
            more = (factors[5, rows, :] - rate * factors[0, rows, :]) * mid
            more += factors[1, rows, :] * wide[STRIP + i - 1 : 2 * STRIP + i - 1, :]
            more += factors[2, rows, :] * wide[STRIP + i + 1 : 2 * STRIP + i + 1, :]
            prior = jnp.where(lane == 0, cols[rows, 0:1], pltpu.roll(mid, 1, 1))
            later = jnp.where(lane == cells_y - 1, cols[rows, 1:2], pltpu.roll(mid, cells_y - 1, 1))
            more += factors[3, rows, :] * prior + factors[4, rows, :] * later
            base[f, rows, :] = base[f, rows, :] + mix_b * (2.0 * mid + more)
        base_out.start()
        return carry

    lax.fori_loop(0, count, one_field, 0)
    for f in range(count):
        for copy in out_copies(f):
            copy.wait()


def finished(first, new_state, remapped, recv, rims, gamma, mix, factors, received):
    count, cells_x, cells_y = recv.shape
    chan = gamma.shape[1]
    anywhere = pl.BlockSpec(memory_space=pl.ANY)
    operands = [gamma, mix, *received, *rims, factors, new_state, recv]
    specs = [pl.BlockSpec(memory_space=pltpu.SMEM)] * 2
    specs += [pl.BlockSpec(memory_space=pltpu.VMEM)] * 8 + [anywhere] * 3
    aliases = {11: 0}
    if remapped is not None:
        aliases[len(operands)] = 1
        operands.append(remapped)
        specs.append(anywhere)
    return pl.pallas_call(
        functools.partial(finish_kernel, first),
        in_specs=specs,
        out_specs=[anywhere, anywhere],
        out_shape=[
            jax.ShapeDtypeStruct(new_state.shape, jnp.float32),
            jax.ShapeDtypeStruct((1, chan, cells_x, cells_y), jnp.float32),
        ],
        input_output_aliases=aliases,
        scratch_shapes=[
            pltpu.VMEM(factors.shape, jnp.float32),
            pltpu.VMEM((count, cells_x, cells_y), jnp.float32),
            pltpu.VMEM((count, cells_x, cells_y), jnp.float32),
            pltpu.VMEM((cells_x + 2 * STRIP, cells_y), jnp.float32),
            pltpu.VMEM((2 * count, cells_y), jnp.float32),
            pltpu.VMEM((2 * count, cells_x), jnp.float32),
            pltpu.SemaphoreType.DMA,
            pltpu.SemaphoreType.DMA((2, count)),
            pltpu.SemaphoreType.DMA((2, count)),
        ],
        compiler_params=pltpu.CompilerParams(vmem_limit_bytes=24 * 1024 * 1024),
        cost_estimate=pl.CostEstimate(
            flops=20 * recv.size, bytes_accessed=20 * recv.size, transcendentals=0
        ),
        name="finish",
    )(*operands)


def body(state, coefs, land_sea, gamma, pair_src, pair_dev, pair_blk, weights):
    tx, ty = lax.axis_size("tx"), lax.axis_size("ty")
    tiles = tx * ty
    nfield, cells_x, cells_y = state.shape[1:]
    chan = gamma.shape[1]
    pairs, width = weights.shape[1], weights.shape[2]
    capacity = max(2, 2 * pairs // tiles)
    half = chan // 2
    early, late = contributions(
        state, pair_src, pair_dev, pair_blk, weights, tiles, capacity, chan
    )
    swap = [(0, 1), (1, 0)]

    def exchanged(rows):
        rows = rows.reshape(tiles, capacity + 1, rows.shape[1], width)
        return lax.all_to_all(rows, ("tx", "ty"), split_axis=0, concat_axis=0, tiled=True)

    def add_up(rows, grant):
        return summed(rows, tiles, capacity, half, cells_x, cells_y, width, grant)

    late_in = exchanged(late)
    early = lax.ppermute(early, "comp", swap)
    early_in = placed_rows(early, tiles, capacity, pairs, cells_x * cells_y // width)

    land_after, _ = lax.optimization_barrier((land_sea, late))
    is_atmos = lax.axis_index("comp") == 0
    mix = jnp.where(is_atmos, jnp.array([[0.0, 1.0]]), jnp.array([[0.5, 0.5]]))
    mix = mix.astype(jnp.float32)
    rates = jnp.concatenate([gamma, jnp.zeros((1, nfield - chan), jnp.float32)], axis=1)
    x_low, x_high, y_low, y_high = edges_of(state, coefs, land_after, mix)
    left = lax.ppermute(y_high, "ty", shift_pairs(ty, 1))
    right = lax.ppermute(y_low, "ty", shift_pairs(ty, -1))
    above = lax.ppermute(x_high, "tx", shift_pairs(tx, 1))
    below = lax.ppermute(x_low, "tx", shift_pairs(tx, -1))
    early_in, above, below, left, right = lax.optimization_barrier(
        (early_in, above, below, left, right)
    )
    received = (above, below, left, right)
    early_in = exchanged(early_in)

    ends = jnp.concatenate([above[:, cells_y - LANES :], below[:, cells_y - LANES :]], axis=0)
    starts = jnp.concatenate([above[:, :LANES], below[:, :LANES]], axis=0)
    corners_left = lax.ppermute(ends, "ty", shift_pairs(ty, 1))
    corners_right = lax.ppermute(starts, "ty", shift_pairs(ty, -1))
    base, factors = base_of(
        state, coefs, land_after, rates, mix, (x_low, x_high, y_low, y_high), received,
        (corners_left, corners_right),
    )

    recv_late, top, bottom, left, right = add_up(late_in, 56)
    recv_late = lax.ppermute(recv_late, "comp", swap)
    rims_late = (
        lax.ppermute(bottom, ("comp", "tx"), crossed("tx", 1)),
        lax.ppermute(top, ("comp", "tx"), crossed("tx", -1)),
        lax.ppermute(right, ("comp", "ty"), crossed("ty", 1)),
        lax.ppermute(left, ("comp", "ty"), crossed("ty", -1)),
    )
    early_in, factors = lax.optimization_barrier((early_in, factors))
    recv_early, top, bottom, left, right = add_up(early_in, 24)
    rims_early = (
        lax.ppermute(bottom, "tx", shift_pairs(tx, 1)),
        lax.ppermute(top, "tx", shift_pairs(tx, -1)),
        lax.ppermute(right, "ty", shift_pairs(ty, 1)),
        lax.ppermute(left, "ty", shift_pairs(ty, -1)),
    )
    rest = (gamma, mix, factors, received)
    new_state, remapped = finished(half, base, None, recv_late, rims_late, *rest)
    new_state, remapped = finished(0, new_state, remapped, recv_early, rims_early, *rest)
    return new_state, remapped


def solution(mesh):
    placed = (
        P("comp", None, "tx", "ty"),
        P("comp", None, "tx", "ty"),
        P("tx", "ty"),
        P("comp", None),
        P("comp", ("tx", "ty")),
        P("comp", ("tx", "ty"), None),
        P("comp", ("tx", "ty")),
        P("comp", ("tx", "ty"), None, None),
    )
    return jax.shard_map(
        body,
        mesh=mesh,
        in_specs=placed,
        out_specs=(P("comp", None, "tx", "ty"), P("comp", None, "tx", "ty")),
        check_vma=False,
    )
```

```python
import functools

import jax
import jax.numpy as jnp
from jax import lax
from jax.experimental import pallas as pl
from jax.experimental.pallas import tpu as pltpu
from jax.sharding import PartitionSpec as P

LANES = 128
STEP_PAIRS = 64
STRIP = 8
NT = (((1,), (1,)), ((), ()))


def shift_pairs(count, by):
    return [(i, i + by) for i in range(count) if 0 <= i + by < count]


def crossed(axis, by):
    count = lax.axis_size(axis)
    return [
        (c * count + i, (1 - c) * count + j) for c in range(2) for i, j in shift_pairs(count, by)
    ]


def split(value, parts):
    if parts & (parts - 1) == 0:
        return lax.shift_right_logical(value, parts.bit_length() - 1), value & (parts - 1)
    return lax.div(value, parts), lax.rem(value, parts)


def ranks(dev, tiles):
    pairs = dev.shape[1]
    tile_of = lax.broadcasted_iota(jnp.int32, (tiles, pairs), 0)
    lane_of = lax.broadcasted_iota(jnp.int32, (tiles, pairs), 1)
    member = (tile_of == dev).astype(jnp.float32)
    total = member
    shift = 1
    while shift < pairs:
        total = total + jnp.where(lane_of >= shift, pltpu.roll(total, shift, 1), 0.0)
        shift *= 2
    return member, (jnp.sum(member * total, axis=0, keepdims=True) - 1.0).astype(jnp.int32)


def slot_blocks(dev, blk, tiles, capacity):
    member, rank = ranks(dev, tiles)
    pairs = dev.shape[1]
    slot_of = lax.broadcasted_iota(jnp.int32, (LANES, pairs), 0) % capacity
    chosen = (slot_of == rank).astype(jnp.bfloat16)

    def spread(values):
        return lax.dot_general(
            (member * values).astype(jnp.bfloat16), chosen, NT, preferred_element_type=jnp.float32
        )

    high, low = split(blk, 256)
    ids = spread(high.astype(jnp.float32)) * 256.0 + spread(low.astype(jnp.float32))
    return jnp.where(spread(jnp.ones(dev.shape, jnp.float32)) > 0.5, ids, -1.0)


def contribution_kernel(
    dims, src_ref, dev_ref, blk_ref, state_ref, weights_ref, early_ref, late_ref,
    cells, w_ref, pair_v, pair_s, taken, field_sems, weight_sems, pair_sems,
):
    tiles, capacity, pairs, fields, cells_x, cells_y, width = dims
    half = fields // 2
    parts = cells_y // width
    steps = pairs // STEP_PAIRS

    scalar_copies = [
        pltpu.make_async_copy(ref, pair_s.at[pl.ds(i, 1), :], pair_sems.at[i])
        for i, ref in enumerate((src_ref, dev_ref))
    ]
    vector_copies = [
        pltpu.make_async_copy(ref, pair_v.at[i], pair_sems.at[2 + i])
        for i, ref in enumerate((dev_ref, blk_ref))
    ]
    field_copies = [
        pltpu.make_async_copy(
            state_ref.at[0, f, :, pl.ds(q * width, width)],
            cells.at[q, :, f, :],
            field_sems.at[f * parts + q],
        )
        for f in range(fields)
        for q in range(parts)
    ]

    def weight_copy(step):
        some = pl.ds(step * STEP_PAIRS, STEP_PAIRS)
        return pltpu.make_async_copy(
            weights_ref.at[0, some], w_ref.at[some], weight_sems.at[step]
        )

    for copy in scalar_copies + vector_copies + field_copies:
        copy.start()
    for step in range(steps):
        weight_copy(step).start()
    late_ref[...] = jnp.zeros_like(late_ref)
    for t in range(tiles):
        taken[t] = t * (capacity + 1)

    for copy in vector_copies:
        copy.wait()
    dev, blk = pair_v[0], pair_v[1]
    ids = slot_blocks(dev, blk, tiles, capacity)
    for t in range(tiles):
        row = jnp.broadcast_to(ids[t : t + 1, :], late_ref.shape[1:])
        late_ref[t * (capacity + 1) + capacity] = row
    code = (dev * (cells_x * parts) + blk).astype(jnp.float32)
    for i in range(pairs // width):
        place = (pairs + i // half, slice(i % half, i % half + 1), slice(None))
        early_ref[place] = code[:, i * width : (i + 1) * width]
    for copy in scalar_copies + field_copies:
        copy.wait()

    def cells_of(p):
        x, part = split(pair_s[0, p], parts)
        return cells[part, x]

    zeros = jnp.zeros((fields, width), jnp.float32)

    def some_pairs(step, carry):
        weight_copy(step).wait()
        for i in range(0, STEP_PAIRS, 4):
            p = step * STEP_PAIRS + i
            left = [
                jnp.concatenate([cells_of(p + j), zeros][:: 1 - j % 2 * 2], axis=1) for j in range(4)
            ]
            left = jnp.concatenate(left, axis=0).astype(jnp.bfloat16)
            w = [w_ref[p + j] for j in range(4)]
            right = jnp.concatenate(
                [jnp.concatenate(w[:2], axis=1), jnp.concatenate(w[2:], axis=1)], axis=0
            )
            four = lax.dot_general(left, right, NT, preferred_element_type=jnp.float32)
            for j in range(4):
                tile = pair_s[1, p + j]
                slot = taken[tile]
                taken[tile] = slot + 1
                at = j // 2 * width
                one = four[j * fields : (j + 1) * fields, at : at + width]
                early_ref[p + j] = one[:half]
                late_ref[slot] = one[half:]
        return carry

    lax.fori_loop(0, steps, some_pairs, 0)


def contributions(state, pair_src, pair_dev, pair_blk, weights, tiles, capacity, fields):
    _, _, cells_x, cells_y = state.shape
    half = fields // 2
    pairs, width = weights.shape[1], weights.shape[2]
    rows = tiles * (capacity + 1)
    dims = (tiles, capacity, pairs, fields, cells_x, cells_y, width)
    parts = cells_y // width
    shapes = [(pairs + -(-pairs // (half * width)), half, width), (rows, half, width)]
    return pl.pallas_call(
        functools.partial(contribution_kernel, dims),
        in_specs=[pl.BlockSpec(memory_space=pltpu.HBM)] * 5,
        out_specs=[pl.BlockSpec(memory_space=pltpu.VMEM) for _ in shapes],
        out_shape=[jax.ShapeDtypeStruct(shape, jnp.float32) for shape in shapes],
        scratch_shapes=[
            pltpu.VMEM((parts, cells_x, fields, width), jnp.float32),
            pltpu.VMEM((pairs, width, width), jnp.bfloat16),
            pltpu.VMEM((2, 1, pairs), jnp.int32),
            pltpu.SMEM((2, pairs), jnp.int32),
            pltpu.SMEM((tiles,), jnp.int32),
            pltpu.SemaphoreType.DMA((parts * fields,)),
            pltpu.SemaphoreType.DMA((pairs // STEP_PAIRS,)),
            pltpu.SemaphoreType.DMA((4,)),
        ],
        compiler_params=pltpu.CompilerParams(vmem_limit_bytes=56 * 1024 * 1024),
        cost_estimate=pl.CostEstimate(
            flops=2 * pairs * fields * width * width,
            bytes_accessed=2 * pairs * width * width + 8 * rows * fields * width,
            transcendentals=0,
        ),
        name="contributions",
    )(pair_src, pair_dev.reshape(1, pairs), pair_blk, state, weights)


def place_kernel(dims, in_ref, out_ref, place_v, place_s, place_sem):
    tiles, capacity, pairs, blocks = dims
    half, width = in_ref.shape[1:]
    code = jnp.concatenate(
        [in_ref[pairs + i // half][i % half : i % half + 1] for i in range(pairs // width)], axis=1
    ).astype(jnp.int32)
    dev, _ = split(code, blocks)
    rank = ranks(dev, tiles)[1]
    place_v[...] = jnp.broadcast_to(dev * capacity + rank, place_v.shape)
    copy = pltpu.make_async_copy(place_v, place_s, place_sem)
    copy.start()
    out_ref[...] = jnp.zeros_like(out_ref)
    copy.wait()

    def some_rows(step, carry):
        for i in range(STEP_PAIRS):
            p = step * STEP_PAIRS + i
            out_ref[place_s[0, p]] = in_ref[p]
        return carry

    lax.fori_loop(0, pairs // STEP_PAIRS, some_rows, 0)


def placed_rows(rows, tiles, capacity, pairs, blocks):
    half, width = rows.shape[1:]
    shape = (tiles * capacity, half, width)
    return pl.pallas_call(
        functools.partial(place_kernel, (tiles, capacity, pairs, blocks)),
        out_shape=jax.ShapeDtypeStruct(shape, jnp.float32),
        scratch_shapes=[
            pltpu.VMEM((8, pairs), jnp.int32),
            pltpu.SMEM((8, pairs), jnp.int32),
            pltpu.SemaphoreType.DMA,
        ],
        compiler_params=pltpu.CompilerParams(vmem_limit_bytes=10 * 1024 * 1024),
        cost_estimate=pl.CostEstimate(
            flops=4 * rows.size, bytes_accessed=12 * rows.size, transcendentals=0
        ),
        name="place_in_slots",
    )(rows)


def sum_kernel(dims, ids_ref, in_ref, out_ref, top_ref, bottom_ref, left_ref, right_ref, pick, high, low):
    tiles, capacity, fields, cells_x, cells_y, width = dims
    parts = cells_y // width
    group = LANES // capacity
    stride = in_ref.shape[0] // tiles
    block_of = lax.broadcasted_iota(jnp.int32, (cells_x * parts, LANES), 0)
    block_of = (block_of % cells_x) * parts + block_of // cells_x
    block_of = block_of.astype(jnp.float32)
    lane = lax.broadcasted_iota(jnp.int32, (1, LANES), 1)
    for k in range(tiles // group):
        columns = pl.ds(k * LANES, LANES)
        ids = None
        for i in range(group):
            source = k * group + i
            row = ids_ref[pl.ds(source, 1), :]
            ids = row if ids is None else jnp.where(lane // capacity == i, row, ids)
            for f in range(fields):
                x = in_ref[pl.ds(source * stride + f, capacity, stride=fields), :]
                rounded = x.astype(jnp.bfloat16)
                place = (
                    pl.ds(source * capacity, capacity),
                    pl.ds(f * width, width),
                )
                high[place] = rounded
                low[place] = (x - rounded.astype(jnp.float32)).astype(jnp.bfloat16)
        pick[:, columns] = (block_of == ids).astype(jnp.bfloat16)
    for q in range(parts):
        chosen = pick[pl.ds(q * cells_x, cells_x), :]
        total = jnp.dot(chosen, high[...], preferred_element_type=jnp.float32)
        total = total + jnp.dot(chosen, low[...], preferred_element_type=jnp.float32)
        for f in range(fields):
            tile = total[:, f * width : (f + 1) * width]
            out_ref[f, :, pl.ds(q * width, width)] = tile
            top_ref[pl.ds(f, 1), pl.ds(q * width, width)] = tile[:1]
            bottom_ref[pl.ds(f, 1), pl.ds(q * width, width)] = tile[cells_x - 1 :]
            if q == 0:
                left_ref[pl.ds(f, 1), :] = tile.T[:1]
            if q == parts - 1:
                right_ref[pl.ds(f, 1), :] = tile.T[width - 1 :]


def summed(ids, rows, tiles, capacity, fields, cells_x, cells_y, width, grant):
    dims = (tiles, capacity, fields, cells_x, cells_y, width)
    slots = tiles * capacity
    blocks = cells_x * cells_y // width
    shapes = [
        (fields, cells_x, cells_y),
        (fields, cells_y),
        (fields, cells_y),
        (fields, cells_x),
        (fields, cells_x),
    ]
    return pl.pallas_call(
        functools.partial(sum_kernel, dims),
        out_shape=[jax.ShapeDtypeStruct(shape, jnp.float32) for shape in shapes],
        scratch_shapes=[
            pltpu.VMEM((blocks, slots), jnp.bfloat16),
            pltpu.VMEM((slots, fields * width), jnp.bfloat16),
            pltpu.VMEM((slots, fields * width), jnp.bfloat16),
        ],
        compiler_params=pltpu.CompilerParams(vmem_limit_bytes=grant * 1024 * 1024),
        cost_estimate=pl.CostEstimate(
            flops=4 * blocks * slots * fields * width,
            bytes_accessed=4 * fields * width * (slots + blocks),
            transcendentals=0,
        ),
        name="sum_by_block",
    )(ids, rows.reshape(-1, width))


def stencil_factors(coefs, keep):
    u, v, kappa = coefs
    return [
        keep,
        keep * (jnp.maximum(u, 0.0) + kappa),
        keep * (kappa - jnp.minimum(u, 0.0)),
        keep * (jnp.maximum(v, 0.0) + kappa),
        keep * (kappa - jnp.minimum(v, 0.0)),
        -keep * (jnp.abs(u) + jnp.abs(v) + 4.0 * kappa),
    ]


def tendency(s, rate, factors, top, bottom, left, right):
    cells_x, cells_y = s.shape
    x_of = lax.broadcasted_iota(jnp.int32, s.shape, 0)
    y_of = lax.broadcasted_iota(jnp.int32, s.shape, 1)
    out = (factors[5] - rate * factors[0]) * s
    out += factors[1] * jnp.where(x_of == 0, top, pltpu.roll(s, 1, 0))
    out += factors[2] * jnp.where(x_of == cells_x - 1, bottom, pltpu.roll(s, cells_x - 1, 0))
    out += factors[3] * jnp.where(y_of == 0, left, pltpu.roll(s, 1, 1))
    out += factors[4] * jnp.where(y_of == cells_y - 1, right, pltpu.roll(s, cells_y - 1, 1))
    return out


def columns_of(rows):
    spare = 8 - rows.shape[0]
    if spare:
        rows = jnp.concatenate([rows, jnp.zeros((spare, rows.shape[1]), rows.dtype)], axis=0)
    return rows.T


def line_count(nfield):
    return 2 * nfield + 8


def edge_kernel(mix_ref, state_tops, state_ends, state_lefts, state_rights, coefs_tops, coefs_ends,
                coefs_lefts, coefs_rights, land_tops, land_ends, land_lefts, land_rights,
                x_low, x_high, y_low, y_high):
    nfield = state_tops.shape[1]
    last_row, last_lane = state_tops.shape[2] - 1, state_lefts.shape[3] - 1
    atmos = mix_ref[0, 1] == 1.0

    def kept(land):
        return jnp.where(atmos, 1.0, land.astype(jnp.float32))

    for out, state, coefs, land, lines in (
        (x_low, state_tops, coefs_tops, land_tops, (0, 1)),
        (x_high, state_ends, coefs_ends, land_ends, (last_row - 1, last_row)),
    ):
        outer = lines[0] if lines[0] == 0 else lines[1]
        out[2 * nfield :, :] = jnp.zeros((8, out.shape[1]), jnp.float32)
        for j, line in enumerate(lines):
            for f in range(nfield):
                out[j * nfield + f : j * nfield + f + 1, :] = state[0, f, line : line + 1, :]
        for c in range(3):
            out[2 * nfield + c : 2 * nfield + c + 1, :] = coefs[0, c, outer : outer + 1, :]
        out[2 * nfield + 3 : 2 * nfield + 4, :] = kept(land[outer : outer + 1, :])

    for out, state, coefs, land, lines in (
        (y_low, state_lefts, coefs_lefts, land_lefts, (0, 1)),
        (y_high, state_rights, coefs_rights, land_rights, (last_lane - 1, last_lane)),
    ):
        outer = lines[0] if lines[0] == 0 else lines[1]
        lane = lax.broadcasted_iota(jnp.int32, land.shape, 1)
        packed = jnp.zeros(land.shape, jnp.float32)

        def put(packed, tile, at, to):
            moved = (to - at) % LANES
            tile = pltpu.roll(tile, moved, 1) if moved else tile
            return jnp.where(lane == to, tile, packed)

        for j, line in enumerate(lines):
            for f in range(nfield):
                packed = put(packed, state[0, f], line, j * nfield + f)
        for c in range(3):
            packed = put(packed, coefs[0, c], outer, 2 * nfield + c)
        packed = put(packed, kept(land[...]), outer, 2 * nfield + 3)
        out[...] = packed.T[: out.shape[0]]


def edges_of(state, coefs, land_sea, mix):
    _, nfield, cells_x, cells_y = state.shape
    lines = line_count(nfield)
    ends = [
        ((8, cells_y), (0, 0)),
        ((8, cells_y), (cells_x // 8 - 1, 0)),
        ((cells_x, LANES), (0, 0)),
        ((cells_x, LANES), (0, cells_y // LANES - 1)),
    ]
    at = lambda lead, place: lambda i: (0,) * len(lead) + place
    specs = [pl.BlockSpec(memory_space=pltpu.SMEM)]
    for lead in ((1, nfield), (1, 3), ()):
        specs += [pl.BlockSpec(lead + shape, at(lead, place)) for shape, place in ends]
    shapes = [(lines, cells_y)] * 2 + [(lines, cells_x)] * 2
    return pl.pallas_call(
        edge_kernel,
        grid=(1,),
        in_specs=specs,
        out_specs=[pl.BlockSpec(shape, lambda i: (0, 0)) for shape in shapes],
        out_shape=[jax.ShapeDtypeStruct(shape, jnp.float32) for shape in shapes],
        compiler_params=pltpu.CompilerParams(vmem_limit_bytes=24 * 1024 * 1024),
        cost_estimate=pl.CostEstimate(
            flops=state.size, bytes_accessed=4 * 1024 * 1024, transcendentals=0
        ),
        name="edges",
    )(mix, *[state] * 4, *[coefs] * 4, *[land_sea] * 4)


def outer_section(center, across, along, factors, rate):
    lane = lax.broadcasted_iota(jnp.int32, center.shape, 1)
    count = center.shape[1]
    before = jnp.where(lane == 0, along[0], pltpu.roll(center, 1, 1))
    after = jnp.where(lane == count - 1, along[1], pltpu.roll(center, count - 1, 1))
    keep, low, high, back, ahead, middle = factors
    out = center + low * across[0] + high * across[1] + back * before + ahead * after
    return out + (middle - rate * keep) * center


def base_kernel(rate_ref, mix_ref, rates_ref, coefs_ref, land_ref, x_low, x_high, y_low, y_high,
                above, below, left, right, corners_left, corners_right, state_ref,
                out_ref, factors, rows, cols):
    f = pl.program_id(0)
    nfield = rates_ref.shape[0]
    lines = line_count(nfield)

    @pl.when(f == 0)
    def _():
        keep = jnp.where(mix_ref[0, 1] == 1.0, 1.0, land_ref[...].astype(jnp.float32))
        for i, factor in enumerate(stencil_factors([coefs_ref[0, c] for c in range(3)], keep)):
            factors[i] = factor
        rate = rates_ref[:, 0:1]
        near, far = pl.ds(0, nfield), pl.ds(nfield, nfield)
        last = corners_left.shape[1] - 1
        corner = (
            (corners_left[nfield : 2 * nfield, last:], corners_left[lines : lines + nfield, last:]),
            (corners_right[nfield : 2 * nfield, 0:1], corners_right[lines : lines + nfield, 0:1]),
        )
        for i, (ref, center, across, along, is_column) in enumerate(
            (
                (above, above[far, :], (above[near, :], x_low[near, :]), (corner[0][0], corner[1][0]), False),
                (below, below[near, :], (x_high[far, :], below[far, :]), (corner[0][1], corner[1][1]), False),
                (left, left[far, :], (left[near, :], y_low[near, :]), corner[0], True),
                (right, right[near, :], (y_high[far, :], right[far, :]), corner[1], True),
            )
        ):
            first = 2 * nfield
            of_line = stencil_factors(
                [ref[first + c : first + c + 1, :] for c in range(3)],
                ref[first + 3 : first + 4, :],
            )
            if is_column:
                of_line = [of_line[j] for j in (0, 3, 4, 1, 2, 5)]
            section = outer_section(center, across, along, of_line, rate)
            kept = cols if is_column else rows
            kept[pl.ds(i % 2 * nfield, nfield), :] = center
            kept[pl.ds((2 + i % 2) * nfield, nfield), :] = section

    rate = rate_ref[0, f]
    mix_a, mix_b = mix_ref[0, 0], mix_ref[0, 1]
    s = state_ref[0, 0]
    row = [rows[pl.ds(i * nfield + f, 1), :] for i in range(4)]
    col = columns_of(
        jnp.concatenate([cols[pl.ds(i * nfield + f, 1), :] for i in range(4)], axis=0)
    )
    s1 = s + tendency(s, rate, factors, row[0], row[1], col[:, 0:1], col[:, 1:2])
    more = tendency(s1, rate, factors, row[2], row[3], col[:, 2:3], col[:, 3:4])
    out_ref[0, 0] = mix_a * s + (1.0 - mix_a) * s1 + mix_b * more


def base_of(state, coefs, land_sea, rates, mix, edges, received, corners):
    _, nfield, cells_x, cells_y = state.shape
    field = pl.BlockSpec((1, 1, cells_x, cells_y), lambda f: (0, f, 0, 0))
    whole = lambda a: pl.BlockSpec(a.shape, lambda f: (0,) * a.ndim)
    rates_wide = jnp.broadcast_to(rates.T, (nfield, LANES))
    operands = [rates_wide, coefs, land_sea, *edges, *received, *corners]
    return pl.pallas_call(
        base_kernel,
        grid=(nfield,),
        in_specs=[
            pl.BlockSpec(memory_space=pltpu.SMEM),
            pl.BlockSpec(memory_space=pltpu.SMEM),
            *[whole(a) for a in operands],
            field,
        ],
        out_specs=[field, pl.BlockSpec((6, cells_x, cells_y), lambda f: (0, 0, 0))],
        out_shape=[
            jax.ShapeDtypeStruct(state.shape, jnp.float32),
            jax.ShapeDtypeStruct((6, cells_x, cells_y), jnp.float32),
        ],
        scratch_shapes=[
            pltpu.VMEM((4 * nfield, cells_y), jnp.float32),
            pltpu.VMEM((4 * nfield, cells_x), jnp.float32),
        ],
        compiler_params=pltpu.CompilerParams(vmem_limit_bytes=16 * 1024 * 1024),
        cost_estimate=pl.CostEstimate(
            flops=40 * state.size, bytes_accessed=8 * state.size, transcendentals=0
        ),
        name="base",
    )(rates, mix, *operands, state)


def finish_kernel(first, with_x, gamma_ref, mix_ref, above, below, before, after, factors, recv,
                  left, right, *rest):
    tops, rest = (rest[:2], rest[2:]) if with_x else (None, rest)
    late, rest = (rest[:2], rest[2:]) if with_x else (None, rest)
    base_ref, rest = rest[0], rest[1:]
    new_ref, out_ref, done_ref = rest[-11:-8]
    base, wide, lines, sides, outer, base_sems, out_sems, outer_sems = rest[-8:]
    count, cells_x, cells_y = base.shape
    mix_b = mix_ref[0, 1]
    keep_row = above.shape[0] - 5
    keep = slice(keep_row, keep_row + 1)
    ends = (0, cells_x - STRIP)

    def base_copy(f):
        return pltpu.make_async_copy(base_ref.at[0, first + f], base.at[f], base_sems.at[f])

    def out_copies(f):
        return (
            pltpu.make_async_copy(recv.at[f], out_ref.at[0, first + f], out_sems.at[0, f]),
            pltpu.make_async_copy(base.at[f], new_ref.at[0, first + f], out_sems.at[1, f]),
        )

    def outer_copy(f, i, back):
        there = (new_ref if back else base_ref).at[0, count + f, pl.ds(ends[i], STRIP), :]
        here = outer.at[f, i]
        pair = (here, there) if back else (there, here)
        return pltpu.make_async_copy(*pair, outer_sems.at[f, i])

    outer_rows = [(f, i) for f in range(count) for i in range(2)] if with_x else []
    for f in range(count):
        base_copy(f).start()
    for f, i in outer_rows:
        outer_copy(f, i, False).start()
    done_ref[...] = jnp.zeros_like(done_ref)
    if with_x:
        lines[:count, :] = tops[0][...] * above[keep, :]
        lines[count:, :] = tops[1][...] * below[keep, :]
    else:
        lines[...] = jnp.zeros_like(lines)
    sides[:count, :] = left[...] * before[keep, :]
    sides[count:, :] = right[...] * after[keep, :]
    lane = lax.broadcasted_iota(jnp.int32, (STRIP, cells_y), 1)

    def one_field(f, carry):
        rate = gamma_ref[0, first + f]
        both = [sides[pl.ds(f, 1), :] * rate, sides[pl.ds(count + f, 1), :] * rate]
        cols = columns_of(jnp.concatenate(both, axis=0))
        wide[STRIP - 1 : STRIP, :] = lines[pl.ds(f, 1), :] * rate
        wide[STRIP + cells_x : STRIP + cells_x + 1, :] = lines[pl.ds(count + f, 1), :] * rate
        to_out, to_new = out_copies(f)
        to_out.start()
        for i in range(0, cells_x, STRIP):
            rows = slice(i, i + STRIP)
            wide[STRIP + i : 2 * STRIP + i, :] = factors[0, rows, :] * recv[f, rows, :] * rate
        base_copy(f).wait()
        for i in range(0, cells_x, STRIP):
            rows = slice(i, i + STRIP)
            mid = wide[STRIP + i : 2 * STRIP + i, :]
            more = (factors[5, rows, :] - rate * factors[0, rows, :]) * mid
            more += factors[1, rows, :] * wide[STRIP + i - 1 : 2 * STRIP + i - 1, :]
            more += factors[2, rows, :] * wide[STRIP + i + 1 : 2 * STRIP + i + 1, :]
            prior = jnp.where(lane == 0, cols[rows, 0:1], pltpu.roll(mid, 1, 1))
            later = jnp.where(lane == cells_y - 1, cols[rows, 1:2], pltpu.roll(mid, cells_y - 1, 1))
            more += factors[3, rows, :] * prior + factors[4, rows, :] * later
            base[f, rows, :] = base[f, rows, :] + mix_b * (2.0 * mid + more)
        to_new.start()
        return carry

    lax.fori_loop(0, count, one_field, 0)
    for f, i in outer_rows:
        outer_copy(f, i, False).wait()
        row = i * (STRIP - 1)
        at = ends[i] + row
        line = late[i][f : f + 1, :] * (above, below)[i][keep, :] * gamma_ref[0, count + f]
        more = mix_b * factors[1 + i, at : at + 1, :] * line
        outer[f, i, row : row + 1, :] = outer[f, i, row : row + 1, :] + more
        outer_copy(f, i, True).start()
    for f in range(count):
        for copy in out_copies(f):
            copy.wait()
    for f, i in outer_rows:
        outer_copy(f, i, True).wait()


def finished(
    first, new_state, remapped, recv, x_rims, y_rims, late_rims, late_done, gamma, mix, factors, received
):
    count, cells_x, cells_y = recv.shape
    chan = gamma.shape[1]
    with_x = x_rims is not None
    anywhere = pl.BlockSpec(memory_space=pl.ANY)
    operands = [gamma, mix, *received, factors, recv, *y_rims]
    if with_x:
        operands += [*x_rims, *late_rims]
    specs = [pl.BlockSpec(memory_space=pltpu.SMEM)] * 2
    specs += [pl.BlockSpec(memory_space=pltpu.VMEM)] * (len(operands) - 2) + [anywhere]
    aliases = {len(operands): 0}
    operands.append(new_state)
    if remapped is not None:
        aliases[len(operands)] = 1
        operands += [remapped, late_done]
        specs += [anywhere, anywhere]
    return pl.pallas_call(
        functools.partial(finish_kernel, first, with_x),
        in_specs=specs,
        out_specs=[anywhere, anywhere, pl.BlockSpec(memory_space=pltpu.VMEM)],
        out_shape=[
            jax.ShapeDtypeStruct(new_state.shape, jnp.float32),
            jax.ShapeDtypeStruct((1, chan, cells_x, cells_y), jnp.float32),
            jax.ShapeDtypeStruct((8, LANES), jnp.float32),
        ],
        input_output_aliases=aliases,
        scratch_shapes=[
            pltpu.VMEM((count, cells_x, cells_y), jnp.float32),
            pltpu.VMEM((cells_x + 2 * STRIP, cells_y), jnp.float32),
            pltpu.VMEM((2 * count, cells_y), jnp.float32),
            pltpu.VMEM((2 * count, cells_x), jnp.float32),
            pltpu.VMEM((count, 2, STRIP, cells_y), jnp.float32),
            pltpu.SemaphoreType.DMA((count,)),
            pltpu.SemaphoreType.DMA((2, count)),
            pltpu.SemaphoreType.DMA((count, 2)),
        ],
        compiler_params=pltpu.CompilerParams(vmem_limit_bytes=12 * 1024 * 1024),
        cost_estimate=pl.CostEstimate(
            flops=20 * recv.size, bytes_accessed=20 * recv.size, transcendentals=0
        ),
        name="finish",
    )(*operands)


def body(state, coefs, land_sea, gamma, pair_src, pair_dev, pair_blk, weights):
    tx, ty = lax.axis_size("tx"), lax.axis_size("ty")
    tiles = tx * ty
    nfield, cells_x, cells_y = state.shape[1:]
    chan = gamma.shape[1]
    pairs, width = weights.shape[1], weights.shape[2]
    capacity = max(2, 2 * pairs // tiles)
    half = chan // 2
    early, late = contributions(
        state, pair_src, pair_dev, pair_blk, weights, tiles, capacity, chan
    )
    swap = [(0, 1), (1, 0)]

    def exchanged(rows):
        rows = rows.reshape(tiles, -1, half, width)
        return lax.all_to_all(rows, ("tx", "ty"), split_axis=0, concat_axis=0, tiled=True)

    def add_up(ids, rows, grant):
        return summed(ids, rows, tiles, capacity, half, cells_x, cells_y, width, grant)

    late_in = exchanged(late)
    early = lax.ppermute(early, "comp", swap)
    early_in = placed_rows(early, tiles, capacity, pairs, cells_x * cells_y // width)

    land_after, _ = lax.optimization_barrier((land_sea, late))
    is_atmos = lax.axis_index("comp") == 0
    mix = jnp.where(is_atmos, jnp.array([[0.0, 1.0]]), jnp.array([[0.5, 0.5]]))
    mix = mix.astype(jnp.float32)
    rates = jnp.concatenate([gamma, jnp.zeros((1, nfield - chan), jnp.float32)], axis=1)
    x_low, x_high, y_low, y_high = edges_of(state, coefs, land_after, mix)
    left = lax.ppermute(y_high, "ty", shift_pairs(ty, 1))
    right = lax.ppermute(y_low, "ty", shift_pairs(ty, -1))
    above = lax.ppermute(x_high, "tx", shift_pairs(tx, 1))
    below = lax.ppermute(x_low, "tx", shift_pairs(tx, -1))
    early_in, above, below, left, right = lax.optimization_barrier(
        (early_in, above, below, left, right)
    )
    received = (above, below, left, right)
    early_in = exchanged(early_in)

    ends = jnp.concatenate([above[:, cells_y - LANES :], below[:, cells_y - LANES :]], axis=0)
    starts = jnp.concatenate([above[:, :LANES], below[:, :LANES]], axis=0)
    corners_left = lax.ppermute(ends, "ty", shift_pairs(ty, 1))
    corners_right = lax.ppermute(starts, "ty", shift_pairs(ty, -1))
    base, factors = base_of(
        state, coefs, land_after, rates, mix, (x_low, x_high, y_low, y_high), received,
        (corners_left, corners_right),
    )

    ids_late = late_in[:, capacity, 0, :]
    ids_early = lax.ppermute(ids_late, "comp", swap)
    recv_late, top, bottom, left, right = add_up(ids_late, late_in, 56)
    recv_late = lax.ppermute(recv_late, "comp", swap)
    late_x = (
        lax.ppermute(bottom, ("comp", "tx"), crossed("tx", 1)),
        lax.ppermute(top, ("comp", "tx"), crossed("tx", -1)),
    )
    late_y = (
        lax.ppermute(right, ("comp", "ty"), crossed("ty", 1)),
        lax.ppermute(left, ("comp", "ty"), crossed("ty", -1)),
    )
    rest = (gamma, mix, factors, received)
    new_state, remapped, done = finished(
        half, base, None, recv_late, None, late_y, None, None, *rest
    )
    early_in, done = lax.optimization_barrier((early_in, done))
    recv_early, top, bottom, left, right = add_up(ids_early, early_in, 16)
    early_x = (
        lax.ppermute(bottom, "tx", shift_pairs(tx, 1)),
        lax.ppermute(top, "tx", shift_pairs(tx, -1)),
    )
    early_y = (
        lax.ppermute(right, "ty", shift_pairs(ty, 1)),
        lax.ppermute(left, "ty", shift_pairs(ty, -1)),
    )
    new_state, remapped, _ = finished(
        0, new_state, remapped, recv_early, early_x, early_y, late_x, done, *rest
    )
    return new_state, remapped


def solution(mesh):
    placed = (
        P("comp", None, "tx", "ty"),
        P("comp", None, "tx", "ty"),
        P("tx", "ty"),
        P("comp", None),
        P("comp", ("tx", "ty")),
        P("comp", ("tx", "ty"), None),
        P("comp", ("tx", "ty")),
        P("comp", ("tx", "ty"), None, None),
    )
    return jax.shard_map(
        body,
        mesh=mesh,
        in_specs=placed,
        out_specs=(P("comp", None, "tx", "ty"), P("comp", None, "tx", "ty")),
        check_vma=False,
    )
```

```python
import functools

import jax
import jax.numpy as jnp
from jax import lax
from jax.experimental import pallas as pl
from jax.experimental.pallas import tpu as pltpu
from jax.sharding import PartitionSpec as P

LANES = 128
STEP_PAIRS = 64
STRIP = 8
NT = (((1,), (1,)), ((), ()))


def shift_pairs(count, by):
    return [(i, i + by) for i in range(count) if 0 <= i + by < count]


def crossed(axis, by):
    count = lax.axis_size(axis)
    return [
        (c * count + i, (1 - c) * count + j) for c in range(2) for i, j in shift_pairs(count, by)
    ]


def split(value, parts):
    if parts & (parts - 1) == 0:
        return lax.shift_right_logical(value, parts.bit_length() - 1), value & (parts - 1)
    return lax.div(value, parts), lax.rem(value, parts)


def ranks(dev, tiles):
    pairs = dev.shape[1]
    tile_of = lax.broadcasted_iota(jnp.int32, (tiles, pairs), 0)
    lane_of = lax.broadcasted_iota(jnp.int32, (tiles, pairs), 1)
    member = (tile_of == dev).astype(jnp.float32)
    total = member
    shift = 1
    while shift < pairs:
        total = total + jnp.where(lane_of >= shift, pltpu.roll(total, shift, 1), 0.0)
        shift *= 2
    return member, (jnp.sum(member * total, axis=0, keepdims=True) - 1.0).astype(jnp.int32)


def slot_blocks(dev, blk, tiles, capacity):
    member, rank = ranks(dev, tiles)
    pairs = dev.shape[1]
    slot_of = lax.broadcasted_iota(jnp.int32, (LANES, pairs), 0) % capacity
    chosen = (slot_of == rank).astype(jnp.bfloat16)

    def spread(values):
        return lax.dot_general(
            (member * values).astype(jnp.bfloat16), chosen, NT, preferred_element_type=jnp.float32
        )

    high, low = split(blk, 256)
    ids = spread(high.astype(jnp.float32)) * 256.0 + spread(low.astype(jnp.float32))
    return jnp.where(spread(jnp.ones(dev.shape, jnp.float32)) > 0.5, ids, -1.0)


def contribution_kernel(
    dims, src_ref, dev_ref, blk_ref, state_ref, weights_ref, early_ref, late_ref,
    cells, w_ref, pair_v, pair_s, taken, field_sems, weight_sems, pair_sems,
):
    tiles, capacity, pairs, fields, cells_x, cells_y, width = dims
    half = fields // 2
    parts = cells_y // width
    steps = pairs // STEP_PAIRS

    scalar_copies = [
        pltpu.make_async_copy(ref, pair_s.at[pl.ds(i, 1), :], pair_sems.at[i])
        for i, ref in enumerate((src_ref, dev_ref))
    ]
    vector_copies = [
        pltpu.make_async_copy(ref, pair_v.at[i], pair_sems.at[2 + i])
        for i, ref in enumerate((dev_ref, blk_ref))
    ]
    field_copies = [
        pltpu.make_async_copy(
            state_ref.at[0, f, :, pl.ds(q * width, width)],
            cells.at[q, :, f, :],
            field_sems.at[f * parts + q],
        )
        for f in range(fields)
        for q in range(parts)
    ]

    def weight_copy(step):
        some = pl.ds(step * STEP_PAIRS, STEP_PAIRS)
        return pltpu.make_async_copy(
            weights_ref.at[0, some], w_ref.at[some], weight_sems.at[step]
        )

    for copy in scalar_copies + vector_copies + field_copies:
        copy.start()
    for step in range(steps):
        weight_copy(step).start()
    late_ref[...] = jnp.zeros_like(late_ref)
    for t in range(tiles):
        taken[t] = t * (capacity + 1)

    for copy in vector_copies:
        copy.wait()
    dev, blk = pair_v[0], pair_v[1]
    ids = slot_blocks(dev, blk, tiles, capacity)
    for t in range(tiles):
        row = jnp.broadcast_to(ids[t : t + 1, :], late_ref.shape[1:])
        late_ref[t * (capacity + 1) + capacity] = row
    code = (dev * (cells_x * parts) + blk).astype(jnp.float32)
    for i in range(pairs // width):
        place = (pairs + i // half, slice(i % half, i % half + 1), slice(None))
        early_ref[place] = code[:, i * width : (i + 1) * width]
    for copy in scalar_copies + field_copies:
        copy.wait()

    def cells_of(p):
        x, part = split(pair_s[0, p], parts)
        return cells[part, x]

    zeros = jnp.zeros((fields, width), jnp.float32)

    def some_pairs(step, carry):
        weight_copy(step).wait()
        for i in range(0, STEP_PAIRS, 4):
            p = step * STEP_PAIRS + i
            left = [
                jnp.concatenate([cells_of(p + j), zeros][:: 1 - j % 2 * 2], axis=1) for j in range(4)
            ]
            left = jnp.concatenate(left, axis=0).astype(jnp.bfloat16)
            w = [w_ref[p + j] for j in range(4)]
            right = jnp.concatenate(
                [jnp.concatenate(w[:2], axis=1), jnp.concatenate(w[2:], axis=1)], axis=0
            )
            four = lax.dot_general(left, right, NT, preferred_element_type=jnp.float32)
            for j in range(4):
                tile = pair_s[1, p + j]
                slot = taken[tile]
                taken[tile] = slot + 1
                at = j // 2 * width
                one = four[j * fields : (j + 1) * fields, at : at + width]
                early_ref[p + j] = one[:half]
                late_ref[slot] = one[half:]
        return carry

    lax.fori_loop(0, steps, some_pairs, 0)


def contributions(state, pair_src, pair_dev, pair_blk, weights, tiles, capacity, fields):
    _, _, cells_x, cells_y = state.shape
    half = fields // 2
    pairs, width = weights.shape[1], weights.shape[2]
    rows = tiles * (capacity + 1)
    dims = (tiles, capacity, pairs, fields, cells_x, cells_y, width)
    parts = cells_y // width
    shapes = [(pairs + -(-pairs // (half * width)), half, width), (rows, half, width)]
    return pl.pallas_call(
        functools.partial(contribution_kernel, dims),
        in_specs=[pl.BlockSpec(memory_space=pltpu.HBM)] * 5,
        out_specs=[pl.BlockSpec(memory_space=pltpu.VMEM) for _ in shapes],
        out_shape=[jax.ShapeDtypeStruct(shape, jnp.float32) for shape in shapes],
        scratch_shapes=[
            pltpu.VMEM((parts, cells_x, fields, width), jnp.float32),
            pltpu.VMEM((pairs, width, width), jnp.bfloat16),
            pltpu.VMEM((2, 1, pairs), jnp.int32),
            pltpu.SMEM((2, pairs), jnp.int32),
            pltpu.SMEM((tiles,), jnp.int32),
            pltpu.SemaphoreType.DMA((parts * fields,)),
            pltpu.SemaphoreType.DMA((pairs // STEP_PAIRS,)),
            pltpu.SemaphoreType.DMA((4,)),
        ],
        compiler_params=pltpu.CompilerParams(vmem_limit_bytes=56 * 1024 * 1024),
        cost_estimate=pl.CostEstimate(
            flops=2 * pairs * fields * width * width,
            bytes_accessed=2 * pairs * width * width + 8 * rows * fields * width,
            transcendentals=0,
        ),
        name="contributions",
    )(pair_src, pair_dev.reshape(1, pairs), pair_blk, state, weights)


def place_kernel(dims, in_ref, out_ref, place_v, place_s, place_sem):
    tiles, capacity, pairs, blocks = dims
    half, width = in_ref.shape[1:]
    code = jnp.concatenate(
        [in_ref[pairs + i // half][i % half : i % half + 1] for i in range(pairs // width)], axis=1
    ).astype(jnp.int32)
    dev, _ = split(code, blocks)
    rank = ranks(dev, tiles)[1]
    place_v[...] = jnp.broadcast_to(dev * capacity + rank, place_v.shape)
    copy = pltpu.make_async_copy(place_v, place_s, place_sem)
    copy.start()
    out_ref[...] = jnp.zeros_like(out_ref)
    copy.wait()

    def some_rows(step, carry):
        for i in range(STEP_PAIRS):
            p = step * STEP_PAIRS + i
            out_ref[place_s[0, p]] = in_ref[p]
        return carry

    lax.fori_loop(0, pairs // STEP_PAIRS, some_rows, 0)


def placed_rows(rows, tiles, capacity, pairs, blocks):
    half, width = rows.shape[1:]
    shape = (tiles * capacity, half, width)
    return pl.pallas_call(
        functools.partial(place_kernel, (tiles, capacity, pairs, blocks)),
        out_shape=jax.ShapeDtypeStruct(shape, jnp.float32),
        scratch_shapes=[
            pltpu.VMEM((8, pairs), jnp.int32),
            pltpu.SMEM((8, pairs), jnp.int32),
            pltpu.SemaphoreType.DMA,
        ],
        compiler_params=pltpu.CompilerParams(vmem_limit_bytes=10 * 1024 * 1024),
        cost_estimate=pl.CostEstimate(
            flops=4 * rows.size, bytes_accessed=12 * rows.size, transcendentals=0
        ),
        name="place_in_slots",
    )(rows)


def sum_kernel(dims, ids_ref, rows_ref, out_ref, top_ref, bottom_ref, left_ref, right_ref,
               in_ref, pick, high, low, row_sems):
    tiles, capacity, fields, cells_x, cells_y, width = dims
    parts = cells_y // width
    group = LANES // capacity
    stride = in_ref.shape[0] // tiles

    def rows_copy(k):
        some = pl.ds(k * group * stride, group * stride)
        return pltpu.make_async_copy(rows_ref.at[some, :], in_ref.at[some, :], row_sems.at[k])

    for k in range(tiles // group):
        rows_copy(k).start()
    block_of = lax.broadcasted_iota(jnp.int32, (cells_x * parts, LANES), 0)
    block_of = (block_of % cells_x) * parts + block_of // cells_x
    block_of = block_of.astype(jnp.float32)
    lane = lax.broadcasted_iota(jnp.int32, (1, LANES), 1)
    for k in range(tiles // group):
        columns = pl.ds(k * LANES, LANES)
        rows_copy(k).wait()
        ids = None
        for i in range(group):
            source = k * group + i
            row = ids_ref[pl.ds(source, 1), :]
            ids = row if ids is None else jnp.where(lane // capacity == i, row, ids)
            for f in range(fields):
                x = in_ref[pl.ds(source * stride + f, capacity, stride=fields), :]
                rounded = x.astype(jnp.bfloat16)
                place = (
                    pl.ds(source * capacity, capacity),
                    pl.ds(f * width, width),
                )
                high[place] = rounded
                low[place] = (x - rounded.astype(jnp.float32)).astype(jnp.bfloat16)
        pick[:, columns] = (block_of == ids).astype(jnp.bfloat16)
    for q in range(parts):
        chosen = pick[pl.ds(q * cells_x, cells_x), :]
        total = jnp.dot(chosen, high[...], preferred_element_type=jnp.float32)
        total = total + jnp.dot(chosen, low[...], preferred_element_type=jnp.float32)
        for f in range(fields):
            tile = total[:, f * width : (f + 1) * width]
            out_ref[f, :, pl.ds(q * width, width)] = tile
            top_ref[pl.ds(f, 1), pl.ds(q * width, width)] = tile[:1]
            bottom_ref[pl.ds(f, 1), pl.ds(q * width, width)] = tile[cells_x - 1 :]
            if q == 0:
                left_ref[pl.ds(f, 1), :] = tile.T[:1]
            if q == parts - 1:
                right_ref[pl.ds(f, 1), :] = tile.T[width - 1 :]


def summed(ids, rows, tiles, capacity, fields, cells_x, cells_y, width, grant):
    dims = (tiles, capacity, fields, cells_x, cells_y, width)
    rows = rows.reshape(-1, width)
    slots = tiles * capacity
    blocks = cells_x * cells_y // width
    shapes = [
        (fields, cells_x, cells_y),
        (fields, cells_y),
        (fields, cells_y),
        (fields, cells_x),
        (fields, cells_x),
    ]
    return pl.pallas_call(
        functools.partial(sum_kernel, dims),
        in_specs=[pl.BlockSpec(memory_space=pltpu.VMEM), pl.BlockSpec(memory_space=pl.ANY)],
        out_shape=[jax.ShapeDtypeStruct(shape, jnp.float32) for shape in shapes],
        scratch_shapes=[
            pltpu.VMEM(rows.shape, jnp.float32),
            pltpu.VMEM((blocks, slots), jnp.bfloat16),
            pltpu.VMEM((slots, fields * width), jnp.bfloat16),
            pltpu.VMEM((slots, fields * width), jnp.bfloat16),
            pltpu.SemaphoreType.DMA((tiles * capacity // LANES,)),
        ],
        compiler_params=pltpu.CompilerParams(vmem_limit_bytes=grant * 1024 * 1024),
        cost_estimate=pl.CostEstimate(
            flops=4 * blocks * slots * fields * width,
            bytes_accessed=4 * fields * width * (slots + blocks),
            transcendentals=0,
        ),
        name="sum_by_block",
    )(ids, rows)


def stencil_factors(coefs, keep):
    u, v, kappa = coefs
    return [
        keep,
        keep * (jnp.maximum(u, 0.0) + kappa),
        keep * (kappa - jnp.minimum(u, 0.0)),
        keep * (jnp.maximum(v, 0.0) + kappa),
        keep * (kappa - jnp.minimum(v, 0.0)),
        -keep * (jnp.abs(u) + jnp.abs(v) + 4.0 * kappa),
    ]


def tendency(s, rate, factors, top, bottom, left, right):
    cells_x, cells_y = s.shape
    x_of = lax.broadcasted_iota(jnp.int32, s.shape, 0)
    y_of = lax.broadcasted_iota(jnp.int32, s.shape, 1)
    out = (factors[5] - rate * factors[0]) * s
    out += factors[1] * jnp.where(x_of == 0, top, pltpu.roll(s, 1, 0))
    out += factors[2] * jnp.where(x_of == cells_x - 1, bottom, pltpu.roll(s, cells_x - 1, 0))
    out += factors[3] * jnp.where(y_of == 0, left, pltpu.roll(s, 1, 1))
    out += factors[4] * jnp.where(y_of == cells_y - 1, right, pltpu.roll(s, cells_y - 1, 1))
    return out


def columns_of(rows):
    spare = 8 - rows.shape[0]
    if spare:
        rows = jnp.concatenate([rows, jnp.zeros((spare, rows.shape[1]), rows.dtype)], axis=0)
    return rows.T


def line_count(nfield):
    return 2 * nfield + 8


def edge_kernel(mix_ref, state_tops, state_ends, state_lefts, state_rights, coefs_tops, coefs_ends,
                coefs_lefts, coefs_rights, land_tops, land_ends, land_lefts, land_rights,
                x_low, x_high, y_low, y_high):
    nfield = state_tops.shape[1]
    last_row, last_lane = state_tops.shape[2] - 1, state_lefts.shape[3] - 1
    atmos = mix_ref[0, 1] == 1.0

    def kept(land):
        return jnp.where(atmos, 1.0, land.astype(jnp.float32))

    for out, state, coefs, land, lines in (
        (x_low, state_tops, coefs_tops, land_tops, (0, 1)),
        (x_high, state_ends, coefs_ends, land_ends, (last_row - 1, last_row)),
    ):
        outer = lines[0] if lines[0] == 0 else lines[1]
        out[2 * nfield :, :] = jnp.zeros((8, out.shape[1]), jnp.float32)
        for j, line in enumerate(lines):
            for f in range(nfield):
                out[j * nfield + f : j * nfield + f + 1, :] = state[0, f, line : line + 1, :]
        for c in range(3):
            out[2 * nfield + c : 2 * nfield + c + 1, :] = coefs[0, c, outer : outer + 1, :]
        out[2 * nfield + 3 : 2 * nfield + 4, :] = kept(land[outer : outer + 1, :])

    for out, state, coefs, land, lines in (
        (y_low, state_lefts, coefs_lefts, land_lefts, (0, 1)),
        (y_high, state_rights, coefs_rights, land_rights, (last_lane - 1, last_lane)),
    ):
        outer = lines[0] if lines[0] == 0 else lines[1]
        lane = lax.broadcasted_iota(jnp.int32, land.shape, 1)
        packed = jnp.zeros(land.shape, jnp.float32)

        def put(packed, tile, at, to):
            moved = (to - at) % LANES
            tile = pltpu.roll(tile, moved, 1) if moved else tile
            return jnp.where(lane == to, tile, packed)

        for j, line in enumerate(lines):
            for f in range(nfield):
                packed = put(packed, state[0, f], line, j * nfield + f)
        for c in range(3):
            packed = put(packed, coefs[0, c], outer, 2 * nfield + c)
        packed = put(packed, kept(land[...]), outer, 2 * nfield + 3)
        out[...] = packed.T[: out.shape[0]]


def edges_of(state, coefs, land_sea, mix):
    _, nfield, cells_x, cells_y = state.shape
    lines = line_count(nfield)
    ends = [
        ((8, cells_y), (0, 0)),
        ((8, cells_y), (cells_x // 8 - 1, 0)),
        ((cells_x, LANES), (0, 0)),
        ((cells_x, LANES), (0, cells_y // LANES - 1)),
    ]
    at = lambda lead, place: lambda i: (0,) * len(lead) + place
    specs = [pl.BlockSpec(memory_space=pltpu.SMEM)]
    for lead in ((1, nfield), (1, 3), ()):
        specs += [pl.BlockSpec(lead + shape, at(lead, place)) for shape, place in ends]
    shapes = [(lines, cells_y)] * 2 + [(lines, cells_x)] * 2
    return pl.pallas_call(
        edge_kernel,
        grid=(1,),
        in_specs=specs,
        out_specs=[pl.BlockSpec(shape, lambda i: (0, 0)) for shape in shapes],
        out_shape=[jax.ShapeDtypeStruct(shape, jnp.float32) for shape in shapes],
        compiler_params=pltpu.CompilerParams(vmem_limit_bytes=24 * 1024 * 1024),
        cost_estimate=pl.CostEstimate(
            flops=state.size, bytes_accessed=4 * 1024 * 1024, transcendentals=0
        ),
        name="edges",
    )(mix, *[state] * 4, *[coefs] * 4, *[land_sea] * 4)


def outer_section(center, across, along, factors, rate):
    lane = lax.broadcasted_iota(jnp.int32, center.shape, 1)
    count = center.shape[1]
    before = jnp.where(lane == 0, along[0], pltpu.roll(center, 1, 1))
    after = jnp.where(lane == count - 1, along[1], pltpu.roll(center, count - 1, 1))
    keep, low, high, back, ahead, middle = factors
    out = center + low * across[0] + high * across[1] + back * before + ahead * after
    return out + (middle - rate * keep) * center


def base_kernel(half, rate_ref, mix_ref, rates_ref, coefs_ref, land_ref, x_low, x_high, y_low, y_high,
                above, below, left, right, corners_left, corners_right, state_ref,
                out_ref, early_ref, factors, rows, cols):
    f = pl.program_id(0)
    nfield = rates_ref.shape[0]
    lines = line_count(nfield)

    @pl.when(f == 0)
    def _():
        keep = jnp.where(mix_ref[0, 1] == 1.0, 1.0, land_ref[...].astype(jnp.float32))
        for i, factor in enumerate(stencil_factors([coefs_ref[0, c] for c in range(3)], keep)):
            factors[i] = factor
        rate = rates_ref[:, 0:1]
        near, far = pl.ds(0, nfield), pl.ds(nfield, nfield)
        last = corners_left.shape[1] - 1
        corner = (
            (corners_left[nfield : 2 * nfield, last:], corners_left[lines : lines + nfield, last:]),
            (corners_right[nfield : 2 * nfield, 0:1], corners_right[lines : lines + nfield, 0:1]),
        )
        for i, (ref, center, across, along, is_column) in enumerate(
            (
                (above, above[far, :], (above[near, :], x_low[near, :]), (corner[0][0], corner[1][0]), False),
                (below, below[near, :], (x_high[far, :], below[far, :]), (corner[0][1], corner[1][1]), False),
                (left, left[far, :], (left[near, :], y_low[near, :]), corner[0], True),
                (right, right[near, :], (y_high[far, :], right[far, :]), corner[1], True),
            )
        ):
            first = 2 * nfield
            of_line = stencil_factors(
                [ref[first + c : first + c + 1, :] for c in range(3)],
                ref[first + 3 : first + 4, :],
            )
            if is_column:
                of_line = [of_line[j] for j in (0, 3, 4, 1, 2, 5)]
            section = outer_section(center, across, along, of_line, rate)
            kept = cols if is_column else rows
            kept[pl.ds(i % 2 * nfield, nfield), :] = center
            kept[pl.ds((2 + i % 2) * nfield, nfield), :] = section

    rate = rate_ref[0, f]
    mix_a, mix_b = mix_ref[0, 0], mix_ref[0, 1]
    s = state_ref[0, 0]
    row = [rows[pl.ds(i * nfield + f, 1), :] for i in range(4)]
    col = columns_of(
        jnp.concatenate([cols[pl.ds(i * nfield + f, 1), :] for i in range(4)], axis=0)
    )
    s1 = s + tendency(s, rate, factors, row[0], row[1], col[:, 0:1], col[:, 1:2])
    more = tendency(s1, rate, factors, row[2], row[3], col[:, 2:3], col[:, 3:4])
    total = mix_a * s + (1.0 - mix_a) * s1 + mix_b * more
    out_ref[0, 0] = total

    @pl.when(f < half)
    def _():
        early_ref[0] = total


def base_of(state, coefs, land_sea, rates, mix, edges, received, corners, half):
    _, nfield, cells_x, cells_y = state.shape
    field = pl.BlockSpec((1, 1, cells_x, cells_y), lambda f: (0, f, 0, 0))
    whole = lambda a: pl.BlockSpec(a.shape, lambda f: (0,) * a.ndim)
    rates_wide = jnp.broadcast_to(rates.T, (nfield, LANES))
    operands = [rates_wide, coefs, land_sea, *edges, *received, *corners]
    return pl.pallas_call(
        functools.partial(base_kernel, half),
        grid=(nfield,),
        in_specs=[
            pl.BlockSpec(memory_space=pltpu.SMEM),
            pl.BlockSpec(memory_space=pltpu.SMEM),
            *[whole(a) for a in operands],
            field,
        ],
        out_specs=[
            field,
            pl.BlockSpec((1, cells_x, cells_y), lambda f: (jnp.minimum(f, half - 1), 0, 0)),
            pl.BlockSpec((6, cells_x, cells_y), lambda f: (0, 0, 0)),
        ],
        out_shape=[
            jax.ShapeDtypeStruct(state.shape, jnp.float32),
            jax.ShapeDtypeStruct((half, cells_x, cells_y), jnp.float32),
            jax.ShapeDtypeStruct((6, cells_x, cells_y), jnp.float32),
        ],
        scratch_shapes=[
            pltpu.VMEM((4 * nfield, cells_y), jnp.float32),
            pltpu.VMEM((4 * nfield, cells_x), jnp.float32),
        ],
        compiler_params=pltpu.CompilerParams(vmem_limit_bytes=16 * 1024 * 1024),
        cost_estimate=pl.CostEstimate(
            flops=40 * state.size, bytes_accessed=8 * state.size, transcendentals=0
        ),
        name="base",
    )(rates, mix, *operands, state)


def finish_kernel(first, with_x, gamma_ref, mix_ref, above, below, before, after, factors, recv,
                  left, right, *rest):
    tops, rest = (rest[:2], rest[2:]) if with_x else (None, rest)
    late, rest = (rest[:2], rest[2:]) if with_x else (None, rest)
    early_base, rest = (rest[0], rest[1:]) if with_x else (None, rest)
    base_ref, rest = rest[0], rest[1:]
    new_ref, out_ref, done_ref = rest[-11:-8]
    base, wide, lines, sides, outer, base_sems, out_sems, outer_sems = rest[-8:]
    count, cells_x, cells_y = base.shape
    mix_b = mix_ref[0, 1]
    keep_row = above.shape[0] - 5
    keep = slice(keep_row, keep_row + 1)
    ends = (0, cells_x - STRIP)

    def base_copy(f):
        return pltpu.make_async_copy(base_ref.at[0, first + f], base.at[f], base_sems.at[f])

    def out_copies(f):
        return (
            pltpu.make_async_copy(recv.at[f], out_ref.at[0, first + f], out_sems.at[0, f]),
            pltpu.make_async_copy(base.at[f], new_ref.at[0, first + f], out_sems.at[1, f]),
        )

    def outer_copy(f, i, back):
        there = (new_ref if back else base_ref).at[0, count + f, pl.ds(ends[i], STRIP), :]
        here = outer.at[f, i]
        pair = (here, there) if back else (there, here)
        return pltpu.make_async_copy(*pair, outer_sems.at[f, i])

    outer_rows = [(f, i) for f in range(count) for i in range(2)] if with_x else []
    if not with_x:
        for f in range(count):
            base_copy(f).start()
    for f, i in outer_rows:
        outer_copy(f, i, False).start()
    done_ref[...] = jnp.zeros_like(done_ref)
    if with_x:
        lines[:count, :] = tops[0][...] * above[keep, :]
        lines[count:, :] = tops[1][...] * below[keep, :]
    else:
        lines[...] = jnp.zeros_like(lines)
    sides[:count, :] = left[...] * before[keep, :]
    sides[count:, :] = right[...] * after[keep, :]
    lane = lax.broadcasted_iota(jnp.int32, (STRIP, cells_y), 1)

    def one_field(f, carry):
        rate = gamma_ref[0, first + f]
        both = [sides[pl.ds(f, 1), :] * rate, sides[pl.ds(count + f, 1), :] * rate]
        cols = columns_of(jnp.concatenate(both, axis=0))
        wide[STRIP - 1 : STRIP, :] = lines[pl.ds(f, 1), :] * rate
        wide[STRIP + cells_x : STRIP + cells_x + 1, :] = lines[pl.ds(count + f, 1), :] * rate
        to_out, to_new = out_copies(f)
        to_out.start()
        for i in range(0, cells_x, STRIP):
            rows = slice(i, i + STRIP)
            wide[STRIP + i : 2 * STRIP + i, :] = factors[0, rows, :] * recv[f, rows, :] * rate
        if not with_x:
            base_copy(f).wait()
        start = early_base if with_x else base
        for i in range(0, cells_x, STRIP):
            rows = slice(i, i + STRIP)
            mid = wide[STRIP + i : 2 * STRIP + i, :]
            more = (factors[5, rows, :] - rate * factors[0, rows, :]) * mid
            more += factors[1, rows, :] * wide[STRIP + i - 1 : 2 * STRIP + i - 1, :]
            more += factors[2, rows, :] * wide[STRIP + i + 1 : 2 * STRIP + i + 1, :]
            prior = jnp.where(lane == 0, cols[rows, 0:1], pltpu.roll(mid, 1, 1))
            later = jnp.where(lane == cells_y - 1, cols[rows, 1:2], pltpu.roll(mid, cells_y - 1, 1))
            more += factors[3, rows, :] * prior + factors[4, rows, :] * later
            base[f, rows, :] = start[f, rows, :] + mix_b * (2.0 * mid + more)
        to_new.start()
        return carry

    def add_lines():
        for f, i in outer_rows:
            outer_copy(f, i, False).wait()
            row = i * (STRIP - 1)
            at = ends[i] + row
            line = late[i][f : f + 1, :] * (above, below)[i][keep, :] * gamma_ref[0, count + f]
            more = mix_b * factors[1 + i, at : at + 1, :] * line
            outer[f, i, row : row + 1, :] = outer[f, i, row : row + 1, :] + more
            outer_copy(f, i, True).start()

    lax.fori_loop(0, count - 1, one_field, 0)
    add_lines()
    one_field(count - 1, 0)
    for f in range(count):
        for copy in out_copies(f):
            copy.wait()
    for f, i in outer_rows:
        outer_copy(f, i, True).wait()


def finished(
    first, new_state, remapped, recv, x_rims, y_rims, closing, gamma, mix, factors, received
):
    count, cells_x, cells_y = recv.shape
    chan = gamma.shape[1]
    with_x = x_rims is not None
    anywhere = pl.BlockSpec(memory_space=pl.ANY)
    operands = [gamma, mix, *received, factors, recv, *y_rims]
    if with_x:
        late_rims, base_early, late_done = closing
        operands += [*x_rims, *late_rims, base_early]
    specs = [pl.BlockSpec(memory_space=pltpu.SMEM)] * 2
    specs += [pl.BlockSpec(memory_space=pltpu.VMEM)] * (len(operands) - 2) + [anywhere]
    aliases = {len(operands): 0}
    operands.append(new_state)
    if remapped is not None:
        aliases[len(operands)] = 1
        operands += [remapped, late_done]
        specs += [anywhere, anywhere]
    return pl.pallas_call(
        functools.partial(finish_kernel, first, with_x),
        in_specs=specs,
        out_specs=[anywhere, anywhere, pl.BlockSpec(memory_space=pltpu.VMEM)],
        out_shape=[
            jax.ShapeDtypeStruct(new_state.shape, jnp.float32),
            jax.ShapeDtypeStruct((1, chan, cells_x, cells_y), jnp.float32),
            jax.ShapeDtypeStruct((8, LANES), jnp.float32),
        ],
        input_output_aliases=aliases,
        scratch_shapes=[
            pltpu.VMEM((count, cells_x, cells_y), jnp.float32),
            pltpu.VMEM((cells_x + 2 * STRIP, cells_y), jnp.float32),
            pltpu.VMEM((2 * count, cells_y), jnp.float32),
            pltpu.VMEM((2 * count, cells_x), jnp.float32),
            pltpu.VMEM((count, 2, STRIP, cells_y), jnp.float32),
            pltpu.SemaphoreType.DMA((count,)),
            pltpu.SemaphoreType.DMA((2, count)),
            pltpu.SemaphoreType.DMA((count, 2)),
        ],
        compiler_params=pltpu.CompilerParams(vmem_limit_bytes=12 * 1024 * 1024),
        cost_estimate=pl.CostEstimate(
            flops=20 * recv.size, bytes_accessed=20 * recv.size, transcendentals=0
        ),
        name="finish",
    )(*operands)


def body(state, coefs, land_sea, gamma, pair_src, pair_dev, pair_blk, weights):
    tx, ty = lax.axis_size("tx"), lax.axis_size("ty")
    tiles = tx * ty
    nfield, cells_x, cells_y = state.shape[1:]
    chan = gamma.shape[1]
    pairs, width = weights.shape[1], weights.shape[2]
    capacity = max(2, 2 * pairs // tiles)
    half = chan // 2
    early, late = contributions(
        state, pair_src, pair_dev, pair_blk, weights, tiles, capacity, chan
    )
    swap = [(0, 1), (1, 0)]

    def exchanged(rows):
        rows = rows.reshape(tiles, -1, half, width)
        return lax.all_to_all(rows, ("tx", "ty"), split_axis=0, concat_axis=0, tiled=True)

    def add_up(ids, rows, grant):
        return summed(ids, rows, tiles, capacity, half, cells_x, cells_y, width, grant)

    late_in = exchanged(late)
    early = lax.ppermute(early, "comp", swap)
    early_in = placed_rows(early, tiles, capacity, pairs, cells_x * cells_y // width)

    land_after, _ = lax.optimization_barrier((land_sea, late))
    is_atmos = lax.axis_index("comp") == 0
    mix = jnp.where(is_atmos, jnp.array([[0.0, 1.0]]), jnp.array([[0.5, 0.5]]))
    mix = mix.astype(jnp.float32)
    rates = jnp.concatenate([gamma, jnp.zeros((1, nfield - chan), jnp.float32)], axis=1)
    x_low, x_high, y_low, y_high = edges_of(state, coefs, land_after, mix)
    left = lax.ppermute(y_high, "ty", shift_pairs(ty, 1))
    right = lax.ppermute(y_low, "ty", shift_pairs(ty, -1))
    above = lax.ppermute(x_high, "tx", shift_pairs(tx, 1))
    below = lax.ppermute(x_low, "tx", shift_pairs(tx, -1))
    early_in, above, below, left, right = lax.optimization_barrier(
        (early_in, above, below, left, right)
    )
    received = (above, below, left, right)
    early_in = exchanged(early_in)

    ends = jnp.concatenate([above[:, cells_y - LANES :], below[:, cells_y - LANES :]], axis=0)
    starts = jnp.concatenate([above[:, :LANES], below[:, :LANES]], axis=0)
    corners_left = lax.ppermute(ends, "ty", shift_pairs(ty, 1))
    corners_right = lax.ppermute(starts, "ty", shift_pairs(ty, -1))
    base, base_early, factors = base_of(
        state, coefs, land_after, rates, mix, (x_low, x_high, y_low, y_high), received,
        (corners_left, corners_right), half,
    )

    ids_late = late_in[:, capacity, 0, :]
    ids_early = lax.ppermute(ids_late, "comp", swap)
    recv_late, top, bottom, left, right = add_up(ids_late, late_in, 56)
    recv_late = lax.ppermute(recv_late, "comp", swap)
    late_x = (
        lax.ppermute(bottom, ("comp", "tx"), crossed("tx", 1)),
        lax.ppermute(top, ("comp", "tx"), crossed("tx", -1)),
    )
    late_y = (
        lax.ppermute(right, ("comp", "ty"), crossed("ty", 1)),
        lax.ppermute(left, ("comp", "ty"), crossed("ty", -1)),
    )
    rest = (gamma, mix, factors, received)
    new_state, remapped, done = finished(
        half, base, None, recv_late, None, late_y, None, *rest
    )
    early_in, done = lax.optimization_barrier((early_in, done))
    recv_early, top, bottom, left, right = add_up(ids_early, early_in, 16)
    early_x = (
        lax.ppermute(bottom, "tx", shift_pairs(tx, 1)),
        lax.ppermute(top, "tx", shift_pairs(tx, -1)),
    )
    early_y = (
        lax.ppermute(right, "ty", shift_pairs(ty, 1)),
        lax.ppermute(left, "ty", shift_pairs(ty, -1)),
    )
    new_state, remapped, _ = finished(
        0, new_state, remapped, recv_early, early_x, early_y, (late_x, base_early, done), *rest
    )
    return new_state, remapped


def solution(mesh):
    placed = (
        P("comp", None, "tx", "ty"),
        P("comp", None, "tx", "ty"),
        P("tx", "ty"),
        P("comp", None),
        P("comp", ("tx", "ty")),
        P("comp", ("tx", "ty"), None),
        P("comp", ("tx", "ty")),
        P("comp", ("tx", "ty"), None, None),
    )
    return jax.shard_map(
        body,
        mesh=mesh,
        in_specs=placed,
        out_specs=(P("comp", None, "tx", "ty"), P("comp", None, "tx", "ty")),
        check_vma=False,
    )
```

```python
import functools

import jax
import jax.numpy as jnp
from jax import lax
from jax.experimental import pallas as pl
from jax.experimental.pallas import tpu as pltpu
from jax.sharding import PartitionSpec as P

LANES = 128
STEP_PAIRS = 128
STRIP = 8
NT = (((1,), (1,)), ((), ()))


def shift_pairs(count, by):
    return [(i, i + by) for i in range(count) if 0 <= i + by < count]


def crossed(axis, by):
    count = lax.axis_size(axis)
    return [
        (c * count + i, (1 - c) * count + j) for c in range(2) for i, j in shift_pairs(count, by)
    ]


def split(value, parts):
    if parts & (parts - 1) == 0:
        return lax.shift_right_logical(value, parts.bit_length() - 1), value & (parts - 1)
    return lax.div(value, parts), lax.rem(value, parts)


def ranks(dev, tiles):
    pairs = dev.shape[1]
    tile_of = lax.broadcasted_iota(jnp.int32, (tiles, pairs), 0)
    lane_of = lax.broadcasted_iota(jnp.int32, (tiles, pairs), 1)
    member = (tile_of == dev).astype(jnp.float32)
    total = member
    shift = 1
    while shift < pairs:
        total = total + jnp.where(lane_of >= shift, pltpu.roll(total, shift, 1), 0.0)
        shift *= 2
    return member, (jnp.sum(member * total, axis=0, keepdims=True) - 1.0).astype(jnp.int32)


def slot_blocks(dev, blk, tiles, capacity):
    member, rank = ranks(dev, tiles)
    pairs = dev.shape[1]
    slot_of = lax.broadcasted_iota(jnp.int32, (LANES, pairs), 0) % capacity
    chosen = (slot_of == rank).astype(jnp.bfloat16)

    def spread(values):
        return lax.dot_general(
            (member * values).astype(jnp.bfloat16), chosen, NT, preferred_element_type=jnp.float32
        )

    high, low = split(blk, 256)
    ids = spread(high.astype(jnp.float32)) * 256.0 + spread(low.astype(jnp.float32))
    return jnp.where(spread(jnp.ones(dev.shape, jnp.float32)) > 0.5, ids, -1.0)


def contribution_kernel(
    dims, src_ref, dev_ref, blk_ref, state_ref, weights_ref, early_ref, late_ref,
    cells, w_ref, pair_v, pair_s, taken, field_sems, weight_sems, pair_sems,
):
    tiles, capacity, pairs, fields, cells_x, cells_y, width = dims
    half = fields // 2
    parts = cells_y // width
    steps = pairs // STEP_PAIRS

    scalar_copies = [
        pltpu.make_async_copy(ref, pair_s.at[pl.ds(i, 1), :], pair_sems.at[i])
        for i, ref in enumerate((src_ref, dev_ref))
    ]
    vector_copies = [
        pltpu.make_async_copy(ref, pair_v.at[i], pair_sems.at[2 + i])
        for i, ref in enumerate((dev_ref, blk_ref))
    ]
    field_copies = [
        pltpu.make_async_copy(
            state_ref.at[0, f, :, pl.ds(q * width, width)],
            cells.at[q, :, f, :],
            field_sems.at[f * parts + q],
        )
        for f in range(fields)
        for q in range(parts)
    ]

    def weight_copy(step):
        some = pl.ds(step * STEP_PAIRS, STEP_PAIRS)
        return pltpu.make_async_copy(
            weights_ref.at[0, some], w_ref.at[some], weight_sems.at[step]
        )

    for copy in scalar_copies + vector_copies + field_copies:
        copy.start()
    for step in range(steps):
        weight_copy(step).start()
    late_ref[...] = jnp.zeros_like(late_ref)
    for t in range(tiles):
        taken[t] = t * (capacity + 1)

    for copy in vector_copies:
        copy.wait()
    dev, blk = pair_v[0], pair_v[1]
    ids = slot_blocks(dev, blk, tiles, capacity)
    for t in range(tiles):
        row = jnp.broadcast_to(ids[t : t + 1, :], late_ref.shape[1:])
        late_ref[t * (capacity + 1) + capacity] = row
    code = (dev * (cells_x * parts) + blk).astype(jnp.float32)
    for i in range(pairs // width):
        place = (pairs + i // half, slice(i % half, i % half + 1), slice(None))
        early_ref[place] = code[:, i * width : (i + 1) * width]
    for copy in scalar_copies + field_copies:
        copy.wait()

    def cells_of(p):
        x, part = split(pair_s[0, p], parts)
        return cells[part, x]

    zeros = jnp.zeros((fields, width), jnp.float32)

    def some_pairs(step, carry):
        weight_copy(step).wait()
        for i in range(0, STEP_PAIRS, 4):
            p = step * STEP_PAIRS + i
            left = [
                jnp.concatenate([cells_of(p + j), zeros][:: 1 - j % 2 * 2], axis=1) for j in range(4)
            ]
            left = jnp.concatenate(left, axis=0).astype(jnp.bfloat16)
            w = [w_ref[p + j] for j in range(4)]
            right = jnp.concatenate(
                [jnp.concatenate(w[:2], axis=1), jnp.concatenate(w[2:], axis=1)], axis=0
            )
            four = lax.dot_general(left, right, NT, preferred_element_type=jnp.float32)
            for j in range(4):
                tile = pair_s[1, p + j]
                slot = taken[tile]
                taken[tile] = slot + 1
                at = j // 2 * width
                one = four[j * fields : (j + 1) * fields, at : at + width]
                early_ref[p + j] = one[:half]
                late_ref[slot] = one[half:]
        return carry

    lax.fori_loop(0, steps, some_pairs, 0)


def contributions(state, pair_src, pair_dev, pair_blk, weights, tiles, capacity, fields):
    _, _, cells_x, cells_y = state.shape
    half = fields // 2
    pairs, width = weights.shape[1], weights.shape[2]
    rows = tiles * (capacity + 1)
    dims = (tiles, capacity, pairs, fields, cells_x, cells_y, width)
    parts = cells_y // width
    shapes = [(pairs + -(-pairs // (half * width)), half, width), (rows, half, width)]
    return pl.pallas_call(
        functools.partial(contribution_kernel, dims),
        in_specs=[pl.BlockSpec(memory_space=pltpu.HBM)] * 5,
        out_specs=[pl.BlockSpec(memory_space=pltpu.VMEM) for _ in shapes],
        out_shape=[jax.ShapeDtypeStruct(shape, jnp.float32) for shape in shapes],
        scratch_shapes=[
            pltpu.VMEM((parts, cells_x, fields, width), jnp.float32),
            pltpu.VMEM((pairs, width, width), jnp.bfloat16),
            pltpu.VMEM((2, 1, pairs), jnp.int32),
            pltpu.SMEM((2, pairs), jnp.int32),
            pltpu.SMEM((tiles,), jnp.int32),
            pltpu.SemaphoreType.DMA((parts * fields,)),
            pltpu.SemaphoreType.DMA((pairs // STEP_PAIRS,)),
            pltpu.SemaphoreType.DMA((4,)),
        ],
        compiler_params=pltpu.CompilerParams(vmem_limit_bytes=56 * 1024 * 1024),
        cost_estimate=pl.CostEstimate(
            flops=2 * pairs * fields * width * width,
            bytes_accessed=2 * pairs * width * width + 8 * rows * fields * width,
            transcendentals=0,
        ),
        name="contributions",
    )(pair_src, pair_dev.reshape(1, pairs), pair_blk, state, weights)


def place_kernel(dims, in_ref, out_ref, place_v, place_s, place_sem):
    tiles, capacity, pairs, blocks = dims
    half, width = in_ref.shape[1:]
    code = jnp.concatenate(
        [in_ref[pairs + i // half][i % half : i % half + 1] for i in range(pairs // width)], axis=1
    ).astype(jnp.int32)
    dev, _ = split(code, blocks)
    rank = ranks(dev, tiles)[1]
    place_v[...] = jnp.broadcast_to(dev * capacity + rank, place_v.shape)
    copy = pltpu.make_async_copy(place_v, place_s, place_sem)
    copy.start()
    out_ref[...] = jnp.zeros_like(out_ref)
    copy.wait()

    def some_rows(step, carry):
        for i in range(STEP_PAIRS):
            p = step * STEP_PAIRS + i
            out_ref[place_s[0, p]] = in_ref[p]
        return carry

    lax.fori_loop(0, pairs // STEP_PAIRS, some_rows, 0)


def placed_rows(rows, tiles, capacity, pairs, blocks):
    half, width = rows.shape[1:]
    shape = (tiles * capacity, half, width)
    return pl.pallas_call(
        functools.partial(place_kernel, (tiles, capacity, pairs, blocks)),
        out_shape=jax.ShapeDtypeStruct(shape, jnp.float32),
        scratch_shapes=[
            pltpu.VMEM((8, pairs), jnp.int32),
            pltpu.SMEM((8, pairs), jnp.int32),
            pltpu.SemaphoreType.DMA,
        ],
        compiler_params=pltpu.CompilerParams(vmem_limit_bytes=10 * 1024 * 1024),
        cost_estimate=pl.CostEstimate(
            flops=4 * rows.size, bytes_accessed=12 * rows.size, transcendentals=0
        ),
        name="place_in_slots",
    )(rows)


def sum_kernel(dims, ids_ref, rows_ref, out_ref, top_ref, bottom_ref, left_ref, right_ref,
               in_ref, pick, high, low, row_sems):
    tiles, capacity, fields, cells_x, cells_y, width = dims
    parts = cells_y // width
    group = LANES // capacity
    stride = in_ref.shape[0] // tiles

    def rows_copy(k):
        some = pl.ds(k * group * stride, group * stride)
        return pltpu.make_async_copy(rows_ref.at[some, :], in_ref.at[some, :], row_sems.at[k])

    for k in range(tiles // group):
        rows_copy(k).start()
    block_of = lax.broadcasted_iota(jnp.int32, (cells_x * parts, LANES), 0)
    block_of = (block_of % cells_x) * parts + block_of // cells_x
    block_of = block_of.astype(jnp.float32)
    lane = lax.broadcasted_iota(jnp.int32, (1, LANES), 1)
    for k in range(tiles // group):
        columns = pl.ds(k * LANES, LANES)
        rows_copy(k).wait()
        ids = None
        for i in range(group):
            source = k * group + i
            row = ids_ref[pl.ds(source, 1), :]
            ids = row if ids is None else jnp.where(lane // capacity == i, row, ids)
            for f in range(fields):
                x = in_ref[pl.ds(source * stride + f, capacity, stride=fields), :]
                rounded = x.astype(jnp.bfloat16)
                place = (
                    pl.ds(source * capacity, capacity),
                    pl.ds(f * width, width),
                )
                high[place] = rounded
                low[place] = (x - rounded.astype(jnp.float32)).astype(jnp.bfloat16)
        pick[:, columns] = (block_of == ids).astype(jnp.bfloat16)
    for q in range(parts):
        chosen = pick[pl.ds(q * cells_x, cells_x), :]
        total = jnp.dot(chosen, high[...], preferred_element_type=jnp.float32)
        total = total + jnp.dot(chosen, low[...], preferred_element_type=jnp.float32)
        for f in range(fields):
            tile = total[:, f * width : (f + 1) * width]
            out_ref[f, :, pl.ds(q * width, width)] = tile
            top_ref[pl.ds(f, 1), pl.ds(q * width, width)] = tile[:1]
            bottom_ref[pl.ds(f, 1), pl.ds(q * width, width)] = tile[cells_x - 1 :]
            if q == 0:
                left_ref[pl.ds(f, 1), :] = tile.T[:1]
            if q == parts - 1:
                right_ref[pl.ds(f, 1), :] = tile.T[width - 1 :]


def summed(ids, rows, tiles, capacity, fields, cells_x, cells_y, width, grant):
    dims = (tiles, capacity, fields, cells_x, cells_y, width)
    rows = rows.reshape(-1, width)
    slots = tiles * capacity
    blocks = cells_x * cells_y // width
    shapes = [
        (fields, cells_x, cells_y),
        (fields, cells_y),
        (fields, cells_y),
        (fields, cells_x),
        (fields, cells_x),
    ]
    return pl.pallas_call(
        functools.partial(sum_kernel, dims),
        in_specs=[pl.BlockSpec(memory_space=pltpu.VMEM), pl.BlockSpec(memory_space=pl.ANY)],
        out_shape=[jax.ShapeDtypeStruct(shape, jnp.float32) for shape in shapes],
        scratch_shapes=[
            pltpu.VMEM(rows.shape, jnp.float32),
            pltpu.VMEM((blocks, slots), jnp.bfloat16),
            pltpu.VMEM((slots, fields * width), jnp.bfloat16),
            pltpu.VMEM((slots, fields * width), jnp.bfloat16),
            pltpu.SemaphoreType.DMA((tiles * capacity // LANES,)),
        ],
        compiler_params=pltpu.CompilerParams(vmem_limit_bytes=grant * 1024 * 1024),
        cost_estimate=pl.CostEstimate(
            flops=4 * blocks * slots * fields * width,
            bytes_accessed=4 * fields * width * (slots + blocks),
            transcendentals=0,
        ),
        name="sum_by_block",
    )(ids, rows)


def stencil_factors(coefs, keep):
    u, v, kappa = coefs
    return [
        keep,
        keep * (jnp.maximum(u, 0.0) + kappa),
        keep * (kappa - jnp.minimum(u, 0.0)),
        keep * (jnp.maximum(v, 0.0) + kappa),
        keep * (kappa - jnp.minimum(v, 0.0)),
        -keep * (jnp.abs(u) + jnp.abs(v) + 4.0 * kappa),
    ]


def tendency(s, rate, factors, top, bottom, left, right):
    cells_x, cells_y = s.shape
    x_of = lax.broadcasted_iota(jnp.int32, s.shape, 0)
    y_of = lax.broadcasted_iota(jnp.int32, s.shape, 1)
    out = (factors[5] - rate * factors[0]) * s
    out += factors[1] * jnp.where(x_of == 0, top, pltpu.roll(s, 1, 0))
    out += factors[2] * jnp.where(x_of == cells_x - 1, bottom, pltpu.roll(s, cells_x - 1, 0))
    out += factors[3] * jnp.where(y_of == 0, left, pltpu.roll(s, 1, 1))
    out += factors[4] * jnp.where(y_of == cells_y - 1, right, pltpu.roll(s, cells_y - 1, 1))
    return out


def columns_of(rows):
    spare = 8 - rows.shape[0]
    if spare:
        rows = jnp.concatenate([rows, jnp.zeros((spare, rows.shape[1]), rows.dtype)], axis=0)
    return rows.T


def line_count(nfield):
    return 2 * nfield + 8


def edge_kernel(mix_ref, state_tops, state_ends, state_lefts, state_rights, coefs_tops, coefs_ends,
                coefs_lefts, coefs_rights, land_tops, land_ends, land_lefts, land_rights,
                x_low, x_high, y_low, y_high):
    nfield = state_tops.shape[1]
    last_row, last_lane = state_tops.shape[2] - 1, state_lefts.shape[3] - 1
    atmos = mix_ref[0, 1] == 1.0

    def kept(land):
        return jnp.where(atmos, 1.0, land.astype(jnp.float32))

    for out, state, coefs, land, lines in (
        (x_low, state_tops, coefs_tops, land_tops, (0, 1)),
        (x_high, state_ends, coefs_ends, land_ends, (last_row - 1, last_row)),
    ):
        outer = lines[0] if lines[0] == 0 else lines[1]
        out[2 * nfield :, :] = jnp.zeros((8, out.shape[1]), jnp.float32)
        for j, line in enumerate(lines):
            for f in range(nfield):
                out[j * nfield + f : j * nfield + f + 1, :] = state[0, f, line : line + 1, :]
        for c in range(3):
            out[2 * nfield + c : 2 * nfield + c + 1, :] = coefs[0, c, outer : outer + 1, :]
        out[2 * nfield + 3 : 2 * nfield + 4, :] = kept(land[outer : outer + 1, :])

    for out, state, coefs, land, lines in (
        (y_low, state_lefts, coefs_lefts, land_lefts, (0, 1)),
        (y_high, state_rights, coefs_rights, land_rights, (last_lane - 1, last_lane)),
    ):
        outer = lines[0] if lines[0] == 0 else lines[1]
        lane = lax.broadcasted_iota(jnp.int32, land.shape, 1)
        packed = jnp.zeros(land.shape, jnp.float32)

        def put(packed, tile, at, to):
            moved = (to - at) % LANES
            tile = pltpu.roll(tile, moved, 1) if moved else tile
            return jnp.where(lane == to, tile, packed)

        for j, line in enumerate(lines):
            for f in range(nfield):
                packed = put(packed, state[0, f], line, j * nfield + f)
        for c in range(3):
            packed = put(packed, coefs[0, c], outer, 2 * nfield + c)
        packed = put(packed, kept(land[...]), outer, 2 * nfield + 3)
        out[...] = packed.T[: out.shape[0]]


def edges_of(state, coefs, land_sea, mix):
    _, nfield, cells_x, cells_y = state.shape
    lines = line_count(nfield)
    ends = [
        ((8, cells_y), (0, 0)),
        ((8, cells_y), (cells_x // 8 - 1, 0)),
        ((cells_x, LANES), (0, 0)),
        ((cells_x, LANES), (0, cells_y // LANES - 1)),
    ]
    at = lambda lead, place: lambda i: (0,) * len(lead) + place
    specs = [pl.BlockSpec(memory_space=pltpu.SMEM)]
    for lead in ((1, nfield), (1, 3), ()):
        specs += [pl.BlockSpec(lead + shape, at(lead, place)) for shape, place in ends]
    shapes = [(lines, cells_y)] * 2 + [(lines, cells_x)] * 2
    return pl.pallas_call(
        edge_kernel,
        grid=(1,),
        in_specs=specs,
        out_specs=[pl.BlockSpec(shape, lambda i: (0, 0)) for shape in shapes],
        out_shape=[jax.ShapeDtypeStruct(shape, jnp.float32) for shape in shapes],
        compiler_params=pltpu.CompilerParams(vmem_limit_bytes=24 * 1024 * 1024),
        cost_estimate=pl.CostEstimate(
            flops=state.size, bytes_accessed=4 * 1024 * 1024, transcendentals=0
        ),
        name="edges",
    )(mix, *[state] * 4, *[coefs] * 4, *[land_sea] * 4)


def outer_section(center, across, along, factors, rate):
    lane = lax.broadcasted_iota(jnp.int32, center.shape, 1)
    count = center.shape[1]
    before = jnp.where(lane == 0, along[0], pltpu.roll(center, 1, 1))
    after = jnp.where(lane == count - 1, along[1], pltpu.roll(center, count - 1, 1))
    keep, low, high, back, ahead, middle = factors
    out = center + low * across[0] + high * across[1] + back * before + ahead * after
    return out + (middle - rate * keep) * center


def base_kernel(half, rate_ref, mix_ref, rates_ref, coefs_ref, land_ref, x_low, x_high, y_low, y_high,
                above, below, left, right, corners_left, corners_right, state_ref,
                out_ref, early_ref, factors, rows, cols):
    f = pl.program_id(0)
    nfield = rates_ref.shape[0]
    lines = line_count(nfield)

    @pl.when(f == 0)
    def _():
        keep = jnp.where(mix_ref[0, 1] == 1.0, 1.0, land_ref[...].astype(jnp.float32))
        for i, factor in enumerate(stencil_factors([coefs_ref[0, c] for c in range(3)], keep)):
            factors[i] = factor
        rate = rates_ref[:, 0:1]
        near, far = pl.ds(0, nfield), pl.ds(nfield, nfield)
        last = corners_left.shape[1] - 1
        corner = (
            (corners_left[nfield : 2 * nfield, last:], corners_left[lines : lines + nfield, last:]),
            (corners_right[nfield : 2 * nfield, 0:1], corners_right[lines : lines + nfield, 0:1]),
        )
        for i, (ref, center, across, along, is_column) in enumerate(
            (
                (above, above[far, :], (above[near, :], x_low[near, :]), (corner[0][0], corner[1][0]), False),
                (below, below[near, :], (x_high[far, :], below[far, :]), (corner[0][1], corner[1][1]), False),
                (left, left[far, :], (left[near, :], y_low[near, :]), corner[0], True),
                (right, right[near, :], (y_high[far, :], right[far, :]), corner[1], True),
            )
        ):
            first = 2 * nfield
            of_line = stencil_factors(
                [ref[first + c : first + c + 1, :] for c in range(3)],
                ref[first + 3 : first + 4, :],
            )
            if is_column:
                of_line = [of_line[j] for j in (0, 3, 4, 1, 2, 5)]
            section = outer_section(center, across, along, of_line, rate)
            kept = cols if is_column else rows
            kept[pl.ds(i % 2 * nfield, nfield), :] = center
            kept[pl.ds((2 + i % 2) * nfield, nfield), :] = section

    rate = rate_ref[0, f]
    mix_a, mix_b = mix_ref[0, 0], mix_ref[0, 1]
    s = state_ref[0, 0]
    row = [rows[pl.ds(i * nfield + f, 1), :] for i in range(4)]
    col = columns_of(
        jnp.concatenate([cols[pl.ds(i * nfield + f, 1), :] for i in range(4)], axis=0)
    )
    s1 = s + tendency(s, rate, factors, row[0], row[1], col[:, 0:1], col[:, 1:2])
    more = tendency(s1, rate, factors, row[2], row[3], col[:, 2:3], col[:, 3:4])
    total = mix_a * s + (1.0 - mix_a) * s1 + mix_b * more
    out_ref[0, 0] = total

    @pl.when(f < half)
    def _():
        early_ref[0] = total


def base_of(state, coefs, land_sea, rates, mix, edges, received, corners, half):
    _, nfield, cells_x, cells_y = state.shape
    field = pl.BlockSpec((1, 1, cells_x, cells_y), lambda f: (0, f, 0, 0))
    whole = lambda a: pl.BlockSpec(a.shape, lambda f: (0,) * a.ndim)
    rates_wide = jnp.broadcast_to(rates.T, (nfield, LANES))
    operands = [rates_wide, coefs, land_sea, *edges, *received, *corners]
    return pl.pallas_call(
        functools.partial(base_kernel, half),
        grid=(nfield,),
        in_specs=[
            pl.BlockSpec(memory_space=pltpu.SMEM),
            pl.BlockSpec(memory_space=pltpu.SMEM),
            *[whole(a) for a in operands],
            field,
        ],
        out_specs=[
            field,
            pl.BlockSpec((1, cells_x, cells_y), lambda f: (jnp.minimum(f, half - 1), 0, 0)),
            pl.BlockSpec((6, cells_x, cells_y), lambda f: (0, 0, 0)),
        ],
        out_shape=[
            jax.ShapeDtypeStruct(state.shape, jnp.float32),
            jax.ShapeDtypeStruct((half, cells_x, cells_y), jnp.float32),
            jax.ShapeDtypeStruct((6, cells_x, cells_y), jnp.float32),
        ],
        scratch_shapes=[
            pltpu.VMEM((4 * nfield, cells_y), jnp.float32),
            pltpu.VMEM((4 * nfield, cells_x), jnp.float32),
        ],
        compiler_params=pltpu.CompilerParams(vmem_limit_bytes=16 * 1024 * 1024),
        cost_estimate=pl.CostEstimate(
            flops=40 * state.size, bytes_accessed=8 * state.size, transcendentals=0
        ),
        name="base",
    )(rates, mix, *operands, state)


def finish_kernel(first, with_x, gamma_ref, mix_ref, above, below, before, after, factors, recv,
                  left, right, *rest):
    tops, rest = (rest[:2], rest[2:]) if with_x else (None, rest)
    late, rest = (rest[:2], rest[2:]) if with_x else (None, rest)
    early_base, rest = (rest[0], rest[1:]) if with_x else (None, rest)
    base_ref, rest = rest[0], rest[1:]
    new_ref, out_ref, done_ref = rest[-11:-8]
    base, wide, lines, sides, outer, base_sems, out_sems, outer_sems = rest[-8:]
    count, cells_x, cells_y = base.shape
    mix_b = mix_ref[0, 1]
    keep_row = above.shape[0] - 5
    keep = slice(keep_row, keep_row + 1)
    ends = (0, cells_x - STRIP)

    def base_copy(f):
        return pltpu.make_async_copy(base_ref.at[0, first + f], base.at[f], base_sems.at[f])

    def out_copies(f):
        return (
            pltpu.make_async_copy(recv.at[f], out_ref.at[0, first + f], out_sems.at[0, f]),
            pltpu.make_async_copy(base.at[f], new_ref.at[0, first + f], out_sems.at[1, f]),
        )

    def outer_copy(f, i, back):
        there = (new_ref if back else base_ref).at[0, count + f, pl.ds(ends[i], STRIP), :]
        here = outer.at[f, i]
        pair = (here, there) if back else (there, here)
        return pltpu.make_async_copy(*pair, outer_sems.at[f, i])

    outer_rows = [(f, i) for f in range(count) for i in range(2)] if with_x else []
    if not with_x:
        for f in range(count):
            base_copy(f).start()
    for f, i in outer_rows:
        outer_copy(f, i, False).start()
    done_ref[...] = jnp.zeros_like(done_ref)
    if with_x:
        lines[:count, :] = tops[0][...] * above[keep, :]
        lines[count:, :] = tops[1][...] * below[keep, :]
    else:
        lines[...] = jnp.zeros_like(lines)
    sides[:count, :] = left[...] * before[keep, :]
    sides[count:, :] = right[...] * after[keep, :]
    lane = lax.broadcasted_iota(jnp.int32, (STRIP, cells_y), 1)

    def one_field(f, carry):
        rate = gamma_ref[0, first + f]
        both = [sides[pl.ds(f, 1), :] * rate, sides[pl.ds(count + f, 1), :] * rate]
        cols = columns_of(jnp.concatenate(both, axis=0))
        wide[STRIP - 1 : STRIP, :] = lines[pl.ds(f, 1), :] * rate
        wide[STRIP + cells_x : STRIP + cells_x + 1, :] = lines[pl.ds(count + f, 1), :] * rate
        to_out, to_new = out_copies(f)
        to_out.start()
        for i in range(0, cells_x, STRIP):
            rows = slice(i, i + STRIP)
            wide[STRIP + i : 2 * STRIP + i, :] = factors[0, rows, :] * recv[f, rows, :] * rate
        if not with_x:
            base_copy(f).wait()
        start = early_base if with_x else base
        for i in range(0, cells_x, STRIP):
            rows = slice(i, i + STRIP)
            mid = wide[STRIP + i : 2 * STRIP + i, :]
            more = (factors[5, rows, :] - rate * factors[0, rows, :]) * mid
            more += factors[1, rows, :] * wide[STRIP + i - 1 : 2 * STRIP + i - 1, :]
            more += factors[2, rows, :] * wide[STRIP + i + 1 : 2 * STRIP + i + 1, :]
            prior = jnp.where(lane == 0, cols[rows, 0:1], pltpu.roll(mid, 1, 1))
            later = jnp.where(lane == cells_y - 1, cols[rows, 1:2], pltpu.roll(mid, cells_y - 1, 1))
            more += factors[3, rows, :] * prior + factors[4, rows, :] * later
            base[f, rows, :] = start[f, rows, :] + mix_b * (2.0 * mid + more)
        to_new.start()
        return carry

    def add_lines():
        for f, i in outer_rows:
            outer_copy(f, i, False).wait()
            row = i * (STRIP - 1)
            at = ends[i] + row
            line = late[i][f : f + 1, :] * (above, below)[i][keep, :] * gamma_ref[0, count + f]
            more = mix_b * factors[1 + i, at : at + 1, :] * line
            outer[f, i, row : row + 1, :] = outer[f, i, row : row + 1, :] + more
            outer_copy(f, i, True).start()

    lax.fori_loop(0, count - 1, one_field, 0)
    add_lines()
    one_field(count - 1, 0)
    for f in range(count):
        for copy in out_copies(f):
            copy.wait()
    for f, i in outer_rows:
        outer_copy(f, i, True).wait()


def finished(
    first, new_state, remapped, recv, x_rims, y_rims, closing, gamma, mix, factors, received
):
    count, cells_x, cells_y = recv.shape
    chan = gamma.shape[1]
    with_x = x_rims is not None
    anywhere = pl.BlockSpec(memory_space=pl.ANY)
    operands = [gamma, mix, *received, factors, recv, *y_rims]
    if with_x:
        late_rims, base_early, late_done = closing
        operands += [*x_rims, *late_rims, base_early]
    specs = [pl.BlockSpec(memory_space=pltpu.SMEM)] * 2
    specs += [pl.BlockSpec(memory_space=pltpu.VMEM)] * (len(operands) - 2) + [anywhere]
    aliases = {len(operands): 0}
    operands.append(new_state)
    if remapped is not None:
        aliases[len(operands)] = 1
        operands += [remapped, late_done]
        specs += [anywhere, anywhere]
    return pl.pallas_call(
        functools.partial(finish_kernel, first, with_x),
        in_specs=specs,
        out_specs=[anywhere, anywhere, pl.BlockSpec(memory_space=pltpu.VMEM)],
        out_shape=[
            jax.ShapeDtypeStruct(new_state.shape, jnp.float32),
            jax.ShapeDtypeStruct((1, chan, cells_x, cells_y), jnp.float32),
            jax.ShapeDtypeStruct((8, LANES), jnp.float32),
        ],
        input_output_aliases=aliases,
        scratch_shapes=[
            pltpu.VMEM((count, cells_x, cells_y), jnp.float32),
            pltpu.VMEM((cells_x + 2 * STRIP, cells_y), jnp.float32),
            pltpu.VMEM((2 * count, cells_y), jnp.float32),
            pltpu.VMEM((2 * count, cells_x), jnp.float32),
            pltpu.VMEM((count, 2, STRIP, cells_y), jnp.float32),
            pltpu.SemaphoreType.DMA((count,)),
            pltpu.SemaphoreType.DMA((2, count)),
            pltpu.SemaphoreType.DMA((count, 2)),
        ],
        compiler_params=pltpu.CompilerParams(vmem_limit_bytes=12 * 1024 * 1024),
        cost_estimate=pl.CostEstimate(
            flops=20 * recv.size, bytes_accessed=20 * recv.size, transcendentals=0
        ),
        name="finish",
    )(*operands)


def body(state, coefs, land_sea, gamma, pair_src, pair_dev, pair_blk, weights):
    tx, ty = lax.axis_size("tx"), lax.axis_size("ty")
    tiles = tx * ty
    nfield, cells_x, cells_y = state.shape[1:]
    chan = gamma.shape[1]
    pairs, width = weights.shape[1], weights.shape[2]
    capacity = max(2, 2 * pairs // tiles)
    half = chan // 2
    early, late = contributions(
        state, pair_src, pair_dev, pair_blk, weights, tiles, capacity, chan
    )
    swap = [(0, 1), (1, 0)]

    def exchanged(rows):
        rows = rows.reshape(tiles, -1, half, width)
        return lax.all_to_all(rows, ("tx", "ty"), split_axis=0, concat_axis=0, tiled=True)

    def add_up(ids, rows, grant):
        return summed(ids, rows, tiles, capacity, half, cells_x, cells_y, width, grant)

    late_in = exchanged(late)
    early = lax.ppermute(early, "comp", swap)
    early_in = placed_rows(early, tiles, capacity, pairs, cells_x * cells_y // width)

    land_after, _ = lax.optimization_barrier((land_sea, late))
    is_atmos = lax.axis_index("comp") == 0
    mix = jnp.where(is_atmos, jnp.array([[0.0, 1.0]]), jnp.array([[0.5, 0.5]]))
    mix = mix.astype(jnp.float32)
    rates = jnp.concatenate([gamma, jnp.zeros((1, nfield - chan), jnp.float32)], axis=1)
    x_low, x_high, y_low, y_high = edges_of(state, coefs, land_after, mix)
    left = lax.ppermute(y_high, "ty", shift_pairs(ty, 1))
    right = lax.ppermute(y_low, "ty", shift_pairs(ty, -1))
    above = lax.ppermute(x_high, "tx", shift_pairs(tx, 1))
    below = lax.ppermute(x_low, "tx", shift_pairs(tx, -1))
    early_in, above, below, left, right = lax.optimization_barrier(
        (early_in, above, below, left, right)
    )
    received = (above, below, left, right)
    early_in = exchanged(early_in)

    ends = jnp.concatenate([above[:, cells_y - LANES :], below[:, cells_y - LANES :]], axis=0)
    starts = jnp.concatenate([above[:, :LANES], below[:, :LANES]], axis=0)
    corners_left = lax.ppermute(ends, "ty", shift_pairs(ty, 1))
    corners_right = lax.ppermute(starts, "ty", shift_pairs(ty, -1))
    base, base_early, factors = base_of(
        state, coefs, land_after, rates, mix, (x_low, x_high, y_low, y_high), received,
        (corners_left, corners_right), half,
    )

    ids_late = late_in[:, capacity, 0, :]
    ids_early = lax.ppermute(ids_late, "comp", swap)
    recv_late, top, bottom, left, right = add_up(ids_late, late_in, 56)
    recv_late = lax.ppermute(recv_late, "comp", swap)
    late_x = (
        lax.ppermute(bottom, ("comp", "tx"), crossed("tx", 1)),
        lax.ppermute(top, ("comp", "tx"), crossed("tx", -1)),
    )
    late_y = (
        lax.ppermute(right, ("comp", "ty"), crossed("ty", 1)),
        lax.ppermute(left, ("comp", "ty"), crossed("ty", -1)),
    )
    rest = (gamma, mix, factors, received)
    new_state, remapped, done = finished(
        half, base, None, recv_late, None, late_y, None, *rest
    )
    early_in, done = lax.optimization_barrier((early_in, done))
    recv_early, top, bottom, left, right = add_up(ids_early, early_in, 16)
    early_y = (
        lax.ppermute(right, "ty", shift_pairs(ty, 1)),
        lax.ppermute(left, "ty", shift_pairs(ty, -1)),
    )
    early_x = (
        lax.ppermute(bottom, "tx", shift_pairs(tx, 1)),
        lax.ppermute(top, "tx", shift_pairs(tx, -1)),
    )
    new_state, remapped, _ = finished(
        0, new_state, remapped, recv_early, early_x, early_y, (late_x, base_early, done), *rest
    )
    return new_state, remapped


def solution(mesh):
    placed = (
        P("comp", None, "tx", "ty"),
        P("comp", None, "tx", "ty"),
        P("tx", "ty"),
        P("comp", None),
        P("comp", ("tx", "ty")),
        P("comp", ("tx", "ty"), None),
        P("comp", ("tx", "ty")),
        P("comp", ("tx", "ty"), None, None),
    )
    return jax.shard_map(
        body,
        mesh=mesh,
        in_specs=placed,
        out_specs=(P("comp", None, "tx", "ty"), P("comp", None, "tx", "ty")),
        check_vma=False,
    )
```

```python
import functools

import jax
import jax.numpy as jnp
from jax import lax
from jax.experimental import pallas as pl
from jax.experimental.pallas import tpu as pltpu
from jax.sharding import PartitionSpec as P

LANES = 128
STEP_PAIRS = 64
STRIP = 8
NT = (((1,), (1,)), ((), ()))


def shift_pairs(count, by):
    return [(i, i + by) for i in range(count) if 0 <= i + by < count]


def neighbour_pairs(count, first):
    lows = range(first, count - 1, 2)
    return [(i, i + 1) for i in lows] + [(i + 1, i) for i in lows]


def crossed(axis, by):
    count = lax.axis_size(axis)
    return [
        (c * count + i, (1 - c) * count + j) for c in range(2) for i, j in shift_pairs(count, by)
    ]


def split(value, parts):
    if parts & (parts - 1) == 0:
        return lax.shift_right_logical(value, parts.bit_length() - 1), value & (parts - 1)
    return lax.div(value, parts), lax.rem(value, parts)


def ranks(dev, tiles):
    pairs = dev.shape[1]
    tile_of = lax.broadcasted_iota(jnp.int32, (tiles, pairs), 0)
    lane_of = lax.broadcasted_iota(jnp.int32, (tiles, pairs), 1)
    member = (tile_of == dev).astype(jnp.float32)
    total = member
    shift = 1
    while shift < pairs:
        total = total + jnp.where(lane_of >= shift, pltpu.roll(total, shift, 1), 0.0)
        shift *= 2
    return member, (jnp.sum(member * total, axis=0, keepdims=True) - 1.0).astype(jnp.int32)


def slot_blocks(dev, blk, tiles, capacity):
    member, rank = ranks(dev, tiles)
    pairs = dev.shape[1]
    slot_of = lax.broadcasted_iota(jnp.int32, (LANES, pairs), 0) % capacity
    chosen = (slot_of == rank).astype(jnp.bfloat16)

    def spread(values):
        return lax.dot_general(
            (member * values).astype(jnp.bfloat16), chosen, NT, preferred_element_type=jnp.float32
        )

    high, low = split(blk, 256)
    ids = spread(high.astype(jnp.float32)) * 256.0 + spread(low.astype(jnp.float32))
    return jnp.where(spread(jnp.ones(dev.shape, jnp.float32)) > 0.5, ids, -1.0)


def contribution_kernel(
    dims, src_ref, dev_ref, blk_ref, state_ref, weights_ref, early_out, late_ref,
    cells, w_ref, early_ref, pair_v, pair_s, taken, field_sems, weight_sems, early_sems, pair_sems,
):
    tiles, capacity, pairs, fields, cells_x, cells_y, width = dims
    half = fields // 2
    parts = cells_y // width
    steps = pairs // STEP_PAIRS

    scalar_copies = [
        pltpu.make_async_copy(ref, pair_s.at[pl.ds(i, 1), :], pair_sems.at[i])
        for i, ref in enumerate((src_ref, dev_ref))
    ]
    vector_copies = [
        pltpu.make_async_copy(ref, pair_v.at[i], pair_sems.at[2 + i])
        for i, ref in enumerate((dev_ref, blk_ref))
    ]
    field_copies = [
        pltpu.make_async_copy(
            state_ref.at[0, f, :, pl.ds(q * width, width)],
            cells.at[q, :, f, :],
            field_sems.at[f * parts + q],
        )
        for f in range(fields)
        for q in range(parts)
    ]

    def weight_copy(step):
        some = pl.ds(step * STEP_PAIRS, STEP_PAIRS)
        return pltpu.make_async_copy(
            weights_ref.at[0, some], w_ref.at[some], weight_sems.at[step]
        )

    def early_copy(step):
        first, count = step * STEP_PAIRS, STEP_PAIRS
        if isinstance(step, int) and step == steps:
            count = early_ref.shape[0] - pairs
        some = pl.ds(first, count)
        return pltpu.make_async_copy(early_ref.at[some], early_out.at[some], early_sems.at[step])

    for copy in scalar_copies + vector_copies + field_copies:
        copy.start()
    for step in range(steps):
        weight_copy(step).start()
    late_ref[...] = jnp.zeros_like(late_ref)
    for t in range(tiles):
        taken[t] = t * (capacity + 1)

    for copy in vector_copies:
        copy.wait()
    dev, blk = pair_v[0], pair_v[1]
    ids = slot_blocks(dev, blk, tiles, capacity)
    for t in range(tiles):
        row = jnp.broadcast_to(ids[t : t + 1, :], late_ref.shape[1:])
        late_ref[t * (capacity + 1) + capacity] = row
    code = (dev * (cells_x * parts) + blk).astype(jnp.float32)
    for i in range(pairs // width):
        place = (pairs + i // half, slice(i % half, i % half + 1), slice(None))
        early_ref[place] = code[:, i * width : (i + 1) * width]
    early_copy(steps).start()
    for copy in scalar_copies + field_copies:
        copy.wait()

    def cells_of(p):
        x, part = split(pair_s[0, p], parts)
        return cells[part, x]

    zeros = jnp.zeros((fields, width), jnp.float32)

    def some_pairs(step, carry):
        weight_copy(step).wait()
        for i in range(0, STEP_PAIRS, 4):
            p = step * STEP_PAIRS + i
            left = [
                jnp.concatenate([cells_of(p + j), zeros][:: 1 - j % 2 * 2], axis=1) for j in range(4)
            ]
            left = jnp.concatenate(left, axis=0).astype(jnp.bfloat16)
            w = [w_ref[p + j] for j in range(4)]
            right = jnp.concatenate(
                [jnp.concatenate(w[:2], axis=1), jnp.concatenate(w[2:], axis=1)], axis=0
            )
            four = lax.dot_general(left, right, NT, preferred_element_type=jnp.float32)
            for j in range(4):
                tile = pair_s[1, p + j]
                slot = taken[tile]
                taken[tile] = slot + 1
                at = j // 2 * width
                one = four[j * fields : (j + 1) * fields, at : at + width]
                early_ref[p + j] = one[:half]
                late_ref[slot] = one[half:]
        early_copy(step).start()
        return carry

    lax.fori_loop(0, steps, some_pairs, 0)
    for step in range(steps + 1):
        early_copy(step).wait()


def contributions(state, pair_src, pair_dev, pair_blk, weights, tiles, capacity, fields):
    _, _, cells_x, cells_y = state.shape
    half = fields // 2
    pairs, width = weights.shape[1], weights.shape[2]
    rows = tiles * (capacity + 1)
    dims = (tiles, capacity, pairs, fields, cells_x, cells_y, width)
    parts = cells_y // width
    shapes = [(pairs + -(-pairs // (half * width)), half, width), (rows, half, width)]
    return pl.pallas_call(
        functools.partial(contribution_kernel, dims),
        in_specs=[pl.BlockSpec(memory_space=pltpu.HBM)] * 5,
        out_specs=[
            pl.BlockSpec(memory_space=pl.ANY),
            pl.BlockSpec(memory_space=pltpu.VMEM),
        ],
        out_shape=[jax.ShapeDtypeStruct(shape, jnp.float32) for shape in shapes],
        scratch_shapes=[
            pltpu.VMEM((parts, cells_x, fields, width), jnp.float32),
            pltpu.VMEM((pairs, width, width), jnp.bfloat16),
            pltpu.VMEM(shapes[0], jnp.float32),
            pltpu.VMEM((2, 1, pairs), jnp.int32),
            pltpu.SMEM((2, pairs), jnp.int32),
            pltpu.SMEM((tiles,), jnp.int32),
            pltpu.SemaphoreType.DMA((parts * fields,)),
            pltpu.SemaphoreType.DMA((pairs // STEP_PAIRS,)),
            pltpu.SemaphoreType.DMA((pairs // STEP_PAIRS + 1,)),
            pltpu.SemaphoreType.DMA((4,)),
        ],
        compiler_params=pltpu.CompilerParams(vmem_limit_bytes=56 * 1024 * 1024),
        cost_estimate=pl.CostEstimate(
            flops=2 * pairs * fields * width * width,
            bytes_accessed=2 * pairs * width * width + 8 * rows * fields * width,
            transcendentals=0,
        ),
        name="contributions",
    )(pair_src, pair_dev.reshape(1, pairs), pair_blk, state, weights)


def place_kernel(dims, in_ref, out_ref, place_v, place_s, place_sem):
    tiles, capacity, pairs, blocks = dims
    half, width = in_ref.shape[1:]
    code = jnp.concatenate(
        [in_ref[pairs + i // half][i % half : i % half + 1] for i in range(pairs // width)], axis=1
    ).astype(jnp.int32)
    dev, _ = split(code, blocks)
    rank = ranks(dev, tiles)[1]
    place_v[...] = jnp.broadcast_to(dev * capacity + rank, place_v.shape)
    copy = pltpu.make_async_copy(place_v, place_s, place_sem)
    copy.start()
    out_ref[...] = jnp.zeros_like(out_ref)
    copy.wait()

    def some_rows(step, carry):
        for i in range(STEP_PAIRS):
            p = step * STEP_PAIRS + i
            out_ref[place_s[0, p]] = in_ref[p]
        return carry

    lax.fori_loop(0, pairs // STEP_PAIRS, some_rows, 0)


def placed_rows(rows, tiles, capacity, pairs, blocks):
    half, width = rows.shape[1:]
    shape = (tiles * capacity, half, width)
    return pl.pallas_call(
        functools.partial(place_kernel, (tiles, capacity, pairs, blocks)),
        out_shape=jax.ShapeDtypeStruct(shape, jnp.float32),
        scratch_shapes=[
            pltpu.VMEM((8, pairs), jnp.int32),
            pltpu.SMEM((8, pairs), jnp.int32),
            pltpu.SemaphoreType.DMA,
        ],
        compiler_params=pltpu.CompilerParams(vmem_limit_bytes=10 * 1024 * 1024),
        cost_estimate=pl.CostEstimate(
            flops=4 * rows.size, bytes_accessed=12 * rows.size, transcendentals=0
        ),
        name="place_in_slots",
    )(rows)


def sum_kernel(dims, odd_ref, ids_ref, rows_ref, out_ref, x0_ref, x1_ref, y0_ref, y1_ref,
               in_ref, pick, high, low, row_sems):
    tiles, capacity, fields, cells_x, cells_y, width = dims
    parts = cells_y // width
    group = LANES // capacity
    stride = in_ref.shape[0] // tiles

    def rows_copy(k):
        some = pl.ds(k * group * stride, group * stride)
        return pltpu.make_async_copy(rows_ref.at[some, :], in_ref.at[some, :], row_sems.at[k])

    for k in range(tiles // group):
        rows_copy(k).start()
    block_of = lax.broadcasted_iota(jnp.int32, (cells_x * parts, LANES), 0)
    block_of = (block_of % cells_x) * parts + block_of // cells_x
    block_of = block_of.astype(jnp.float32)
    lane = lax.broadcasted_iota(jnp.int32, (1, LANES), 1)
    for k in range(tiles // group):
        ids = None
        for i in range(group):
            row = ids_ref[pl.ds(k * group + i, 1), :]
            ids = row if ids is None else jnp.where(lane // capacity == i, row, ids)
        pick[:, pl.ds(k * LANES, LANES)] = (block_of == ids).astype(jnp.bfloat16)
    for k in range(tiles // group):
        rows_copy(k).wait()
        for source in range(k * group, (k + 1) * group):
            for f in range(fields):
                x = in_ref[pl.ds(source * stride + f, capacity, stride=fields), :]
                rounded = x.astype(jnp.bfloat16)
                place = (
                    pl.ds(source * capacity, capacity),
                    pl.ds(f * width, width),
                )
                high[place] = rounded
                low[place] = (x - rounded.astype(jnp.float32)).astype(jnp.bfloat16)
    odd_x, odd_y = odd_ref[0, 0] == 1, odd_ref[0, 1] == 1
    columns = {}
    for q in range(parts):
        chosen = pick[pl.ds(q * cells_x, cells_x), :]
        total = jnp.dot(chosen, high[...], preferred_element_type=jnp.float32)
        total = total + jnp.dot(chosen, low[...], preferred_element_type=jnp.float32)
        for f in range(fields):
            tile = total[:, f * width : (f + 1) * width]
            out_ref[f, :, pl.ds(q * width, width)] = tile
            top, bottom = tile[:1], tile[cells_x - 1 :]
            x0_ref[pl.ds(f, 1), pl.ds(q * width, width)] = jnp.where(odd_x, bottom, top)
            x1_ref[pl.ds(f, 1), pl.ds(q * width, width)] = jnp.where(odd_x, top, bottom)
            if q in (0, parts - 1):
                columns[q, f] = tile.T[:1] if q == 0 else tile.T[width - 1 :]
    for f in range(fields):
        left, right = columns[0, f], columns[parts - 1, f]
        y0_ref[pl.ds(f, 1), :] = jnp.where(odd_y, right, left)
        y1_ref[pl.ds(f, 1), :] = jnp.where(odd_y, left, right)


def summed(odd, ids, rows, tiles, capacity, fields, cells_x, cells_y, width, grant):
    dims = (tiles, capacity, fields, cells_x, cells_y, width)
    rows = rows.reshape(-1, width)
    slots = tiles * capacity
    blocks = cells_x * cells_y // width
    shapes = [
        (fields, cells_x, cells_y),
        (fields, cells_y),
        (fields, cells_y),
        (fields, cells_x),
        (fields, cells_x),
    ]
    return pl.pallas_call(
        functools.partial(sum_kernel, dims),
        in_specs=[
            pl.BlockSpec(memory_space=pltpu.SMEM),
            pl.BlockSpec(memory_space=pltpu.VMEM),
            pl.BlockSpec(memory_space=pl.ANY),
        ],
        out_shape=[jax.ShapeDtypeStruct(shape, jnp.float32) for shape in shapes],
        scratch_shapes=[
            pltpu.VMEM(rows.shape, jnp.float32),
            pltpu.VMEM((blocks, slots), jnp.bfloat16),
            pltpu.VMEM((slots, fields * width), jnp.bfloat16),
            pltpu.VMEM((slots, fields * width), jnp.bfloat16),
            pltpu.SemaphoreType.DMA((tiles * capacity // LANES,)),
        ],
        compiler_params=pltpu.CompilerParams(vmem_limit_bytes=grant * 1024 * 1024),
        cost_estimate=pl.CostEstimate(
            flops=4 * blocks * slots * fields * width,
            bytes_accessed=4 * fields * width * (slots + blocks),
            transcendentals=0,
        ),
        name="sum_by_block",
    )(odd, ids, rows)


def stencil_factors(coefs, keep):
    u, v, kappa = coefs
    return [
        keep,
        keep * (jnp.maximum(u, 0.0) + kappa),
        keep * (kappa - jnp.minimum(u, 0.0)),
        keep * (jnp.maximum(v, 0.0) + kappa),
        keep * (kappa - jnp.minimum(v, 0.0)),
        -keep * (jnp.abs(u) + jnp.abs(v) + 4.0 * kappa),
    ]


def tendency(s, rate, factors, top, bottom, left, right):
    cells_x, cells_y = s.shape
    x_of = lax.broadcasted_iota(jnp.int32, s.shape, 0)
    y_of = lax.broadcasted_iota(jnp.int32, s.shape, 1)
    out = (factors[5] - rate * factors[0]) * s
    out += factors[1] * jnp.where(x_of == 0, top, pltpu.roll(s, 1, 0))
    out += factors[2] * jnp.where(x_of == cells_x - 1, bottom, pltpu.roll(s, cells_x - 1, 0))
    out += factors[3] * jnp.where(y_of == 0, left, pltpu.roll(s, 1, 1))
    out += factors[4] * jnp.where(y_of == cells_y - 1, right, pltpu.roll(s, cells_y - 1, 1))
    return out


def columns_of(rows):
    spare = 8 - rows.shape[0]
    if spare:
        rows = jnp.concatenate([rows, jnp.zeros((spare, rows.shape[1]), rows.dtype)], axis=0)
    return rows.T


def line_count(nfield):
    return 2 * nfield + 8


def edge_kernel(mix_ref, state_tops, state_ends, state_lefts, state_rights, coefs_tops, coefs_ends,
                coefs_lefts, coefs_rights, land_tops, land_ends, land_lefts, land_rights,
                x_low, x_high, y_low, y_high):
    nfield = state_tops.shape[1]
    last_row, last_lane = state_tops.shape[2] - 1, state_lefts.shape[3] - 1
    atmos = mix_ref[0, 1] == 1.0

    def kept(land):
        return jnp.where(atmos, 1.0, land.astype(jnp.float32))

    for out, state, coefs, land, lines in (
        (x_low, state_tops, coefs_tops, land_tops, (0, 1)),
        (x_high, state_ends, coefs_ends, land_ends, (last_row - 1, last_row)),
    ):
        outer = lines[0] if lines[0] == 0 else lines[1]
        out[2 * nfield :, :] = jnp.zeros((8, out.shape[1]), jnp.float32)
        for j, line in enumerate(lines):
            for f in range(nfield):
                out[j * nfield + f : j * nfield + f + 1, :] = state[0, f, line : line + 1, :]
        for c in range(3):
            out[2 * nfield + c : 2 * nfield + c + 1, :] = coefs[0, c, outer : outer + 1, :]
        out[2 * nfield + 3 : 2 * nfield + 4, :] = kept(land[outer : outer + 1, :])

    for out, state, coefs, land, lines in (
        (y_low, state_lefts, coefs_lefts, land_lefts, (0, 1)),
        (y_high, state_rights, coefs_rights, land_rights, (last_lane - 1, last_lane)),
    ):
        outer = lines[0] if lines[0] == 0 else lines[1]
        lane = lax.broadcasted_iota(jnp.int32, land.shape, 1)
        packed = jnp.zeros(land.shape, jnp.float32)

        def put(packed, tile, at, to):
            moved = (to - at) % LANES
            tile = pltpu.roll(tile, moved, 1) if moved else tile
            return jnp.where(lane == to, tile, packed)

        for j, line in enumerate(lines):
            for f in range(nfield):
                packed = put(packed, state[0, f], line, j * nfield + f)
        for c in range(3):
            packed = put(packed, coefs[0, c], outer, 2 * nfield + c)
        packed = put(packed, kept(land[...]), outer, 2 * nfield + 3)
        out[...] = packed.T[: out.shape[0]]


def edges_of(state, coefs, land_sea, mix):
    _, nfield, cells_x, cells_y = state.shape
    lines = line_count(nfield)
    ends = [
        ((8, cells_y), (0, 0)),
        ((8, cells_y), (cells_x // 8 - 1, 0)),
        ((cells_x, LANES), (0, 0)),
        ((cells_x, LANES), (0, cells_y // LANES - 1)),
    ]
    at = lambda lead, place: lambda i: (0,) * len(lead) + place
    specs = [pl.BlockSpec(memory_space=pltpu.SMEM)]
    for lead in ((1, nfield), (1, 3), ()):
        specs += [pl.BlockSpec(lead + shape, at(lead, place)) for shape, place in ends]
    shapes = [(lines, cells_y)] * 2 + [(lines, cells_x)] * 2
    return pl.pallas_call(
        edge_kernel,
        grid=(1,),
        in_specs=specs,
        out_specs=[pl.BlockSpec(shape, lambda i: (0, 0)) for shape in shapes],
        out_shape=[jax.ShapeDtypeStruct(shape, jnp.float32) for shape in shapes],
        compiler_params=pltpu.CompilerParams(vmem_limit_bytes=24 * 1024 * 1024),
        cost_estimate=pl.CostEstimate(
            flops=state.size, bytes_accessed=4 * 1024 * 1024, transcendentals=0
        ),
        name="edges",
    )(mix, *[state] * 4, *[coefs] * 4, *[land_sea] * 4)


def outer_section(center, across, along, factors, rate):
    lane = lax.broadcasted_iota(jnp.int32, center.shape, 1)
    count = center.shape[1]
    before = jnp.where(lane == 0, along[0], pltpu.roll(center, 1, 1))
    after = jnp.where(lane == count - 1, along[1], pltpu.roll(center, count - 1, 1))
    keep, low, high, back, ahead, middle = factors
    out = center + low * across[0] + high * across[1] + back * before + ahead * after
    return out + (middle - rate * keep) * center


def base_kernel(half, rate_ref, mix_ref, rates_ref, coefs_ref, land_ref, x_low, x_high, y_low, y_high,
                above, below, left, right, corners_left, corners_right, state_ref,
                out_ref, early_ref, factors, rows, cols):
    f = pl.program_id(0)
    nfield = rates_ref.shape[0]
    lines = line_count(nfield)

    @pl.when(f == 0)
    def _():
        keep = jnp.where(mix_ref[0, 1] == 1.0, 1.0, land_ref[...].astype(jnp.float32))
        for i, factor in enumerate(stencil_factors([coefs_ref[0, c] for c in range(3)], keep)):
            factors[i] = factor
        rate = rates_ref[:, 0:1]
        near, far = pl.ds(0, nfield), pl.ds(nfield, nfield)
        last = corners_left.shape[1] - 1
        corner = (
            (corners_left[nfield : 2 * nfield, last:], corners_left[lines : lines + nfield, last:]),
            (corners_right[nfield : 2 * nfield, 0:1], corners_right[lines : lines + nfield, 0:1]),
        )
        for i, (ref, center, across, along, is_column) in enumerate(
            (
                (above, above[far, :], (above[near, :], x_low[near, :]), (corner[0][0], corner[1][0]), False),
                (below, below[near, :], (x_high[far, :], below[far, :]), (corner[0][1], corner[1][1]), False),
                (left, left[far, :], (left[near, :], y_low[near, :]), corner[0], True),
                (right, right[near, :], (y_high[far, :], right[far, :]), corner[1], True),
            )
        ):
            first = 2 * nfield
            of_line = stencil_factors(
                [ref[first + c : first + c + 1, :] for c in range(3)],
                ref[first + 3 : first + 4, :],
            )
            if is_column:
                of_line = [of_line[j] for j in (0, 3, 4, 1, 2, 5)]
            section = outer_section(center, across, along, of_line, rate)
            kept = cols if is_column else rows
            kept[pl.ds(i % 2 * nfield, nfield), :] = center
            kept[pl.ds((2 + i % 2) * nfield, nfield), :] = section

    rate = rate_ref[0, f]
    mix_a, mix_b = mix_ref[0, 0], mix_ref[0, 1]
    s = state_ref[0, 0]
    row = [rows[pl.ds(i * nfield + f, 1), :] for i in range(4)]
    col = columns_of(
        jnp.concatenate([cols[pl.ds(i * nfield + f, 1), :] for i in range(4)], axis=0)
    )
    s1 = s + tendency(s, rate, factors, row[0], row[1], col[:, 0:1], col[:, 1:2])
    more = tendency(s1, rate, factors, row[2], row[3], col[:, 2:3], col[:, 3:4])
    total = mix_a * s + (1.0 - mix_a) * s1 + mix_b * more
    out_ref[0, 0] = total

    @pl.when(f < half)
    def _():
        early_ref[0] = total


def base_of(state, coefs, land_sea, rates, mix, edges, received, corners, half):
    _, nfield, cells_x, cells_y = state.shape
    field = pl.BlockSpec((1, 1, cells_x, cells_y), lambda f: (0, f, 0, 0))
    whole = lambda a: pl.BlockSpec(a.shape, lambda f: (0,) * a.ndim)
    rates_wide = jnp.broadcast_to(rates.T, (nfield, LANES))
    operands = [rates_wide, coefs, land_sea, *edges, *received, *corners]
    return pl.pallas_call(
        functools.partial(base_kernel, half),
        grid=(nfield,),
        in_specs=[
            pl.BlockSpec(memory_space=pltpu.SMEM),
            pl.BlockSpec(memory_space=pltpu.SMEM),
            *[whole(a) for a in operands],
            field,
        ],
        out_specs=[
            field,
            pl.BlockSpec((1, cells_x, cells_y), lambda f: (jnp.minimum(f, half - 1), 0, 0)),
            pl.BlockSpec((6, cells_x, cells_y), lambda f: (0, 0, 0)),
        ],
        out_shape=[
            jax.ShapeDtypeStruct(state.shape, jnp.float32),
            jax.ShapeDtypeStruct((half, cells_x, cells_y), jnp.float32),
            jax.ShapeDtypeStruct((6, cells_x, cells_y), jnp.float32),
        ],
        scratch_shapes=[
            pltpu.VMEM((4 * nfield, cells_y), jnp.float32),
            pltpu.VMEM((4 * nfield, cells_x), jnp.float32),
        ],
        compiler_params=pltpu.CompilerParams(vmem_limit_bytes=16 * 1024 * 1024),
        cost_estimate=pl.CostEstimate(
            flops=40 * state.size, bytes_accessed=8 * state.size, transcendentals=0
        ),
        name="base",
    )(rates, mix, *operands, state)


def finish_kernel(first, with_x, gamma_ref, mix_ref, above, below, before, after, factors, recv,
                  left, right, *rest):
    tops, rest = (rest[:2], rest[2:]) if with_x else (None, rest)
    late, rest = (rest[:2], rest[2:]) if with_x else (None, rest)
    early_base, odd_ref, rest = (*rest[:2], rest[2:]) if with_x else (None, None, rest)
    base_ref, rest = rest[0], rest[1:]
    new_ref, out_ref, done_ref = rest[-11:-8]
    base, wide, lines, sides, outer, base_sems, out_sems, outer_sems = rest[-8:]
    count, cells_x, cells_y = base.shape
    mix_b = mix_ref[0, 1]
    keep_row = above.shape[0] - 5
    keep = slice(keep_row, keep_row + 1)
    ends = (0, cells_x - STRIP)

    def base_copy(f):
        return pltpu.make_async_copy(base_ref.at[0, first + f], base.at[f], base_sems.at[f])

    def out_copies(f):
        return (
            pltpu.make_async_copy(recv.at[f], out_ref.at[0, first + f], out_sems.at[0, f]),
            pltpu.make_async_copy(base.at[f], new_ref.at[0, first + f], out_sems.at[1, f]),
        )

    def outer_copy(f, i, back):
        there = (new_ref if back else base_ref).at[0, count + f, pl.ds(ends[i], STRIP), :]
        here = outer.at[f, i]
        pair = (here, there) if back else (there, here)
        return pltpu.make_async_copy(*pair, outer_sems.at[f, i])

    outer_rows = [(f, i) for f in range(count) for i in range(2)] if with_x else []
    if not with_x:
        for f in range(count):
            base_copy(f).start()
    for f, i in outer_rows:
        outer_copy(f, i, False).start()
    done_ref[...] = jnp.zeros_like(done_ref)
    if with_x:
        for i, (pair, kept, low_keep, high_keep) in enumerate(
            ((tops, lines, above, below), ((left, right), sides, before, after))
        ):
            odd = odd_ref[0, i] == 1
            in_odd, in_even = pair[0][...], pair[1][...]
            kept[:count, :] = jnp.where(odd, in_even, in_odd) * low_keep[keep, :]
            kept[count:, :] = jnp.where(odd, in_odd, in_even) * high_keep[keep, :]
    else:
        lines[...] = jnp.zeros_like(lines)
        sides[:count, :] = left[...] * before[keep, :]
        sides[count:, :] = right[...] * after[keep, :]
    lane = lax.broadcasted_iota(jnp.int32, (STRIP, cells_y), 1)

    def one_field(f, carry):
        rate = gamma_ref[0, first + f]
        both = [sides[pl.ds(f, 1), :] * rate, sides[pl.ds(count + f, 1), :] * rate]
        cols = columns_of(jnp.concatenate(both, axis=0))
        wide[STRIP - 1 : STRIP, :] = lines[pl.ds(f, 1), :] * rate
        wide[STRIP + cells_x : STRIP + cells_x + 1, :] = lines[pl.ds(count + f, 1), :] * rate
        to_out, to_new = out_copies(f)
        to_out.start()
        for i in range(0, cells_x, STRIP):
            rows = slice(i, i + STRIP)
            wide[STRIP + i : 2 * STRIP + i, :] = factors[0, rows, :] * recv[f, rows, :] * rate
        if not with_x:
            base_copy(f).wait()
        start = early_base if with_x else base
        for i in range(0, cells_x, STRIP):
            rows = slice(i, i + STRIP)
            mid = wide[STRIP + i : 2 * STRIP + i, :]
            more = (factors[5, rows, :] - rate * factors[0, rows, :]) * mid
            more += factors[1, rows, :] * wide[STRIP + i - 1 : 2 * STRIP + i - 1, :]
            more += factors[2, rows, :] * wide[STRIP + i + 1 : 2 * STRIP + i + 1, :]
            prior = jnp.where(lane == 0, cols[rows, 0:1], pltpu.roll(mid, 1, 1))
            later = jnp.where(lane == cells_y - 1, cols[rows, 1:2], pltpu.roll(mid, cells_y - 1, 1))
            more += factors[3, rows, :] * prior + factors[4, rows, :] * later
            base[f, rows, :] = start[f, rows, :] + mix_b * (2.0 * mid + more)
        to_new.start()
        return carry

    def add_lines():
        for f, i in outer_rows:
            outer_copy(f, i, False).wait()
            row = i * (STRIP - 1)
            at = ends[i] + row
            line = late[i][f : f + 1, :] * (above, below)[i][keep, :] * gamma_ref[0, count + f]
            more = mix_b * factors[1 + i, at : at + 1, :] * line
            outer[f, i, row : row + 1, :] = outer[f, i, row : row + 1, :] + more
            outer_copy(f, i, True).start()

    lax.fori_loop(0, count - 1, one_field, 0)
    add_lines()
    one_field(count - 1, 0)
    for f in range(count):
        for copy in out_copies(f):
            copy.wait()
    for f, i in outer_rows:
        outer_copy(f, i, True).wait()


def finished(
    first, new_state, remapped, recv, x_rims, y_rims, closing, gamma, mix, factors, received
):
    count, cells_x, cells_y = recv.shape
    chan = gamma.shape[1]
    with_x = x_rims is not None
    anywhere = pl.BlockSpec(memory_space=pl.ANY)
    operands = [gamma, mix, *received, factors, recv, *y_rims]
    if with_x:
        late_rims, base_early, odd, late_done = closing
        operands += [*x_rims, *late_rims, base_early]
    scalars = pl.BlockSpec(memory_space=pltpu.SMEM)
    specs = [scalars] * 2 + [pl.BlockSpec(memory_space=pltpu.VMEM)] * (len(operands) - 2)
    if with_x:
        operands.append(odd)
        specs.append(scalars)
    specs.append(anywhere)
    aliases = {len(operands): 0}
    operands.append(new_state)
    if remapped is not None:
        aliases[len(operands)] = 1
        operands += [remapped, late_done]
        specs += [anywhere, anywhere]
    return pl.pallas_call(
        functools.partial(finish_kernel, first, with_x),
        in_specs=specs,
        out_specs=[anywhere, anywhere, pl.BlockSpec(memory_space=pltpu.VMEM)],
        out_shape=[
            jax.ShapeDtypeStruct(new_state.shape, jnp.float32),
            jax.ShapeDtypeStruct((1, chan, cells_x, cells_y), jnp.float32),
            jax.ShapeDtypeStruct((8, LANES), jnp.float32),
        ],
        input_output_aliases=aliases,
        scratch_shapes=[
            pltpu.VMEM((count, cells_x, cells_y), jnp.float32),
            pltpu.VMEM((cells_x + 2 * STRIP, cells_y), jnp.float32),
            pltpu.VMEM((2 * count, cells_y), jnp.float32),
            pltpu.VMEM((2 * count, cells_x), jnp.float32),
            pltpu.VMEM((count, 2, STRIP, cells_y), jnp.float32),
            pltpu.SemaphoreType.DMA((count,)),
            pltpu.SemaphoreType.DMA((2, count)),
            pltpu.SemaphoreType.DMA((count, 2)),
        ],
        compiler_params=pltpu.CompilerParams(vmem_limit_bytes=12 * 1024 * 1024),
        cost_estimate=pl.CostEstimate(
            flops=20 * recv.size, bytes_accessed=20 * recv.size, transcendentals=0
        ),
        name="finish",
    )(*operands)


def body(state, coefs, land_sea, gamma, pair_src, pair_dev, pair_blk, weights):
    tx, ty = lax.axis_size("tx"), lax.axis_size("ty")
    tiles = tx * ty
    nfield, cells_x, cells_y = state.shape[1:]
    chan = gamma.shape[1]
    pairs, width = weights.shape[1], weights.shape[2]
    capacity = max(2, 2 * pairs // tiles)
    half = chan // 2
    early, late = contributions(
        state, pair_src, pair_dev, pair_blk, weights, tiles, capacity, chan
    )
    swap = [(0, 1), (1, 0)]

    def exchanged(rows):
        rows = rows.reshape(tiles, -1, half, width)
        return lax.all_to_all(rows, ("tx", "ty"), split_axis=0, concat_axis=0, tiled=True)

    def add_up(odd, ids, rows, grant):
        return summed(odd, ids, rows, tiles, capacity, half, cells_x, cells_y, width, grant)

    late_in = exchanged(late)
    early = lax.ppermute(early, "comp", swap)
    early_in = placed_rows(early, tiles, capacity, pairs, cells_x * cells_y // width)

    land_after, _ = lax.optimization_barrier((land_sea, late))
    is_atmos = lax.axis_index("comp") == 0
    mix = jnp.where(is_atmos, jnp.array([[0.0, 1.0]]), jnp.array([[0.5, 0.5]]))
    mix = mix.astype(jnp.float32)
    rates = jnp.concatenate([gamma, jnp.zeros((1, nfield - chan), jnp.float32)], axis=1)
    x_low, x_high, y_low, y_high = edges_of(state, coefs, land_after, mix)
    left = lax.ppermute(y_high, "ty", shift_pairs(ty, 1))
    right = lax.ppermute(y_low, "ty", shift_pairs(ty, -1))
    above = lax.ppermute(x_high, "tx", shift_pairs(tx, 1))
    below = lax.ppermute(x_low, "tx", shift_pairs(tx, -1))
    early_in, above, below, left, right = lax.optimization_barrier(
        (early_in, above, below, left, right)
    )
    received = (above, below, left, right)
    early_in = exchanged(early_in)

    ends = jnp.concatenate([above[:, cells_y - LANES :], below[:, cells_y - LANES :]], axis=0)
    starts = jnp.concatenate([above[:, :LANES], below[:, :LANES]], axis=0)
    corners_left = lax.ppermute(ends, "ty", shift_pairs(ty, 1))
    corners_right = lax.ppermute(starts, "ty", shift_pairs(ty, -1))
    base, base_early, factors = base_of(
        state, coefs, land_after, rates, mix, (x_low, x_high, y_low, y_high), received,
        (corners_left, corners_right), half,
    )

    ids_late = late_in[:, capacity, 0, :]
    ids_early = lax.ppermute(ids_late, "comp", swap)
    recv_late, top, bottom, left, right = add_up(jnp.zeros((1, 2), jnp.int32), ids_late, late_in, 56)
    recv_late = lax.ppermute(recv_late, "comp", swap)
    late_x = (
        lax.ppermute(bottom, ("comp", "tx"), crossed("tx", 1)),
        lax.ppermute(top, ("comp", "tx"), crossed("tx", -1)),
    )
    late_y = (
        lax.ppermute(right, ("comp", "ty"), crossed("ty", 1)),
        lax.ppermute(left, ("comp", "ty"), crossed("ty", -1)),
    )
    rest = (gamma, mix, factors, received)
    new_state, remapped, done = finished(
        half, base, None, recv_late, None, late_y, None, *rest
    )
    early_in, done = lax.optimization_barrier((early_in, done))
    odd = jnp.stack([lax.axis_index("tx"), lax.axis_index("ty")]).astype(jnp.int32)[None] & 1
    recv_early, x_odd, x_even, y_odd, y_even = add_up(odd, ids_early, early_in, 16)
    early_x = (
        lax.ppermute(x_odd, "tx", neighbour_pairs(tx, 1)),
        lax.ppermute(x_even, "tx", neighbour_pairs(tx, 0)),
    )
    early_y = (
        lax.ppermute(y_odd, "ty", neighbour_pairs(ty, 1)),
        lax.ppermute(y_even, "ty", neighbour_pairs(ty, 0)),
    )
    new_state, remapped, _ = finished(
        0, new_state, remapped, recv_early, early_x, early_y, (late_x, base_early, odd, done), *rest
    )
    return new_state, remapped


def solution(mesh):
    placed = (
        P("comp", None, "tx", "ty"),
        P("comp", None, "tx", "ty"),
        P("tx", "ty"),
        P("comp", None),
        P("comp", ("tx", "ty")),
        P("comp", ("tx", "ty"), None),
        P("comp", ("tx", "ty")),
        P("comp", ("tx", "ty"), None, None),
    )
    return jax.shard_map(
        body,
        mesh=mesh,
        in_specs=placed,
        out_specs=(P("comp", None, "tx", "ty"), P("comp", None, "tx", "ty")),
        check_vma=False,
    )
```

```python
import functools

import jax
import jax.numpy as jnp
from jax import lax
from jax.experimental import pallas as pl
from jax.experimental.pallas import tpu as pltpu
from jax.sharding import PartitionSpec as P

LANES = 128
STEP_PAIRS = 64
STRIP = 8
NT = (((1,), (1,)), ((), ()))


def shift_pairs(count, by):
    return [(i, i + by) for i in range(count) if 0 <= i + by < count]


def neighbour_pairs(count, first):
    lows = range(first, count - 1, 2)
    return [(i, i + 1) for i in lows] + [(i + 1, i) for i in lows]


def crossed(axis, by):
    count = lax.axis_size(axis)
    return [
        (c * count + i, (1 - c) * count + j) for c in range(2) for i, j in shift_pairs(count, by)
    ]


def split(value, parts):
    if parts & (parts - 1) == 0:
        return lax.shift_right_logical(value, parts.bit_length() - 1), value & (parts - 1)
    return lax.div(value, parts), lax.rem(value, parts)


def ranks(dev, tiles):
    pairs = dev.shape[1]
    tile_of = lax.broadcasted_iota(jnp.int32, (tiles, pairs), 0)
    lane_of = lax.broadcasted_iota(jnp.int32, (tiles, pairs), 1)
    member = (tile_of == dev).astype(jnp.float32)
    total = member
    shift = 1
    while shift < pairs:
        total = total + jnp.where(lane_of >= shift, pltpu.roll(total, shift, 1), 0.0)
        shift *= 2
    return member, (jnp.sum(member * total, axis=0, keepdims=True) - 1.0).astype(jnp.int32)


def slot_blocks(dev, blk, tiles, capacity):
    member, rank = ranks(dev, tiles)
    pairs = dev.shape[1]
    slot_of = lax.broadcasted_iota(jnp.int32, (LANES, pairs), 0) % capacity
    chosen = (slot_of == rank).astype(jnp.bfloat16)

    def spread(values):
        return lax.dot_general(
            (member * values).astype(jnp.bfloat16), chosen, NT, preferred_element_type=jnp.float32
        )

    high, low = split(blk, 256)
    ids = spread(high.astype(jnp.float32)) * 256.0 + spread(low.astype(jnp.float32))
    return jnp.where(spread(jnp.ones(dev.shape, jnp.float32)) > 0.5, ids, -1.0)


def contribution_kernel(
    dims, src_ref, dev_ref, blk_ref, state_ref, weights_ref, early_ref, late_ref,
    cells, w_ref, pair_v, pair_s, taken, field_sems, weight_sems, pair_sems,
):
    tiles, capacity, pairs, fields, cells_x, cells_y, width = dims
    half = fields // 2
    parts = cells_y // width
    steps = pairs // STEP_PAIRS

    scalar_copies = [
        pltpu.make_async_copy(ref, pair_s.at[pl.ds(i, 1), :], pair_sems.at[i])
        for i, ref in enumerate((src_ref, dev_ref))
    ]
    vector_copies = [
        pltpu.make_async_copy(ref, pair_v.at[i], pair_sems.at[2 + i])
        for i, ref in enumerate((dev_ref, blk_ref))
    ]
    field_copies = [
        pltpu.make_async_copy(
            state_ref.at[0, f, :, pl.ds(q * width, width)],
            cells.at[q, :, f, :],
            field_sems.at[f * parts + q],
        )
        for f in range(fields)
        for q in range(parts)
    ]

    def weight_copy(step):
        some = pl.ds(step * STEP_PAIRS, STEP_PAIRS)
        return pltpu.make_async_copy(
            weights_ref.at[0, some], w_ref.at[some], weight_sems.at[step]
        )

    for copy in scalar_copies + vector_copies + field_copies:
        copy.start()
    for step in range(steps):
        weight_copy(step).start()
    late_ref[...] = jnp.zeros_like(late_ref)
    for t in range(tiles):
        taken[t] = t * (capacity + 1)

    for copy in vector_copies:
        copy.wait()
    dev, blk = pair_v[0], pair_v[1]
    ids = slot_blocks(dev, blk, tiles, capacity)
    for t in range(tiles):
        row = jnp.broadcast_to(ids[t : t + 1, :], late_ref.shape[1:])
        late_ref[t * (capacity + 1) + capacity] = row
    code = (dev * (cells_x * parts) + blk).astype(jnp.float32)
    for i in range(pairs // width):
        place = (pairs + i // half, slice(i % half, i % half + 1), slice(None))
        early_ref[place] = code[:, i * width : (i + 1) * width]
    for copy in scalar_copies + field_copies:
        copy.wait()

    def cells_of(p):
        x, part = split(pair_s[0, p], parts)
        return cells[part, x]

    zeros = jnp.zeros((fields, width), jnp.float32)

    def some_pairs(step, carry):
        weight_copy(step).wait()
        for i in range(0, STEP_PAIRS, 4):
            p = step * STEP_PAIRS + i
            left = [
                jnp.concatenate([cells_of(p + j), zeros][:: 1 - j % 2 * 2], axis=1) for j in range(4)
            ]
            left = jnp.concatenate(left, axis=0).astype(jnp.bfloat16)
            w = [w_ref[p + j] for j in range(4)]
            right = jnp.concatenate(
                [jnp.concatenate(w[:2], axis=1), jnp.concatenate(w[2:], axis=1)], axis=0
            )
            four = lax.dot_general(left, right, NT, preferred_element_type=jnp.float32)
            for j in range(4):
                tile = pair_s[1, p + j]
                slot = taken[tile]
                taken[tile] = slot + 1
                at = j // 2 * width
                one = four[j * fields : (j + 1) * fields, at : at + width]
                early_ref[p + j] = one[:half]
                late_ref[slot] = one[half:]
        return carry

    lax.fori_loop(0, steps, some_pairs, 0)


def contributions(state, pair_src, pair_dev, pair_blk, weights, tiles, capacity, fields):
    _, _, cells_x, cells_y = state.shape
    half = fields // 2
    pairs, width = weights.shape[1], weights.shape[2]
    rows = tiles * (capacity + 1)
    dims = (tiles, capacity, pairs, fields, cells_x, cells_y, width)
    parts = cells_y // width
    shapes = [(pairs + -(-pairs // (half * width)), half, width), (rows, half, width)]
    return pl.pallas_call(
        functools.partial(contribution_kernel, dims),
        in_specs=[pl.BlockSpec(memory_space=pltpu.HBM)] * 5,
        out_specs=[pl.BlockSpec(memory_space=pltpu.VMEM) for _ in shapes],
        out_shape=[jax.ShapeDtypeStruct(shape, jnp.float32) for shape in shapes],
        scratch_shapes=[
            pltpu.VMEM((parts, cells_x, fields, width), jnp.float32),
            pltpu.VMEM((pairs, width, width), jnp.bfloat16),
            pltpu.VMEM((2, 1, pairs), jnp.int32),
            pltpu.SMEM((2, pairs), jnp.int32),
            pltpu.SMEM((tiles,), jnp.int32),
            pltpu.SemaphoreType.DMA((parts * fields,)),
            pltpu.SemaphoreType.DMA((pairs // STEP_PAIRS,)),
            pltpu.SemaphoreType.DMA((4,)),
        ],
        compiler_params=pltpu.CompilerParams(vmem_limit_bytes=56 * 1024 * 1024),
        cost_estimate=pl.CostEstimate(
            flops=2 * pairs * fields * width * width,
            bytes_accessed=2 * pairs * width * width + 8 * rows * fields * width,
            transcendentals=0,
        ),
        name="contributions",
    )(pair_src, pair_dev.reshape(1, pairs), pair_blk, state, weights)


def place_kernel(dims, in_ref, out_ref, place_v, place_s, place_sem):
    tiles, capacity, pairs, blocks = dims
    half, width = in_ref.shape[1:]
    code = jnp.concatenate(
        [in_ref[pairs + i // half][i % half : i % half + 1] for i in range(pairs // width)], axis=1
    ).astype(jnp.int32)
    dev, _ = split(code, blocks)
    rank = ranks(dev, tiles)[1]
    place_v[...] = jnp.broadcast_to(dev * capacity + rank, place_v.shape)
    copy = pltpu.make_async_copy(place_v, place_s, place_sem)
    copy.start()
    out_ref[...] = jnp.zeros_like(out_ref)
    copy.wait()

    def some_rows(step, carry):
        for i in range(STEP_PAIRS):
            p = step * STEP_PAIRS + i
            out_ref[place_s[0, p]] = in_ref[p]
        return carry

    lax.fori_loop(0, pairs // STEP_PAIRS, some_rows, 0)


def placed_rows(rows, tiles, capacity, pairs, blocks):
    half, width = rows.shape[1:]
    shape = (tiles * capacity, half, width)
    return pl.pallas_call(
        functools.partial(place_kernel, (tiles, capacity, pairs, blocks)),
        out_shape=jax.ShapeDtypeStruct(shape, jnp.float32),
        scratch_shapes=[
            pltpu.VMEM((8, pairs), jnp.int32),
            pltpu.SMEM((8, pairs), jnp.int32),
            pltpu.SemaphoreType.DMA,
        ],
        compiler_params=pltpu.CompilerParams(vmem_limit_bytes=10 * 1024 * 1024),
        cost_estimate=pl.CostEstimate(
            flops=4 * rows.size, bytes_accessed=12 * rows.size, transcendentals=0
        ),
        name="place_in_slots",
    )(rows)


def sum_kernel(dims, paired, *refs):
    odd_ref, refs = (refs[0], refs[1:]) if paired else (None, refs)
    ids_ref, rows_ref, out_ref, x0_ref, x1_ref, y0_ref, y1_ref = refs[:7]
    in_ref, pick, high, low, row_sems = refs[7:]
    tiles, capacity, fields, cells_x, cells_y, width = dims
    parts = cells_y // width
    group = LANES // capacity
    stride = in_ref.shape[0] // tiles

    def rows_copy(k):
        some = pl.ds(k * group * stride, group * stride)
        return pltpu.make_async_copy(rows_ref.at[some, :], in_ref.at[some, :], row_sems.at[k])

    for k in range(tiles // group):
        rows_copy(k).start()
    block_of = lax.broadcasted_iota(jnp.int32, (cells_x * parts, LANES), 0)
    block_of = (block_of % cells_x) * parts + block_of // cells_x
    block_of = block_of.astype(jnp.float32)
    lane = lax.broadcasted_iota(jnp.int32, (1, LANES), 1)
    for k in range(tiles // group):
        rows_copy(k).wait()
        ids = None
        for i in range(group):
            source = k * group + i
            row = ids_ref[pl.ds(source, 1), :]
            ids = row if ids is None else jnp.where(lane // capacity == i, row, ids)
            for f in range(fields):
                x = in_ref[pl.ds(source * stride + f, capacity, stride=fields), :]
                rounded = x.astype(jnp.bfloat16)
                place = (
                    pl.ds(source * capacity, capacity),
                    pl.ds(f * width, width),
                )
                high[place] = rounded
                low[place] = (x - rounded.astype(jnp.float32)).astype(jnp.bfloat16)
        pick[:, pl.ds(k * LANES, LANES)] = (block_of == ids).astype(jnp.bfloat16)

    def in_order(i, low_rim, high_rim):
        if not paired:
            return low_rim, high_rim
        odd = odd_ref[0, i] == 1
        return jnp.where(odd, high_rim, low_rim), jnp.where(odd, low_rim, high_rim)

    columns = {}
    for q in range(parts):
        chosen = pick[pl.ds(q * cells_x, cells_x), :]
        total = jnp.dot(chosen, high[...], preferred_element_type=jnp.float32)
        total = total + jnp.dot(chosen, low[...], preferred_element_type=jnp.float32)
        for f in range(fields):
            tile = total[:, f * width : (f + 1) * width]
            out_ref[f, :, pl.ds(q * width, width)] = tile
            rims = in_order(0, tile[:1], tile[cells_x - 1 :])
            for rim_ref, rim in zip((x0_ref, x1_ref), rims):
                rim_ref[pl.ds(f, 1), pl.ds(q * width, width)] = rim
            if q in (0, parts - 1):
                columns[q, f] = tile.T[:1] if q == 0 else tile.T[width - 1 :]
    for f in range(fields):
        rims = in_order(1, columns[0, f], columns[parts - 1, f])
        y0_ref[pl.ds(f, 1), :], y1_ref[pl.ds(f, 1), :] = rims


def summed(odd, ids, rows, tiles, capacity, fields, cells_x, cells_y, width, grant):
    dims = (tiles, capacity, fields, cells_x, cells_y, width)
    rows = rows.reshape(-1, width)
    flags = [] if odd is None else [pl.BlockSpec(memory_space=pltpu.SMEM)]
    slots = tiles * capacity
    blocks = cells_x * cells_y // width
    shapes = [
        (fields, cells_x, cells_y),
        (fields, cells_y),
        (fields, cells_y),
        (fields, cells_x),
        (fields, cells_x),
    ]
    return pl.pallas_call(
        functools.partial(sum_kernel, dims, odd is not None),
        in_specs=flags
        + [pl.BlockSpec(memory_space=pltpu.VMEM), pl.BlockSpec(memory_space=pl.ANY)],
        out_shape=[jax.ShapeDtypeStruct(shape, jnp.float32) for shape in shapes],
        scratch_shapes=[
            pltpu.VMEM(rows.shape, jnp.float32),
            pltpu.VMEM((blocks, slots), jnp.bfloat16),
            pltpu.VMEM((slots, fields * width), jnp.bfloat16),
            pltpu.VMEM((slots, fields * width), jnp.bfloat16),
            pltpu.SemaphoreType.DMA((tiles * capacity // LANES,)),
        ],
        compiler_params=pltpu.CompilerParams(vmem_limit_bytes=grant * 1024 * 1024),
        cost_estimate=pl.CostEstimate(
            flops=4 * blocks * slots * fields * width,
            bytes_accessed=4 * fields * width * (slots + blocks),
            transcendentals=0,
        ),
        name="sum_by_block",
    )(*([] if odd is None else [odd]), ids, rows)


def stencil_factors(coefs, keep):
    u, v, kappa = coefs
    return [
        keep,
        keep * (jnp.maximum(u, 0.0) + kappa),
        keep * (kappa - jnp.minimum(u, 0.0)),
        keep * (jnp.maximum(v, 0.0) + kappa),
        keep * (kappa - jnp.minimum(v, 0.0)),
        -keep * (jnp.abs(u) + jnp.abs(v) + 4.0 * kappa),
    ]


def tendency(s, rate, factors, top, bottom, left, right):
    cells_x, cells_y = s.shape
    x_of = lax.broadcasted_iota(jnp.int32, s.shape, 0)
    y_of = lax.broadcasted_iota(jnp.int32, s.shape, 1)
    out = (factors[5] - rate * factors[0]) * s
    out += factors[1] * jnp.where(x_of == 0, top, pltpu.roll(s, 1, 0))
    out += factors[2] * jnp.where(x_of == cells_x - 1, bottom, pltpu.roll(s, cells_x - 1, 0))
    out += factors[3] * jnp.where(y_of == 0, left, pltpu.roll(s, 1, 1))
    out += factors[4] * jnp.where(y_of == cells_y - 1, right, pltpu.roll(s, cells_y - 1, 1))
    return out


def columns_of(rows):
    spare = 8 - rows.shape[0]
    if spare:
        rows = jnp.concatenate([rows, jnp.zeros((spare, rows.shape[1]), rows.dtype)], axis=0)
    return rows.T


def line_count(nfield):
    return 2 * nfield + 8


def edge_kernel(mix_ref, state_tops, state_ends, state_lefts, state_rights, coefs_tops, coefs_ends,
                coefs_lefts, coefs_rights, land_tops, land_ends, land_lefts, land_rights,
                x_low, x_high, y_low, y_high):
    nfield = state_tops.shape[1]
    last_row, last_lane = state_tops.shape[2] - 1, state_lefts.shape[3] - 1
    atmos = mix_ref[0, 1] == 1.0

    def kept(land):
        return jnp.where(atmos, 1.0, land.astype(jnp.float32))

    for out, state, coefs, land, lines in (
        (x_low, state_tops, coefs_tops, land_tops, (0, 1)),
        (x_high, state_ends, coefs_ends, land_ends, (last_row - 1, last_row)),
    ):
        outer = lines[0] if lines[0] == 0 else lines[1]
        out[2 * nfield :, :] = jnp.zeros((8, out.shape[1]), jnp.float32)
        for j, line in enumerate(lines):
            for f in range(nfield):
                out[j * nfield + f : j * nfield + f + 1, :] = state[0, f, line : line + 1, :]
        for c in range(3):
            out[2 * nfield + c : 2 * nfield + c + 1, :] = coefs[0, c, outer : outer + 1, :]
        out[2 * nfield + 3 : 2 * nfield + 4, :] = kept(land[outer : outer + 1, :])

    for out, state, coefs, land, lines in (
        (y_low, state_lefts, coefs_lefts, land_lefts, (0, 1)),
        (y_high, state_rights, coefs_rights, land_rights, (last_lane - 1, last_lane)),
    ):
        outer = lines[0] if lines[0] == 0 else lines[1]
        lane = lax.broadcasted_iota(jnp.int32, land.shape, 1)
        packed = jnp.zeros(land.shape, jnp.float32)

        def put(packed, tile, at, to):
            moved = (to - at) % LANES
            tile = pltpu.roll(tile, moved, 1) if moved else tile
            return jnp.where(lane == to, tile, packed)

        for j, line in enumerate(lines):
            for f in range(nfield):
                packed = put(packed, state[0, f], line, j * nfield + f)
        for c in range(3):
            packed = put(packed, coefs[0, c], outer, 2 * nfield + c)
        packed = put(packed, kept(land[...]), outer, 2 * nfield + 3)
        out[...] = packed.T[: out.shape[0]]


def edges_of(state, coefs, land_sea, mix):
    _, nfield, cells_x, cells_y = state.shape
    lines = line_count(nfield)
    ends = [
        ((8, cells_y), (0, 0)),
        ((8, cells_y), (cells_x // 8 - 1, 0)),
        ((cells_x, LANES), (0, 0)),
        ((cells_x, LANES), (0, cells_y // LANES - 1)),
    ]
    at = lambda lead, place: lambda i: (0,) * len(lead) + place
    specs = [pl.BlockSpec(memory_space=pltpu.SMEM)]
    for lead in ((1, nfield), (1, 3), ()):
        specs += [pl.BlockSpec(lead + shape, at(lead, place)) for shape, place in ends]
    shapes = [(lines, cells_y)] * 2 + [(lines, cells_x)] * 2
    return pl.pallas_call(
        edge_kernel,
        grid=(1,),
        in_specs=specs,
        out_specs=[pl.BlockSpec(shape, lambda i: (0, 0)) for shape in shapes],
        out_shape=[jax.ShapeDtypeStruct(shape, jnp.float32) for shape in shapes],
        compiler_params=pltpu.CompilerParams(vmem_limit_bytes=24 * 1024 * 1024),
        cost_estimate=pl.CostEstimate(
            flops=state.size, bytes_accessed=4 * 1024 * 1024, transcendentals=0
        ),
        name="edges",
    )(mix, *[state] * 4, *[coefs] * 4, *[land_sea] * 4)


def outer_section(center, across, along, factors, rate):
    lane = lax.broadcasted_iota(jnp.int32, center.shape, 1)
    count = center.shape[1]
    before = jnp.where(lane == 0, along[0], pltpu.roll(center, 1, 1))
    after = jnp.where(lane == count - 1, along[1], pltpu.roll(center, count - 1, 1))
    keep, low, high, back, ahead, middle = factors
    out = center + low * across[0] + high * across[1] + back * before + ahead * after
    return out + (middle - rate * keep) * center


def base_kernel(half, rate_ref, mix_ref, rates_ref, coefs_ref, land_ref, x_low, x_high, y_low, y_high,
                above, below, left, right, corners_left, corners_right, state_ref,
                out_ref, early_ref, factors, rows, cols):
    f = pl.program_id(0)
    nfield = rates_ref.shape[0]
    lines = line_count(nfield)

    @pl.when(f == 0)
    def _():
        keep = jnp.where(mix_ref[0, 1] == 1.0, 1.0, land_ref[...].astype(jnp.float32))
        for i, factor in enumerate(stencil_factors([coefs_ref[0, c] for c in range(3)], keep)):
            factors[i] = factor
        rate = rates_ref[:, 0:1]
        near, far = pl.ds(0, nfield), pl.ds(nfield, nfield)
        last = corners_left.shape[1] - 1
        corner = (
            (corners_left[nfield : 2 * nfield, last:], corners_left[lines : lines + nfield, last:]),
            (corners_right[nfield : 2 * nfield, 0:1], corners_right[lines : lines + nfield, 0:1]),
        )
        for i, (ref, center, across, along, is_column) in enumerate(
            (
                (above, above[far, :], (above[near, :], x_low[near, :]), (corner[0][0], corner[1][0]), False),
                (below, below[near, :], (x_high[far, :], below[far, :]), (corner[0][1], corner[1][1]), False),
                (left, left[far, :], (left[near, :], y_low[near, :]), corner[0], True),
                (right, right[near, :], (y_high[far, :], right[far, :]), corner[1], True),
            )
        ):
            first = 2 * nfield
            of_line = stencil_factors(
                [ref[first + c : first + c + 1, :] for c in range(3)],
                ref[first + 3 : first + 4, :],
            )
            if is_column:
                of_line = [of_line[j] for j in (0, 3, 4, 1, 2, 5)]
            section = outer_section(center, across, along, of_line, rate)
            kept = cols if is_column else rows
            kept[pl.ds(i % 2 * nfield, nfield), :] = center
            kept[pl.ds((2 + i % 2) * nfield, nfield), :] = section

    rate = rate_ref[0, f]
    mix_a, mix_b = mix_ref[0, 0], mix_ref[0, 1]
    s = state_ref[0, 0]
    row = [rows[pl.ds(i * nfield + f, 1), :] for i in range(4)]
    col = columns_of(
        jnp.concatenate([cols[pl.ds(i * nfield + f, 1), :] for i in range(4)], axis=0)
    )
    s1 = s + tendency(s, rate, factors, row[0], row[1], col[:, 0:1], col[:, 1:2])
    more = tendency(s1, rate, factors, row[2], row[3], col[:, 2:3], col[:, 3:4])
    total = mix_a * s + (1.0 - mix_a) * s1 + mix_b * more
    out_ref[0, 0] = total

    @pl.when(f < half)
    def _():
        early_ref[0] = total


def base_of(state, coefs, land_sea, rates, mix, edges, received, corners, half):
    _, nfield, cells_x, cells_y = state.shape
    field = pl.BlockSpec((1, 1, cells_x, cells_y), lambda f: (0, f, 0, 0))
    whole = lambda a: pl.BlockSpec(a.shape, lambda f: (0,) * a.ndim)
    rates_wide = jnp.broadcast_to(rates.T, (nfield, LANES))
    operands = [rates_wide, coefs, land_sea, *edges, *received, *corners]
    return pl.pallas_call(
        functools.partial(base_kernel, half),
        grid=(nfield,),
        in_specs=[
            pl.BlockSpec(memory_space=pltpu.SMEM),
            pl.BlockSpec(memory_space=pltpu.SMEM),
            *[whole(a) for a in operands],
            field,
        ],
        out_specs=[
            field,
            pl.BlockSpec((1, cells_x, cells_y), lambda f: (jnp.minimum(f, half - 1), 0, 0)),
            pl.BlockSpec((6, cells_x, cells_y), lambda f: (0, 0, 0)),
        ],
        out_shape=[
            jax.ShapeDtypeStruct(state.shape, jnp.float32),
            jax.ShapeDtypeStruct((half, cells_x, cells_y), jnp.float32),
            jax.ShapeDtypeStruct((6, cells_x, cells_y), jnp.float32),
        ],
        scratch_shapes=[
            pltpu.VMEM((4 * nfield, cells_y), jnp.float32),
            pltpu.VMEM((4 * nfield, cells_x), jnp.float32),
        ],
        compiler_params=pltpu.CompilerParams(vmem_limit_bytes=56 * 1024 * 1024),
        cost_estimate=pl.CostEstimate(
            flops=40 * state.size, bytes_accessed=8 * state.size, transcendentals=0
        ),
        name="base",
    )(rates, mix, *operands, state)


def finish_kernel(first, with_x, gamma_ref, mix_ref, above, below, before, after, factors, recv,
                  left, right, *rest):
    tops, rest = (rest[:2], rest[2:]) if with_x else (None, rest)
    late, rest = (rest[:2], rest[2:]) if with_x else (None, rest)
    early_base, odd_ref, rest = (*rest[:2], rest[2:]) if with_x else (None, None, rest)
    base_ref, rest = rest[0], rest[1:]
    new_ref, out_ref, done_ref = rest[-11:-8]
    base, wide, lines, sides, outer, base_sems, out_sems, outer_sems = rest[-8:]
    count, cells_x, cells_y = base.shape
    mix_b = mix_ref[0, 1]
    keep_row = above.shape[0] - 5
    keep = slice(keep_row, keep_row + 1)
    ends = (0, cells_x - STRIP)

    def base_copy(f):
        return pltpu.make_async_copy(base_ref.at[0, first + f], base.at[f], base_sems.at[f])

    def out_copies(f):
        return (
            pltpu.make_async_copy(recv.at[f], out_ref.at[0, first + f], out_sems.at[0, f]),
            pltpu.make_async_copy(base.at[f], new_ref.at[0, first + f], out_sems.at[1, f]),
        )

    def outer_copy(f, i, back):
        there = (new_ref if back else base_ref).at[0, count + f, pl.ds(ends[i], STRIP), :]
        here = outer.at[f, i]
        pair = (here, there) if back else (there, here)
        return pltpu.make_async_copy(*pair, outer_sems.at[f, i])

    outer_rows = [(f, i) for f in range(count) for i in range(2)] if with_x else []
    if not with_x:
        for f in range(count):
            base_copy(f).start()
    for f, i in outer_rows:
        outer_copy(f, i, False).start()
    done_ref[...] = jnp.zeros_like(done_ref)
    if with_x:
        for i, (pair, kept, low_keep, high_keep) in enumerate(
            ((tops, lines, above, below), ((left, right), sides, before, after))
        ):
            odd = odd_ref[0, i] == 1
            in_odd, in_even = pair[0][...], pair[1][...]
            kept[:count, :] = jnp.where(odd, in_even, in_odd) * low_keep[keep, :]
            kept[count:, :] = jnp.where(odd, in_odd, in_even) * high_keep[keep, :]
    else:
        lines[...] = jnp.zeros_like(lines)
        sides[:count, :] = left[...] * before[keep, :]
        sides[count:, :] = right[...] * after[keep, :]
    lane = lax.broadcasted_iota(jnp.int32, (STRIP, cells_y), 1)

    def one_field(f, carry):
        rate = gamma_ref[0, first + f]
        both = [sides[pl.ds(f, 1), :] * rate, sides[pl.ds(count + f, 1), :] * rate]
        cols = columns_of(jnp.concatenate(both, axis=0))
        wide[STRIP - 1 : STRIP, :] = lines[pl.ds(f, 1), :] * rate
        wide[STRIP + cells_x : STRIP + cells_x + 1, :] = lines[pl.ds(count + f, 1), :] * rate
        to_out, to_new = out_copies(f)
        to_out.start()
        for i in range(0, cells_x, STRIP):
            rows = slice(i, i + STRIP)
            wide[STRIP + i : 2 * STRIP + i, :] = factors[0, rows, :] * recv[f, rows, :] * rate
        if not with_x:
            base_copy(f).wait()
        start = early_base if with_x else base
        for i in range(0, cells_x, STRIP):
            rows = slice(i, i + STRIP)
            mid = wide[STRIP + i : 2 * STRIP + i, :]
            more = (factors[5, rows, :] - rate * factors[0, rows, :]) * mid
            more += factors[1, rows, :] * wide[STRIP + i - 1 : 2 * STRIP + i - 1, :]
            more += factors[2, rows, :] * wide[STRIP + i + 1 : 2 * STRIP + i + 1, :]
            prior = jnp.where(lane == 0, cols[rows, 0:1], pltpu.roll(mid, 1, 1))
            later = jnp.where(lane == cells_y - 1, cols[rows, 1:2], pltpu.roll(mid, cells_y - 1, 1))
            more += factors[3, rows, :] * prior + factors[4, rows, :] * later
            base[f, rows, :] = start[f, rows, :] + mix_b * (2.0 * mid + more)
        to_new.start()
        return carry

    def add_lines():
        for f, i in outer_rows:
            outer_copy(f, i, False).wait()
            row = i * (STRIP - 1)
            at = ends[i] + row
            line = late[i][f : f + 1, :] * (above, below)[i][keep, :] * gamma_ref[0, count + f]
            more = mix_b * factors[1 + i, at : at + 1, :] * line
            outer[f, i, row : row + 1, :] = outer[f, i, row : row + 1, :] + more
            outer_copy(f, i, True).start()

    lax.fori_loop(0, count - 1, one_field, 0)
    add_lines()
    one_field(count - 1, 0)
    for f in range(count):
        for copy in out_copies(f):
            copy.wait()
    for f, i in outer_rows:
        outer_copy(f, i, True).wait()


def finished(
    first, new_state, remapped, recv, x_rims, y_rims, closing, gamma, mix, factors, received
):
    count, cells_x, cells_y = recv.shape
    chan = gamma.shape[1]
    with_x = x_rims is not None
    anywhere = pl.BlockSpec(memory_space=pl.ANY)
    operands = [gamma, mix, *received, factors, recv, *y_rims]
    if with_x:
        late_rims, base_early, odd, late_done = closing
        operands += [*x_rims, *late_rims, base_early]
    scalars = pl.BlockSpec(memory_space=pltpu.SMEM)
    specs = [scalars] * 2 + [pl.BlockSpec(memory_space=pltpu.VMEM)] * (len(operands) - 2)
    if with_x:
        operands.append(odd)
        specs.append(scalars)
    specs.append(anywhere)
    aliases = {len(operands): 0}
    operands.append(new_state)
    if remapped is not None:
        aliases[len(operands)] = 1
        operands += [remapped, late_done]
        specs += [anywhere, anywhere]
    return pl.pallas_call(
        functools.partial(finish_kernel, first, with_x),
        in_specs=specs,
        out_specs=[anywhere, anywhere, pl.BlockSpec(memory_space=pltpu.VMEM)],
        out_shape=[
            jax.ShapeDtypeStruct(new_state.shape, jnp.float32),
            jax.ShapeDtypeStruct((1, chan, cells_x, cells_y), jnp.float32),
            jax.ShapeDtypeStruct((8, LANES), jnp.float32),
        ],
        input_output_aliases=aliases,
        scratch_shapes=[
            pltpu.VMEM((count, cells_x, cells_y), jnp.float32),
            pltpu.VMEM((cells_x + 2 * STRIP, cells_y), jnp.float32),
            pltpu.VMEM((2 * count, cells_y), jnp.float32),
            pltpu.VMEM((2 * count, cells_x), jnp.float32),
            pltpu.VMEM((count, 2, STRIP, cells_y), jnp.float32),
            pltpu.SemaphoreType.DMA((count,)),
            pltpu.SemaphoreType.DMA((2, count)),
            pltpu.SemaphoreType.DMA((count, 2)),
        ],
        compiler_params=pltpu.CompilerParams(vmem_limit_bytes=12 * 1024 * 1024),
        cost_estimate=pl.CostEstimate(
            flops=20 * recv.size, bytes_accessed=20 * recv.size, transcendentals=0
        ),
        name="finish",
    )(*operands)


def body(state, coefs, land_sea, gamma, pair_src, pair_dev, pair_blk, weights):
    tx, ty = lax.axis_size("tx"), lax.axis_size("ty")
    tiles = tx * ty
    nfield, cells_x, cells_y = state.shape[1:]
    chan = gamma.shape[1]
    pairs, width = weights.shape[1], weights.shape[2]
    capacity = max(2, 2 * pairs // tiles)
    half = chan // 2
    early, late = contributions(
        state, pair_src, pair_dev, pair_blk, weights, tiles, capacity, chan
    )
    swap = [(0, 1), (1, 0)]

    def exchanged(rows):
        rows = rows.reshape(tiles, -1, half, width)
        return lax.all_to_all(rows, ("tx", "ty"), split_axis=0, concat_axis=0, tiled=True)

    def add_up(odd, ids, rows, grant):
        return summed(odd, ids, rows, tiles, capacity, half, cells_x, cells_y, width, grant)

    late_in = exchanged(late)
    early = lax.ppermute(early, "comp", swap)
    early_in = placed_rows(early, tiles, capacity, pairs, cells_x * cells_y // width)

    land_after, _ = lax.optimization_barrier((land_sea, late))
    is_atmos = lax.axis_index("comp") == 0
    mix = jnp.where(is_atmos, jnp.array([[0.0, 1.0]]), jnp.array([[0.5, 0.5]]))
    mix = mix.astype(jnp.float32)
    rates = jnp.concatenate([gamma, jnp.zeros((1, nfield - chan), jnp.float32)], axis=1)
    x_low, x_high, y_low, y_high = edges_of(state, coefs, land_after, mix)
    left = lax.ppermute(y_high, "ty", shift_pairs(ty, 1))
    right = lax.ppermute(y_low, "ty", shift_pairs(ty, -1))
    above = lax.ppermute(x_high, "tx", shift_pairs(tx, 1))
    below = lax.ppermute(x_low, "tx", shift_pairs(tx, -1))
    early_in, above, below, left, right = lax.optimization_barrier(
        (early_in, above, below, left, right)
    )
    received = (above, below, left, right)
    early_in = exchanged(early_in)

    ends = jnp.concatenate([above[:, cells_y - LANES :], below[:, cells_y - LANES :]], axis=0)
    starts = jnp.concatenate([above[:, :LANES], below[:, :LANES]], axis=0)
    corners_left = lax.ppermute(ends, "ty", shift_pairs(ty, 1))
    corners_right = lax.ppermute(starts, "ty", shift_pairs(ty, -1))
    base, base_early, factors = base_of(
        state, coefs, land_after, rates, mix, (x_low, x_high, y_low, y_high), received,
        (corners_left, corners_right), half,
    )

    ids_late = late_in[:, capacity, 0, :]
    ids_early = lax.ppermute(ids_late, "comp", swap)
    recv_late, top, bottom, left, right = add_up(None, ids_late, late_in, 50)
    recv_late = lax.ppermute(recv_late, "comp", swap)
    late_x = (
        lax.ppermute(bottom, ("comp", "tx"), crossed("tx", 1)),
        lax.ppermute(top, ("comp", "tx"), crossed("tx", -1)),
    )
    late_y = (
        lax.ppermute(right, ("comp", "ty"), crossed("ty", 1)),
        lax.ppermute(left, ("comp", "ty"), crossed("ty", -1)),
    )
    rest = (gamma, mix, factors, received)
    new_state, remapped, done = finished(
        half, base, None, recv_late, None, late_y, None, *rest
    )
    early_in, done = lax.optimization_barrier((early_in, done))
    odd = jnp.stack([lax.axis_index("tx"), lax.axis_index("ty")]).astype(jnp.int32)[None] & 1
    recv_early, x_odd, x_even, y_odd, y_even = add_up(odd, ids_early, early_in, 16)
    early_x = (
        lax.ppermute(x_odd, "tx", neighbour_pairs(tx, 1)),
        lax.ppermute(x_even, "tx", neighbour_pairs(tx, 0)),
    )
    early_y = (
        lax.ppermute(y_odd, "ty", neighbour_pairs(ty, 1)),
        lax.ppermute(y_even, "ty", neighbour_pairs(ty, 0)),
    )
    new_state, remapped, _ = finished(
        0, new_state, remapped, recv_early, early_x, early_y, (late_x, base_early, odd, done), *rest
    )
    return new_state, remapped


def solution(mesh):
    placed = (
        P("comp", None, "tx", "ty"),
        P("comp", None, "tx", "ty"),
        P("tx", "ty"),
        P("comp", None),
        P("comp", ("tx", "ty")),
        P("comp", ("tx", "ty"), None),
        P("comp", ("tx", "ty")),
        P("comp", ("tx", "ty"), None, None),
    )
    return jax.shard_map(
        body,
        mesh=mesh,
        in_specs=placed,
        out_specs=(P("comp", None, "tx", "ty"), P("comp", None, "tx", "ty")),
        check_vma=False,
    )
```

```python
import functools

import jax
import jax.numpy as jnp
from jax import lax
from jax.experimental import pallas as pl
from jax.experimental.pallas import tpu as pltpu
from jax.sharding import PartitionSpec as P

LANES = 128
STEP_PAIRS = 64
STRIP = 8
PER_STEP = 2
NT = (((1,), (1,)), ((), ()))


def pinned(space, *arrays):
    return [pltpu.with_memory_space_constraint(a, space) for a in arrays]


def shift_pairs(count, by):
    return [(i, i + by) for i in range(count) if 0 <= i + by < count]


def neighbour_pairs(count, first):
    lows = range(first, count - 1, 2)
    return [(i, i + 1) for i in lows] + [(i + 1, i) for i in lows]


def crossed(axis, first):
    count = lax.axis_size(axis)
    pairs = neighbour_pairs(count, first)
    return [(c * count + i, (1 - c) * count + j) for c in range(2) for i, j in pairs]


def split(value, parts):
    if parts & (parts - 1) == 0:
        return lax.shift_right_logical(value, parts.bit_length() - 1), value & (parts - 1)
    return lax.div(value, parts), lax.rem(value, parts)


def ranks(dev, tiles):
    pairs = dev.shape[1]
    tile_of = lax.broadcasted_iota(jnp.int32, (tiles, pairs), 0)
    lane_of = lax.broadcasted_iota(jnp.int32, (tiles, pairs), 1)
    member = (tile_of == dev).astype(jnp.float32)
    total = member
    shift = 1
    while shift < pairs:
        total = total + jnp.where(lane_of >= shift, pltpu.roll(total, shift, 1), 0.0)
        shift *= 2
    return member, (jnp.sum(member * total, axis=0, keepdims=True) - 1.0).astype(jnp.int32)


def slot_blocks(dev, blk, tiles, capacity):
    member, rank = ranks(dev, tiles)
    pairs = dev.shape[1]
    slot_of = lax.broadcasted_iota(jnp.int32, (LANES, pairs), 0) % capacity
    chosen = (slot_of == rank).astype(jnp.bfloat16)

    def spread(values):
        return lax.dot_general(
            (member * values).astype(jnp.bfloat16), chosen, NT, preferred_element_type=jnp.float32
        )

    high, low = split(blk, 256)
    ids = spread(high.astype(jnp.float32)) * 256.0 + spread(low.astype(jnp.float32))
    return jnp.where(spread(jnp.ones(dev.shape, jnp.float32)) > 0.5, ids, -1.0)


def contribution_kernel(
    dims, src_ref, dev_ref, blk_ref, state_ref, weights_ref, early_ref, late_ref,
    cells, w_ref, pair_v, pair_s, taken, field_sems, weight_sems, pair_sems,
):
    tiles, capacity, pairs, fields, cells_x, cells_y, width = dims
    half = fields // 2
    parts = cells_y // width
    steps = pairs // STEP_PAIRS

    scalar_copies = [
        pltpu.make_async_copy(ref, pair_s.at[pl.ds(i, 1), :], pair_sems.at[i])
        for i, ref in enumerate((src_ref, dev_ref))
    ]
    vector_copies = [
        pltpu.make_async_copy(ref, pair_v.at[i], pair_sems.at[2 + i])
        for i, ref in enumerate((dev_ref, blk_ref))
    ]
    field_copies = [
        pltpu.make_async_copy(
            state_ref.at[0, f, :, pl.ds(q * width, width)],
            cells.at[q, :, f, :],
            field_sems.at[f * parts + q],
        )
        for f in range(fields)
        for q in range(parts)
    ]

    def weight_copy(step):
        some = pl.ds(step * STEP_PAIRS, STEP_PAIRS)
        return pltpu.make_async_copy(
            weights_ref.at[0, some], w_ref.at[some], weight_sems.at[step]
        )

    for copy in scalar_copies + vector_copies + field_copies:
        copy.start()
    for step in range(steps):
        weight_copy(step).start()
    late_ref[...] = jnp.zeros_like(late_ref)
    for t in range(tiles):
        taken[t] = t * (capacity + 1)

    for copy in vector_copies:
        copy.wait()
    dev, blk = pair_v[0], pair_v[1]
    ids = slot_blocks(dev, blk, tiles, capacity)
    for t in range(tiles):
        row = jnp.broadcast_to(ids[t : t + 1, :], late_ref.shape[1:])
        late_ref[t * (capacity + 1) + capacity] = row
    code = (dev * (cells_x * parts) + blk).astype(jnp.float32)
    for i in range(pairs // width):
        place = (pairs + i // half, slice(i % half, i % half + 1), slice(None))
        early_ref[place] = code[:, i * width : (i + 1) * width]
    for copy in scalar_copies + field_copies:
        copy.wait()

    def cells_of(p):
        x, part = split(pair_s[0, p], parts)
        return cells[part, x]

    zeros = jnp.zeros((fields, width), jnp.float32)

    def some_pairs(step, carry):
        weight_copy(step).wait()
        for i in range(0, STEP_PAIRS, 4):
            p = step * STEP_PAIRS + i
            left = [
                jnp.concatenate([cells_of(p + j), zeros][:: 1 - j % 2 * 2], axis=1) for j in range(4)
            ]
            left = jnp.concatenate(left, axis=0).astype(jnp.bfloat16)
            w = [w_ref[p + j] for j in range(4)]
            right = jnp.concatenate(
                [jnp.concatenate(w[:2], axis=1), jnp.concatenate(w[2:], axis=1)], axis=0
            )
            four = lax.dot_general(left, right, NT, preferred_element_type=jnp.float32)
            for j in range(4):
                tile = pair_s[1, p + j]
                slot = taken[tile]
                taken[tile] = slot + 1
                at = j // 2 * width
                one = four[j * fields : (j + 1) * fields, at : at + width]
                early_ref[p + j] = one[:half]
                late_ref[slot] = one[half:]
        return carry

    lax.fori_loop(0, steps, some_pairs, 0)


def contributions(state, pair_src, pair_dev, pair_blk, weights, tiles, capacity, fields):
    _, _, cells_x, cells_y = state.shape
    half = fields // 2
    pairs, width = weights.shape[1], weights.shape[2]
    rows = tiles * (capacity + 1)
    dims = (tiles, capacity, pairs, fields, cells_x, cells_y, width)
    parts = cells_y // width
    shapes = [(pairs + -(-pairs // (half * width)), half, width), (rows, half, width)]
    return pl.pallas_call(
        functools.partial(contribution_kernel, dims),
        in_specs=[pl.BlockSpec(memory_space=pltpu.HBM)] * 5,
        out_specs=[pl.BlockSpec(memory_space=pltpu.VMEM) for _ in shapes],
        out_shape=[jax.ShapeDtypeStruct(shape, jnp.float32) for shape in shapes],
        scratch_shapes=[
            pltpu.VMEM((parts, cells_x, fields, width), jnp.float32),
            pltpu.VMEM((pairs, width, width), jnp.bfloat16),
            pltpu.VMEM((2, 1, pairs), jnp.int32),
            pltpu.SMEM((2, pairs), jnp.int32),
            pltpu.SMEM((tiles,), jnp.int32),
            pltpu.SemaphoreType.DMA((parts * fields,)),
            pltpu.SemaphoreType.DMA((pairs // STEP_PAIRS,)),
            pltpu.SemaphoreType.DMA((4,)),
        ],
        compiler_params=pltpu.CompilerParams(vmem_limit_bytes=40 * 1024 * 1024),
        cost_estimate=pl.CostEstimate(
            flops=2 * pairs * fields * width * width,
            bytes_accessed=2 * pairs * width * width + 8 * rows * fields * width,
            transcendentals=0,
        ),
        name="contributions",
    )(*pinned(pltpu.HBM, pair_src, pair_dev.reshape(1, pairs), pair_blk, state, weights))


def place_kernel(dims, in_ref, out_ref, place_v, place_s, place_sem):
    tiles, capacity, pairs, blocks = dims
    half, width = in_ref.shape[1:]
    code = jnp.concatenate(
        [in_ref[pairs + i // half][i % half : i % half + 1] for i in range(pairs // width)], axis=1
    ).astype(jnp.int32)
    dev, _ = split(code, blocks)
    rank = ranks(dev, tiles)[1]
    place_v[...] = jnp.broadcast_to(dev * capacity + rank, place_v.shape)
    copy = pltpu.make_async_copy(place_v, place_s, place_sem)
    copy.start()
    out_ref[...] = jnp.zeros_like(out_ref)
    copy.wait()

    def some_rows(step, carry):
        for i in range(STEP_PAIRS):
            p = step * STEP_PAIRS + i
            out_ref[place_s[0, p]] = in_ref[p]
        return carry

    lax.fori_loop(0, pairs // STEP_PAIRS, some_rows, 0)


def placed_rows(rows, tiles, capacity, pairs, blocks):
    half, width = rows.shape[1:]
    shape = (tiles * capacity, half, width)
    return pl.pallas_call(
        functools.partial(place_kernel, (tiles, capacity, pairs, blocks)),
        out_shape=jax.ShapeDtypeStruct(shape, jnp.float32),
        scratch_shapes=[
            pltpu.VMEM((8, pairs), jnp.int32),
            pltpu.SMEM((8, pairs), jnp.int32),
            pltpu.SemaphoreType.DMA,
        ],
        compiler_params=pltpu.CompilerParams(vmem_limit_bytes=10 * 1024 * 1024),
        cost_estimate=pl.CostEstimate(
            flops=4 * rows.size, bytes_accessed=12 * rows.size, transcendentals=0
        ),
        name="place_in_slots",
    )(rows)


def sum_kernel(dims, paired, *refs):
    odd_ref, refs = (refs[0], refs[1:]) if paired else (None, refs)
    ids_ref, rows_ref, out_ref, x0_ref, x1_ref, y0_ref, y1_ref = refs[:7]
    pick, high, low, *copied = refs[7:]
    in_ref, row_sems = copied if copied else (rows_ref, None)
    tiles, capacity, fields, cells_x, cells_y, width = dims
    parts = cells_y // width
    group = LANES // capacity
    stride = in_ref.shape[0] // tiles

    def rows_copy(k):
        some = pl.ds(k * group * stride, group * stride)
        return pltpu.make_async_copy(rows_ref.at[some, :], in_ref.at[some, :], row_sems.at[k])

    for k in range(tiles // group if copied else 0):
        rows_copy(k).start()
    block_of = lax.broadcasted_iota(jnp.int32, (cells_x * parts, LANES), 0)
    block_of = (block_of % cells_x) * parts + block_of // cells_x
    block_of = block_of.astype(jnp.float32)
    lane = lax.broadcasted_iota(jnp.int32, (1, LANES), 1)
    for k in range(tiles // group):
        if copied:
            rows_copy(k).wait()
        ids = None
        for i in range(group):
            source = k * group + i
            row = ids_ref[pl.ds(source, 1), :]
            ids = row if ids is None else jnp.where(lane // capacity == i, row, ids)
            for f in range(fields):
                x = in_ref[pl.ds(source * stride + f, capacity, stride=fields), :]
                rounded = x.astype(jnp.bfloat16)
                place = (
                    pl.ds(source * capacity, capacity),
                    pl.ds(f * width, width),
                )
                high[place] = rounded
                low[place] = (x - rounded.astype(jnp.float32)).astype(jnp.bfloat16)
        pick[:, pl.ds(k * LANES, LANES)] = (block_of == ids).astype(jnp.bfloat16)

    def in_order(i, low_rim, high_rim):
        if not paired:
            return low_rim, high_rim
        odd = odd_ref[0, i] == 1
        return jnp.where(odd, high_rim, low_rim), jnp.where(odd, low_rim, high_rim)

    columns = {}
    for q in range(parts):
        chosen = pick[pl.ds(q * cells_x, cells_x), :]
        total = jnp.dot(chosen, high[...], preferred_element_type=jnp.float32)
        total = total + jnp.dot(chosen, low[...], preferred_element_type=jnp.float32)
        for f in range(fields):
            tile = total[:, f * width : (f + 1) * width]
            out_ref[f, :, pl.ds(q * width, width)] = tile
            rims = in_order(0, tile[:1], tile[cells_x - 1 :])
            for rim_ref, rim in zip((x0_ref, x1_ref), rims):
                rim_ref[pl.ds(f, 1), pl.ds(q * width, width)] = rim
            if q in (0, parts - 1):
                columns[q, f] = tile.T[:1] if q == 0 else tile.T[width - 1 :]
    for f in range(fields):
        rims = in_order(1, columns[0, f], columns[parts - 1, f])
        y0_ref[pl.ds(f, 1), :], y1_ref[pl.ds(f, 1), :] = rims


def summed(odd, ids, rows, tiles, capacity, fields, cells_x, cells_y, width, space):
    dims = (tiles, capacity, fields, cells_x, cells_y, width)
    rows = rows.reshape(-1, width)
    flags = [] if odd is None else [pl.BlockSpec(memory_space=pltpu.SMEM)]
    copied = []
    if space is pltpu.HBM:
        copied = [
            pltpu.VMEM(rows.shape, jnp.float32),
            pltpu.SemaphoreType.DMA((tiles * capacity // LANES,)),
        ]
    slots = tiles * capacity
    blocks = cells_x * cells_y // width
    shapes = [
        (fields, cells_x, cells_y),
        (fields, cells_y),
        (fields, cells_y),
        (fields, cells_x),
        (fields, cells_x),
    ]
    return pl.pallas_call(
        functools.partial(sum_kernel, dims, odd is not None),
        in_specs=flags
        + [pl.BlockSpec(memory_space=pltpu.VMEM), pl.BlockSpec(memory_space=space)],
        out_shape=[jax.ShapeDtypeStruct(shape, jnp.float32) for shape in shapes],
        scratch_shapes=[
            pltpu.VMEM((blocks, slots), jnp.bfloat16),
            pltpu.VMEM((slots, fields * width), jnp.bfloat16),
            pltpu.VMEM((slots, fields * width), jnp.bfloat16),
        ]
        + copied,
        compiler_params=pltpu.CompilerParams(vmem_limit_bytes=24 * 1024 * 1024),
        cost_estimate=pl.CostEstimate(
            flops=4 * blocks * slots * fields * width,
            bytes_accessed=4 * fields * width * (slots + blocks),
            transcendentals=0,
        ),
        name="sum_by_block",
    )(*([] if odd is None else [odd]), ids, *pinned(space, rows))


def stencil_factors(coefs, keep):
    u, v, kappa = coefs
    return [
        keep,
        keep * (jnp.maximum(u, 0.0) + kappa),
        keep * (kappa - jnp.minimum(u, 0.0)),
        keep * (jnp.maximum(v, 0.0) + kappa),
        keep * (kappa - jnp.minimum(v, 0.0)),
        -keep * (jnp.abs(u) + jnp.abs(v) + 4.0 * kappa),
    ]


def tendency(s, rate, factors, top, bottom, left, right):
    cells_x, cells_y = s.shape
    x_of = lax.broadcasted_iota(jnp.int32, s.shape, 0)
    y_of = lax.broadcasted_iota(jnp.int32, s.shape, 1)
    out = (factors[5] - rate * factors[0]) * s
    out += factors[1] * jnp.where(x_of == 0, top, pltpu.roll(s, 1, 0))
    out += factors[2] * jnp.where(x_of == cells_x - 1, bottom, pltpu.roll(s, cells_x - 1, 0))
    out += factors[3] * jnp.where(y_of == 0, left, pltpu.roll(s, 1, 1))
    out += factors[4] * jnp.where(y_of == cells_y - 1, right, pltpu.roll(s, cells_y - 1, 1))
    return out


def columns_of(rows):
    spare = 8 - rows.shape[0]
    if spare:
        rows = jnp.concatenate([rows, jnp.zeros((spare, rows.shape[1]), rows.dtype)], axis=0)
    return rows.T


def line_count(nfield):
    return 2 * nfield + 8


def edge_kernel(mix_ref, state_tops, state_ends, state_lefts, state_rights, coefs_tops, coefs_ends,
                coefs_lefts, coefs_rights, land_tops, land_ends, land_lefts, land_rights,
                x_low, x_high, y_low, y_high):
    nfield = state_tops.shape[1]
    last_row, last_lane = state_tops.shape[2] - 1, state_lefts.shape[3] - 1
    atmos = mix_ref[0, 1] == 1.0

    def kept(land):
        return jnp.where(atmos, 1.0, land.astype(jnp.float32))

    for out, state, coefs, land, lines in (
        (x_low, state_tops, coefs_tops, land_tops, (0, 1)),
        (x_high, state_ends, coefs_ends, land_ends, (last_row - 1, last_row)),
    ):
        outer = lines[0] if lines[0] == 0 else lines[1]
        out[2 * nfield :, :] = jnp.zeros((8, out.shape[1]), jnp.float32)
        for j, line in enumerate(lines):
            for f in range(nfield):
                out[j * nfield + f : j * nfield + f + 1, :] = state[0, f, line : line + 1, :]
        for c in range(3):
            out[2 * nfield + c : 2 * nfield + c + 1, :] = coefs[0, c, outer : outer + 1, :]
        out[2 * nfield + 3 : 2 * nfield + 4, :] = kept(land[outer : outer + 1, :])

    for out, state, coefs, land, lines in (
        (y_low, state_lefts, coefs_lefts, land_lefts, (0, 1)),
        (y_high, state_rights, coefs_rights, land_rights, (last_lane - 1, last_lane)),
    ):
        outer = lines[0] if lines[0] == 0 else lines[1]
        lane = lax.broadcasted_iota(jnp.int32, land.shape, 1)
        packed = jnp.zeros(land.shape, jnp.float32)

        def put(packed, tile, at, to):
            moved = (to - at) % LANES
            tile = pltpu.roll(tile, moved, 1) if moved else tile
            return jnp.where(lane == to, tile, packed)

        for j, line in enumerate(lines):
            for f in range(nfield):
                packed = put(packed, state[0, f], line, j * nfield + f)
        for c in range(3):
            packed = put(packed, coefs[0, c], outer, 2 * nfield + c)
        packed = put(packed, kept(land[...]), outer, 2 * nfield + 3)
        out[...] = packed.T[: out.shape[0]]


def edges_of(state, coefs, land_sea, mix):
    _, nfield, cells_x, cells_y = state.shape
    lines = line_count(nfield)
    ends = [
        ((8, cells_y), (0, 0)),
        ((8, cells_y), (cells_x // 8 - 1, 0)),
        ((cells_x, LANES), (0, 0)),
        ((cells_x, LANES), (0, cells_y // LANES - 1)),
    ]
    at = lambda lead, place: lambda i: (0,) * len(lead) + place
    specs = [pl.BlockSpec(memory_space=pltpu.SMEM)]
    for lead in ((1, nfield), (1, 3), ()):
        specs += [pl.BlockSpec(lead + shape, at(lead, place)) for shape, place in ends]
    shapes = [(lines, cells_y)] * 2 + [(lines, cells_x)] * 2
    return pl.pallas_call(
        edge_kernel,
        grid=(1,),
        in_specs=specs,
        out_specs=[pl.BlockSpec(shape, lambda i: (0, 0)) for shape in shapes],
        out_shape=[jax.ShapeDtypeStruct(shape, jnp.float32) for shape in shapes],
        compiler_params=pltpu.CompilerParams(vmem_limit_bytes=24 * 1024 * 1024),
        cost_estimate=pl.CostEstimate(
            flops=state.size, bytes_accessed=4 * 1024 * 1024, transcendentals=0
        ),
        name="edges",
    )(mix, *pinned(pltpu.HBM, *[state] * 4), *[coefs] * 4, *[land_sea] * 4)


def outer_section(center, across, along, factors, rate):
    lane = lax.broadcasted_iota(jnp.int32, center.shape, 1)
    count = center.shape[1]
    before = jnp.where(lane == 0, along[0], pltpu.roll(center, 1, 1))
    after = jnp.where(lane == count - 1, along[1], pltpu.roll(center, count - 1, 1))
    keep, low, high, back, ahead, middle = factors
    out = center + low * across[0] + high * across[1] + back * before + ahead * after
    return out + (middle - rate * keep) * center


def base_kernel(half, rate_ref, mix_ref, rates_ref, coefs_ref, land_ref, x_low, x_high, y_low, y_high,
                above, below, left, right, corners_left, corners_right, state_ref,
                out_ref, early_ref, factors, rows, cols):
    f = pl.program_id(0)
    nfield = rates_ref.shape[0]
    lines = line_count(nfield)

    @pl.when(f == 0)
    def _():
        keep = jnp.where(mix_ref[0, 1] == 1.0, 1.0, land_ref[...].astype(jnp.float32))
        for i, factor in enumerate(stencil_factors([coefs_ref[0, c] for c in range(3)], keep)):
            factors[i] = factor
        rate = rates_ref[:, 0:1]
        near, far = pl.ds(0, nfield), pl.ds(nfield, nfield)
        last = corners_left.shape[1] - 1
        corner = (
            (corners_left[nfield : 2 * nfield, last:], corners_left[lines : lines + nfield, last:]),
            (corners_right[nfield : 2 * nfield, 0:1], corners_right[lines : lines + nfield, 0:1]),
        )
        for i, (ref, center, across, along, is_column) in enumerate(
            (
                (above, above[far, :], (above[near, :], x_low[near, :]), (corner[0][0], corner[1][0]), False),
                (below, below[near, :], (x_high[far, :], below[far, :]), (corner[0][1], corner[1][1]), False),
                (left, left[far, :], (left[near, :], y_low[near, :]), corner[0], True),
                (right, right[near, :], (y_high[far, :], right[far, :]), corner[1], True),
            )
        ):
            first = 2 * nfield
            of_line = stencil_factors(
                [ref[first + c : first + c + 1, :] for c in range(3)],
                ref[first + 3 : first + 4, :],
            )
            if is_column:
                of_line = [of_line[j] for j in (0, 3, 4, 1, 2, 5)]
            section = outer_section(center, across, along, of_line, rate)
            kept = cols if is_column else rows
            kept[pl.ds(i % 2 * nfield, nfield), :] = center
            kept[pl.ds((2 + i % 2) * nfield, nfield), :] = section

    mix_a, mix_b = mix_ref[0, 0], mix_ref[0, 1]
    for j in range(PER_STEP):
        field = f * PER_STEP + j
        rate = rate_ref[0, field]
        s = state_ref[0, j]
        row = [rows[pl.ds(i * nfield + field, 1), :] for i in range(4)]
        col = columns_of(
            jnp.concatenate([cols[pl.ds(i * nfield + field, 1), :] for i in range(4)], axis=0)
        )
        s1 = s + tendency(s, rate, factors, row[0], row[1], col[:, 0:1], col[:, 1:2])
        more = tendency(s1, rate, factors, row[2], row[3], col[:, 2:3], col[:, 3:4])
        total = mix_a * s + (1.0 - mix_a) * s1 + mix_b * more
        out_ref[0, j] = total

        @pl.when(field < half)
        def _():
            early_ref[j] = total


def base_of(state, coefs, land_sea, rates, mix, edges, received, corners, half):
    _, nfield, cells_x, cells_y = state.shape
    field = pl.BlockSpec((1, PER_STEP, cells_x, cells_y), lambda f: (0, f, 0, 0))
    early = pl.BlockSpec(
        (PER_STEP, cells_x, cells_y), lambda f: (jnp.minimum(f, half // PER_STEP - 1), 0, 0)
    )
    whole = lambda a: pl.BlockSpec(a.shape, lambda f: (0,) * a.ndim)
    rates_wide = jnp.broadcast_to(rates.T, (nfield, LANES))
    operands = [rates_wide, coefs, land_sea, *edges, *received, *corners]
    return pl.pallas_call(
        functools.partial(base_kernel, half),
        grid=(nfield // PER_STEP,),
        in_specs=[
            pl.BlockSpec(memory_space=pltpu.SMEM),
            pl.BlockSpec(memory_space=pltpu.SMEM),
            *[whole(a) for a in operands],
            field,
        ],
        out_specs=[
            field,
            early,
            pl.BlockSpec((6, cells_x, cells_y), lambda f: (0, 0, 0)),
        ],
        out_shape=[
            jax.ShapeDtypeStruct(state.shape, jnp.float32),
            jax.ShapeDtypeStruct((half, cells_x, cells_y), jnp.float32),
            jax.ShapeDtypeStruct((6, cells_x, cells_y), jnp.float32),
        ],
        scratch_shapes=[
            pltpu.VMEM((4 * nfield, cells_y), jnp.float32),
            pltpu.VMEM((4 * nfield, cells_x), jnp.float32),
        ],
        compiler_params=pltpu.CompilerParams(vmem_limit_bytes=24 * 1024 * 1024),
        cost_estimate=pl.CostEstimate(
            flops=40 * state.size, bytes_accessed=8 * state.size, transcendentals=0
        ),
        name="base",
    )(rates, mix, *operands, *pinned(pltpu.HBM, state))


def finish_kernel(first, with_x, gamma_ref, mix_ref, above, below, before, after, factors, recv,
                  left, right, *rest):
    tops, rest = (rest[:2], rest[2:]) if with_x else (None, rest)
    late, rest = (rest[:2], rest[2:]) if with_x else (None, rest)
    early_base, rest = (rest[0], rest[1:]) if with_x else (None, rest)
    odd_ref, base_ref, rest = rest[0], rest[1], rest[2:]
    new_ref, out_ref, done_ref = rest[-11:-8]
    base, wide, lines, sides, outer, base_sems, out_sems, outer_sems = rest[-8:]
    count, cells_x, cells_y = base.shape
    mix_b = mix_ref[0, 1]
    keep_row = above.shape[0] - 5
    keep = slice(keep_row, keep_row + 1)
    ends = (0, cells_x - STRIP)

    def base_copy(f):
        return pltpu.make_async_copy(base_ref.at[0, first + f], base.at[f], base_sems.at[f])

    def out_copies(f):
        return (
            pltpu.make_async_copy(recv.at[f], out_ref.at[0, first + f], out_sems.at[0, f]),
            pltpu.make_async_copy(base.at[f], new_ref.at[0, first + f], out_sems.at[1, f]),
        )

    def outer_copy(f, i, back):
        there = (new_ref if back else base_ref).at[0, count + f, pl.ds(ends[i], STRIP), :]
        here = outer.at[f, i]
        pair = (here, there) if back else (there, here)
        return pltpu.make_async_copy(*pair, outer_sems.at[f, i])

    outer_rows = [(f, i) for f in range(count) for i in range(2)] if with_x else []
    if not with_x:
        for f in range(count):
            base_copy(f).start()
    for f, i in outer_rows:
        outer_copy(f, i, False).start()
    done_ref[...] = jnp.zeros_like(done_ref)
    def in_order(i, pair):
        odd = odd_ref[0, i] == 1
        in_odd, in_even = pair[0][...], pair[1][...]
        return jnp.where(odd, in_even, in_odd), jnp.where(odd, in_odd, in_even)

    if with_x:
        top, bottom = in_order(0, tops)
        lines[:count, :] = top * above[keep, :]
        lines[count:, :] = bottom * below[keep, :]
        late = in_order(0, late)
    else:
        lines[...] = jnp.zeros_like(lines)
    left, right = in_order(1, (left, right))
    sides[:count, :] = left * before[keep, :]
    sides[count:, :] = right * after[keep, :]
    lane = lax.broadcasted_iota(jnp.int32, (STRIP, cells_y), 1)

    def one_field(f, carry):
        rate = gamma_ref[0, first + f]
        both = [sides[pl.ds(f, 1), :] * rate, sides[pl.ds(count + f, 1), :] * rate]
        cols = columns_of(jnp.concatenate(both, axis=0))
        wide[STRIP - 1 : STRIP, :] = lines[pl.ds(f, 1), :] * rate
        wide[STRIP + cells_x : STRIP + cells_x + 1, :] = lines[pl.ds(count + f, 1), :] * rate
        to_out, to_new = out_copies(f)
        to_out.start()
        for i in range(0, cells_x, STRIP):
            rows = slice(i, i + STRIP)
            wide[STRIP + i : 2 * STRIP + i, :] = factors[0, rows, :] * recv[f, rows, :] * rate
        if not with_x:
            base_copy(f).wait()
        start = early_base if with_x else base
        for i in range(0, cells_x, STRIP):
            rows = slice(i, i + STRIP)
            mid = wide[STRIP + i : 2 * STRIP + i, :]
            more = (factors[5, rows, :] - rate * factors[0, rows, :]) * mid
            more += factors[1, rows, :] * wide[STRIP + i - 1 : 2 * STRIP + i - 1, :]
            more += factors[2, rows, :] * wide[STRIP + i + 1 : 2 * STRIP + i + 1, :]
            prior = jnp.where(lane == 0, cols[rows, 0:1], pltpu.roll(mid, 1, 1))
            later = jnp.where(lane == cells_y - 1, cols[rows, 1:2], pltpu.roll(mid, cells_y - 1, 1))
            more += factors[3, rows, :] * prior + factors[4, rows, :] * later
            base[f, rows, :] = start[f, rows, :] + mix_b * (2.0 * mid + more)
        to_new.start()
        return carry

    def add_lines():
        for f, i in outer_rows:
            outer_copy(f, i, False).wait()
            row = i * (STRIP - 1)
            at = ends[i] + row
            line = late[i][f : f + 1, :] * (above, below)[i][keep, :] * gamma_ref[0, count + f]
            more = mix_b * factors[1 + i, at : at + 1, :] * line
            outer[f, i, row : row + 1, :] = outer[f, i, row : row + 1, :] + more
            outer_copy(f, i, True).start()

    lax.fori_loop(0, count - 1, one_field, 0)
    add_lines()
    one_field(count - 1, 0)
    for f in range(count):
        for copy in out_copies(f):
            copy.wait()
    for f, i in outer_rows:
        outer_copy(f, i, True).wait()


def finished(
    first, new_state, remapped, recv, odd, x_rims, y_rims, closing, gamma, mix, factors, received
):
    count, cells_x, cells_y = recv.shape
    chan = gamma.shape[1]
    with_x = x_rims is not None
    anywhere = pl.BlockSpec(memory_space=pl.ANY)
    operands = [gamma, mix, *received, factors, recv, *y_rims]
    if with_x:
        late_rims, base_early, late_done = closing
        operands += [*x_rims, *late_rims, base_early]
    scalars = pl.BlockSpec(memory_space=pltpu.SMEM)
    specs = [scalars] * 2 + [pl.BlockSpec(memory_space=pltpu.VMEM)] * (len(operands) - 2)
    operands.append(odd)
    specs += [scalars, anywhere]
    aliases = {len(operands): 0}
    operands.append(new_state)
    if remapped is not None:
        aliases[len(operands)] = 1
        operands += [remapped, late_done]
        specs += [anywhere, anywhere]
    return pl.pallas_call(
        functools.partial(finish_kernel, first, with_x),
        in_specs=specs,
        out_specs=[anywhere, anywhere, pl.BlockSpec(memory_space=pltpu.VMEM)],
        out_shape=[
            jax.ShapeDtypeStruct(new_state.shape, jnp.float32),
            jax.ShapeDtypeStruct((1, chan, cells_x, cells_y), jnp.float32),
            jax.ShapeDtypeStruct((8, LANES), jnp.float32),
        ],
        input_output_aliases=aliases,
        scratch_shapes=[
            pltpu.VMEM((count, cells_x, cells_y), jnp.float32),
            pltpu.VMEM((cells_x + 2 * STRIP, cells_y), jnp.float32),
            pltpu.VMEM((2 * count, cells_y), jnp.float32),
            pltpu.VMEM((2 * count, cells_x), jnp.float32),
            pltpu.VMEM((count, 2, STRIP, cells_y), jnp.float32),
            pltpu.SemaphoreType.DMA((count,)),
            pltpu.SemaphoreType.DMA((2, count)),
            pltpu.SemaphoreType.DMA((count, 2)),
        ],
        compiler_params=pltpu.CompilerParams(vmem_limit_bytes=12 * 1024 * 1024),
        cost_estimate=pl.CostEstimate(
            flops=20 * recv.size, bytes_accessed=20 * recv.size, transcendentals=0
        ),
        name="finish",
    )(*operands)


def body(state, coefs, land_sea, gamma, pair_src, pair_dev, pair_blk, weights):
    tx, ty = lax.axis_size("tx"), lax.axis_size("ty")
    tiles = tx * ty
    nfield, cells_x, cells_y = state.shape[1:]
    chan = gamma.shape[1]
    pairs, width = weights.shape[1], weights.shape[2]
    capacity = max(2, 2 * pairs // tiles)
    half = chan // 2
    early, late = contributions(
        state, pair_src, pair_dev, pair_blk, weights, tiles, capacity, chan
    )
    swap = [(0, 1), (1, 0)]

    def exchanged(rows):
        rows = rows.reshape(tiles, -1, half, width)
        return lax.all_to_all(rows, ("tx", "ty"), split_axis=0, concat_axis=0, tiled=True)

    def add_up(odd, ids, rows, space):
        return summed(odd, ids, rows, tiles, capacity, half, cells_x, cells_y, width, space)

    late_in = exchanged(late)
    early = lax.ppermute(early, "comp", swap)
    early_in = placed_rows(early, tiles, capacity, pairs, cells_x * cells_y // width)

    land_after, _ = lax.optimization_barrier((land_sea, late))
    is_atmos = lax.axis_index("comp") == 0
    mix = jnp.where(is_atmos, jnp.array([[0.0, 1.0]]), jnp.array([[0.5, 0.5]]))
    mix = mix.astype(jnp.float32)
    rates = jnp.concatenate([gamma, jnp.zeros((1, nfield - chan), jnp.float32)], axis=1)
    x_low, x_high, y_low, y_high = edges_of(state, coefs, land_after, mix)
    left = lax.ppermute(y_high, "ty", shift_pairs(ty, 1))
    right = lax.ppermute(y_low, "ty", shift_pairs(ty, -1))
    above = lax.ppermute(x_high, "tx", shift_pairs(tx, 1))
    below = lax.ppermute(x_low, "tx", shift_pairs(tx, -1))
    early_in, above, below, left, right = lax.optimization_barrier(
        (early_in, above, below, left, right)
    )
    received = (above, below, left, right)
    early_in = exchanged(early_in)

    ends = jnp.concatenate([above[:, cells_y - LANES :], below[:, cells_y - LANES :]], axis=0)
    starts = jnp.concatenate([above[:, :LANES], below[:, :LANES]], axis=0)
    corners_left = lax.ppermute(ends, "ty", shift_pairs(ty, 1))
    corners_right = lax.ppermute(starts, "ty", shift_pairs(ty, -1))
    base, base_early, factors = base_of(
        state, coefs, land_after, rates, mix, (x_low, x_high, y_low, y_high), received,
        (corners_left, corners_right), half,
    )

    ids_late = late_in[:, capacity, 0, :]
    ids_early = lax.ppermute(ids_late, "comp", swap)
    odd = jnp.stack([lax.axis_index("tx"), lax.axis_index("ty")]).astype(jnp.int32)[None] & 1
    recv_late, x_odd, x_even, y_odd, y_even = add_up(odd, ids_late, late_in, pltpu.HBM)
    recv_late = lax.ppermute(recv_late, "comp", swap)
    late_x = (
        lax.ppermute(x_odd, ("comp", "tx"), crossed("tx", 1)),
        lax.ppermute(x_even, ("comp", "tx"), crossed("tx", 0)),
    )
    late_y = (
        lax.ppermute(y_odd, ("comp", "ty"), crossed("ty", 1)),
        lax.ppermute(y_even, ("comp", "ty"), crossed("ty", 0)),
    )
    rest = (gamma, mix, factors, received)
    new_state, remapped, done = finished(
        half, base, None, recv_late, odd, None, late_y, None, *rest
    )
    early_in, done = lax.optimization_barrier((early_in, done))
    recv_early, x_odd, x_even, y_odd, y_even = add_up(odd, ids_early, early_in, pltpu.VMEM)
    early_x = (
        lax.ppermute(x_odd, "tx", neighbour_pairs(tx, 1)),
        lax.ppermute(x_even, "tx", neighbour_pairs(tx, 0)),
    )
    early_y = (
        lax.ppermute(y_odd, "ty", neighbour_pairs(ty, 1)),
        lax.ppermute(y_even, "ty", neighbour_pairs(ty, 0)),
    )
    new_state, remapped, _ = finished(
        0, new_state, remapped, recv_early, odd, early_x, early_y, (late_x, base_early, done), *rest
    )
    return new_state, remapped


def solution(mesh):
    placed = (
        P("comp", None, "tx", "ty"),
        P("comp", None, "tx", "ty"),
        P("tx", "ty"),
        P("comp", None),
        P("comp", ("tx", "ty")),
        P("comp", ("tx", "ty"), None),
        P("comp", ("tx", "ty")),
        P("comp", ("tx", "ty"), None, None),
    )
    return jax.shard_map(
        body,
        mesh=mesh,
        in_specs=placed,
        out_specs=(P("comp", None, "tx", "ty"), P("comp", None, "tx", "ty")),
        check_vma=False,
    )
```

```python
import functools

import jax
import jax.numpy as jnp
from jax import lax
from jax.experimental import pallas as pl
from jax.experimental.pallas import tpu as pltpu
from jax.sharding import PartitionSpec as P

LANES = 128
STEP_PAIRS = 64
STRIP = 8
PER_STEP = 2
NT = (((1,), (1,)), ((), ()))


def pinned(space, *arrays):
    return [pltpu.with_memory_space_constraint(a, space) for a in arrays]


def shift_pairs(count, by):
    return [(i, i + by) for i in range(count) if 0 <= i + by < count]


def neighbour_pairs(count, first):
    lows = range(first, count - 1, 2)
    return [(i, i + 1) for i in lows] + [(i + 1, i) for i in lows]


def crossed(axis, first):
    count = lax.axis_size(axis)
    pairs = neighbour_pairs(count, first)
    return [(c * count + i, (1 - c) * count + j) for c in range(2) for i, j in pairs]


def split(value, parts):
    if parts & (parts - 1) == 0:
        return lax.shift_right_logical(value, parts.bit_length() - 1), value & (parts - 1)
    return lax.div(value, parts), lax.rem(value, parts)


def ranks(dev, tiles):
    pairs = dev.shape[1]
    tile_of = lax.broadcasted_iota(jnp.int32, (tiles, pairs), 0)
    lane_of = lax.broadcasted_iota(jnp.int32, (tiles, pairs), 1)
    member = (tile_of == dev).astype(jnp.float32)
    total = member
    shift = 1
    while shift < pairs:
        total = total + jnp.where(lane_of >= shift, pltpu.roll(total, shift, 1), 0.0)
        shift *= 2
    return member, (jnp.sum(member * total, axis=0, keepdims=True) - 1.0).astype(jnp.int32)


def slot_blocks(dev, blk, tiles, capacity):
    member, rank = ranks(dev, tiles)
    pairs = dev.shape[1]
    slot_of = lax.broadcasted_iota(jnp.int32, (LANES, pairs), 0) % capacity
    chosen = (slot_of == rank).astype(jnp.bfloat16)

    def spread(values):
        return lax.dot_general(
            (member * values).astype(jnp.bfloat16), chosen, NT, preferred_element_type=jnp.float32
        )

    high, low = split(blk, 256)
    ids = spread(high.astype(jnp.float32)) * 256.0 + spread(low.astype(jnp.float32))
    return jnp.where(spread(jnp.ones(dev.shape, jnp.float32)) > 0.5, ids, -1.0)


def contribution_kernel(
    dims, src_ref, dev_ref, blk_ref, state_ref, weights_ref, early_ref, late_ref,
    cells, w_ref, pair_v, pair_s, taken, field_sems, weight_sems, pair_sems,
):
    tiles, capacity, pairs, fields, cells_x, cells_y, width = dims
    half = fields // 2
    parts = cells_y // width
    steps = pairs // STEP_PAIRS

    scalar_copies = [
        pltpu.make_async_copy(ref, pair_s.at[pl.ds(i, 1), :], pair_sems.at[i])
        for i, ref in enumerate((src_ref, dev_ref))
    ]
    vector_copies = [
        pltpu.make_async_copy(ref, pair_v.at[i], pair_sems.at[2 + i])
        for i, ref in enumerate((dev_ref, blk_ref))
    ]
    field_copies = [
        pltpu.make_async_copy(
            state_ref.at[0, f, :, pl.ds(q * width, width)],
            cells.at[q, :, f, :],
            field_sems.at[f * parts + q],
        )
        for f in range(fields)
        for q in range(parts)
    ]

    def weight_copy(step):
        some = pl.ds(step * STEP_PAIRS, STEP_PAIRS)
        return pltpu.make_async_copy(
            weights_ref.at[0, some], w_ref.at[some], weight_sems.at[step]
        )

    for copy in scalar_copies + vector_copies + field_copies:
        copy.start()
    for step in range(steps):
        weight_copy(step).start()
    late_ref[...] = jnp.zeros_like(late_ref)
    for t in range(tiles):
        taken[t] = t * (capacity + 1)

    for copy in vector_copies:
        copy.wait()
    dev, blk = pair_v[0], pair_v[1]
    ids = slot_blocks(dev, blk, tiles, capacity)
    for t in range(tiles):
        row = jnp.broadcast_to(ids[t : t + 1, :], late_ref.shape[1:])
        late_ref[t * (capacity + 1) + capacity] = row
    code = (dev * (cells_x * parts) + blk).astype(jnp.float32)
    for i in range(pairs // width):
        place = (pairs + i // half, slice(i % half, i % half + 1), slice(None))
        early_ref[place] = code[:, i * width : (i + 1) * width]
    for copy in scalar_copies + field_copies:
        copy.wait()

    def cells_of(p):
        x, part = split(pair_s[0, p], parts)
        return cells[part, x]

    zeros = jnp.zeros((fields, width), jnp.float32)

    def some_pairs(step, carry):
        weight_copy(step).wait()
        for i in range(0, STEP_PAIRS, 4):
            p = step * STEP_PAIRS + i
            left = [
                jnp.concatenate([cells_of(p + j), zeros][:: 1 - j % 2 * 2], axis=1) for j in range(4)
            ]
            left = jnp.concatenate(left, axis=0).astype(jnp.bfloat16)
            w = [w_ref[p + j] for j in range(4)]
            right = jnp.concatenate(
                [jnp.concatenate(w[:2], axis=1), jnp.concatenate(w[2:], axis=1)], axis=0
            )
            four = lax.dot_general(left, right, NT, preferred_element_type=jnp.float32)
            for j in range(4):
                tile = pair_s[1, p + j]
                slot = taken[tile]
                taken[tile] = slot + 1
                at = j // 2 * width
                one = four[j * fields : (j + 1) * fields, at : at + width]
                early_ref[p + j] = one[:half]
                late_ref[slot] = one[half:]
        return carry

    lax.fori_loop(0, steps, some_pairs, 0)


def contributions(state, pair_src, pair_dev, pair_blk, weights, tiles, capacity, fields):
    _, _, cells_x, cells_y = state.shape
    half = fields // 2
    pairs, width = weights.shape[1], weights.shape[2]
    rows = tiles * (capacity + 1)
    dims = (tiles, capacity, pairs, fields, cells_x, cells_y, width)
    parts = cells_y // width
    shapes = [(pairs + -(-pairs // (half * width)), half, width), (rows, half, width)]
    return pl.pallas_call(
        functools.partial(contribution_kernel, dims),
        in_specs=[pl.BlockSpec(memory_space=pltpu.HBM)] * 5,
        out_specs=[pl.BlockSpec(memory_space=pltpu.VMEM) for _ in shapes],
        out_shape=[jax.ShapeDtypeStruct(shape, jnp.float32) for shape in shapes],
        scratch_shapes=[
            pltpu.VMEM((parts, cells_x, fields, width), jnp.float32),
            pltpu.VMEM((pairs, width, width), jnp.bfloat16),
            pltpu.VMEM((2, 1, pairs), jnp.int32),
            pltpu.SMEM((2, pairs), jnp.int32),
            pltpu.SMEM((tiles,), jnp.int32),
            pltpu.SemaphoreType.DMA((parts * fields,)),
            pltpu.SemaphoreType.DMA((pairs // STEP_PAIRS,)),
            pltpu.SemaphoreType.DMA((4,)),
        ],
        compiler_params=pltpu.CompilerParams(vmem_limit_bytes=40 * 1024 * 1024),
        cost_estimate=pl.CostEstimate(
            flops=2 * pairs * fields * width * width,
            bytes_accessed=2 * pairs * width * width + 8 * rows * fields * width,
            transcendentals=0,
        ),
        name="contributions",
    )(*pinned(pltpu.HBM, pair_src, pair_dev.reshape(1, pairs), pair_blk, state, weights))


def place_kernel(dims, in_ref, out_ref, place_v, place_s, place_sem):
    tiles, capacity, pairs, blocks = dims
    half, width = in_ref.shape[1:]
    code = jnp.concatenate(
        [in_ref[pairs + i // half][i % half : i % half + 1] for i in range(pairs // width)], axis=1
    ).astype(jnp.int32)
    dev, _ = split(code, blocks)
    rank = ranks(dev, tiles)[1]
    place_v[...] = jnp.broadcast_to(dev * capacity + rank, place_v.shape)
    copy = pltpu.make_async_copy(place_v, place_s, place_sem)
    copy.start()
    out_ref[...] = jnp.zeros_like(out_ref)
    copy.wait()

    def some_rows(step, carry):
        for i in range(STEP_PAIRS):
            p = step * STEP_PAIRS + i
            out_ref[place_s[0, p]] = in_ref[p]
        return carry

    lax.fori_loop(0, pairs // STEP_PAIRS, some_rows, 0)


def placed_rows(rows, tiles, capacity, pairs, blocks):
    half, width = rows.shape[1:]
    shape = (tiles * capacity, half, width)
    return pl.pallas_call(
        functools.partial(place_kernel, (tiles, capacity, pairs, blocks)),
        out_shape=jax.ShapeDtypeStruct(shape, jnp.float32),
        scratch_shapes=[
            pltpu.VMEM((8, pairs), jnp.int32),
            pltpu.SMEM((8, pairs), jnp.int32),
            pltpu.SemaphoreType.DMA,
        ],
        compiler_params=pltpu.CompilerParams(vmem_limit_bytes=10 * 1024 * 1024),
        cost_estimate=pl.CostEstimate(
            flops=4 * rows.size, bytes_accessed=12 * rows.size, transcendentals=0
        ),
        name="place_in_slots",
    )(rows)


def sum_kernel(dims, odd_ref, ids_ref, rows_ref, out_ref, x0_ref, x1_ref, y0_ref, y1_ref,
               pick, high, low, in_ref, row_sems):
    tiles, capacity, fields, cells_x, cells_y, width = dims
    parts = cells_y // width
    group = LANES // capacity
    stride = in_ref.shape[0] // tiles

    def rows_copy(k):
        some = pl.ds(k * group * stride, group * stride)
        return pltpu.make_async_copy(rows_ref.at[some, :], in_ref.at[some, :], row_sems.at[k])

    for k in range(tiles // group):
        rows_copy(k).start()
    block_of = lax.broadcasted_iota(jnp.int32, (cells_x * parts, LANES), 0)
    block_of = (block_of % cells_x) * parts + block_of // cells_x
    block_of = block_of.astype(jnp.float32)
    lane = lax.broadcasted_iota(jnp.int32, (1, LANES), 1)
    for k in range(tiles // group):
        ids = None
        for i in range(group):
            row = ids_ref[pl.ds(k * group + i, 1), :]
            ids = row if ids is None else jnp.where(lane // capacity == i, row, ids)
        pick[:, pl.ds(k * LANES, LANES)] = (block_of == ids).astype(jnp.bfloat16)
    for k in range(tiles // group):
        rows_copy(k).wait()
        for source in range(k * group, (k + 1) * group):
            for f in range(fields):
                x = in_ref[pl.ds(source * stride + f, capacity, stride=fields), :]
                rounded = x.astype(jnp.bfloat16)
                place = (
                    pl.ds(source * capacity, capacity),
                    pl.ds(f * width, width),
                )
                high[place] = rounded
                low[place] = (x - rounded.astype(jnp.float32)).astype(jnp.bfloat16)

    def in_order(i, low_rim, high_rim):
        odd = odd_ref[i : i + 1, :] == 1.0
        return jnp.where(odd, high_rim, low_rim), jnp.where(odd, low_rim, high_rim)

    columns = {}
    for q in range(parts):
        chosen = pick[pl.ds(q * cells_x, cells_x), :]
        total = jnp.dot(chosen, high[...], preferred_element_type=jnp.float32)
        total = total + jnp.dot(chosen, low[...], preferred_element_type=jnp.float32)
        for f in range(fields):
            tile = total[:, f * width : (f + 1) * width]
            out_ref[f, :, pl.ds(q * width, width)] = tile
            rims = in_order(0, tile[:1], tile[cells_x - 1 :])
            for rim_ref, rim in zip((x0_ref, x1_ref), rims):
                rim_ref[pl.ds(f, 1), pl.ds(q * width, width)] = rim
            if q in (0, parts - 1):
                columns[q, f] = tile.T[:1] if q == 0 else tile.T[width - 1 :]
    for f in range(fields):
        rims = in_order(1, columns[0, f], columns[parts - 1, f])
        y0_ref[pl.ds(f, 1), :], y1_ref[pl.ds(f, 1), :] = rims


def summed(odd, ids, rows, tiles, capacity, fields, cells_x, cells_y, width):
    dims = (tiles, capacity, fields, cells_x, cells_y, width)
    rows = rows.reshape(-1, width)
    slots = tiles * capacity
    blocks = cells_x * cells_y // width
    shapes = [
        (fields, cells_x, cells_y),
        (fields, cells_y),
        (fields, cells_y),
        (fields, cells_x),
        (fields, cells_x),
    ]
    return pl.pallas_call(
        functools.partial(sum_kernel, dims),
        in_specs=[pl.BlockSpec(memory_space=pltpu.VMEM)] * 2
        + [pl.BlockSpec(memory_space=pltpu.HBM)],
        out_shape=[jax.ShapeDtypeStruct(shape, jnp.float32) for shape in shapes],
        scratch_shapes=[
            pltpu.VMEM((blocks, slots), jnp.bfloat16),
            pltpu.VMEM((slots, fields * width), jnp.bfloat16),
            pltpu.VMEM((slots, fields * width), jnp.bfloat16),
            pltpu.VMEM(rows.shape, jnp.float32),
            pltpu.SemaphoreType.DMA((tiles * capacity // LANES,)),
        ],
        compiler_params=pltpu.CompilerParams(vmem_limit_bytes=24 * 1024 * 1024),
        cost_estimate=pl.CostEstimate(
            flops=4 * blocks * slots * fields * width,
            bytes_accessed=4 * fields * width * (slots + blocks),
            transcendentals=0,
        ),
        name="sum_by_block",
    )(odd, ids, *pinned(pltpu.HBM, rows))


def stencil_factors(coefs, keep):
    u, v, kappa = coefs
    return [
        keep,
        keep * (jnp.maximum(u, 0.0) + kappa),
        keep * (kappa - jnp.minimum(u, 0.0)),
        keep * (jnp.maximum(v, 0.0) + kappa),
        keep * (kappa - jnp.minimum(v, 0.0)),
        -keep * (jnp.abs(u) + jnp.abs(v) + 4.0 * kappa),
    ]


def tendency(s, rate, factors, top, bottom, left, right):
    cells_x, cells_y = s.shape
    x_of = lax.broadcasted_iota(jnp.int32, s.shape, 0)
    y_of = lax.broadcasted_iota(jnp.int32, s.shape, 1)
    out = (factors[5] - rate * factors[0]) * s
    out += factors[1] * jnp.where(x_of == 0, top, pltpu.roll(s, 1, 0))
    out += factors[2] * jnp.where(x_of == cells_x - 1, bottom, pltpu.roll(s, cells_x - 1, 0))
    out += factors[3] * jnp.where(y_of == 0, left, pltpu.roll(s, 1, 1))
    out += factors[4] * jnp.where(y_of == cells_y - 1, right, pltpu.roll(s, cells_y - 1, 1))
    return out


def columns_of(rows):
    spare = 8 - rows.shape[0]
    if spare:
        rows = jnp.concatenate([rows, jnp.zeros((spare, rows.shape[1]), rows.dtype)], axis=0)
    return rows.T


def line_count(nfield):
    return 2 * nfield + 8


def edge_kernel(mix_ref, state_tops, state_ends, state_lefts, state_rights, coefs_tops, coefs_ends,
                coefs_lefts, coefs_rights, land_tops, land_ends, land_lefts, land_rights,
                x_low, x_high, y_low, y_high):
    nfield = state_tops.shape[1]
    last_row, last_lane = state_tops.shape[2] - 1, state_lefts.shape[3] - 1
    atmos = mix_ref[0, 1] == 1.0

    def kept(land):
        return jnp.where(atmos, 1.0, land.astype(jnp.float32))

    for out, state, coefs, land, lines in (
        (x_low, state_tops, coefs_tops, land_tops, (0, 1)),
        (x_high, state_ends, coefs_ends, land_ends, (last_row - 1, last_row)),
    ):
        outer = lines[0] if lines[0] == 0 else lines[1]
        out[2 * nfield :, :] = jnp.zeros((8, out.shape[1]), jnp.float32)
        for j, line in enumerate(lines):
            for f in range(nfield):
                out[j * nfield + f : j * nfield + f + 1, :] = state[0, f, line : line + 1, :]
        for c in range(3):
            out[2 * nfield + c : 2 * nfield + c + 1, :] = coefs[0, c, outer : outer + 1, :]
        out[2 * nfield + 3 : 2 * nfield + 4, :] = kept(land[outer : outer + 1, :])

    for out, state, coefs, land, lines in (
        (y_low, state_lefts, coefs_lefts, land_lefts, (0, 1)),
        (y_high, state_rights, coefs_rights, land_rights, (last_lane - 1, last_lane)),
    ):
        outer = lines[0] if lines[0] == 0 else lines[1]
        lane = lax.broadcasted_iota(jnp.int32, land.shape, 1)
        packed = jnp.zeros(land.shape, jnp.float32)

        def put(packed, tile, at, to):
            moved = (to - at) % LANES
            tile = pltpu.roll(tile, moved, 1) if moved else tile
            return jnp.where(lane == to, tile, packed)

        for j, line in enumerate(lines):
            for f in range(nfield):
                packed = put(packed, state[0, f], line, j * nfield + f)
        for c in range(3):
            packed = put(packed, coefs[0, c], outer, 2 * nfield + c)
        packed = put(packed, kept(land[...]), outer, 2 * nfield + 3)
        out[...] = packed.T[: out.shape[0]]


def edges_of(state, coefs, land_sea, mix):
    _, nfield, cells_x, cells_y = state.shape
    lines = line_count(nfield)
    ends = [
        ((8, cells_y), (0, 0)),
        ((8, cells_y), (cells_x // 8 - 1, 0)),
        ((cells_x, LANES), (0, 0)),
        ((cells_x, LANES), (0, cells_y // LANES - 1)),
    ]
    at = lambda lead, place: lambda i: (0,) * len(lead) + place
    specs = [pl.BlockSpec(memory_space=pltpu.SMEM)]
    for lead in ((1, nfield), (1, 3), ()):
        specs += [pl.BlockSpec(lead + shape, at(lead, place)) for shape, place in ends]
    shapes = [(lines, cells_y)] * 2 + [(lines, cells_x)] * 2
    return pl.pallas_call(
        edge_kernel,
        grid=(1,),
        in_specs=specs,
        out_specs=[pl.BlockSpec(shape, lambda i: (0, 0)) for shape in shapes],
        out_shape=[jax.ShapeDtypeStruct(shape, jnp.float32) for shape in shapes],
        compiler_params=pltpu.CompilerParams(vmem_limit_bytes=24 * 1024 * 1024),
        cost_estimate=pl.CostEstimate(
            flops=state.size, bytes_accessed=4 * 1024 * 1024, transcendentals=0
        ),
        name="edges",
    )(mix, *pinned(pltpu.HBM, *[state] * 4), *[coefs] * 4, *[land_sea] * 4)


def outer_section(center, across, along, factors, rate):
    lane = lax.broadcasted_iota(jnp.int32, center.shape, 1)
    count = center.shape[1]
    before = jnp.where(lane == 0, along[0], pltpu.roll(center, 1, 1))
    after = jnp.where(lane == count - 1, along[1], pltpu.roll(center, count - 1, 1))
    keep, low, high, back, ahead, middle = factors
    out = center + low * across[0] + high * across[1] + back * before + ahead * after
    return out + (middle - rate * keep) * center


def base_kernel(half, rate_ref, mix_ref, rates_ref, coefs_ref, land_ref, x_low, x_high, y_low, y_high,
                above, below, left, right, corners_left, corners_right, state_ref,
                out_ref, early_ref, factors, rows, cols):
    f = pl.program_id(0)
    nfield = rates_ref.shape[0]
    lines = line_count(nfield)

    @pl.when(f == 0)
    def _():
        keep = jnp.where(mix_ref[0, 1] == 1.0, 1.0, land_ref[...].astype(jnp.float32))
        for i, factor in enumerate(stencil_factors([coefs_ref[0, c] for c in range(3)], keep)):
            factors[i] = factor
        rate = rates_ref[:, 0:1]
        near, far = pl.ds(0, nfield), pl.ds(nfield, nfield)
        last = corners_left.shape[1] - 1
        corner = (
            (corners_left[nfield : 2 * nfield, last:], corners_left[lines : lines + nfield, last:]),
            (corners_right[nfield : 2 * nfield, 0:1], corners_right[lines : lines + nfield, 0:1]),
        )
        for i, (ref, center, across, along, is_column) in enumerate(
            (
                (above, above[far, :], (above[near, :], x_low[near, :]), (corner[0][0], corner[1][0]), False),
                (below, below[near, :], (x_high[far, :], below[far, :]), (corner[0][1], corner[1][1]), False),
                (left, left[far, :], (left[near, :], y_low[near, :]), corner[0], True),
                (right, right[near, :], (y_high[far, :], right[far, :]), corner[1], True),
            )
        ):
            first = 2 * nfield
            of_line = stencil_factors(
                [ref[first + c : first + c + 1, :] for c in range(3)],
                ref[first + 3 : first + 4, :],
            )
            if is_column:
                of_line = [of_line[j] for j in (0, 3, 4, 1, 2, 5)]
            section = outer_section(center, across, along, of_line, rate)
            kept = cols if is_column else rows
            kept[pl.ds(i % 2 * nfield, nfield), :] = center
            kept[pl.ds((2 + i % 2) * nfield, nfield), :] = section

    mix_a, mix_b = mix_ref[0, 0], mix_ref[0, 1]
    for j in range(PER_STEP):
        field = f * PER_STEP + j
        rate = rate_ref[0, field]
        s = state_ref[0, j]
        row = [rows[pl.ds(i * nfield + field, 1), :] for i in range(4)]
        col = columns_of(
            jnp.concatenate([cols[pl.ds(i * nfield + field, 1), :] for i in range(4)], axis=0)
        )
        s1 = s + tendency(s, rate, factors, row[0], row[1], col[:, 0:1], col[:, 1:2])
        more = tendency(s1, rate, factors, row[2], row[3], col[:, 2:3], col[:, 3:4])
        total = mix_a * s + (1.0 - mix_a) * s1 + mix_b * more
        out_ref[0, j] = total

        @pl.when(field < half)
        def _():
            early_ref[j] = total


def base_of(state, coefs, land_sea, rates, mix, edges, received, corners, half):
    _, nfield, cells_x, cells_y = state.shape
    field = pl.BlockSpec((1, PER_STEP, cells_x, cells_y), lambda f: (0, f, 0, 0))
    early = pl.BlockSpec(
        (PER_STEP, cells_x, cells_y), lambda f: (jnp.minimum(f, half // PER_STEP - 1), 0, 0)
    )
    whole = lambda a: pl.BlockSpec(a.shape, lambda f: (0,) * a.ndim)
    rates_wide = jnp.broadcast_to(rates.T, (nfield, LANES))
    operands = [rates_wide, coefs, land_sea, *edges, *received, *corners]
    return pl.pallas_call(
        functools.partial(base_kernel, half),
        grid=(nfield // PER_STEP,),
        in_specs=[
            pl.BlockSpec(memory_space=pltpu.SMEM),
            pl.BlockSpec(memory_space=pltpu.SMEM),
            *[whole(a) for a in operands],
            field,
        ],
        out_specs=[
            field,
            early,
            pl.BlockSpec((6, cells_x, cells_y), lambda f: (0, 0, 0)),
        ],
        out_shape=[
            jax.ShapeDtypeStruct(state.shape, jnp.float32),
            jax.ShapeDtypeStruct((half, cells_x, cells_y), jnp.float32),
            jax.ShapeDtypeStruct((6, cells_x, cells_y), jnp.float32),
        ],
        scratch_shapes=[
            pltpu.VMEM((4 * nfield, cells_y), jnp.float32),
            pltpu.VMEM((4 * nfield, cells_x), jnp.float32),
        ],
        compiler_params=pltpu.CompilerParams(vmem_limit_bytes=24 * 1024 * 1024),
        cost_estimate=pl.CostEstimate(
            flops=40 * state.size, bytes_accessed=8 * state.size, transcendentals=0
        ),
        name="base",
    )(rates, mix, *operands, *pinned(pltpu.HBM, state))


def finish_kernel(first, with_x, gamma_ref, mix_ref, above, below, before, after, factors, recv,
                  left, right, *rest):
    tops, rest = (rest[:2], rest[2:]) if with_x else (None, rest)
    late, rest = (rest[:2], rest[2:]) if with_x else (None, rest)
    early_base, rest = (rest[0], rest[1:]) if with_x else (None, rest)
    odd_ref, base_ref, rest = rest[0], rest[1], rest[2:]
    new_ref, out_ref, done_ref = rest[-11:-8]
    base, wide, lines, sides, outer, base_sems, out_sems, outer_sems = rest[-8:]
    count, cells_x, cells_y = base.shape
    mix_b = mix_ref[0, 1]
    keep_row = above.shape[0] - 5
    keep = slice(keep_row, keep_row + 1)
    ends = (0, cells_x - STRIP)

    def base_copy(f):
        return pltpu.make_async_copy(base_ref.at[0, first + f], base.at[f], base_sems.at[f])

    def out_copies(f):
        return (
            pltpu.make_async_copy(recv.at[f], out_ref.at[0, first + f], out_sems.at[0, f]),
            pltpu.make_async_copy(base.at[f], new_ref.at[0, first + f], out_sems.at[1, f]),
        )

    def outer_copy(f, i, back):
        there = (new_ref if back else base_ref).at[0, count + f, pl.ds(ends[i], STRIP), :]
        here = outer.at[f, i]
        pair = (here, there) if back else (there, here)
        return pltpu.make_async_copy(*pair, outer_sems.at[f, i])

    outer_rows = [(f, i) for f in range(count) for i in range(2)] if with_x else []
    if not with_x:
        for f in range(count):
            base_copy(f).start()
    for f, i in outer_rows:
        outer_copy(f, i, False).start()
    done_ref[...] = jnp.zeros_like(done_ref)
    def in_order(i, pair):
        odd = odd_ref[0, i] == 1
        in_odd, in_even = pair[0][...], pair[1][...]
        return jnp.where(odd, in_even, in_odd), jnp.where(odd, in_odd, in_even)

    if with_x:
        top, bottom = in_order(0, tops)
        lines[:count, :] = top * above[keep, :]
        lines[count:, :] = bottom * below[keep, :]
        late = in_order(0, late)
    else:
        lines[...] = jnp.zeros_like(lines)
    left, right = in_order(1, (left, right))
    sides[:count, :] = left * before[keep, :]
    sides[count:, :] = right * after[keep, :]
    lane = lax.broadcasted_iota(jnp.int32, (STRIP, cells_y), 1)

    def one_field(f, carry):
        rate = gamma_ref[0, first + f]
        both = [sides[pl.ds(f, 1), :] * rate, sides[pl.ds(count + f, 1), :] * rate]
        cols = columns_of(jnp.concatenate(both, axis=0))
        wide[STRIP - 1 : STRIP, :] = lines[pl.ds(f, 1), :] * rate
        wide[STRIP + cells_x : STRIP + cells_x + 1, :] = lines[pl.ds(count + f, 1), :] * rate
        to_out, to_new = out_copies(f)
        to_out.start()
        for i in range(0, cells_x, STRIP):
            rows = slice(i, i + STRIP)
            wide[STRIP + i : 2 * STRIP + i, :] = factors[0, rows, :] * recv[f, rows, :] * rate
        if not with_x:
            base_copy(f).wait()
        start = early_base if with_x else base
        for i in range(0, cells_x, STRIP):
            rows = slice(i, i + STRIP)
            mid = wide[STRIP + i : 2 * STRIP + i, :]
            more = (factors[5, rows, :] - rate * factors[0, rows, :]) * mid
            more += factors[1, rows, :] * wide[STRIP + i - 1 : 2 * STRIP + i - 1, :]
            more += factors[2, rows, :] * wide[STRIP + i + 1 : 2 * STRIP + i + 1, :]
            prior = jnp.where(lane == 0, cols[rows, 0:1], pltpu.roll(mid, 1, 1))
            later = jnp.where(lane == cells_y - 1, cols[rows, 1:2], pltpu.roll(mid, cells_y - 1, 1))
            more += factors[3, rows, :] * prior + factors[4, rows, :] * later
            base[f, rows, :] = start[f, rows, :] + mix_b * (2.0 * mid + more)
        to_new.start()
        return carry

    def add_lines():
        for f, i in outer_rows:
            outer_copy(f, i, False).wait()
            row = i * (STRIP - 1)
            at = ends[i] + row
            line = late[i][f : f + 1, :] * (above, below)[i][keep, :] * gamma_ref[0, count + f]
            more = mix_b * factors[1 + i, at : at + 1, :] * line
            outer[f, i, row : row + 1, :] = outer[f, i, row : row + 1, :] + more
            outer_copy(f, i, True).start()

    lax.fori_loop(0, count - 1, one_field, 0)
    add_lines()
    one_field(count - 1, 0)
    for f in range(count):
        for copy in out_copies(f):
            copy.wait()
    for f, i in outer_rows:
        outer_copy(f, i, True).wait()


def finished(
    first, new_state, remapped, recv, odd, x_rims, y_rims, closing, gamma, mix, factors, received
):
    count, cells_x, cells_y = recv.shape
    chan = gamma.shape[1]
    with_x = x_rims is not None
    anywhere = pl.BlockSpec(memory_space=pl.ANY)
    operands = [gamma, mix, *received, factors, recv, *y_rims]
    if with_x:
        late_rims, base_early, late_done = closing
        operands += [*x_rims, *late_rims, base_early]
    scalars = pl.BlockSpec(memory_space=pltpu.SMEM)
    specs = [scalars] * 2 + [pl.BlockSpec(memory_space=pltpu.VMEM)] * (len(operands) - 2)
    operands.append(odd)
    specs += [scalars, anywhere]
    aliases = {len(operands): 0}
    operands.append(new_state)
    if remapped is not None:
        aliases[len(operands)] = 1
        operands += [remapped, late_done]
        specs += [anywhere, anywhere]
    return pl.pallas_call(
        functools.partial(finish_kernel, first, with_x),
        in_specs=specs,
        out_specs=[anywhere, anywhere, pl.BlockSpec(memory_space=pltpu.VMEM)],
        out_shape=[
            jax.ShapeDtypeStruct(new_state.shape, jnp.float32),
            jax.ShapeDtypeStruct((1, chan, cells_x, cells_y), jnp.float32),
            jax.ShapeDtypeStruct((8, LANES), jnp.float32),
        ],
        input_output_aliases=aliases,
        scratch_shapes=[
            pltpu.VMEM((count, cells_x, cells_y), jnp.float32),
            pltpu.VMEM((cells_x + 2 * STRIP, cells_y), jnp.float32),
            pltpu.VMEM((2 * count, cells_y), jnp.float32),
            pltpu.VMEM((2 * count, cells_x), jnp.float32),
            pltpu.VMEM((count, 2, STRIP, cells_y), jnp.float32),
            pltpu.SemaphoreType.DMA((count,)),
            pltpu.SemaphoreType.DMA((2, count)),
            pltpu.SemaphoreType.DMA((count, 2)),
        ],
        compiler_params=pltpu.CompilerParams(vmem_limit_bytes=12 * 1024 * 1024),
        cost_estimate=pl.CostEstimate(
            flops=20 * recv.size, bytes_accessed=20 * recv.size, transcendentals=0
        ),
        name="finish",
    )(*operands)


def body(state, coefs, land_sea, gamma, pair_src, pair_dev, pair_blk, weights):
    tx, ty = lax.axis_size("tx"), lax.axis_size("ty")
    tiles = tx * ty
    nfield, cells_x, cells_y = state.shape[1:]
    chan = gamma.shape[1]
    pairs, width = weights.shape[1], weights.shape[2]
    capacity = max(2, 2 * pairs // tiles)
    half = chan // 2
    early, late = contributions(
        state, pair_src, pair_dev, pair_blk, weights, tiles, capacity, chan
    )
    swap = [(0, 1), (1, 0)]

    def exchanged(rows):
        rows = rows.reshape(tiles, -1, half, width)
        return lax.all_to_all(rows, ("tx", "ty"), split_axis=0, concat_axis=0, tiled=True)

    def add_up(odd, ids, rows):
        return summed(odd, ids, rows, tiles, capacity, half, cells_x, cells_y, width)

    late_in = exchanged(late)
    early = lax.ppermute(early, "comp", swap)
    early_in = placed_rows(early, tiles, capacity, pairs, cells_x * cells_y // width)

    land_after, _ = lax.optimization_barrier((land_sea, late))
    is_atmos = lax.axis_index("comp") == 0
    mix = jnp.where(is_atmos, jnp.array([[0.0, 1.0]]), jnp.array([[0.5, 0.5]]))
    mix = mix.astype(jnp.float32)
    rates = jnp.concatenate([gamma, jnp.zeros((1, nfield - chan), jnp.float32)], axis=1)
    x_low, x_high, y_low, y_high = edges_of(state, coefs, land_after, mix)
    left = lax.ppermute(y_high, "ty", shift_pairs(ty, 1))
    right = lax.ppermute(y_low, "ty", shift_pairs(ty, -1))
    above = lax.ppermute(x_high, "tx", shift_pairs(tx, 1))
    below = lax.ppermute(x_low, "tx", shift_pairs(tx, -1))
    early_in, above, below, left, right = lax.optimization_barrier(
        (early_in, above, below, left, right)
    )
    received = (above, below, left, right)
    early_in = exchanged(early_in)

    ends = jnp.concatenate([above[:, cells_y - LANES :], below[:, cells_y - LANES :]], axis=0)
    starts = jnp.concatenate([above[:, :LANES], below[:, :LANES]], axis=0)
    corners_left = lax.ppermute(ends, "ty", shift_pairs(ty, 1))
    corners_right = lax.ppermute(starts, "ty", shift_pairs(ty, -1))
    base, base_early, factors = base_of(
        state, coefs, land_after, rates, mix, (x_low, x_high, y_low, y_high), received,
        (corners_left, corners_right), half,
    )

    ids_late = late_in[:, capacity, 0, :]
    ids_early = lax.ppermute(ids_late, "comp", swap)
    odd = jnp.stack([lax.axis_index("tx"), lax.axis_index("ty")]).astype(jnp.int32)[None] & 1
    odd_lanes = jnp.broadcast_to(odd.T.astype(jnp.float32), (2, LANES))
    recv_late, x_odd, x_even, y_odd, y_even = add_up(odd_lanes, ids_late, late_in)
    recv_late = lax.ppermute(recv_late, "comp", swap)
    late_x = (
        lax.ppermute(x_odd, ("comp", "tx"), crossed("tx", 1)),
        lax.ppermute(x_even, ("comp", "tx"), crossed("tx", 0)),
    )
    late_y = (
        lax.ppermute(y_odd, ("comp", "ty"), crossed("ty", 1)),
        lax.ppermute(y_even, ("comp", "ty"), crossed("ty", 0)),
    )
    rest = (gamma, mix, factors, received)
    new_state, remapped, done = finished(
        half, base, None, recv_late, odd, None, late_y, None, *rest
    )
    early_in, done = lax.optimization_barrier((early_in, done))
    recv_early, x_odd, x_even, y_odd, y_even = add_up(odd_lanes, ids_early, early_in)
    early_x = (
        lax.ppermute(x_odd, "tx", neighbour_pairs(tx, 1)),
        lax.ppermute(x_even, "tx", neighbour_pairs(tx, 0)),
    )
    early_y = (
        lax.ppermute(y_odd, "ty", neighbour_pairs(ty, 1)),
        lax.ppermute(y_even, "ty", neighbour_pairs(ty, 0)),
    )
    new_state, remapped, _ = finished(
        0, new_state, remapped, recv_early, odd, early_x, early_y, (late_x, base_early, done), *rest
    )
    return new_state, remapped


def solution(mesh):
    placed = (
        P("comp", None, "tx", "ty"),
        P("comp", None, "tx", "ty"),
        P("tx", "ty"),
        P("comp", None),
        P("comp", ("tx", "ty")),
        P("comp", ("tx", "ty"), None),
        P("comp", ("tx", "ty")),
        P("comp", ("tx", "ty"), None, None),
    )
    return jax.shard_map(
        body,
        mesh=mesh,
        in_specs=placed,
        out_specs=(P("comp", None, "tx", "ty"), P("comp", None, "tx", "ty")),
        check_vma=False,
    )
```

```python
import functools

import jax
import jax.numpy as jnp
from jax import lax
from jax.experimental import pallas as pl
from jax.experimental.pallas import tpu as pltpu
from jax.sharding import PartitionSpec as P

LANES = 128
STEP_PAIRS = 64
STRIP = 8
PER_STEP = 2
NT = (((1,), (1,)), ((), ()))


def pinned(space, *arrays):
    return [pltpu.with_memory_space_constraint(a, space) for a in arrays]


def shift_pairs(count, by):
    return [(i, i + by) for i in range(count) if 0 <= i + by < count]


def neighbour_pairs(count, first):
    lows = range(first, count - 1, 2)
    return [(i, i + 1) for i in lows] + [(i + 1, i) for i in lows]


def crossed(axis, first):
    count = lax.axis_size(axis)
    pairs = neighbour_pairs(count, first)
    return [(c * count + i, (1 - c) * count + j) for c in range(2) for i, j in pairs]


def split(value, parts):
    if parts & (parts - 1) == 0:
        return lax.shift_right_logical(value, parts.bit_length() - 1), value & (parts - 1)
    return lax.div(value, parts), lax.rem(value, parts)


def ranks(dev, tiles):
    pairs = dev.shape[1]
    tile_of = lax.broadcasted_iota(jnp.int32, (tiles, pairs), 0)
    lane_of = lax.broadcasted_iota(jnp.int32, (tiles, pairs), 1)
    member = (tile_of == dev).astype(jnp.float32)
    total = member
    shift = 1
    while shift < pairs:
        total = total + jnp.where(lane_of >= shift, pltpu.roll(total, shift, 1), 0.0)
        shift *= 2
    return member, (jnp.sum(member * total, axis=0, keepdims=True) - 1.0).astype(jnp.int32)


def slot_blocks(dev, blk, tiles, capacity):
    member, rank = ranks(dev, tiles)
    pairs = dev.shape[1]
    slot_of = lax.broadcasted_iota(jnp.int32, (LANES, pairs), 0) % capacity
    chosen = (slot_of == rank).astype(jnp.bfloat16)

    def spread(values):
        return lax.dot_general(
            (member * values).astype(jnp.bfloat16), chosen, NT, preferred_element_type=jnp.float32
        )

    high, low = split(blk, 256)
    ids = spread(high.astype(jnp.float32)) * 256.0 + spread(low.astype(jnp.float32))
    return jnp.where(spread(jnp.ones(dev.shape, jnp.float32)) > 0.5, ids, -1.0)


def contribution_kernel(
    dims, src_ref, dev_ref, blk_ref, state_ref, weights_ref, early_ref, late_ref,
    cells, w_ref, pair_v, pair_s, taken, field_sems, weight_sems, pair_sems,
):
    tiles, capacity, pairs, fields, cells_x, cells_y, width = dims
    half = fields // 2
    parts = cells_y // width
    steps = pairs // STEP_PAIRS

    scalar_copies = [
        pltpu.make_async_copy(ref, pair_s.at[pl.ds(i, 1), :], pair_sems.at[i])
        for i, ref in enumerate((src_ref, dev_ref))
    ]
    vector_copies = [
        pltpu.make_async_copy(ref, pair_v.at[i], pair_sems.at[2 + i])
        for i, ref in enumerate((dev_ref, blk_ref))
    ]
    field_copies = [
        pltpu.make_async_copy(
            state_ref.at[0, f, :, pl.ds(q * width, width)],
            cells.at[q, :, f, :],
            field_sems.at[f * parts + q],
        )
        for f in range(fields)
        for q in range(parts)
    ]

    def weight_copy(step):
        some = pl.ds(step * STEP_PAIRS, STEP_PAIRS)
        return pltpu.make_async_copy(
            weights_ref.at[0, some], w_ref.at[some], weight_sems.at[step]
        )

    for copy in scalar_copies + vector_copies + field_copies:
        copy.start()
    for step in range(steps):
        weight_copy(step).start()
    late_ref[...] = jnp.zeros_like(late_ref)
    for t in range(tiles):
        taken[t] = t * (capacity + 1)

    for copy in vector_copies + scalar_copies + field_copies:
        copy.wait()

    def cells_of(p):
        x, part = split(pair_s[0, p], parts)
        return cells[part, x]

    zeros = jnp.zeros((fields, width), jnp.float32)

    def work(step):
        for i in range(0, STEP_PAIRS, 4):
            p = step * STEP_PAIRS + i
            left = [
                jnp.concatenate([cells_of(p + j), zeros][:: 1 - j % 2 * 2], axis=1) for j in range(4)
            ]
            left = jnp.concatenate(left, axis=0).astype(jnp.bfloat16)
            w = [w_ref[p + j] for j in range(4)]
            right = jnp.concatenate(
                [jnp.concatenate(w[:2], axis=1), jnp.concatenate(w[2:], axis=1)], axis=0
            )
            four = lax.dot_general(left, right, NT, preferred_element_type=jnp.float32)
            for j in range(4):
                tile = pair_s[1, p + j]
                slot = taken[tile]
                taken[tile] = slot + 1
                at = j // 2 * width
                one = four[j * fields : (j + 1) * fields, at : at + width]
                early_ref[p + j] = one[:half]
                late_ref[slot] = one[half:]

    def some_pairs(step, carry):
        weight_copy(step).wait()
        work(step)
        return carry

    weight_copy(0).wait()
    dev, blk = pair_v[0], pair_v[1]
    ids = slot_blocks(dev, blk, tiles, capacity)
    code = (dev * (cells_x * parts) + blk).astype(jnp.float32)
    work(0)
    for t in range(tiles):
        row = jnp.broadcast_to(ids[t : t + 1, :], late_ref.shape[1:])
        late_ref[t * (capacity + 1) + capacity] = row
    for i in range(pairs // width):
        place = (pairs + i // half, slice(i % half, i % half + 1), slice(None))
        early_ref[place] = code[:, i * width : (i + 1) * width]

    lax.fori_loop(1, steps, some_pairs, 0)


def contributions(state, pair_src, pair_dev, pair_blk, weights, tiles, capacity, fields):
    _, _, cells_x, cells_y = state.shape
    half = fields // 2
    pairs, width = weights.shape[1], weights.shape[2]
    rows = tiles * (capacity + 1)
    dims = (tiles, capacity, pairs, fields, cells_x, cells_y, width)
    parts = cells_y // width
    shapes = [(pairs + -(-pairs // (half * width)), half, width), (rows, half, width)]
    return pl.pallas_call(
        functools.partial(contribution_kernel, dims),
        in_specs=[pl.BlockSpec(memory_space=pltpu.HBM)] * 5,
        out_specs=[pl.BlockSpec(memory_space=pltpu.VMEM) for _ in shapes],
        out_shape=[jax.ShapeDtypeStruct(shape, jnp.float32) for shape in shapes],
        scratch_shapes=[
            pltpu.VMEM((parts, cells_x, fields, width), jnp.float32),
            pltpu.VMEM((pairs, width, width), jnp.bfloat16),
            pltpu.VMEM((2, 1, pairs), jnp.int32),
            pltpu.SMEM((2, pairs), jnp.int32),
            pltpu.SMEM((tiles,), jnp.int32),
            pltpu.SemaphoreType.DMA((parts * fields,)),
            pltpu.SemaphoreType.DMA((pairs // STEP_PAIRS,)),
            pltpu.SemaphoreType.DMA((4,)),
        ],
        compiler_params=pltpu.CompilerParams(vmem_limit_bytes=40 * 1024 * 1024),
        cost_estimate=pl.CostEstimate(
            flops=2 * pairs * fields * width * width,
            bytes_accessed=2 * pairs * width * width + 8 * rows * fields * width,
            transcendentals=0,
        ),
        name="contributions",
    )(*pinned(pltpu.HBM, pair_src, pair_dev.reshape(1, pairs), pair_blk, state, weights))


def place_kernel(dims, in_ref, out_ref, place_v, place_s, place_sem):
    tiles, capacity, pairs, blocks = dims
    half, width = in_ref.shape[1:]
    code = jnp.concatenate(
        [in_ref[pairs + i // half][i % half : i % half + 1] for i in range(pairs // width)], axis=1
    ).astype(jnp.int32)
    dev, _ = split(code, blocks)
    rank = ranks(dev, tiles)[1]
    place_v[...] = jnp.broadcast_to(dev * capacity + rank, place_v.shape)
    copy = pltpu.make_async_copy(place_v, place_s, place_sem)
    copy.start()
    out_ref[...] = jnp.zeros_like(out_ref)
    copy.wait()

    def some_rows(step, carry):
        for i in range(STEP_PAIRS):
            p = step * STEP_PAIRS + i
            out_ref[place_s[0, p]] = in_ref[p]
        return carry

    lax.fori_loop(0, pairs // STEP_PAIRS, some_rows, 0)


def placed_rows(rows, tiles, capacity, pairs, blocks):
    half, width = rows.shape[1:]
    shape = (tiles * capacity, half, width)
    return pl.pallas_call(
        functools.partial(place_kernel, (tiles, capacity, pairs, blocks)),
        out_shape=jax.ShapeDtypeStruct(shape, jnp.float32),
        scratch_shapes=[
            pltpu.VMEM((8, pairs), jnp.int32),
            pltpu.SMEM((8, pairs), jnp.int32),
            pltpu.SemaphoreType.DMA,
        ],
        compiler_params=pltpu.CompilerParams(vmem_limit_bytes=10 * 1024 * 1024),
        cost_estimate=pl.CostEstimate(
            flops=4 * rows.size, bytes_accessed=12 * rows.size, transcendentals=0
        ),
        name="place_in_slots",
    )(rows)


def sum_kernel(dims, odd_ref, ids_ref, rows_ref, out_ref, x0_ref, x1_ref, y0_ref, y1_ref,
               pick, high, low, in_ref, row_sems):
    tiles, capacity, fields, cells_x, cells_y, width = dims
    parts = cells_y // width
    group = LANES // capacity
    stride = in_ref.shape[0] // tiles

    def rows_copy(k):
        some = pl.ds(k * group * stride, group * stride)
        return pltpu.make_async_copy(rows_ref.at[some, :], in_ref.at[some, :], row_sems.at[k])

    for k in range(tiles // group):
        rows_copy(k).start()
    block_of = lax.broadcasted_iota(jnp.int32, (cells_x * parts, LANES), 0)
    block_of = (block_of % cells_x) * parts + block_of // cells_x
    block_of = block_of.astype(jnp.float32)
    lane = lax.broadcasted_iota(jnp.int32, (1, LANES), 1)
    for k in range(tiles // group):
        ids = None
        for i in range(group):
            row = ids_ref[pl.ds(k * group + i, 1), :]
            ids = row if ids is None else jnp.where(lane // capacity == i, row, ids)
        pick[:, pl.ds(k * LANES, LANES)] = (block_of == ids).astype(jnp.bfloat16)
    for k in range(tiles // group):
        rows_copy(k).wait()
        for source in range(k * group, (k + 1) * group):
            for f in range(fields):
                x = in_ref[pl.ds(source * stride + f, capacity, stride=fields), :]
                rounded = x.astype(jnp.bfloat16)
                place = (
                    pl.ds(source * capacity, capacity),
                    pl.ds(f * width, width),
                )
                high[place] = rounded
                low[place] = (x - rounded.astype(jnp.float32)).astype(jnp.bfloat16)

    def in_order(i, low_rim, high_rim):
        odd = odd_ref[i : i + 1, :] == 1.0
        return jnp.where(odd, high_rim, low_rim), jnp.where(odd, low_rim, high_rim)

    columns = {}
    for q in range(parts):
        chosen = pick[pl.ds(q * cells_x, cells_x), :]
        total = jnp.dot(chosen, high[...], preferred_element_type=jnp.float32)
        total = total + jnp.dot(chosen, low[...], preferred_element_type=jnp.float32)
        for f in range(fields):
            tile = total[:, f * width : (f + 1) * width]
            out_ref[f, :, pl.ds(q * width, width)] = tile
            rims = in_order(0, tile[:1], tile[cells_x - 1 :])
            for rim_ref, rim in zip((x0_ref, x1_ref), rims):
                rim_ref[pl.ds(f, 1), pl.ds(q * width, width)] = rim
            if q in (0, parts - 1):
                columns[q, f] = tile.T[:1] if q == 0 else tile.T[width - 1 :]
    for f in range(fields):
        rims = in_order(1, columns[0, f], columns[parts - 1, f])
        y0_ref[pl.ds(f, 1), :], y1_ref[pl.ds(f, 1), :] = rims


def summed(odd, ids, rows, tiles, capacity, fields, cells_x, cells_y, width):
    dims = (tiles, capacity, fields, cells_x, cells_y, width)
    rows = rows.reshape(-1, width)
    slots = tiles * capacity
    blocks = cells_x * cells_y // width
    shapes = [
        (fields, cells_x, cells_y),
        (fields, cells_y),
        (fields, cells_y),
        (fields, cells_x),
        (fields, cells_x),
    ]
    return pl.pallas_call(
        functools.partial(sum_kernel, dims),
        in_specs=[pl.BlockSpec(memory_space=pltpu.VMEM)] * 2
        + [pl.BlockSpec(memory_space=pltpu.HBM)],
        out_shape=[jax.ShapeDtypeStruct(shape, jnp.float32) for shape in shapes],
        scratch_shapes=[
            pltpu.VMEM((blocks, slots), jnp.bfloat16),
            pltpu.VMEM((slots, fields * width), jnp.bfloat16),
            pltpu.VMEM((slots, fields * width), jnp.bfloat16),
            pltpu.VMEM(rows.shape, jnp.float32),
            pltpu.SemaphoreType.DMA((tiles * capacity // LANES,)),
        ],
        compiler_params=pltpu.CompilerParams(vmem_limit_bytes=24 * 1024 * 1024),
        cost_estimate=pl.CostEstimate(
            flops=4 * blocks * slots * fields * width,
            bytes_accessed=4 * fields * width * (slots + blocks),
            transcendentals=0,
        ),
        name="sum_by_block",
    )(odd, ids, *pinned(pltpu.HBM, rows))


def stencil_factors(coefs, keep):
    u, v, kappa = coefs
    return [
        keep,
        keep * (jnp.maximum(u, 0.0) + kappa),
        keep * (kappa - jnp.minimum(u, 0.0)),
        keep * (jnp.maximum(v, 0.0) + kappa),
        keep * (kappa - jnp.minimum(v, 0.0)),
        -keep * (jnp.abs(u) + jnp.abs(v) + 4.0 * kappa),
    ]


def tendency(s, rate, factors, top, bottom, left, right):
    cells_x, cells_y = s.shape
    x_of = lax.broadcasted_iota(jnp.int32, s.shape, 0)
    y_of = lax.broadcasted_iota(jnp.int32, s.shape, 1)
    out = (factors[5] - rate * factors[0]) * s
    out += factors[1] * jnp.where(x_of == 0, top, pltpu.roll(s, 1, 0))
    out += factors[2] * jnp.where(x_of == cells_x - 1, bottom, pltpu.roll(s, cells_x - 1, 0))
    out += factors[3] * jnp.where(y_of == 0, left, pltpu.roll(s, 1, 1))
    out += factors[4] * jnp.where(y_of == cells_y - 1, right, pltpu.roll(s, cells_y - 1, 1))
    return out


def columns_of(rows):
    spare = 8 - rows.shape[0]
    if spare:
        rows = jnp.concatenate([rows, jnp.zeros((spare, rows.shape[1]), rows.dtype)], axis=0)
    return rows.T


def line_count(nfield):
    return 2 * nfield + 8


def edge_kernel(mix_ref, state_tops, state_ends, state_lefts, state_rights, coefs_tops, coefs_ends,
                coefs_lefts, coefs_rights, land_tops, land_ends, land_lefts, land_rights,
                x_low, x_high, y_low, y_high):
    nfield = state_tops.shape[1]
    last_row, last_lane = state_tops.shape[2] - 1, state_lefts.shape[3] - 1
    atmos = mix_ref[0, 1] == 1.0

    def kept(land):
        return jnp.where(atmos, 1.0, land.astype(jnp.float32))

    for out, state, coefs, land, lines in (
        (x_low, state_tops, coefs_tops, land_tops, (0, 1)),
        (x_high, state_ends, coefs_ends, land_ends, (last_row - 1, last_row)),
    ):
        outer = lines[0] if lines[0] == 0 else lines[1]
        out[2 * nfield :, :] = jnp.zeros((8, out.shape[1]), jnp.float32)
        for j, line in enumerate(lines):
            for f in range(nfield):
                out[j * nfield + f : j * nfield + f + 1, :] = state[0, f, line : line + 1, :]
        for c in range(3):
            out[2 * nfield + c : 2 * nfield + c + 1, :] = coefs[0, c, outer : outer + 1, :]
        out[2 * nfield + 3 : 2 * nfield + 4, :] = kept(land[outer : outer + 1, :])

    for out, state, coefs, land, lines in (
        (y_low, state_lefts, coefs_lefts, land_lefts, (0, 1)),
        (y_high, state_rights, coefs_rights, land_rights, (last_lane - 1, last_lane)),
    ):
        outer = lines[0] if lines[0] == 0 else lines[1]
        lane = lax.broadcasted_iota(jnp.int32, land.shape, 1)
        packed = jnp.zeros(land.shape, jnp.float32)

        def put(packed, tile, at, to):
            moved = (to - at) % LANES
            tile = pltpu.roll(tile, moved, 1) if moved else tile
            return jnp.where(lane == to, tile, packed)

        for j, line in enumerate(lines):
            for f in range(nfield):
                packed = put(packed, state[0, f], line, j * nfield + f)
        for c in range(3):
            packed = put(packed, coefs[0, c], outer, 2 * nfield + c)
        packed = put(packed, kept(land[...]), outer, 2 * nfield + 3)
        out[...] = packed.T[: out.shape[0]]


def edges_of(state, coefs, land_sea, mix):
    _, nfield, cells_x, cells_y = state.shape
    lines = line_count(nfield)
    ends = [
        ((8, cells_y), (0, 0)),
        ((8, cells_y), (cells_x // 8 - 1, 0)),
        ((cells_x, LANES), (0, 0)),
        ((cells_x, LANES), (0, cells_y // LANES - 1)),
    ]
    at = lambda lead, place: lambda i: (0,) * len(lead) + place
    specs = [pl.BlockSpec(memory_space=pltpu.SMEM)]
    for lead in ((1, nfield), (1, 3), ()):
        specs += [pl.BlockSpec(lead + shape, at(lead, place)) for shape, place in ends]
    shapes = [(lines, cells_y)] * 2 + [(lines, cells_x)] * 2
    return pl.pallas_call(
        edge_kernel,
        grid=(1,),
        in_specs=specs,
        out_specs=[pl.BlockSpec(shape, lambda i: (0, 0)) for shape in shapes],
        out_shape=[jax.ShapeDtypeStruct(shape, jnp.float32) for shape in shapes],
        compiler_params=pltpu.CompilerParams(vmem_limit_bytes=24 * 1024 * 1024),
        cost_estimate=pl.CostEstimate(
            flops=state.size, bytes_accessed=4 * 1024 * 1024, transcendentals=0
        ),
        name="edges",
    )(mix, *pinned(pltpu.HBM, *[state] * 4), *[coefs] * 4, *[land_sea] * 4)


def outer_section(center, across, along, factors, rate):
    lane = lax.broadcasted_iota(jnp.int32, center.shape, 1)
    count = center.shape[1]
    before = jnp.where(lane == 0, along[0], pltpu.roll(center, 1, 1))
    after = jnp.where(lane == count - 1, along[1], pltpu.roll(center, count - 1, 1))
    keep, low, high, back, ahead, middle = factors
    out = center + low * across[0] + high * across[1] + back * before + ahead * after
    return out + (middle - rate * keep) * center


def base_kernel(half, rate_ref, mix_ref, rates_ref, coefs_ref, land_ref, x_low, x_high, y_low, y_high,
                above, below, left, right, corners_left, corners_right, state_ref,
                out_ref, early_ref, factors, rows, cols):
    f = pl.program_id(0)
    nfield = rates_ref.shape[0]
    lines = line_count(nfield)

    @pl.when(f == 0)
    def _():
        keep = jnp.where(mix_ref[0, 1] == 1.0, 1.0, land_ref[...].astype(jnp.float32))
        for i, factor in enumerate(stencil_factors([coefs_ref[0, c] for c in range(3)], keep)):
            factors[i] = factor
        rate = rates_ref[:, 0:1]
        near, far = pl.ds(0, nfield), pl.ds(nfield, nfield)
        last = corners_left.shape[1] - 1
        corner = (
            (corners_left[nfield : 2 * nfield, last:], corners_left[lines : lines + nfield, last:]),
            (corners_right[nfield : 2 * nfield, 0:1], corners_right[lines : lines + nfield, 0:1]),
        )
        for i, (ref, center, across, along, is_column) in enumerate(
            (
                (above, above[far, :], (above[near, :], x_low[near, :]), (corner[0][0], corner[1][0]), False),
                (below, below[near, :], (x_high[far, :], below[far, :]), (corner[0][1], corner[1][1]), False),
                (left, left[far, :], (left[near, :], y_low[near, :]), corner[0], True),
                (right, right[near, :], (y_high[far, :], right[far, :]), corner[1], True),
            )
        ):
            first = 2 * nfield
            of_line = stencil_factors(
                [ref[first + c : first + c + 1, :] for c in range(3)],
                ref[first + 3 : first + 4, :],
            )
            if is_column:
                of_line = [of_line[j] for j in (0, 3, 4, 1, 2, 5)]
            section = outer_section(center, across, along, of_line, rate)
            kept = cols if is_column else rows
            kept[pl.ds(i % 2 * nfield, nfield), :] = center
            kept[pl.ds((2 + i % 2) * nfield, nfield), :] = section

    mix_a, mix_b = mix_ref[0, 0], mix_ref[0, 1]
    for j in range(PER_STEP):
        field = f * PER_STEP + j
        rate = rate_ref[0, field]
        s = state_ref[0, j]
        row = [rows[pl.ds(i * nfield + field, 1), :] for i in range(4)]
        col = columns_of(
            jnp.concatenate([cols[pl.ds(i * nfield + field, 1), :] for i in range(4)], axis=0)
        )
        s1 = s + tendency(s, rate, factors, row[0], row[1], col[:, 0:1], col[:, 1:2])
        more = tendency(s1, rate, factors, row[2], row[3], col[:, 2:3], col[:, 3:4])
        total = mix_a * s + (1.0 - mix_a) * s1 + mix_b * more
        out_ref[0, j] = total

        @pl.when(field < half)
        def _():
            early_ref[j] = total


def base_of(state, coefs, land_sea, rates, mix, edges, received, corners, half):
    _, nfield, cells_x, cells_y = state.shape
    field = pl.BlockSpec((1, PER_STEP, cells_x, cells_y), lambda f: (0, f, 0, 0))
    early = pl.BlockSpec(
        (PER_STEP, cells_x, cells_y), lambda f: (jnp.minimum(f, half // PER_STEP - 1), 0, 0)
    )
    whole = lambda a: pl.BlockSpec(a.shape, lambda f: (0,) * a.ndim)
    rates_wide = jnp.broadcast_to(rates.T, (nfield, LANES))
    operands = [rates_wide, coefs, land_sea, *edges, *received, *corners]
    return pl.pallas_call(
        functools.partial(base_kernel, half),
        grid=(nfield // PER_STEP,),
        in_specs=[
            pl.BlockSpec(memory_space=pltpu.SMEM),
            pl.BlockSpec(memory_space=pltpu.SMEM),
            *[whole(a) for a in operands],
            field,
        ],
        out_specs=[
            field,
            early,
            pl.BlockSpec((6, cells_x, cells_y), lambda f: (0, 0, 0)),
        ],
        out_shape=[
            jax.ShapeDtypeStruct(state.shape, jnp.float32),
            jax.ShapeDtypeStruct((half, cells_x, cells_y), jnp.float32),
            jax.ShapeDtypeStruct((6, cells_x, cells_y), jnp.float32),
        ],
        scratch_shapes=[
            pltpu.VMEM((4 * nfield, cells_y), jnp.float32),
            pltpu.VMEM((4 * nfield, cells_x), jnp.float32),
        ],
        compiler_params=pltpu.CompilerParams(vmem_limit_bytes=24 * 1024 * 1024),
        cost_estimate=pl.CostEstimate(
            flops=40 * state.size, bytes_accessed=8 * state.size, transcendentals=0
        ),
        name="base",
    )(rates, mix, *operands, *pinned(pltpu.HBM, state))


def finish_kernel(first, with_x, gamma_ref, mix_ref, above, below, before, after, factors, recv,
                  left, right, *rest):
    tops, rest = (rest[:2], rest[2:]) if with_x else (None, rest)
    late, rest = (rest[:2], rest[2:]) if with_x else (None, rest)
    early_base, rest = (rest[0], rest[1:]) if with_x else (None, rest)
    odd_ref, base_ref, rest = rest[0], rest[1], rest[2:]
    new_ref, out_ref, done_ref = rest[-11:-8]
    base, wide, lines, sides, outer, base_sems, out_sems, outer_sems = rest[-8:]
    count, cells_x, cells_y = base.shape
    mix_b = mix_ref[0, 1]
    keep_row = above.shape[0] - 5
    keep = slice(keep_row, keep_row + 1)
    ends = (0, cells_x - STRIP)

    def base_copy(f):
        return pltpu.make_async_copy(base_ref.at[0, first + f], base.at[f], base_sems.at[f])

    def out_copies(f):
        return (
            pltpu.make_async_copy(recv.at[f], out_ref.at[0, first + f], out_sems.at[0, f]),
            pltpu.make_async_copy(base.at[f], new_ref.at[0, first + f], out_sems.at[1, f]),
        )

    def outer_copy(f, i, back):
        there = (new_ref if back else base_ref).at[0, count + f, pl.ds(ends[i], STRIP), :]
        here = outer.at[f, i]
        pair = (here, there) if back else (there, here)
        return pltpu.make_async_copy(*pair, outer_sems.at[f, i])

    outer_rows = [(f, i) for f in range(count) for i in range(2)] if with_x else []
    if not with_x:
        for f in range(count):
            base_copy(f).start()
    for f, i in outer_rows:
        outer_copy(f, i, False).start()
    done_ref[...] = jnp.zeros_like(done_ref)
    def in_order(i, pair):
        odd = odd_ref[0, i] == 1
        in_odd, in_even = pair[0][...], pair[1][...]
        return jnp.where(odd, in_even, in_odd), jnp.where(odd, in_odd, in_even)

    if with_x:
        top, bottom = in_order(0, tops)
        lines[:count, :] = top * above[keep, :]
        lines[count:, :] = bottom * below[keep, :]
        late = in_order(0, late)
    else:
        lines[...] = jnp.zeros_like(lines)
    left, right = in_order(1, (left, right))
    sides[:count, :] = left * before[keep, :]
    sides[count:, :] = right * after[keep, :]
    lane = lax.broadcasted_iota(jnp.int32, (STRIP, cells_y), 1)

    def one_field(f, carry):
        rate = gamma_ref[0, first + f]
        both = [sides[pl.ds(f, 1), :] * rate, sides[pl.ds(count + f, 1), :] * rate]
        cols = columns_of(jnp.concatenate(both, axis=0))
        wide[STRIP - 1 : STRIP, :] = lines[pl.ds(f, 1), :] * rate
        wide[STRIP + cells_x : STRIP + cells_x + 1, :] = lines[pl.ds(count + f, 1), :] * rate
        to_out, to_new = out_copies(f)
        to_out.start()
        for i in range(0, cells_x, STRIP):
            rows = slice(i, i + STRIP)
            wide[STRIP + i : 2 * STRIP + i, :] = factors[0, rows, :] * recv[f, rows, :] * rate
        if not with_x:
            base_copy(f).wait()
        start = early_base if with_x else base
        for i in range(0, cells_x, STRIP):
            rows = slice(i, i + STRIP)
            mid = wide[STRIP + i : 2 * STRIP + i, :]
            more = (factors[5, rows, :] - rate * factors[0, rows, :]) * mid
            more += factors[1, rows, :] * wide[STRIP + i - 1 : 2 * STRIP + i - 1, :]
            more += factors[2, rows, :] * wide[STRIP + i + 1 : 2 * STRIP + i + 1, :]
            prior = jnp.where(lane == 0, cols[rows, 0:1], pltpu.roll(mid, 1, 1))
            later = jnp.where(lane == cells_y - 1, cols[rows, 1:2], pltpu.roll(mid, cells_y - 1, 1))
            more += factors[3, rows, :] * prior + factors[4, rows, :] * later
            base[f, rows, :] = start[f, rows, :] + mix_b * (2.0 * mid + more)
        to_new.start()
        return carry

    def add_lines():
        for f, i in outer_rows:
            outer_copy(f, i, False).wait()
            row = i * (STRIP - 1)
            at = ends[i] + row
            line = late[i][f : f + 1, :] * (above, below)[i][keep, :] * gamma_ref[0, count + f]
            more = mix_b * factors[1 + i, at : at + 1, :] * line
            outer[f, i, row : row + 1, :] = outer[f, i, row : row + 1, :] + more
            outer_copy(f, i, True).start()

    lax.fori_loop(0, count - 1, one_field, 0)
    add_lines()
    one_field(count - 1, 0)
    for f in range(count):
        for copy in out_copies(f):
            copy.wait()
    for f, i in outer_rows:
        outer_copy(f, i, True).wait()


def finished(
    first, new_state, remapped, recv, odd, x_rims, y_rims, closing, gamma, mix, factors, received
):
    count, cells_x, cells_y = recv.shape
    chan = gamma.shape[1]
    with_x = x_rims is not None
    anywhere = pl.BlockSpec(memory_space=pl.ANY)
    operands = [gamma, mix, *received, factors, recv, *y_rims]
    if with_x:
        late_rims, base_early, late_done = closing
        operands += [*x_rims, *late_rims, base_early]
    scalars = pl.BlockSpec(memory_space=pltpu.SMEM)
    specs = [scalars] * 2 + [pl.BlockSpec(memory_space=pltpu.VMEM)] * (len(operands) - 2)
    operands.append(odd)
    specs += [scalars, anywhere]
    aliases = {len(operands): 0}
    operands.append(new_state)
    if remapped is not None:
        aliases[len(operands)] = 1
        operands += [remapped, late_done]
        specs += [anywhere, anywhere]
    return pl.pallas_call(
        functools.partial(finish_kernel, first, with_x),
        in_specs=specs,
        out_specs=[anywhere, anywhere, pl.BlockSpec(memory_space=pltpu.VMEM)],
        out_shape=[
            jax.ShapeDtypeStruct(new_state.shape, jnp.float32),
            jax.ShapeDtypeStruct((1, chan, cells_x, cells_y), jnp.float32),
            jax.ShapeDtypeStruct((8, LANES), jnp.float32),
        ],
        input_output_aliases=aliases,
        scratch_shapes=[
            pltpu.VMEM((count, cells_x, cells_y), jnp.float32),
            pltpu.VMEM((cells_x + 2 * STRIP, cells_y), jnp.float32),
            pltpu.VMEM((2 * count, cells_y), jnp.float32),
            pltpu.VMEM((2 * count, cells_x), jnp.float32),
            pltpu.VMEM((count, 2, STRIP, cells_y), jnp.float32),
            pltpu.SemaphoreType.DMA((count,)),
            pltpu.SemaphoreType.DMA((2, count)),
            pltpu.SemaphoreType.DMA((count, 2)),
        ],
        compiler_params=pltpu.CompilerParams(vmem_limit_bytes=12 * 1024 * 1024),
        cost_estimate=pl.CostEstimate(
            flops=20 * recv.size, bytes_accessed=20 * recv.size, transcendentals=0
        ),
        name="finish",
    )(*operands)


def body(state, coefs, land_sea, gamma, pair_src, pair_dev, pair_blk, weights):
    tx, ty = lax.axis_size("tx"), lax.axis_size("ty")
    tiles = tx * ty
    nfield, cells_x, cells_y = state.shape[1:]
    chan = gamma.shape[1]
    pairs, width = weights.shape[1], weights.shape[2]
    capacity = max(2, 2 * pairs // tiles)
    half = chan // 2
    early, late = contributions(
        state, pair_src, pair_dev, pair_blk, weights, tiles, capacity, chan
    )
    swap = [(0, 1), (1, 0)]

    def exchanged(rows):
        rows = rows.reshape(tiles, -1, half, width)
        return lax.all_to_all(rows, ("tx", "ty"), split_axis=0, concat_axis=0, tiled=True)

    def add_up(odd, ids, rows):
        return summed(odd, ids, rows, tiles, capacity, half, cells_x, cells_y, width)

    late_in = exchanged(late)
    early = lax.ppermute(early, "comp", swap)
    early_in = placed_rows(early, tiles, capacity, pairs, cells_x * cells_y // width)

    land_after, _ = lax.optimization_barrier((land_sea, late))
    is_atmos = lax.axis_index("comp") == 0
    mix = jnp.where(is_atmos, jnp.array([[0.0, 1.0]]), jnp.array([[0.5, 0.5]]))
    mix = mix.astype(jnp.float32)
    rates = jnp.concatenate([gamma, jnp.zeros((1, nfield - chan), jnp.float32)], axis=1)
    x_low, x_high, y_low, y_high = edges_of(state, coefs, land_after, mix)
    left = lax.ppermute(y_high, "ty", shift_pairs(ty, 1))
    right = lax.ppermute(y_low, "ty", shift_pairs(ty, -1))
    above = lax.ppermute(x_high, "tx", shift_pairs(tx, 1))
    below = lax.ppermute(x_low, "tx", shift_pairs(tx, -1))
    early_in, above, below, left, right = lax.optimization_barrier(
        (early_in, above, below, left, right)
    )
    received = (above, below, left, right)
    early_in = exchanged(early_in)

    ends = jnp.concatenate([above[:, cells_y - LANES :], below[:, cells_y - LANES :]], axis=0)
    starts = jnp.concatenate([above[:, :LANES], below[:, :LANES]], axis=0)
    corners_left = lax.ppermute(ends, "ty", shift_pairs(ty, 1))
    corners_right = lax.ppermute(starts, "ty", shift_pairs(ty, -1))
    base, base_early, factors = base_of(
        state, coefs, land_after, rates, mix, (x_low, x_high, y_low, y_high), received,
        (corners_left, corners_right), half,
    )

    ids_late = late_in[:, capacity, 0, :]
    ids_early = lax.ppermute(ids_late, "comp", swap)
    odd = jnp.stack([lax.axis_index("tx"), lax.axis_index("ty")]).astype(jnp.int32)[None] & 1
    odd_lanes = jnp.broadcast_to(odd.T.astype(jnp.float32), (2, LANES))
    recv_late, x_odd, x_even, y_odd, y_even = add_up(odd_lanes, ids_late, late_in)
    recv_late = lax.ppermute(recv_late, "comp", swap)
    late_x = (
        lax.ppermute(x_odd, ("comp", "tx"), crossed("tx", 1)),
        lax.ppermute(x_even, ("comp", "tx"), crossed("tx", 0)),
    )
    late_y = (
        lax.ppermute(y_odd, ("comp", "ty"), crossed("ty", 1)),
        lax.ppermute(y_even, ("comp", "ty"), crossed("ty", 0)),
    )
    rest = (gamma, mix, factors, received)
    new_state, remapped, done = finished(
        half, base, None, recv_late, odd, None, late_y, None, *rest
    )
    early_in, done = lax.optimization_barrier((early_in, done))
    recv_early, x_odd, x_even, y_odd, y_even = add_up(odd_lanes, ids_early, early_in)
    early_x = (
        lax.ppermute(x_odd, "tx", neighbour_pairs(tx, 1)),
        lax.ppermute(x_even, "tx", neighbour_pairs(tx, 0)),
    )
    early_y = (
        lax.ppermute(y_odd, "ty", neighbour_pairs(ty, 1)),
        lax.ppermute(y_even, "ty", neighbour_pairs(ty, 0)),
    )
    new_state, remapped, _ = finished(
        0, new_state, remapped, recv_early, odd, early_x, early_y, (late_x, base_early, done), *rest
    )
    return new_state, remapped


def solution(mesh):
    placed = (
        P("comp", None, "tx", "ty"),
        P("comp", None, "tx", "ty"),
        P("tx", "ty"),
        P("comp", None),
        P("comp", ("tx", "ty")),
        P("comp", ("tx", "ty"), None),
        P("comp", ("tx", "ty")),
        P("comp", ("tx", "ty"), None, None),
    )
    return jax.shard_map(
        body,
        mesh=mesh,
        in_specs=placed,
        out_specs=(P("comp", None, "tx", "ty"), P("comp", None, "tx", "ty")),
        check_vma=False,
    )
```

```python
import functools

import jax
import jax.numpy as jnp
from jax import lax
from jax.experimental import pallas as pl
from jax.experimental.pallas import tpu as pltpu
from jax.sharding import PartitionSpec as P

LANES = 128
STEP_PAIRS = 64
STRIP = 8
PER_STEP = 2
NT = (((1,), (1,)), ((), ()))


def pinned(space, *arrays):
    return [pltpu.with_memory_space_constraint(a, space) for a in arrays]


def shift_pairs(count, by):
    return [(i, i + by) for i in range(count) if 0 <= i + by < count]


def neighbour_pairs(count, first):
    lows = range(first, count - 1, 2)
    return [(i, i + 1) for i in lows] + [(i + 1, i) for i in lows]


def crossed(axis, first):
    count = lax.axis_size(axis)
    pairs = neighbour_pairs(count, first)
    return [(c * count + i, (1 - c) * count + j) for c in range(2) for i, j in pairs]


def split(value, parts):
    if parts & (parts - 1) == 0:
        return lax.shift_right_logical(value, parts.bit_length() - 1), value & (parts - 1)
    return lax.div(value, parts), lax.rem(value, parts)


def ranks(dev, tiles):
    pairs = dev.shape[1]
    tile_of = lax.broadcasted_iota(jnp.int32, (tiles, pairs), 0)
    lane_of = lax.broadcasted_iota(jnp.int32, (tiles, pairs), 1)
    member = (tile_of == dev).astype(jnp.float32)
    total = member
    shift = 1
    while shift < pairs:
        total = total + jnp.where(lane_of >= shift, pltpu.roll(total, shift, 1), 0.0)
        shift *= 2
    return member, (jnp.sum(member * total, axis=0, keepdims=True) - 1.0).astype(jnp.int32)


def slot_blocks(dev, blk, tiles, capacity):
    member, rank = ranks(dev, tiles)
    pairs = dev.shape[1]
    slot_of = lax.broadcasted_iota(jnp.int32, (LANES, pairs), 0) % capacity
    chosen = (slot_of == rank).astype(jnp.bfloat16)

    def spread(values):
        return lax.dot_general(
            (member * values).astype(jnp.bfloat16), chosen, NT, preferred_element_type=jnp.float32
        )

    high, low = split(blk, 256)
    ids = spread(high.astype(jnp.float32)) * 256.0 + spread(low.astype(jnp.float32))
    return jnp.where(spread(jnp.ones(dev.shape, jnp.float32)) > 0.5, ids, -1.0)


def contribution_kernel(
    dims, src_ref, dev_ref, blk_ref, state_ref, weights_ref, early_ref, late_ref,
    cells, w_ref, pair_v, pair_s, taken, field_sems, weight_sems, pair_sems,
):
    tiles, capacity, pairs, fields, cells_x, cells_y, width = dims
    half = fields // 2
    parts = cells_y // width
    steps = pairs // STEP_PAIRS

    scalar_copies = [
        pltpu.make_async_copy(ref, pair_s.at[pl.ds(i, 1), :], pair_sems.at[i])
        for i, ref in enumerate((src_ref, dev_ref))
    ]
    vector_copies = [
        pltpu.make_async_copy(ref, pair_v.at[i], pair_sems.at[2 + i])
        for i, ref in enumerate((dev_ref, blk_ref))
    ]
    field_copies = [
        pltpu.make_async_copy(
            state_ref.at[0, f, :, pl.ds(q * width, width)],
            cells.at[q, :, f, :],
            field_sems.at[f * parts + q],
        )
        for f in range(fields)
        for q in range(parts)
    ]

    def weight_copy(step):
        some = pl.ds(step * STEP_PAIRS, STEP_PAIRS)
        return pltpu.make_async_copy(
            weights_ref.at[0, some], w_ref.at[some], weight_sems.at[step]
        )

    for copy in scalar_copies + vector_copies + field_copies:
        copy.start()
    for step in range(steps):
        weight_copy(step).start()
    late_ref[...] = jnp.zeros_like(late_ref)
    for t in range(tiles):
        taken[t] = t * (capacity + 1)

    for copy in vector_copies:
        copy.wait()
    dev, blk = pair_v[0], pair_v[1]
    ids = slot_blocks(dev, blk, tiles, capacity)
    for t in range(tiles):
        row = jnp.broadcast_to(ids[t : t + 1, :], late_ref.shape[1:])
        late_ref[t * (capacity + 1) + capacity] = row
    code = (dev * (cells_x * parts) + blk).astype(jnp.float32)
    for i in range(pairs // width):
        place = (pairs + i // half, slice(i % half, i % half + 1), slice(None))
        early_ref[place] = code[:, i * width : (i + 1) * width]
    for copy in scalar_copies + field_copies:
        copy.wait()

    def cells_of(p):
        x, part = split(pair_s[0, p], parts)
        return cells[part, x]

    zeros = jnp.zeros((fields, width), jnp.float32)

    def some_pairs(step, carry):
        weight_copy(step).wait()
        for i in range(0, STEP_PAIRS, 4):
            p = step * STEP_PAIRS + i
            left = [
                jnp.concatenate([cells_of(p + j), zeros][:: 1 - j % 2 * 2], axis=1) for j in range(4)
            ]
            left = jnp.concatenate(left, axis=0).astype(jnp.bfloat16)
            w = [w_ref[p + j] for j in range(4)]
            right = jnp.concatenate(
                [jnp.concatenate(w[:2], axis=1), jnp.concatenate(w[2:], axis=1)], axis=0
            )
            four = lax.dot_general(left, right, NT, preferred_element_type=jnp.float32)
            for j in range(4):
                tile = pair_s[1, p + j]
                slot = taken[tile]
                taken[tile] = slot + 1
                at = j // 2 * width
                one = four[j * fields : (j + 1) * fields, at : at + width]
                early_ref[p + j] = one[:half]
                late_ref[slot] = one[half:]
        return carry

    lax.fori_loop(0, steps, some_pairs, 0)


def contributions(state, pair_src, pair_dev, pair_blk, weights, tiles, capacity, fields):
    _, _, cells_x, cells_y = state.shape
    half = fields // 2
    pairs, width = weights.shape[1], weights.shape[2]
    rows = tiles * (capacity + 1)
    dims = (tiles, capacity, pairs, fields, cells_x, cells_y, width)
    parts = cells_y // width
    shapes = [(pairs + -(-pairs // (half * width)), half, width), (rows, half, width)]
    return pl.pallas_call(
        functools.partial(contribution_kernel, dims),
        in_specs=[pl.BlockSpec(memory_space=pltpu.HBM)] * 5,
        out_specs=[pl.BlockSpec(memory_space=pltpu.VMEM) for _ in shapes],
        out_shape=[jax.ShapeDtypeStruct(shape, jnp.float32) for shape in shapes],
        scratch_shapes=[
            pltpu.VMEM((parts, cells_x, fields, width), jnp.float32),
            pltpu.VMEM((pairs, width, width), jnp.bfloat16),
            pltpu.VMEM((2, 1, pairs), jnp.int32),
            pltpu.SMEM((2, pairs), jnp.int32),
            pltpu.SMEM((tiles,), jnp.int32),
            pltpu.SemaphoreType.DMA((parts * fields,)),
            pltpu.SemaphoreType.DMA((pairs // STEP_PAIRS,)),
            pltpu.SemaphoreType.DMA((4,)),
        ],
        compiler_params=pltpu.CompilerParams(vmem_limit_bytes=40 * 1024 * 1024),
        cost_estimate=pl.CostEstimate(
            flops=2 * pairs * fields * width * width,
            bytes_accessed=2 * pairs * width * width + 8 * rows * fields * width,
            transcendentals=0,
        ),
        name="contributions",
    )(*pinned(pltpu.HBM, pair_src, pair_dev.reshape(1, pairs), pair_blk, state, weights))


def place_kernel(dims, in_ref, out_ref, place_v, place_s, place_sem):
    tiles, capacity, pairs, blocks = dims
    half, width = in_ref.shape[1:]
    code = jnp.concatenate(
        [in_ref[pairs + i // half][i % half : i % half + 1] for i in range(pairs // width)], axis=1
    ).astype(jnp.int32)
    dev, _ = split(code, blocks)
    rank = ranks(dev, tiles)[1]
    place_v[...] = jnp.broadcast_to(dev * capacity + rank, place_v.shape)
    copy = pltpu.make_async_copy(place_v, place_s, place_sem)
    copy.start()
    out_ref[...] = jnp.zeros_like(out_ref)
    copy.wait()

    def some_rows(step, carry):
        for i in range(STEP_PAIRS):
            p = step * STEP_PAIRS + i
            out_ref[place_s[0, p]] = in_ref[p]
        return carry

    lax.fori_loop(0, pairs // STEP_PAIRS, some_rows, 0)


def placed_rows(rows, tiles, capacity, pairs, blocks):
    half, width = rows.shape[1:]
    shape = (tiles * capacity, half, width)
    return pl.pallas_call(
        functools.partial(place_kernel, (tiles, capacity, pairs, blocks)),
        out_shape=jax.ShapeDtypeStruct(shape, jnp.float32),
        scratch_shapes=[
            pltpu.VMEM((8, pairs), jnp.int32),
            pltpu.SMEM((8, pairs), jnp.int32),
            pltpu.SemaphoreType.DMA,
        ],
        compiler_params=pltpu.CompilerParams(vmem_limit_bytes=10 * 1024 * 1024),
        cost_estimate=pl.CostEstimate(
            flops=4 * rows.size, bytes_accessed=12 * rows.size, transcendentals=0
        ),
        name="place_in_slots",
    )(rows)


def sum_kernel(dims, odd_ref, ids_ref, rows_ref, out_ref, x0_ref, x1_ref, y0_ref, y1_ref,
               pick, high, low, in_ref, row_sems):
    tiles, capacity, fields, cells_x, cells_y, width = dims
    parts = cells_y // width
    group = LANES // capacity
    stride = in_ref.shape[0] // tiles

    def rows_copy(k):
        some = pl.ds(k * group * stride, group * stride)
        return pltpu.make_async_copy(rows_ref.at[some, :], in_ref.at[some, :], row_sems.at[k])

    for k in range(tiles // group):
        rows_copy(k).start()
    block_of = lax.broadcasted_iota(jnp.int32, (cells_x * parts, LANES), 0)
    block_of = (block_of % cells_x) * parts + block_of // cells_x
    block_of = block_of.astype(jnp.float32)
    lane = lax.broadcasted_iota(jnp.int32, (1, LANES), 1)
    for k in range(tiles // group):
        ids = None
        for i in range(group):
            row = ids_ref[pl.ds(k * group + i, 1), :]
            ids = row if ids is None else jnp.where(lane // capacity == i, row, ids)
        pick[:, pl.ds(k * LANES, LANES)] = (block_of == ids).astype(jnp.bfloat16)
    for k in range(tiles // group):
        rows_copy(k).wait()
        for source in range(k * group, (k + 1) * group):
            for f in range(fields):
                x = in_ref[pl.ds(source * stride + f, capacity, stride=fields), :]
                rounded = x.astype(jnp.bfloat16)
                place = (
                    pl.ds(source * capacity, capacity),
                    pl.ds(f * width, width),
                )
                high[place] = rounded
                low[place] = (x - rounded.astype(jnp.float32)).astype(jnp.bfloat16)

    def in_order(i, low_rim, high_rim):
        odd = odd_ref[i : i + 1, :] == 1.0
        return jnp.where(odd, high_rim, low_rim), jnp.where(odd, low_rim, high_rim)

    columns = {}
    column_of = lax.broadcasted_iota(jnp.int32, (cells_x, width), 1)
    for q in range(parts):
        chosen = pick[pl.ds(q * cells_x, cells_x), :]
        total = jnp.dot(chosen, high[...], preferred_element_type=jnp.float32)
        total = total + jnp.dot(chosen, low[...], preferred_element_type=jnp.float32)
        for f in range(fields):
            tile = total[:, f * width : (f + 1) * width]
            out_ref[f, :, pl.ds(q * width, width)] = tile
            rims = in_order(0, tile[:1], tile[cells_x - 1 :])
            for rim_ref, rim in zip((x0_ref, x1_ref), rims):
                rim_ref[pl.ds(f, 1), pl.ds(q * width, width)] = rim
            for edge, at in ((0, 0), (parts - 1, width - 1)):
                if q == edge:
                    moved = (f - at) % width
                    tile = pltpu.roll(tile, moved, 1) if moved else tile
                    columns[at] = jnp.where(column_of == f, tile, columns.get(at, 0.0))
    low_rims, high_rims = (columns[at].T[:fields] for at in (0, width - 1))
    y0_ref[...], y1_ref[...] = in_order(1, low_rims, high_rims)


def summed(odd, ids, rows, tiles, capacity, fields, cells_x, cells_y, width):
    dims = (tiles, capacity, fields, cells_x, cells_y, width)
    rows = rows.reshape(-1, width)
    slots = tiles * capacity
    blocks = cells_x * cells_y // width
    shapes = [
        (fields, cells_x, cells_y),
        (fields, cells_y),
        (fields, cells_y),
        (fields, cells_x),
        (fields, cells_x),
    ]
    return pl.pallas_call(
        functools.partial(sum_kernel, dims),
        in_specs=[pl.BlockSpec(memory_space=pltpu.VMEM)] * 2
        + [pl.BlockSpec(memory_space=pltpu.HBM)],
        out_shape=[jax.ShapeDtypeStruct(shape, jnp.float32) for shape in shapes],
        scratch_shapes=[
            pltpu.VMEM((blocks, slots), jnp.bfloat16),
            pltpu.VMEM((slots, fields * width), jnp.bfloat16),
            pltpu.VMEM((slots, fields * width), jnp.bfloat16),
            pltpu.VMEM(rows.shape, jnp.float32),
            pltpu.SemaphoreType.DMA((tiles * capacity // LANES,)),
        ],
        compiler_params=pltpu.CompilerParams(vmem_limit_bytes=24 * 1024 * 1024),
        cost_estimate=pl.CostEstimate(
            flops=4 * blocks * slots * fields * width,
            bytes_accessed=4 * fields * width * (slots + blocks),
            transcendentals=0,
        ),
        name="sum_by_block",
    )(odd, ids, *pinned(pltpu.HBM, rows))


def stencil_factors(coefs, keep):
    u, v, kappa = coefs
    return [
        keep,
        keep * (jnp.maximum(u, 0.0) + kappa),
        keep * (kappa - jnp.minimum(u, 0.0)),
        keep * (jnp.maximum(v, 0.0) + kappa),
        keep * (kappa - jnp.minimum(v, 0.0)),
        -keep * (jnp.abs(u) + jnp.abs(v) + 4.0 * kappa),
    ]


def tendency(s, rate, factors, top, bottom, left, right):
    cells_x, cells_y = s.shape
    x_of = lax.broadcasted_iota(jnp.int32, s.shape, 0)
    y_of = lax.broadcasted_iota(jnp.int32, s.shape, 1)
    out = (factors[5] - rate * factors[0]) * s
    out += factors[1] * jnp.where(x_of == 0, top, pltpu.roll(s, 1, 0))
    out += factors[2] * jnp.where(x_of == cells_x - 1, bottom, pltpu.roll(s, cells_x - 1, 0))
    out += factors[3] * jnp.where(y_of == 0, left, pltpu.roll(s, 1, 1))
    out += factors[4] * jnp.where(y_of == cells_y - 1, right, pltpu.roll(s, cells_y - 1, 1))
    return out


def columns_of(rows):
    spare = 8 - rows.shape[0]
    if spare:
        rows = jnp.concatenate([rows, jnp.zeros((spare, rows.shape[1]), rows.dtype)], axis=0)
    return rows.T


def line_count(nfield):
    return 2 * nfield + 8


def edge_kernel(mix_ref, state_tops, state_ends, state_lefts, state_rights, coefs_tops, coefs_ends,
                coefs_lefts, coefs_rights, land_tops, land_ends, land_lefts, land_rights,
                x_low, x_high, y_low, y_high):
    nfield = state_tops.shape[1]
    last_row, last_lane = state_tops.shape[2] - 1, state_lefts.shape[3] - 1
    atmos = mix_ref[0, 1] == 1.0

    def kept(land):
        return jnp.where(atmos, 1.0, land.astype(jnp.float32))

    for out, state, coefs, land, lines in (
        (x_low, state_tops, coefs_tops, land_tops, (0, 1)),
        (x_high, state_ends, coefs_ends, land_ends, (last_row - 1, last_row)),
    ):
        outer = lines[0] if lines[0] == 0 else lines[1]
        out[2 * nfield :, :] = jnp.zeros((8, out.shape[1]), jnp.float32)
        for j, line in enumerate(lines):
            for f in range(nfield):
                out[j * nfield + f : j * nfield + f + 1, :] = state[0, f, line : line + 1, :]
        for c in range(3):
            out[2 * nfield + c : 2 * nfield + c + 1, :] = coefs[0, c, outer : outer + 1, :]
        out[2 * nfield + 3 : 2 * nfield + 4, :] = kept(land[outer : outer + 1, :])

    for out, state, coefs, land, lines in (
        (y_low, state_lefts, coefs_lefts, land_lefts, (0, 1)),
        (y_high, state_rights, coefs_rights, land_rights, (last_lane - 1, last_lane)),
    ):
        outer = lines[0] if lines[0] == 0 else lines[1]
        lane = lax.broadcasted_iota(jnp.int32, land.shape, 1)
        packed = jnp.zeros(land.shape, jnp.float32)

        def put(packed, tile, at, to):
            moved = (to - at) % LANES
            tile = pltpu.roll(tile, moved, 1) if moved else tile
            return jnp.where(lane == to, tile, packed)

        for j, line in enumerate(lines):
            for f in range(nfield):
                packed = put(packed, state[0, f], line, j * nfield + f)
        for c in range(3):
            packed = put(packed, coefs[0, c], outer, 2 * nfield + c)
        packed = put(packed, kept(land[...]), outer, 2 * nfield + 3)
        out[...] = packed.T[: out.shape[0]]


def edges_of(state, coefs, land_sea, mix):
    _, nfield, cells_x, cells_y = state.shape
    lines = line_count(nfield)
    ends = [
        ((8, cells_y), (0, 0)),
        ((8, cells_y), (cells_x // 8 - 1, 0)),
        ((cells_x, LANES), (0, 0)),
        ((cells_x, LANES), (0, cells_y // LANES - 1)),
    ]
    at = lambda lead, place: lambda i: (0,) * len(lead) + place
    specs = [pl.BlockSpec(memory_space=pltpu.SMEM)]
    for lead in ((1, nfield), (1, 3), ()):
        specs += [pl.BlockSpec(lead + shape, at(lead, place)) for shape, place in ends]
    shapes = [(lines, cells_y)] * 2 + [(lines, cells_x)] * 2
    return pl.pallas_call(
        edge_kernel,
        grid=(1,),
        in_specs=specs,
        out_specs=[pl.BlockSpec(shape, lambda i: (0, 0)) for shape in shapes],
        out_shape=[jax.ShapeDtypeStruct(shape, jnp.float32) for shape in shapes],
        compiler_params=pltpu.CompilerParams(vmem_limit_bytes=24 * 1024 * 1024),
        cost_estimate=pl.CostEstimate(
            flops=state.size, bytes_accessed=4 * 1024 * 1024, transcendentals=0
        ),
        name="edges",
    )(mix, *pinned(pltpu.HBM, *[state] * 4), *[coefs] * 4, *[land_sea] * 4)


def outer_section(center, across, along, factors, rate):
    lane = lax.broadcasted_iota(jnp.int32, center.shape, 1)
    count = center.shape[1]
    before = jnp.where(lane == 0, along[0], pltpu.roll(center, 1, 1))
    after = jnp.where(lane == count - 1, along[1], pltpu.roll(center, count - 1, 1))
    keep, low, high, back, ahead, middle = factors
    out = center + low * across[0] + high * across[1] + back * before + ahead * after
    return out + (middle - rate * keep) * center


def base_kernel(half, rate_ref, mix_ref, rates_ref, coefs_ref, land_ref, x_low, x_high, y_low, y_high,
                above, below, left, right, corners_left, corners_right, state_ref,
                out_ref, early_ref, factors, rows, cols):
    f = pl.program_id(0)
    nfield = rates_ref.shape[0]
    lines = line_count(nfield)

    @pl.when(f == 0)
    def _():
        keep = jnp.where(mix_ref[0, 1] == 1.0, 1.0, land_ref[...].astype(jnp.float32))
        for i, factor in enumerate(stencil_factors([coefs_ref[0, c] for c in range(3)], keep)):
            factors[i] = factor
        rate = rates_ref[:, 0:1]
        near, far = pl.ds(0, nfield), pl.ds(nfield, nfield)
        last = corners_left.shape[1] - 1
        corner = (
            (corners_left[nfield : 2 * nfield, last:], corners_left[lines : lines + nfield, last:]),
            (corners_right[nfield : 2 * nfield, 0:1], corners_right[lines : lines + nfield, 0:1]),
        )
        for i, (ref, center, across, along, is_column) in enumerate(
            (
                (above, above[far, :], (above[near, :], x_low[near, :]), (corner[0][0], corner[1][0]), False),
                (below, below[near, :], (x_high[far, :], below[far, :]), (corner[0][1], corner[1][1]), False),
                (left, left[far, :], (left[near, :], y_low[near, :]), corner[0], True),
                (right, right[near, :], (y_high[far, :], right[far, :]), corner[1], True),
            )
        ):
            first = 2 * nfield
            of_line = stencil_factors(
                [ref[first + c : first + c + 1, :] for c in range(3)],
                ref[first + 3 : first + 4, :],
            )
            if is_column:
                of_line = [of_line[j] for j in (0, 3, 4, 1, 2, 5)]
            section = outer_section(center, across, along, of_line, rate)
            kept = cols if is_column else rows
            kept[pl.ds(i % 2 * nfield, nfield), :] = center
            kept[pl.ds((2 + i % 2) * nfield, nfield), :] = section

    mix_a, mix_b = mix_ref[0, 0], mix_ref[0, 1]
    for j in range(PER_STEP):
        field = f * PER_STEP + j
        rate = rate_ref[0, field]
        s = state_ref[0, j]
        row = [rows[pl.ds(i * nfield + field, 1), :] for i in range(4)]
        col = columns_of(
            jnp.concatenate([cols[pl.ds(i * nfield + field, 1), :] for i in range(4)], axis=0)
        )
        s1 = s + tendency(s, rate, factors, row[0], row[1], col[:, 0:1], col[:, 1:2])
        more = tendency(s1, rate, factors, row[2], row[3], col[:, 2:3], col[:, 3:4])
        total = mix_a * s + (1.0 - mix_a) * s1 + mix_b * more
        out_ref[0, j] = total

        @pl.when(field < half)
        def _():
            early_ref[j] = total


def base_of(state, coefs, land_sea, rates, mix, edges, received, corners, half):
    _, nfield, cells_x, cells_y = state.shape
    field = pl.BlockSpec((1, PER_STEP, cells_x, cells_y), lambda f: (0, f, 0, 0))
    early = pl.BlockSpec(
        (PER_STEP, cells_x, cells_y), lambda f: (jnp.minimum(f, half // PER_STEP - 1), 0, 0)
    )
    whole = lambda a: pl.BlockSpec(a.shape, lambda f: (0,) * a.ndim)
    rates_wide = jnp.broadcast_to(rates.T, (nfield, LANES))
    operands = [rates_wide, coefs, land_sea, *edges, *received, *corners]
    return pl.pallas_call(
        functools.partial(base_kernel, half),
        grid=(nfield // PER_STEP,),
        in_specs=[
            pl.BlockSpec(memory_space=pltpu.SMEM),
            pl.BlockSpec(memory_space=pltpu.SMEM),
            *[whole(a) for a in operands],
            field,
        ],
        out_specs=[
            field,
            early,
            pl.BlockSpec((6, cells_x, cells_y), lambda f: (0, 0, 0)),
        ],
        out_shape=[
            jax.ShapeDtypeStruct(state.shape, jnp.float32),
            jax.ShapeDtypeStruct((half, cells_x, cells_y), jnp.float32),
            jax.ShapeDtypeStruct((6, cells_x, cells_y), jnp.float32),
        ],
        scratch_shapes=[
            pltpu.VMEM((4 * nfield, cells_y), jnp.float32),
            pltpu.VMEM((4 * nfield, cells_x), jnp.float32),
        ],
        compiler_params=pltpu.CompilerParams(vmem_limit_bytes=24 * 1024 * 1024),
        cost_estimate=pl.CostEstimate(
            flops=40 * state.size, bytes_accessed=8 * state.size, transcendentals=0
        ),
        name="base",
    )(rates, mix, *operands, *pinned(pltpu.HBM, state))


def finish_kernel(first, with_x, rates_ref, mix_ref, above, below, before, after, factors, recv,
                  left, right, *rest):
    tops, rest = (rest[:2], rest[2:]) if with_x else (None, rest)
    late, rest = (rest[:2], rest[2:]) if with_x else (None, rest)
    early_base, rest = (rest[0], rest[1:]) if with_x else (None, rest)
    odd_ref, base_ref, rest = rest[0], rest[1], rest[2:]
    new_ref, out_ref, done_ref = rest[-11:-8]
    base, wide, lines, sides, outer, base_sems, out_sems, outer_sems = rest[-8:]
    count, cells_x, cells_y = base.shape
    mix_b = jnp.broadcast_to(mix_ref[1:2, 0:1], (STRIP, cells_y))
    keep_row = above.shape[0] - 5
    keep = slice(keep_row, keep_row + 1)
    ends = (0, cells_x - STRIP)

    def base_copy(f):
        return pltpu.make_async_copy(base_ref.at[0, first + f], base.at[f], base_sems.at[f])

    def out_copies(f):
        return (
            pltpu.make_async_copy(recv.at[f], out_ref.at[0, first + f], out_sems.at[0, f]),
            pltpu.make_async_copy(base.at[f], new_ref.at[0, first + f], out_sems.at[1, f]),
        )

    def outer_copy(f, i, back):
        there = (new_ref if back else base_ref).at[0, count + f, pl.ds(ends[i], STRIP), :]
        here = outer.at[f, i]
        pair = (here, there) if back else (there, here)
        return pltpu.make_async_copy(*pair, outer_sems.at[f, i])

    outer_rows = [(f, i) for f in range(count) for i in range(2)] if with_x else []
    if not with_x:
        for f in range(count):
            base_copy(f).start()
    for f, i in outer_rows:
        outer_copy(f, i, False).start()
    done_ref[...] = jnp.zeros_like(done_ref)
    def in_order(i, pair):
        in_odd, in_even = pair[0][...], pair[1][...]
        odd = jnp.broadcast_to(odd_ref[i : i + 1, 0:1], in_odd.shape) == 1.0
        return jnp.where(odd, in_even, in_odd), jnp.where(odd, in_odd, in_even)

    if with_x:
        top, bottom = in_order(0, tops)
        lines[:count, :] = top * above[keep, :]
        lines[count:, :] = bottom * below[keep, :]
        late = in_order(0, late)
    else:
        lines[...] = jnp.zeros_like(lines)
    left, right = in_order(1, (left, right))
    sides[:count, :] = left * before[keep, :]
    sides[count:, :] = right * after[keep, :]
    lane = lax.broadcasted_iota(jnp.int32, (STRIP, cells_y), 1)

    def one_field(f, carry):
        rate = jnp.broadcast_to(rates_ref[pl.ds(first + f, 1), 0:1], (STRIP, cells_y))
        line_rate, side_rate = rate[:1], rate[:1, :cells_x]
        both = [sides[pl.ds(f, 1), :] * side_rate, sides[pl.ds(count + f, 1), :] * side_rate]
        cols = columns_of(jnp.concatenate(both, axis=0))
        wide[STRIP - 1 : STRIP, :] = lines[pl.ds(f, 1), :] * line_rate
        wide[STRIP + cells_x : STRIP + cells_x + 1, :] = lines[pl.ds(count + f, 1), :] * line_rate
        to_out, to_new = out_copies(f)
        to_out.start()
        for i in range(0, cells_x, STRIP):
            rows = slice(i, i + STRIP)
            wide[STRIP + i : 2 * STRIP + i, :] = factors[0, rows, :] * recv[f, rows, :] * rate
        if not with_x:
            base_copy(f).wait()
        start = early_base if with_x else base
        for i in range(0, cells_x, STRIP):
            rows = slice(i, i + STRIP)
            mid = wide[STRIP + i : 2 * STRIP + i, :]
            more = (factors[5, rows, :] - rate * factors[0, rows, :]) * mid
            more += factors[1, rows, :] * wide[STRIP + i - 1 : 2 * STRIP + i - 1, :]
            more += factors[2, rows, :] * wide[STRIP + i + 1 : 2 * STRIP + i + 1, :]
            prior = jnp.where(lane == 0, cols[rows, 0:1], pltpu.roll(mid, 1, 1))
            later = jnp.where(lane == cells_y - 1, cols[rows, 1:2], pltpu.roll(mid, cells_y - 1, 1))
            more += factors[3, rows, :] * prior + factors[4, rows, :] * later
            base[f, rows, :] = start[f, rows, :] + mix_b * (2.0 * mid + more)
        to_new.start()
        return carry

    def add_lines():
        for f, i in outer_rows:
            outer_copy(f, i, False).wait()
            row = i * (STRIP - 1)
            at = ends[i] + row
            rate = jnp.broadcast_to(rates_ref[count + f : count + f + 1, 0:1], (1, cells_y))
            line = late[i][f : f + 1, :] * (above, below)[i][keep, :] * rate
            more = mix_b[:1] * factors[1 + i, at : at + 1, :] * line
            outer[f, i, row : row + 1, :] = outer[f, i, row : row + 1, :] + more
            outer_copy(f, i, True).start()

    lax.fori_loop(0, count - 1, one_field, 0)
    add_lines()
    one_field(count - 1, 0)
    for f in range(count):
        for copy in out_copies(f):
            copy.wait()
    for f, i in outer_rows:
        outer_copy(f, i, True).wait()


def finished(
    first, new_state, remapped, recv, odd, x_rims, y_rims, closing, rates, mix, factors, received
):
    count, cells_x, cells_y = recv.shape
    chan = 2 * count
    with_x = x_rims is not None
    anywhere = pl.BlockSpec(memory_space=pl.ANY)
    operands = [rates, mix, *received, factors, recv, *y_rims]
    if with_x:
        late_rims, base_early, late_done = closing
        operands += [*x_rims, *late_rims, base_early]
    operands.append(odd)
    specs = [pl.BlockSpec(memory_space=pltpu.VMEM)] * len(operands) + [anywhere]
    aliases = {len(operands): 0}
    operands.append(new_state)
    if remapped is not None:
        aliases[len(operands)] = 1
        operands += [remapped, late_done]
        specs += [anywhere, anywhere]
    return pl.pallas_call(
        functools.partial(finish_kernel, first, with_x),
        in_specs=specs,
        out_specs=[anywhere, anywhere, pl.BlockSpec(memory_space=pltpu.VMEM)],
        out_shape=[
            jax.ShapeDtypeStruct(new_state.shape, jnp.float32),
            jax.ShapeDtypeStruct((1, chan, cells_x, cells_y), jnp.float32),
            jax.ShapeDtypeStruct((8, LANES), jnp.float32),
        ],
        input_output_aliases=aliases,
        scratch_shapes=[
            pltpu.VMEM((count, cells_x, cells_y), jnp.float32),
            pltpu.VMEM((cells_x + 2 * STRIP, cells_y), jnp.float32),
            pltpu.VMEM((2 * count, cells_y), jnp.float32),
            pltpu.VMEM((2 * count, cells_x), jnp.float32),
            pltpu.VMEM((count, 2, STRIP, cells_y), jnp.float32),
            pltpu.SemaphoreType.DMA((count,)),
            pltpu.SemaphoreType.DMA((2, count)),
            pltpu.SemaphoreType.DMA((count, 2)),
        ],
        compiler_params=pltpu.CompilerParams(vmem_limit_bytes=12 * 1024 * 1024),
        cost_estimate=pl.CostEstimate(
            flops=20 * recv.size, bytes_accessed=20 * recv.size, transcendentals=0
        ),
        name="finish",
    )(*operands)


def body(state, coefs, land_sea, gamma, pair_src, pair_dev, pair_blk, weights):
    tx, ty = lax.axis_size("tx"), lax.axis_size("ty")
    tiles = tx * ty
    nfield, cells_x, cells_y = state.shape[1:]
    chan = gamma.shape[1]
    pairs, width = weights.shape[1], weights.shape[2]
    capacity = max(2, 2 * pairs // tiles)
    half = chan // 2
    early, late = contributions(
        state, pair_src, pair_dev, pair_blk, weights, tiles, capacity, chan
    )
    swap = [(0, 1), (1, 0)]

    def exchanged(rows):
        rows = rows.reshape(tiles, -1, half, width)
        return lax.all_to_all(rows, ("tx", "ty"), split_axis=0, concat_axis=0, tiled=True)

    def add_up(odd, ids, rows):
        return summed(odd, ids, rows, tiles, capacity, half, cells_x, cells_y, width)

    late_in = exchanged(late)
    early = lax.ppermute(early, "comp", swap)
    early_in = placed_rows(early, tiles, capacity, pairs, cells_x * cells_y // width)

    land_after, _ = lax.optimization_barrier((land_sea, late))
    is_atmos = lax.axis_index("comp") == 0
    mix = jnp.where(is_atmos, jnp.array([[0.0, 1.0]]), jnp.array([[0.5, 0.5]]))
    mix = mix.astype(jnp.float32)
    rates = jnp.concatenate([gamma, jnp.zeros((1, nfield - chan), jnp.float32)], axis=1)
    x_low, x_high, y_low, y_high = edges_of(state, coefs, land_after, mix)
    left = lax.ppermute(y_high, "ty", shift_pairs(ty, 1))
    right = lax.ppermute(y_low, "ty", shift_pairs(ty, -1))
    above = lax.ppermute(x_high, "tx", shift_pairs(tx, 1))
    below = lax.ppermute(x_low, "tx", shift_pairs(tx, -1))
    early_in, above, below, left, right = lax.optimization_barrier(
        (early_in, above, below, left, right)
    )
    received = (above, below, left, right)
    early_in = exchanged(early_in)

    ends = jnp.concatenate([above[:, cells_y - LANES :], below[:, cells_y - LANES :]], axis=0)
    starts = jnp.concatenate([above[:, :LANES], below[:, :LANES]], axis=0)
    corners_left = lax.ppermute(ends, "ty", shift_pairs(ty, 1))
    corners_right = lax.ppermute(starts, "ty", shift_pairs(ty, -1))
    base, base_early, factors = base_of(
        state, coefs, land_after, rates, mix, (x_low, x_high, y_low, y_high), received,
        (corners_left, corners_right), half,
    )

    ids_late = late_in[:, capacity, 0, :]
    ids_early = lax.ppermute(ids_late, "comp", swap)
    odd = jnp.stack([lax.axis_index("tx"), lax.axis_index("ty")]).astype(jnp.int32)[None] & 1
    odd_lanes = jnp.broadcast_to(odd.T.astype(jnp.float32), (2, LANES))
    recv_late, x_odd, x_even, y_odd, y_even = add_up(odd_lanes, ids_late, late_in)
    recv_late = lax.ppermute(recv_late, "comp", swap)
    late_x = (
        lax.ppermute(x_odd, ("comp", "tx"), crossed("tx", 1)),
        lax.ppermute(x_even, ("comp", "tx"), crossed("tx", 0)),
    )
    late_y = (
        lax.ppermute(y_odd, ("comp", "ty"), crossed("ty", 1)),
        lax.ppermute(y_even, ("comp", "ty"), crossed("ty", 0)),
    )
    lanes = lambda a: jnp.broadcast_to(a.T, (a.shape[1], LANES))
    rest = (lanes(rates), lanes(mix), factors, received)
    new_state, remapped, done = finished(
        half, base, None, recv_late, odd_lanes, None, late_y, None, *rest
    )
    early_in, done = lax.optimization_barrier((early_in, done))
    recv_early, x_odd, x_even, y_odd, y_even = add_up(odd_lanes, ids_early, early_in)
    early_x = (
        lax.ppermute(x_odd, "tx", neighbour_pairs(tx, 1)),
        lax.ppermute(x_even, "tx", neighbour_pairs(tx, 0)),
    )
    early_y = (
        lax.ppermute(y_odd, "ty", neighbour_pairs(ty, 1)),
        lax.ppermute(y_even, "ty", neighbour_pairs(ty, 0)),
    )
    new_state, remapped, _ = finished(
        0, new_state, remapped, recv_early, odd_lanes, early_x, early_y, (late_x, base_early, done), *rest
    )
    return new_state, remapped


def solution(mesh):
    placed = (
        P("comp", None, "tx", "ty"),
        P("comp", None, "tx", "ty"),
        P("tx", "ty"),
        P("comp", None),
        P("comp", ("tx", "ty")),
        P("comp", ("tx", "ty"), None),
        P("comp", ("tx", "ty")),
        P("comp", ("tx", "ty"), None, None),
    )
    return jax.shard_map(
        body,
        mesh=mesh,
        in_specs=placed,
        out_specs=(P("comp", None, "tx", "ty"), P("comp", None, "tx", "ty")),
        check_vma=False,
    )
```

```python
import functools

import jax
import jax.numpy as jnp
from jax import lax
from jax.experimental import pallas as pl
from jax.experimental.pallas import tpu as pltpu
from jax.sharding import PartitionSpec as P

LANES = 128
STEP_PAIRS = 64
STRIP = 8
PER_STEP = 2
NT = (((1,), (1,)), ((), ()))


def pinned(space, *arrays):
    return [pltpu.with_memory_space_constraint(a, space) for a in arrays]


def shift_pairs(count, by):
    return [(i, i + by) for i in range(count) if 0 <= i + by < count]


def neighbour_pairs(count, first):
    lows = range(first, count - 1, 2)
    return [(i, i + 1) for i in lows] + [(i + 1, i) for i in lows]


def crossed(axis, first):
    count = lax.axis_size(axis)
    pairs = neighbour_pairs(count, first)
    return [(c * count + i, (1 - c) * count + j) for c in range(2) for i, j in pairs]


def split(value, parts):
    if parts & (parts - 1) == 0:
        return lax.shift_right_logical(value, parts.bit_length() - 1), value & (parts - 1)
    return lax.div(value, parts), lax.rem(value, parts)


def ranks(dev, tiles):
    pairs = dev.shape[1]
    tile_of = lax.broadcasted_iota(jnp.int32, (tiles, pairs), 0)
    lane_of = lax.broadcasted_iota(jnp.int32, (tiles, pairs), 1)
    member = (tile_of == dev).astype(jnp.float32)
    total = member
    shift = 1
    while shift < pairs:
        total = total + jnp.where(lane_of >= shift, pltpu.roll(total, shift, 1), 0.0)
        shift *= 2
    return member, (jnp.sum(member * total, axis=0, keepdims=True) - 1.0).astype(jnp.int32)


def slot_blocks(dev, blk, tiles, capacity):
    member, rank = ranks(dev, tiles)
    pairs = dev.shape[1]
    slot_of = lax.broadcasted_iota(jnp.int32, (LANES, pairs), 0) % capacity
    chosen = (slot_of == rank).astype(jnp.bfloat16)

    def spread(values):
        return lax.dot_general(
            (member * values).astype(jnp.bfloat16), chosen, NT, preferred_element_type=jnp.float32
        )

    high, low = split(blk, 256)
    ids = spread(high.astype(jnp.float32)) * 256.0 + spread(low.astype(jnp.float32))
    return jnp.where(spread(jnp.ones(dev.shape, jnp.float32)) > 0.5, ids, -1.0)


def contribution_kernel(
    dims, src_ref, dev_ref, blk_ref, state_ref, weights_ref, early_ref, late_ref,
    cells, w_ref, pair_v, pair_s, taken, field_sems, weight_sems, pair_sems,
):
    tiles, capacity, pairs, fields, cells_x, cells_y, width = dims
    half = fields // 2
    parts = cells_y // width
    steps = pairs // STEP_PAIRS

    scalar_copies = [
        pltpu.make_async_copy(ref, pair_s.at[pl.ds(i, 1), :], pair_sems.at[i])
        for i, ref in enumerate((src_ref, dev_ref))
    ]
    vector_copies = [
        pltpu.make_async_copy(ref, pair_v.at[i], pair_sems.at[2 + i])
        for i, ref in enumerate((dev_ref, blk_ref))
    ]
    field_copies = [
        pltpu.make_async_copy(
            state_ref.at[0, f, :, pl.ds(q * width, width)],
            cells.at[q, :, f, :],
            field_sems.at[f * parts + q],
        )
        for f in range(fields)
        for q in range(parts)
    ]

    def weight_copy(step):
        some = pl.ds(step * STEP_PAIRS, STEP_PAIRS)
        return pltpu.make_async_copy(
            weights_ref.at[0, some], w_ref.at[some], weight_sems.at[step]
        )

    for copy in scalar_copies + vector_copies + field_copies:
        copy.start()
    for step in range(steps):
        weight_copy(step).start()
    late_ref[...] = jnp.zeros_like(late_ref)
    for t in range(tiles):
        taken[t] = t * (capacity + 1)

    for copy in vector_copies:
        copy.wait()
    dev, blk = pair_v[0], pair_v[1]
    ids = slot_blocks(dev, blk, tiles, capacity)
    for t in range(tiles):
        row = jnp.broadcast_to(ids[t : t + 1, :], late_ref.shape[1:])
        late_ref[t * (capacity + 1) + capacity] = row
    code = (dev * (cells_x * parts) + blk).astype(jnp.float32)
    for i in range(pairs // width):
        place = (pairs + i // half, slice(i % half, i % half + 1), slice(None))
        early_ref[place] = code[:, i * width : (i + 1) * width]
    for copy in scalar_copies + field_copies:
        copy.wait()

    def cells_of(p):
        x, part = split(pair_s[0, p], parts)
        return cells[part, x]

    zeros = jnp.zeros((fields, width), jnp.float32)

    def some_pairs(step, carry):
        weight_copy(step).wait()
        for i in range(0, STEP_PAIRS, 4):
            p = step * STEP_PAIRS + i
            left = [
                jnp.concatenate([cells_of(p + j), zeros][:: 1 - j % 2 * 2], axis=1) for j in range(4)
            ]
            left = jnp.concatenate(left, axis=0).astype(jnp.bfloat16)
            w = [w_ref[p + j] for j in range(4)]
            right = jnp.concatenate(
                [jnp.concatenate(w[:2], axis=1), jnp.concatenate(w[2:], axis=1)], axis=0
            )
            four = lax.dot_general(left, right, NT, preferred_element_type=jnp.float32)
            for j in range(4):
                tile = pair_s[1, p + j]
                slot = taken[tile]
                taken[tile] = slot + 1
                at = j // 2 * width
                one = four[j * fields : (j + 1) * fields, at : at + width]
                early_ref[p + j] = one[:half]
                late_ref[slot] = one[half:]
        return carry

    lax.fori_loop(0, steps, some_pairs, 0)


def contributions(state, pair_src, pair_dev, pair_blk, weights, tiles, capacity, fields):
    _, _, cells_x, cells_y = state.shape
    half = fields // 2
    pairs, width = weights.shape[1], weights.shape[2]
    rows = tiles * (capacity + 1)
    dims = (tiles, capacity, pairs, fields, cells_x, cells_y, width)
    parts = cells_y // width
    shapes = [(pairs + -(-pairs // (half * width)), half, width), (rows, half, width)]
    return pl.pallas_call(
        functools.partial(contribution_kernel, dims),
        in_specs=[pl.BlockSpec(memory_space=pltpu.HBM)] * 5,
        out_specs=[pl.BlockSpec(memory_space=pltpu.VMEM) for _ in shapes],
        out_shape=[jax.ShapeDtypeStruct(shape, jnp.float32) for shape in shapes],
        scratch_shapes=[
            pltpu.VMEM((parts, cells_x, fields, width), jnp.float32),
            pltpu.VMEM((pairs, width, width), jnp.bfloat16),
            pltpu.VMEM((2, 1, pairs), jnp.int32),
            pltpu.SMEM((2, pairs), jnp.int32),
            pltpu.SMEM((tiles,), jnp.int32),
            pltpu.SemaphoreType.DMA((parts * fields,)),
            pltpu.SemaphoreType.DMA((pairs // STEP_PAIRS,)),
            pltpu.SemaphoreType.DMA((4,)),
        ],
        compiler_params=pltpu.CompilerParams(vmem_limit_bytes=40 * 1024 * 1024),
        cost_estimate=pl.CostEstimate(
            flops=2 * pairs * fields * width * width,
            bytes_accessed=2 * pairs * width * width + 8 * rows * fields * width,
            transcendentals=0,
        ),
        name="contributions",
    )(*pinned(pltpu.HBM, pair_src, pair_dev.reshape(1, pairs), pair_blk, state, weights))


def place_kernel(dims, in_ref, out_ref, place_v, place_s, place_sem):
    tiles, capacity, pairs, blocks = dims
    half, width = in_ref.shape[1:]
    code = jnp.concatenate(
        [in_ref[pairs + i // half][i % half : i % half + 1] for i in range(pairs // width)], axis=1
    ).astype(jnp.int32)
    dev, _ = split(code, blocks)
    rank = ranks(dev, tiles)[1]
    place_v[...] = jnp.broadcast_to(dev * capacity + rank, place_v.shape)
    copy = pltpu.make_async_copy(place_v, place_s, place_sem)
    copy.start()
    out_ref[...] = jnp.zeros_like(out_ref)
    copy.wait()

    def some_rows(step, carry):
        for i in range(STEP_PAIRS):
            p = step * STEP_PAIRS + i
            out_ref[place_s[0, p]] = in_ref[p]
        return carry

    lax.fori_loop(0, pairs // STEP_PAIRS, some_rows, 0)


def placed_rows(rows, tiles, capacity, pairs, blocks):
    half, width = rows.shape[1:]
    shape = (tiles * capacity, half, width)
    return pl.pallas_call(
        functools.partial(place_kernel, (tiles, capacity, pairs, blocks)),
        out_shape=jax.ShapeDtypeStruct(shape, jnp.float32),
        scratch_shapes=[
            pltpu.VMEM((8, pairs), jnp.int32),
            pltpu.SMEM((8, pairs), jnp.int32),
            pltpu.SemaphoreType.DMA,
        ],
        compiler_params=pltpu.CompilerParams(vmem_limit_bytes=10 * 1024 * 1024),
        cost_estimate=pl.CostEstimate(
            flops=4 * rows.size, bytes_accessed=12 * rows.size, transcendentals=0
        ),
        name="place_in_slots",
    )(rows)


def sum_kernel(dims, odd_ref, ids_ref, rows_ref, out_ref, x0_ref, x1_ref, y0_ref, y1_ref,
               pick, high, low, in_ref, row_sems):
    tiles, capacity, fields, cells_x, cells_y, width = dims
    parts = cells_y // width
    group = LANES // capacity
    stride = rows_ref.shape[0] // tiles

    def rows_copy(k):
        some = pl.ds(k * group * stride, group * stride)
        return pltpu.make_async_copy(rows_ref.at[some, :], in_ref.at[some, :], row_sems.at[k])

    for k in range(tiles // group):
        rows_copy(k).start()
    block_of = lax.broadcasted_iota(jnp.int32, (cells_x * parts, LANES), 0)
    block_of = (block_of % cells_x) * parts + block_of // cells_x
    block_of = block_of.astype(jnp.float32)
    lane = lax.broadcasted_iota(jnp.int32, (1, LANES), 1)
    for k in range(tiles // group):
        ids = None
        for i in range(group):
            row = ids_ref[pl.ds(k * group + i, 1), :]
            ids = row if ids is None else jnp.where(lane // capacity == i, row, ids)
        pick[:, pl.ds(k * LANES, LANES)] = (block_of == ids).astype(jnp.bfloat16)
    for k in range(tiles // group):
        rows_copy(k).wait()
        for source in range(k * group, (k + 1) * group):
            for f in range(fields):
                x = in_ref[pl.ds(source * stride + f, capacity, stride=fields), :]
                rounded = x.astype(jnp.bfloat16)
                place = (
                    pl.ds(source * capacity, capacity),
                    pl.ds(f * width, width),
                )
                high[place] = rounded
                low[place] = (x - rounded.astype(jnp.float32)).astype(jnp.bfloat16)

    def in_order(i, low_rim, high_rim):
        odd = odd_ref[i : i + 1, :] == 1.0
        return jnp.where(odd, high_rim, low_rim), jnp.where(odd, low_rim, high_rim)

    columns = {}
    column_of = lax.broadcasted_iota(jnp.int32, (cells_x, width), 1)
    for q in range(parts):
        chosen = pick[pl.ds(q * cells_x, cells_x), :]
        total = jnp.dot(chosen, high[...], preferred_element_type=jnp.float32)
        total = total + jnp.dot(chosen, low[...], preferred_element_type=jnp.float32)
        for f in range(fields):
            tile = total[:, f * width : (f + 1) * width]
            out_ref[f, :, pl.ds(q * width, width)] = tile
            rims = in_order(0, tile[:1], tile[cells_x - 1 :])
            for rim_ref, rim in zip((x0_ref, x1_ref), rims):
                rim_ref[pl.ds(f, 1), pl.ds(q * width, width)] = rim
            for edge, at in ((0, 0), (parts - 1, width - 1)):
                if q == edge:
                    moved = (f - at) % width
                    tile = pltpu.roll(tile, moved, 1) if moved else tile
                    columns[at] = jnp.where(column_of == f, tile, columns.get(at, 0.0))
    low_rims, high_rims = (columns[at].T[:fields] for at in (0, width - 1))
    y0_ref[...], y1_ref[...] = in_order(1, low_rims, high_rims)


def summed(odd, ids, rows, tiles, capacity, fields, cells_x, cells_y, width):
    dims = (tiles, capacity, fields, cells_x, cells_y, width)
    rows = rows.reshape(-1, width)
    slots = tiles * capacity
    blocks = cells_x * cells_y // width
    shapes = [
        (fields, cells_x, cells_y),
        (fields, cells_y),
        (fields, cells_y),
        (fields, cells_x),
        (fields, cells_x),
    ]
    return pl.pallas_call(
        functools.partial(sum_kernel, dims),
        in_specs=[pl.BlockSpec(memory_space=pltpu.VMEM)] * 2
        + [pl.BlockSpec(memory_space=pltpu.HBM)],
        out_shape=[jax.ShapeDtypeStruct(shape, jnp.float32) for shape in shapes],
        scratch_shapes=[
            pltpu.VMEM((blocks, slots), jnp.bfloat16),
            pltpu.VMEM((slots, fields * width), jnp.bfloat16),
            pltpu.VMEM((slots, fields * width), jnp.bfloat16),
            pltpu.VMEM((rows.shape[0] + 8, width), jnp.float32),
            pltpu.SemaphoreType.DMA((tiles * capacity // LANES,)),
        ],
        compiler_params=pltpu.CompilerParams(vmem_limit_bytes=24 * 1024 * 1024),
        cost_estimate=pl.CostEstimate(
            flops=4 * blocks * slots * fields * width,
            bytes_accessed=4 * fields * width * (slots + blocks),
            transcendentals=0,
        ),
        name="sum_by_block",
    )(odd, ids, *pinned(pltpu.HBM, rows))


def stencil_factors(coefs, keep):
    u, v, kappa = coefs
    return [
        keep,
        keep * (jnp.maximum(u, 0.0) + kappa),
        keep * (kappa - jnp.minimum(u, 0.0)),
        keep * (jnp.maximum(v, 0.0) + kappa),
        keep * (kappa - jnp.minimum(v, 0.0)),
        -keep * (jnp.abs(u) + jnp.abs(v) + 4.0 * kappa),
    ]


def tendency(s, rate, factors, top, bottom, left, right):
    cells_x, cells_y = s.shape
    x_of = lax.broadcasted_iota(jnp.int32, s.shape, 0)
    y_of = lax.broadcasted_iota(jnp.int32, s.shape, 1)
    out = (factors[5] - rate * factors[0]) * s
    out += factors[1] * jnp.where(x_of == 0, top, pltpu.roll(s, 1, 0))
    out += factors[2] * jnp.where(x_of == cells_x - 1, bottom, pltpu.roll(s, cells_x - 1, 0))
    out += factors[3] * jnp.where(y_of == 0, left, pltpu.roll(s, 1, 1))
    out += factors[4] * jnp.where(y_of == cells_y - 1, right, pltpu.roll(s, cells_y - 1, 1))
    return out


def columns_of(rows):
    spare = 8 - rows.shape[0]
    if spare:
        rows = jnp.concatenate([rows, jnp.zeros((spare, rows.shape[1]), rows.dtype)], axis=0)
    return rows.T


def line_count(nfield):
    return 2 * nfield + 8


def edge_kernel(mix_ref, state_tops, state_ends, state_lefts, state_rights, coefs_tops, coefs_ends,
                coefs_lefts, coefs_rights, land_tops, land_ends, land_lefts, land_rights,
                x_low, x_high, y_low, y_high):
    nfield = state_tops.shape[1]
    last_row, last_lane = state_tops.shape[2] - 1, state_lefts.shape[3] - 1
    atmos = mix_ref[0, 1] == 1.0

    def kept(land):
        return jnp.where(atmos, 1.0, land.astype(jnp.float32))

    for out, state, coefs, land, lines in (
        (x_low, state_tops, coefs_tops, land_tops, (0, 1)),
        (x_high, state_ends, coefs_ends, land_ends, (last_row - 1, last_row)),
    ):
        outer = lines[0] if lines[0] == 0 else lines[1]
        out[2 * nfield :, :] = jnp.zeros((8, out.shape[1]), jnp.float32)
        for j, line in enumerate(lines):
            for f in range(nfield):
                out[j * nfield + f : j * nfield + f + 1, :] = state[0, f, line : line + 1, :]
        for c in range(3):
            out[2 * nfield + c : 2 * nfield + c + 1, :] = coefs[0, c, outer : outer + 1, :]
        out[2 * nfield + 3 : 2 * nfield + 4, :] = kept(land[outer : outer + 1, :])

    for out, state, coefs, land, lines in (
        (y_low, state_lefts, coefs_lefts, land_lefts, (0, 1)),
        (y_high, state_rights, coefs_rights, land_rights, (last_lane - 1, last_lane)),
    ):
        outer = lines[0] if lines[0] == 0 else lines[1]
        lane = lax.broadcasted_iota(jnp.int32, land.shape, 1)
        packed = jnp.zeros(land.shape, jnp.float32)

        def put(packed, tile, at, to):
            moved = (to - at) % LANES
            tile = pltpu.roll(tile, moved, 1) if moved else tile
            return jnp.where(lane == to, tile, packed)

        for j, line in enumerate(lines):
            for f in range(nfield):
                packed = put(packed, state[0, f], line, j * nfield + f)
        for c in range(3):
            packed = put(packed, coefs[0, c], outer, 2 * nfield + c)
        packed = put(packed, kept(land[...]), outer, 2 * nfield + 3)
        out[...] = packed.T[: out.shape[0]]


def edges_of(state, coefs, land_sea, mix):
    _, nfield, cells_x, cells_y = state.shape
    lines = line_count(nfield)
    ends = [
        ((8, cells_y), (0, 0)),
        ((8, cells_y), (cells_x // 8 - 1, 0)),
        ((cells_x, LANES), (0, 0)),
        ((cells_x, LANES), (0, cells_y // LANES - 1)),
    ]
    at = lambda lead, place: lambda i: (0,) * len(lead) + place
    specs = [pl.BlockSpec(memory_space=pltpu.SMEM)]
    for lead in ((1, nfield), (1, 3), ()):
        specs += [pl.BlockSpec(lead + shape, at(lead, place)) for shape, place in ends]
    shapes = [(lines, cells_y)] * 2 + [(lines, cells_x)] * 2
    return pl.pallas_call(
        edge_kernel,
        grid=(1,),
        in_specs=specs,
        out_specs=[pl.BlockSpec(shape, lambda i: (0, 0)) for shape in shapes],
        out_shape=[jax.ShapeDtypeStruct(shape, jnp.float32) for shape in shapes],
        compiler_params=pltpu.CompilerParams(vmem_limit_bytes=24 * 1024 * 1024),
        cost_estimate=pl.CostEstimate(
            flops=state.size, bytes_accessed=4 * 1024 * 1024, transcendentals=0
        ),
        name="edges",
    )(mix, *pinned(pltpu.HBM, *[state] * 4), *[coefs] * 4, *[land_sea] * 4)


def outer_section(center, across, along, factors, rate):
    lane = lax.broadcasted_iota(jnp.int32, center.shape, 1)
    count = center.shape[1]
    before = jnp.where(lane == 0, along[0], pltpu.roll(center, 1, 1))
    after = jnp.where(lane == count - 1, along[1], pltpu.roll(center, count - 1, 1))
    keep, low, high, back, ahead, middle = factors
    out = center + low * across[0] + high * across[1] + back * before + ahead * after
    return out + (middle - rate * keep) * center


def base_kernel(half, rate_ref, mix_ref, rates_ref, coefs_ref, land_ref, x_low, x_high, y_low, y_high,
                above, below, left, right, corners_left, corners_right, state_ref,
                out_ref, early_ref, factors, rows, cols):
    f = pl.program_id(0)
    nfield = rates_ref.shape[0]
    lines = line_count(nfield)

    @pl.when(f == 0)
    def _():
        keep = jnp.where(mix_ref[0, 1] == 1.0, 1.0, land_ref[...].astype(jnp.float32))
        for i, factor in enumerate(stencil_factors([coefs_ref[0, c] for c in range(3)], keep)):
            factors[i] = factor
        rate = rates_ref[:, 0:1]
        near, far = pl.ds(0, nfield), pl.ds(nfield, nfield)
        last = corners_left.shape[1] - 1
        corner = (
            (corners_left[nfield : 2 * nfield, last:], corners_left[lines : lines + nfield, last:]),
            (corners_right[nfield : 2 * nfield, 0:1], corners_right[lines : lines + nfield, 0:1]),
        )
        for i, (ref, center, across, along, is_column) in enumerate(
            (
                (above, above[far, :], (above[near, :], x_low[near, :]), (corner[0][0], corner[1][0]), False),
                (below, below[near, :], (x_high[far, :], below[far, :]), (corner[0][1], corner[1][1]), False),
                (left, left[far, :], (left[near, :], y_low[near, :]), corner[0], True),
                (right, right[near, :], (y_high[far, :], right[far, :]), corner[1], True),
            )
        ):
            first = 2 * nfield
            of_line = stencil_factors(
                [ref[first + c : first + c + 1, :] for c in range(3)],
                ref[first + 3 : first + 4, :],
            )
            if is_column:
                of_line = [of_line[j] for j in (0, 3, 4, 1, 2, 5)]
            section = outer_section(center, across, along, of_line, rate)
            kept = cols if is_column else rows
            kept[pl.ds(i % 2 * nfield, nfield), :] = center
            kept[pl.ds((2 + i % 2) * nfield, nfield), :] = section

    mix_a, mix_b = mix_ref[0, 0], mix_ref[0, 1]
    for j in range(PER_STEP):
        field = f * PER_STEP + j
        rate = rate_ref[0, field]
        s = state_ref[0, j]
        row = [rows[pl.ds(i * nfield + field, 1), :] for i in range(4)]
        col = columns_of(
            jnp.concatenate([cols[pl.ds(i * nfield + field, 1), :] for i in range(4)], axis=0)
        )
        s1 = s + tendency(s, rate, factors, row[0], row[1], col[:, 0:1], col[:, 1:2])
        more = tendency(s1, rate, factors, row[2], row[3], col[:, 2:3], col[:, 3:4])
        total = mix_a * s + (1.0 - mix_a) * s1 + mix_b * more
        out_ref[0, j] = total

        @pl.when(field < half)
        def _():
            early_ref[j] = total


def base_of(state, coefs, land_sea, rates, mix, edges, received, corners, half):
    _, nfield, cells_x, cells_y = state.shape
    field = pl.BlockSpec((1, PER_STEP, cells_x, cells_y), lambda f: (0, f, 0, 0))
    early = pl.BlockSpec(
        (PER_STEP, cells_x, cells_y), lambda f: (jnp.minimum(f, half // PER_STEP - 1), 0, 0)
    )
    whole = lambda a: pl.BlockSpec(a.shape, lambda f: (0,) * a.ndim)
    rates_wide = jnp.broadcast_to(rates.T, (nfield, LANES))
    operands = [rates_wide, coefs, land_sea, *edges, *received, *corners]
    return pl.pallas_call(
        functools.partial(base_kernel, half),
        grid=(nfield // PER_STEP,),
        in_specs=[
            pl.BlockSpec(memory_space=pltpu.SMEM),
            pl.BlockSpec(memory_space=pltpu.SMEM),
            *[whole(a) for a in operands],
            field,
        ],
        out_specs=[
            field,
            early,
            pl.BlockSpec((6, cells_x, cells_y), lambda f: (0, 0, 0)),
        ],
        out_shape=[
            jax.ShapeDtypeStruct(state.shape, jnp.float32),
            jax.ShapeDtypeStruct((half, cells_x, cells_y), jnp.float32),
            jax.ShapeDtypeStruct((6, cells_x, cells_y), jnp.float32),
        ],
        scratch_shapes=[
            pltpu.VMEM((4 * nfield, cells_y), jnp.float32),
            pltpu.VMEM((4 * nfield, cells_x), jnp.float32),
        ],
        compiler_params=pltpu.CompilerParams(vmem_limit_bytes=24 * 1024 * 1024),
        cost_estimate=pl.CostEstimate(
            flops=40 * state.size, bytes_accessed=8 * state.size, transcendentals=0
        ),
        name="base",
    )(rates, mix, *operands, *pinned(pltpu.HBM, state))


def finish_kernel(first, with_x, rates_ref, mix_ref, above, below, before, after, factors, recv,
                  left, right, *rest):
    tops, rest = (rest[:2], rest[2:]) if with_x else (None, rest)
    late, rest = (rest[:2], rest[2:]) if with_x else (None, rest)
    early_base, rest = (rest[0], rest[1:]) if with_x else (None, rest)
    odd_ref, base_ref, rest = rest[0], rest[1], rest[2:]
    new_ref, out_ref, done_ref = rest[-11:-8]
    base, wide, lines, sides, outer, base_sems, out_sems, outer_sems = rest[-8:]
    count, cells_x, cells_y = base.shape
    mix_b = jnp.broadcast_to(mix_ref[1:2, 0:1], (STRIP, cells_y))
    keep_row = above.shape[0] - 5
    keep = slice(keep_row, keep_row + 1)
    ends = (0, cells_x - STRIP)

    def base_copy(f):
        return pltpu.make_async_copy(base_ref.at[0, first + f], base.at[f], base_sems.at[f])

    def out_copies(f):
        return (
            pltpu.make_async_copy(recv.at[f], out_ref.at[0, first + f], out_sems.at[0, f]),
            pltpu.make_async_copy(base.at[f], new_ref.at[0, first + f], out_sems.at[1, f]),
        )

    def outer_copy(f, i, back):
        there = (new_ref if back else base_ref).at[0, count + f, pl.ds(ends[i], STRIP), :]
        here = outer.at[f, i]
        pair = (here, there) if back else (there, here)
        return pltpu.make_async_copy(*pair, outer_sems.at[f, i])

    outer_rows = [(f, i) for f in range(count) for i in range(2)] if with_x else []
    if not with_x:
        for f in range(count):
            base_copy(f).start()
    for f, i in outer_rows:
        outer_copy(f, i, False).start()
    done_ref[...] = jnp.zeros_like(done_ref)
    def in_order(i, pair):
        in_odd, in_even = pair[0][...], pair[1][...]
        odd = jnp.broadcast_to(odd_ref[i : i + 1, 0:1], in_odd.shape) == 1.0
        return jnp.where(odd, in_even, in_odd), jnp.where(odd, in_odd, in_even)

    if with_x:
        top, bottom = in_order(0, tops)
        lines[:count, :] = top * above[keep, :]
        lines[count:, :] = bottom * below[keep, :]
        late = in_order(0, late)
    else:
        lines[...] = jnp.zeros_like(lines)
    left, right = in_order(1, (left, right))
    sides[:count, :] = left * before[keep, :]
    sides[count:, :] = right * after[keep, :]
    lane = lax.broadcasted_iota(jnp.int32, (STRIP, cells_y), 1)

    def one_field(f, carry):
        rate = jnp.broadcast_to(rates_ref[pl.ds(first + f, 1), 0:1], (STRIP, cells_y))
        line_rate, side_rate = rate[:1], rate[:1, :cells_x]
        both = [sides[pl.ds(f, 1), :] * side_rate, sides[pl.ds(count + f, 1), :] * side_rate]
        cols = columns_of(jnp.concatenate(both, axis=0))
        wide[STRIP - 1 : STRIP, :] = lines[pl.ds(f, 1), :] * line_rate
        wide[STRIP + cells_x : STRIP + cells_x + 1, :] = lines[pl.ds(count + f, 1), :] * line_rate
        to_out, to_new = out_copies(f)
        to_out.start()
        for i in range(0, cells_x, STRIP):
            rows = slice(i, i + STRIP)
            wide[STRIP + i : 2 * STRIP + i, :] = factors[0, rows, :] * recv[f, rows, :] * rate
        if not with_x:
            base_copy(f).wait()
        start = early_base if with_x else base
        for i in range(0, cells_x, STRIP):
            rows = slice(i, i + STRIP)
            mid = wide[STRIP + i : 2 * STRIP + i, :]
            more = (factors[5, rows, :] - rate * factors[0, rows, :]) * mid
            more += factors[1, rows, :] * wide[STRIP + i - 1 : 2 * STRIP + i - 1, :]
            more += factors[2, rows, :] * wide[STRIP + i + 1 : 2 * STRIP + i + 1, :]
            prior = jnp.where(lane == 0, cols[rows, 0:1], pltpu.roll(mid, 1, 1))
            later = jnp.where(lane == cells_y - 1, cols[rows, 1:2], pltpu.roll(mid, cells_y - 1, 1))
            more += factors[3, rows, :] * prior + factors[4, rows, :] * later
            base[f, rows, :] = start[f, rows, :] + mix_b * (2.0 * mid + more)
        to_new.start()
        return carry

    def add_lines():
        for f, i in outer_rows:
            outer_copy(f, i, False).wait()
            row = i * (STRIP - 1)
            at = ends[i] + row
            rate = jnp.broadcast_to(rates_ref[count + f : count + f + 1, 0:1], (1, cells_y))
            line = late[i][f : f + 1, :] * (above, below)[i][keep, :] * rate
            more = mix_b[:1] * factors[1 + i, at : at + 1, :] * line
            outer[f, i, row : row + 1, :] = outer[f, i, row : row + 1, :] + more
            outer_copy(f, i, True).start()

    lax.fori_loop(0, count - 1, one_field, 0)
    add_lines()
    one_field(count - 1, 0)
    for f in range(count):
        for copy in out_copies(f):
            copy.wait()
    for f, i in outer_rows:
        outer_copy(f, i, True).wait()


def finished(
    first, new_state, remapped, recv, odd, x_rims, y_rims, closing, rates, mix, factors, received
):
    count, cells_x, cells_y = recv.shape
    chan = 2 * count
    with_x = x_rims is not None
    anywhere = pl.BlockSpec(memory_space=pl.ANY)
    operands = [rates, mix, *received, factors, recv, *y_rims]
    if with_x:
        late_rims, base_early, late_done = closing
        operands += [*x_rims, *late_rims, base_early]
    operands.append(odd)
    specs = [pl.BlockSpec(memory_space=pltpu.VMEM)] * len(operands) + [anywhere]
    aliases = {len(operands): 0}
    operands.append(new_state)
    if remapped is not None:
        aliases[len(operands)] = 1
        operands += [remapped, late_done]
        specs += [anywhere, anywhere]
    return pl.pallas_call(
        functools.partial(finish_kernel, first, with_x),
        in_specs=specs,
        out_specs=[anywhere, anywhere, pl.BlockSpec(memory_space=pltpu.VMEM)],
        out_shape=[
            jax.ShapeDtypeStruct(new_state.shape, jnp.float32),
            jax.ShapeDtypeStruct((1, chan, cells_x, cells_y), jnp.float32),
            jax.ShapeDtypeStruct((8, LANES), jnp.float32),
        ],
        input_output_aliases=aliases,
        scratch_shapes=[
            pltpu.VMEM((count, cells_x, cells_y), jnp.float32),
            pltpu.VMEM((cells_x + 2 * STRIP, cells_y), jnp.float32),
            pltpu.VMEM((2 * count, cells_y), jnp.float32),
            pltpu.VMEM((2 * count, cells_x), jnp.float32),
            pltpu.VMEM((count, 2, STRIP, cells_y), jnp.float32),
            pltpu.SemaphoreType.DMA((count,)),
            pltpu.SemaphoreType.DMA((2, count)),
            pltpu.SemaphoreType.DMA((count, 2)),
        ],
        compiler_params=pltpu.CompilerParams(vmem_limit_bytes=12 * 1024 * 1024),
        cost_estimate=pl.CostEstimate(
            flops=20 * recv.size, bytes_accessed=20 * recv.size, transcendentals=0
        ),
        name="finish",
    )(*operands)


def body(state, coefs, land_sea, gamma, pair_src, pair_dev, pair_blk, weights):
    tx, ty = lax.axis_size("tx"), lax.axis_size("ty")
    tiles = tx * ty
    nfield, cells_x, cells_y = state.shape[1:]
    chan = gamma.shape[1]
    pairs, width = weights.shape[1], weights.shape[2]
    capacity = max(2, 2 * pairs // tiles)
    half = chan // 2
    early, late = contributions(
        state, pair_src, pair_dev, pair_blk, weights, tiles, capacity, chan
    )
    swap = [(0, 1), (1, 0)]

    def exchanged(rows):
        rows = rows.reshape(tiles, -1, half, width)
        return lax.all_to_all(rows, ("tx", "ty"), split_axis=0, concat_axis=0, tiled=True)

    def add_up(odd, ids, rows):
        return summed(odd, ids, rows, tiles, capacity, half, cells_x, cells_y, width)

    late_in = exchanged(late)
    early = lax.ppermute(early, "comp", swap)
    early_in = placed_rows(early, tiles, capacity, pairs, cells_x * cells_y // width)

    land_after, _ = lax.optimization_barrier((land_sea, late))
    is_atmos = lax.axis_index("comp") == 0
    mix = jnp.where(is_atmos, jnp.array([[0.0, 1.0]]), jnp.array([[0.5, 0.5]]))
    mix = mix.astype(jnp.float32)
    rates = jnp.concatenate([gamma, jnp.zeros((1, nfield - chan), jnp.float32)], axis=1)
    x_low, x_high, y_low, y_high = edges_of(state, coefs, land_after, mix)
    left = lax.ppermute(y_high, "ty", shift_pairs(ty, 1))
    right = lax.ppermute(y_low, "ty", shift_pairs(ty, -1))
    above = lax.ppermute(x_high, "tx", shift_pairs(tx, 1))
    below = lax.ppermute(x_low, "tx", shift_pairs(tx, -1))
    early_in, above, below, left, right = lax.optimization_barrier(
        (early_in, above, below, left, right)
    )
    received = (above, below, left, right)
    early_in = exchanged(early_in)

    ends = jnp.concatenate([above[:, cells_y - LANES :], below[:, cells_y - LANES :]], axis=0)
    starts = jnp.concatenate([above[:, :LANES], below[:, :LANES]], axis=0)
    corners_left = lax.ppermute(ends, "ty", shift_pairs(ty, 1))
    corners_right = lax.ppermute(starts, "ty", shift_pairs(ty, -1))
    base, base_early, factors = base_of(
        state, coefs, land_after, rates, mix, (x_low, x_high, y_low, y_high), received,
        (corners_left, corners_right), half,
    )

    ids_late = late_in[:, capacity, 0, :]
    ids_early = lax.ppermute(ids_late, "comp", swap)
    odd = jnp.stack([lax.axis_index("tx"), lax.axis_index("ty")]).astype(jnp.int32)[None] & 1
    odd_lanes = jnp.broadcast_to(odd.T.astype(jnp.float32), (2, LANES))
    recv_late, x_odd, x_even, y_odd, y_even = add_up(odd_lanes, ids_late, late_in)
    recv_late = lax.ppermute(recv_late, "comp", swap)
    late_x = (
        lax.ppermute(x_odd, ("comp", "tx"), crossed("tx", 1)),
        lax.ppermute(x_even, ("comp", "tx"), crossed("tx", 0)),
    )
    late_y = (
        lax.ppermute(y_odd, ("comp", "ty"), crossed("ty", 1)),
        lax.ppermute(y_even, ("comp", "ty"), crossed("ty", 0)),
    )
    lanes = lambda a: jnp.broadcast_to(a.T, (a.shape[1], LANES))
    rest = (lanes(rates), lanes(mix), factors, received)
    new_state, remapped, done = finished(
        half, base, None, recv_late, odd_lanes, None, late_y, None, *rest
    )
    early_in, done = lax.optimization_barrier((early_in, done))
    recv_early, x_odd, x_even, y_odd, y_even = add_up(odd_lanes, ids_early, early_in)
    early_x = (
        lax.ppermute(x_odd, "tx", neighbour_pairs(tx, 1)),
        lax.ppermute(x_even, "tx", neighbour_pairs(tx, 0)),
    )
    early_y = (
        lax.ppermute(y_odd, "ty", neighbour_pairs(ty, 1)),
        lax.ppermute(y_even, "ty", neighbour_pairs(ty, 0)),
    )
    new_state, remapped, _ = finished(
        0, new_state, remapped, recv_early, odd_lanes, early_x, early_y, (late_x, base_early, done), *rest
    )
    return new_state, remapped


def solution(mesh):
    placed = (
        P("comp", None, "tx", "ty"),
        P("comp", None, "tx", "ty"),
        P("tx", "ty"),
        P("comp", None),
        P("comp", ("tx", "ty")),
        P("comp", ("tx", "ty"), None),
        P("comp", ("tx", "ty")),
        P("comp", ("tx", "ty"), None, None),
    )
    return jax.shard_map(
        body,
        mesh=mesh,
        in_specs=placed,
        out_specs=(P("comp", None, "tx", "ty"), P("comp", None, "tx", "ty")),
        check_vma=False,
    )
```

```python
import functools

import jax
import jax.numpy as jnp
from jax import lax
from jax.experimental import pallas as pl
from jax.experimental.pallas import tpu as pltpu
from jax.sharding import PartitionSpec as P

LANES = 128
STEP_PAIRS = 64
STRIP = 8
PER_STEP = 2
NT = (((1,), (1,)), ((), ()))


def pinned(space, *arrays):
    return [pltpu.with_memory_space_constraint(a, space) for a in arrays]


def shift_pairs(count, by):
    return [(i, i + by) for i in range(count) if 0 <= i + by < count]


def neighbour_pairs(count, first):
    lows = range(first, count - 1, 2)
    return [(i, i + 1) for i in lows] + [(i + 1, i) for i in lows]


def crossed(axis, first):
    count = lax.axis_size(axis)
    pairs = neighbour_pairs(count, first)
    return [(c * count + i, (1 - c) * count + j) for c in range(2) for i, j in pairs]


def split(value, parts):
    if parts & (parts - 1) == 0:
        return lax.shift_right_logical(value, parts.bit_length() - 1), value & (parts - 1)
    return lax.div(value, parts), lax.rem(value, parts)


def ranks(dev, tiles):
    pairs = dev.shape[1]
    tile_of = lax.broadcasted_iota(jnp.int32, (tiles, pairs), 0)
    lane_of = lax.broadcasted_iota(jnp.int32, (tiles, pairs), 1)
    member = (tile_of == dev).astype(jnp.float32)
    total = member
    shift = 1
    while shift < pairs:
        total = total + jnp.where(lane_of >= shift, pltpu.roll(total, shift, 1), 0.0)
        shift *= 2
    return member, (jnp.sum(member * total, axis=0, keepdims=True) - 1.0).astype(jnp.int32)


def slot_blocks(dev, blk, tiles, capacity):
    member, rank = ranks(dev, tiles)
    pairs = dev.shape[1]
    slot_of = lax.broadcasted_iota(jnp.int32, (LANES, pairs), 0) % capacity
    chosen = (slot_of == rank).astype(jnp.bfloat16)

    def spread(values):
        return lax.dot_general(
            (member * values).astype(jnp.bfloat16), chosen, NT, preferred_element_type=jnp.float32
        )

    high, low = split(blk, 256)
    ids = spread(high.astype(jnp.float32)) * 256.0 + spread(low.astype(jnp.float32))
    return jnp.where(spread(jnp.ones(dev.shape, jnp.float32)) > 0.5, ids, -1.0)


def contribution_kernel(
    dims, src_ref, dev_ref, blk_ref, state_ref, weights_ref, early_ref, late_ref,
    cells, w_ref, pair_v, pair_s, taken, field_sems, weight_sems, pair_sems,
):
    tiles, capacity, pairs, fields, cells_x, cells_y, width = dims
    half = fields // 2
    parts = cells_y // width
    steps = pairs // STEP_PAIRS

    scalar_copies = [
        pltpu.make_async_copy(ref, pair_s.at[pl.ds(i, 1), :], pair_sems.at[i])
        for i, ref in enumerate((src_ref, dev_ref))
    ]
    vector_copies = [
        pltpu.make_async_copy(ref, pair_v.at[i], pair_sems.at[2 + i])
        for i, ref in enumerate((dev_ref, blk_ref))
    ]
    field_copies = [
        pltpu.make_async_copy(
            state_ref.at[0, f, :, pl.ds(q * width, width)],
            cells.at[q, :, f, :],
            field_sems.at[f * parts + q],
        )
        for f in range(fields)
        for q in range(parts)
    ]

    def weight_copy(step):
        some = pl.ds(step * STEP_PAIRS, STEP_PAIRS)
        return pltpu.make_async_copy(
            weights_ref.at[0, some], w_ref.at[some], weight_sems.at[step]
        )

    for copy in scalar_copies + vector_copies + field_copies:
        copy.start()
    for step in range(steps):
        weight_copy(step).start()
    late_ref[...] = jnp.zeros_like(late_ref)
    for t in range(tiles):
        taken[t] = t * (capacity + 1)

    for copy in vector_copies:
        copy.wait()
    dev, blk = pair_v[0], pair_v[1]
    ids = slot_blocks(dev, blk, tiles, capacity)
    for t in range(tiles):
        row = jnp.broadcast_to(ids[t : t + 1, :], late_ref.shape[1:])
        late_ref[t * (capacity + 1) + capacity] = row
    code = (dev * (cells_x * parts) + blk).astype(jnp.float32)
    for i in range(pairs // width):
        place = (pairs + i // half, slice(i % half, i % half + 1), slice(None))
        early_ref[place] = code[:, i * width : (i + 1) * width]
    for copy in scalar_copies + field_copies:
        copy.wait()

    def cells_of(p):
        x, part = split(pair_s[0, p], parts)
        return cells[part, x]

    zeros = jnp.zeros((fields, width), jnp.float32)

    def some_pairs(step, carry):
        weight_copy(step).wait()
        for i in range(0, STEP_PAIRS, 4):
            p = step * STEP_PAIRS + i
            left = [
                jnp.concatenate([cells_of(p + j), zeros][:: 1 - j % 2 * 2], axis=1) for j in range(4)
            ]
            left = jnp.concatenate(left, axis=0).astype(jnp.bfloat16)
            w = [w_ref[p + j] for j in range(4)]
            right = jnp.concatenate(
                [jnp.concatenate(w[:2], axis=1), jnp.concatenate(w[2:], axis=1)], axis=0
            )
            four = lax.dot_general(left, right, NT, preferred_element_type=jnp.float32)
            for j in range(4):
                tile = pair_s[1, p + j]
                slot = taken[tile]
                taken[tile] = slot + 1
                at = j // 2 * width
                one = four[j * fields : (j + 1) * fields, at : at + width]
                early_ref[p + j] = one[:half]
                late_ref[slot] = one[half:]
        return carry

    lax.fori_loop(0, steps, some_pairs, 0)


def contributions(state, pair_src, pair_dev, pair_blk, weights, tiles, capacity, fields):
    _, _, cells_x, cells_y = state.shape
    half = fields // 2
    pairs, width = weights.shape[1], weights.shape[2]
    rows = tiles * (capacity + 1)
    dims = (tiles, capacity, pairs, fields, cells_x, cells_y, width)
    parts = cells_y // width
    shapes = [(pairs + -(-pairs // (half * width)), half, width), (rows, half, width)]
    return pl.pallas_call(
        functools.partial(contribution_kernel, dims),
        in_specs=[pl.BlockSpec(memory_space=pltpu.HBM)] * 5,
        out_specs=[pl.BlockSpec(memory_space=pltpu.VMEM) for _ in shapes],
        out_shape=[jax.ShapeDtypeStruct(shape, jnp.float32) for shape in shapes],
        scratch_shapes=[
            pltpu.VMEM((parts, cells_x, fields, width), jnp.float32),
            pltpu.VMEM((pairs, width, width), jnp.bfloat16),
            pltpu.VMEM((2, 1, pairs), jnp.int32),
            pltpu.SMEM((2, pairs), jnp.int32),
            pltpu.SMEM((tiles,), jnp.int32),
            pltpu.SemaphoreType.DMA((parts * fields,)),
            pltpu.SemaphoreType.DMA((pairs // STEP_PAIRS,)),
            pltpu.SemaphoreType.DMA((4,)),
        ],
        compiler_params=pltpu.CompilerParams(vmem_limit_bytes=40 * 1024 * 1024),
        cost_estimate=pl.CostEstimate(
            flops=2 * pairs * fields * width * width,
            bytes_accessed=2 * pairs * width * width + 8 * rows * fields * width,
            transcendentals=0,
        ),
        name="contributions",
    )(*pinned(pltpu.HBM, pair_src, pair_dev.reshape(1, pairs), pair_blk, state, weights))


def place_kernel(dims, in_ref, out_ref, place_v, place_s, place_sem):
    tiles, capacity, pairs, blocks = dims
    half, width = in_ref.shape[1:]
    code = jnp.concatenate(
        [in_ref[pairs + i // half][i % half : i % half + 1] for i in range(pairs // width)], axis=1
    ).astype(jnp.int32)
    dev, _ = split(code, blocks)
    rank = ranks(dev, tiles)[1]
    place_v[...] = jnp.broadcast_to(dev * capacity + rank, place_v.shape)
    copy = pltpu.make_async_copy(place_v, place_s, place_sem)
    copy.start()
    out_ref[...] = jnp.zeros_like(out_ref)
    copy.wait()

    def some_rows(step, carry):
        for i in range(STEP_PAIRS):
            p = step * STEP_PAIRS + i
            out_ref[place_s[0, p]] = in_ref[p]
        return carry

    lax.fori_loop(0, pairs // STEP_PAIRS, some_rows, 0)


def placed_rows(rows, tiles, capacity, pairs, blocks):
    half, width = rows.shape[1:]
    shape = (tiles * capacity, half, width)
    return pl.pallas_call(
        functools.partial(place_kernel, (tiles, capacity, pairs, blocks)),
        out_shape=jax.ShapeDtypeStruct(shape, jnp.float32),
        scratch_shapes=[
            pltpu.VMEM((8, pairs), jnp.int32),
            pltpu.SMEM((8, pairs), jnp.int32),
            pltpu.SemaphoreType.DMA,
        ],
        compiler_params=pltpu.CompilerParams(vmem_limit_bytes=10 * 1024 * 1024),
        cost_estimate=pl.CostEstimate(
            flops=4 * rows.size, bytes_accessed=12 * rows.size, transcendentals=0
        ),
        name="place_in_slots",
    )(rows)


def sum_kernel(dims, odd_ref, ids_ref, rows_ref, out_ref, x0_ref, x1_ref, y0_ref, y1_ref,
               pick, high, low, in_ref, row_sems):
    tiles, capacity, fields, cells_x, cells_y, width = dims
    parts = cells_y // width
    group = LANES // capacity
    stride = rows_ref.shape[0] // tiles

    def rows_copy(k):
        some = pl.ds(k * group * stride, group * stride)
        return pltpu.make_async_copy(rows_ref.at[some, :], in_ref.at[some, :], row_sems.at[k])

    for k in range(tiles // group):
        rows_copy(k).start()
    block_of = lax.broadcasted_iota(jnp.int32, (cells_x * parts, LANES), 0)
    block_of = (block_of % cells_x) * parts + block_of // cells_x
    block_of = block_of.astype(jnp.float32)
    lane = lax.broadcasted_iota(jnp.int32, (1, LANES), 1)
    for k in range(tiles // group):
        ids = None
        for i in range(group):
            row = ids_ref[pl.ds(k * group + i, 1), :]
            ids = row if ids is None else jnp.where(lane // capacity == i, row, ids)
        pick[:, pl.ds(k * LANES, LANES)] = (block_of == ids).astype(jnp.bfloat16)
    for k in range(tiles // group):
        rows_copy(k).wait()
        for source in range(k * group, (k + 1) * group):
            for f in range(fields):
                x = in_ref[pl.ds(source * stride + f, capacity, stride=fields), :]
                rounded = x.astype(jnp.bfloat16)
                place = (
                    pl.ds(source * capacity, capacity),
                    pl.ds(f * width, width),
                )
                high[place] = rounded
                low[place] = (x - rounded.astype(jnp.float32)).astype(jnp.bfloat16)

    def in_order(i, low_rim, high_rim):
        odd = odd_ref[i : i + 1, :] == 1.0
        return jnp.where(odd, high_rim, low_rim), jnp.where(odd, low_rim, high_rim)

    columns = {}
    column_of = lax.broadcasted_iota(jnp.int32, (cells_x, width), 1)
    for q in range(parts):
        chosen = pick[pl.ds(q * cells_x, cells_x), :]
        total = jnp.dot(chosen, high[...], preferred_element_type=jnp.float32)
        total = total + jnp.dot(chosen, low[...], preferred_element_type=jnp.float32)
        for f in range(fields):
            tile = total[:, f * width : (f + 1) * width]
            out_ref[f, :, pl.ds(q * width, width)] = tile
            rims = in_order(0, tile[:1], tile[cells_x - 1 :])
            for rim_ref, rim in zip((x0_ref, x1_ref), rims):
                rim_ref[pl.ds(f, 1), pl.ds(q * width, width)] = rim
            for edge, at in ((0, 0), (parts - 1, width - 1)):
                if q == edge:
                    moved = (f - at) % width
                    tile = pltpu.roll(tile, moved, 1) if moved else tile
                    columns[at] = jnp.where(column_of == f, tile, columns.get(at, 0.0))
    low_rims, high_rims = (columns[at].T[:fields] for at in (0, width - 1))
    y0_ref[...], y1_ref[...] = in_order(1, low_rims, high_rims)


def summed(odd, ids, rows, tiles, capacity, fields, cells_x, cells_y, width):
    dims = (tiles, capacity, fields, cells_x, cells_y, width)
    rows = rows.reshape(-1, width)
    slots = tiles * capacity
    blocks = cells_x * cells_y // width
    shapes = [
        (fields, cells_x, cells_y),
        (fields, cells_y),
        (fields, cells_y),
        (fields, cells_x),
        (fields, cells_x),
    ]
    return pl.pallas_call(
        functools.partial(sum_kernel, dims),
        in_specs=[pl.BlockSpec(memory_space=pltpu.VMEM)] * 2
        + [pl.BlockSpec(memory_space=pltpu.HBM)],
        out_shape=[jax.ShapeDtypeStruct(shape, jnp.float32) for shape in shapes],
        scratch_shapes=[
            pltpu.VMEM((blocks, slots), jnp.bfloat16),
            pltpu.VMEM((slots, fields * width), jnp.bfloat16),
            pltpu.VMEM((slots, fields * width), jnp.bfloat16),
            pltpu.VMEM((rows.shape[0] + 8, width), jnp.float32),
            pltpu.SemaphoreType.DMA((tiles * capacity // LANES,)),
        ],
        compiler_params=pltpu.CompilerParams(vmem_limit_bytes=24 * 1024 * 1024),
        cost_estimate=pl.CostEstimate(
            flops=4 * blocks * slots * fields * width,
            bytes_accessed=4 * fields * width * (slots + blocks),
            transcendentals=0,
        ),
        name="sum_by_block",
    )(odd, ids, *pinned(pltpu.HBM, rows))


def stencil_factors(coefs, keep):
    u, v, kappa = coefs
    return [
        keep,
        keep * (jnp.maximum(u, 0.0) + kappa),
        keep * (kappa - jnp.minimum(u, 0.0)),
        keep * (jnp.maximum(v, 0.0) + kappa),
        keep * (kappa - jnp.minimum(v, 0.0)),
        -keep * (jnp.abs(u) + jnp.abs(v) + 4.0 * kappa),
    ]


def tendency(s, rate, factors, top, bottom, left, right):
    cells_x, cells_y = s.shape
    x_of = lax.broadcasted_iota(jnp.int32, s.shape, 0)
    y_of = lax.broadcasted_iota(jnp.int32, s.shape, 1)
    out = (factors[5] - rate * factors[0]) * s
    out += factors[1] * jnp.where(x_of == 0, top, pltpu.roll(s, 1, 0))
    out += factors[2] * jnp.where(x_of == cells_x - 1, bottom, pltpu.roll(s, cells_x - 1, 0))
    out += factors[3] * jnp.where(y_of == 0, left, pltpu.roll(s, 1, 1))
    out += factors[4] * jnp.where(y_of == cells_y - 1, right, pltpu.roll(s, cells_y - 1, 1))
    return out


def columns_of(rows):
    spare = 8 - rows.shape[0]
    if spare:
        rows = jnp.concatenate([rows, jnp.zeros((spare, rows.shape[1]), rows.dtype)], axis=0)
    return rows.T


def line_count(nfield):
    return 2 * nfield + 8


def edge_kernel(mix_ref, state_tops, state_ends, state_lefts, state_rights, coefs_tops, coefs_ends,
                coefs_lefts, coefs_rights, land_tops, land_ends, land_lefts, land_rights,
                x_low, x_high, y_low, y_high):
    nfield = state_tops.shape[1]
    last_row, last_lane = state_tops.shape[2] - 1, state_lefts.shape[3] - 1
    atmos = mix_ref[0, 1] == 1.0

    def kept(land):
        return jnp.where(atmos, 1.0, land.astype(jnp.float32))

    for out, state, coefs, land, lines in (
        (x_low, state_tops, coefs_tops, land_tops, (0, 1)),
        (x_high, state_ends, coefs_ends, land_ends, (last_row - 1, last_row)),
    ):
        outer = lines[0] if lines[0] == 0 else lines[1]
        out[2 * nfield :, :] = jnp.zeros((8, out.shape[1]), jnp.float32)
        for j, line in enumerate(lines):
            for f in range(nfield):
                out[j * nfield + f : j * nfield + f + 1, :] = state[0, f, line : line + 1, :]
        for c in range(3):
            out[2 * nfield + c : 2 * nfield + c + 1, :] = coefs[0, c, outer : outer + 1, :]
        out[2 * nfield + 3 : 2 * nfield + 4, :] = kept(land[outer : outer + 1, :])

    for out, state, coefs, land, lines in (
        (y_low, state_lefts, coefs_lefts, land_lefts, (0, 1)),
        (y_high, state_rights, coefs_rights, land_rights, (last_lane - 1, last_lane)),
    ):
        outer = lines[0] if lines[0] == 0 else lines[1]
        lane = lax.broadcasted_iota(jnp.int32, land.shape, 1)
        packed = jnp.zeros(land.shape, jnp.float32)

        def put(packed, tile, at, to):
            moved = (to - at) % LANES
            tile = pltpu.roll(tile, moved, 1) if moved else tile
            return jnp.where(lane == to, tile, packed)

        for j, line in enumerate(lines):
            for f in range(nfield):
                packed = put(packed, state[0, f], line, j * nfield + f)
        for c in range(3):
            packed = put(packed, coefs[0, c], outer, 2 * nfield + c)
        packed = put(packed, kept(land[...]), outer, 2 * nfield + 3)
        out[...] = packed.T[: out.shape[0]]


def edges_of(state, coefs, land_sea, mix):
    _, nfield, cells_x, cells_y = state.shape
    lines = line_count(nfield)
    ends = [
        ((8, cells_y), (0, 0)),
        ((8, cells_y), (cells_x // 8 - 1, 0)),
        ((cells_x, LANES), (0, 0)),
        ((cells_x, LANES), (0, cells_y // LANES - 1)),
    ]
    at = lambda lead, place: lambda i: (0,) * len(lead) + place
    specs = [pl.BlockSpec(memory_space=pltpu.SMEM)]
    for lead in ((1, nfield), (1, 3), ()):
        specs += [pl.BlockSpec(lead + shape, at(lead, place)) for shape, place in ends]
    shapes = [(lines, cells_y)] * 2 + [(lines, cells_x)] * 2
    return pl.pallas_call(
        edge_kernel,
        grid=(1,),
        in_specs=specs,
        out_specs=[pl.BlockSpec(shape, lambda i: (0, 0)) for shape in shapes],
        out_shape=[jax.ShapeDtypeStruct(shape, jnp.float32) for shape in shapes],
        compiler_params=pltpu.CompilerParams(vmem_limit_bytes=24 * 1024 * 1024),
        cost_estimate=pl.CostEstimate(
            flops=state.size, bytes_accessed=4 * 1024 * 1024, transcendentals=0
        ),
        name="edges",
    )(mix, *pinned(pltpu.HBM, *[state] * 4), *[coefs] * 4, *[land_sea] * 4)


def outer_section(center, across, along, factors, rate):
    lane = lax.broadcasted_iota(jnp.int32, center.shape, 1)
    count = center.shape[1]
    before = jnp.where(lane == 0, along[0], pltpu.roll(center, 1, 1))
    after = jnp.where(lane == count - 1, along[1], pltpu.roll(center, count - 1, 1))
    keep, low, high, back, ahead, middle = factors
    out = center + low * across[0] + high * across[1] + back * before + ahead * after
    return out + (middle - rate * keep) * center


def base_kernel(half, rate_ref, mix_ref, rates_ref, coefs_ref, land_ref, x_low, x_high, y_low, y_high,
                above, below, left, right, corners_left, corners_right, state_ref,
                out_ref, early_ref, factors, rows, cols):
    f = pl.program_id(0)
    nfield = rates_ref.shape[0]
    lines = line_count(nfield)

    @pl.when(f == 0)
    def _():
        keep = jnp.where(mix_ref[0, 1] == 1.0, 1.0, land_ref[...].astype(jnp.float32))
        for i, factor in enumerate(stencil_factors([coefs_ref[0, c] for c in range(3)], keep)):
            factors[i] = factor
        rate = rates_ref[:, 0:1]
        near, far = pl.ds(0, nfield), pl.ds(nfield, nfield)
        last = corners_left.shape[1] - 1
        corner = (
            (corners_left[nfield : 2 * nfield, last:], corners_left[lines : lines + nfield, last:]),
            (corners_right[nfield : 2 * nfield, 0:1], corners_right[lines : lines + nfield, 0:1]),
        )
        for i, (ref, center, across, along, is_column) in enumerate(
            (
                (above, above[far, :], (above[near, :], x_low[near, :]), (corner[0][0], corner[1][0]), False),
                (below, below[near, :], (x_high[far, :], below[far, :]), (corner[0][1], corner[1][1]), False),
                (left, left[far, :], (left[near, :], y_low[near, :]), corner[0], True),
                (right, right[near, :], (y_high[far, :], right[far, :]), corner[1], True),
            )
        ):
            first = 2 * nfield
            of_line = stencil_factors(
                [ref[first + c : first + c + 1, :] for c in range(3)],
                ref[first + 3 : first + 4, :],
            )
            if is_column:
                of_line = [of_line[j] for j in (0, 3, 4, 1, 2, 5)]
            section = outer_section(center, across, along, of_line, rate)
            kept = cols if is_column else rows
            kept[pl.ds(i % 2 * nfield, nfield), :] = center
            kept[pl.ds((2 + i % 2) * nfield, nfield), :] = section

    mix_a, mix_b = mix_ref[0, 0], mix_ref[0, 1]
    for j in range(PER_STEP):
        field = f * PER_STEP + j
        rate = rate_ref[0, field]
        s = state_ref[0, j]
        row = [rows[pl.ds(i * nfield + field, 1), :] for i in range(4)]
        col = columns_of(
            jnp.concatenate([cols[pl.ds(i * nfield + field, 1), :] for i in range(4)], axis=0)
        )
        s1 = s + tendency(s, rate, factors, row[0], row[1], col[:, 0:1], col[:, 1:2])
        more = tendency(s1, rate, factors, row[2], row[3], col[:, 2:3], col[:, 3:4])
        total = mix_a * s + (1.0 - mix_a) * s1 + mix_b * more
        out_ref[0, j] = total

        @pl.when(field < half)
        def _():
            early_ref[j] = total


def base_of(state, coefs, land_sea, rates, mix, edges, received, corners, half):
    _, nfield, cells_x, cells_y = state.shape
    field = pl.BlockSpec((1, PER_STEP, cells_x, cells_y), lambda f: (0, f, 0, 0))
    early = pl.BlockSpec(
        (PER_STEP, cells_x, cells_y), lambda f: (jnp.minimum(f, half // PER_STEP - 1), 0, 0)
    )
    whole = lambda a: pl.BlockSpec(a.shape, lambda f: (0,) * a.ndim)
    rates_wide = jnp.broadcast_to(rates.T, (nfield, LANES))
    operands = [rates_wide, coefs, land_sea, *edges, *received, *corners]
    return pl.pallas_call(
        functools.partial(base_kernel, half),
        grid=(nfield // PER_STEP,),
        in_specs=[
            pl.BlockSpec(memory_space=pltpu.SMEM),
            pl.BlockSpec(memory_space=pltpu.SMEM),
            *[whole(a) for a in operands],
            field,
        ],
        out_specs=[
            field,
            early,
            pl.BlockSpec((6, cells_x, cells_y), lambda f: (0, 0, 0)),
        ],
        out_shape=[
            jax.ShapeDtypeStruct(state.shape, jnp.float32),
            jax.ShapeDtypeStruct((half, cells_x, cells_y), jnp.float32),
            jax.ShapeDtypeStruct((6, cells_x, cells_y), jnp.float32),
        ],
        scratch_shapes=[
            pltpu.VMEM((4 * nfield, cells_y), jnp.float32),
            pltpu.VMEM((4 * nfield, cells_x), jnp.float32),
        ],
        compiler_params=pltpu.CompilerParams(vmem_limit_bytes=24 * 1024 * 1024),
        cost_estimate=pl.CostEstimate(
            flops=40 * state.size, bytes_accessed=8 * state.size, transcendentals=0
        ),
        name="base",
    )(rates, mix, *operands, *pinned(pltpu.HBM, state))


def finish_kernel(first, with_x, rates_ref, mix_ref, above, below, before, after, factors, recv,
                  left, right, *rest):
    tops, rest = (rest[:2], rest[2:]) if with_x else (None, rest)
    late, rest = (rest[:2], rest[2:]) if with_x else (None, rest)
    early_base, rest = (rest[0], rest[1:]) if with_x else (None, rest)
    odd_ref, base_ref, rest = rest[0], rest[1], rest[2:]
    new_ref, out_ref, done_ref = rest[-11:-8]
    base, wide, lines, sides, outer, base_sems, out_sems, outer_sems = rest[-8:]
    count, cells_x, cells_y = base.shape
    mix_b = jnp.broadcast_to(mix_ref[1:2, 0:1], (STRIP, cells_y))
    keep_row = above.shape[0] - 5
    keep = slice(keep_row, keep_row + 1)
    ends = (0, cells_x - STRIP)

    def base_copy(f):
        return pltpu.make_async_copy(base_ref.at[0, first + f], base.at[f], base_sems.at[f])

    def out_copies(f):
        return (
            pltpu.make_async_copy(recv.at[f], out_ref.at[0, first + f], out_sems.at[0, f]),
            pltpu.make_async_copy(base.at[f], new_ref.at[0, first + f], out_sems.at[1, f]),
        )

    def outer_copy(f, i, back):
        there = (new_ref if back else base_ref).at[0, count + f, pl.ds(ends[i], STRIP), :]
        here = outer.at[f, i]
        pair = (here, there) if back else (there, here)
        return pltpu.make_async_copy(*pair, outer_sems.at[f, i])

    outer_rows = [(f, i) for f in range(count) for i in range(2)] if with_x else []
    if not with_x:
        for f in range(count):
            base_copy(f).start()
    for f, i in outer_rows:
        outer_copy(f, i, False).start()
    done_ref[...] = jnp.zeros_like(done_ref)
    def in_order(i, pair):
        in_odd, in_even = pair[0][...], pair[1][...]
        odd = jnp.broadcast_to(odd_ref[i : i + 1, 0:1], in_odd.shape) == 1.0
        return jnp.where(odd, in_even, in_odd), jnp.where(odd, in_odd, in_even)

    if with_x:
        top, bottom = in_order(0, tops)
        lines[:count, :] = top * above[keep, :]
        lines[count:, :] = bottom * below[keep, :]
        late = in_order(0, late)
    else:
        lines[...] = jnp.zeros_like(lines)
    left, right = in_order(1, (left, right))
    sides[:count, :] = left * before[keep, :]
    sides[count:, :] = right * after[keep, :]
    lane = lax.broadcasted_iota(jnp.int32, (STRIP, cells_y), 1)

    def one_field(f, carry):
        rate = jnp.broadcast_to(rates_ref[pl.ds(first + f, 1), 0:1], (STRIP, cells_y))
        line_rate, side_rate = rate[:1], rate[:1, :cells_x]
        both = [sides[pl.ds(f, 1), :] * side_rate, sides[pl.ds(count + f, 1), :] * side_rate]
        cols = columns_of(jnp.concatenate(both, axis=0))
        wide[STRIP - 1 : STRIP, :] = lines[pl.ds(f, 1), :] * line_rate
        wide[STRIP + cells_x : STRIP + cells_x + 1, :] = lines[pl.ds(count + f, 1), :] * line_rate
        to_out, to_new = out_copies(f)
        to_out.start()
        for i in range(0, cells_x, STRIP):
            rows = slice(i, i + STRIP)
            wide[STRIP + i : 2 * STRIP + i, :] = factors[0, rows, :] * recv[f, rows, :] * rate
        if not with_x:
            base_copy(f).wait()
        start = early_base if with_x else base
        for i in range(0, cells_x, STRIP):
            rows = slice(i, i + STRIP)
            mid = wide[STRIP + i : 2 * STRIP + i, :]
            more = (factors[5, rows, :] - rate * factors[0, rows, :]) * mid
            more += factors[1, rows, :] * wide[STRIP + i - 1 : 2 * STRIP + i - 1, :]
            more += factors[2, rows, :] * wide[STRIP + i + 1 : 2 * STRIP + i + 1, :]
            prior = jnp.where(lane == 0, cols[rows, 0:1], pltpu.roll(mid, 1, 1))
            later = jnp.where(lane == cells_y - 1, cols[rows, 1:2], pltpu.roll(mid, cells_y - 1, 1))
            more += factors[3, rows, :] * prior + factors[4, rows, :] * later
            base[f, rows, :] = start[f, rows, :] + mix_b * (2.0 * mid + more)
        to_new.start()
        return carry

    def add_lines():
        for f, i in outer_rows:
            outer_copy(f, i, False).wait()
            row = i * (STRIP - 1)
            at = ends[i] + row
            rate = jnp.broadcast_to(rates_ref[count + f : count + f + 1, 0:1], (1, cells_y))
            line = late[i][f : f + 1, :] * (above, below)[i][keep, :] * rate
            more = mix_b[:1] * factors[1 + i, at : at + 1, :] * line
            outer[f, i, row : row + 1, :] = outer[f, i, row : row + 1, :] + more
            outer_copy(f, i, True).start()

    lax.fori_loop(0, count - 1, one_field, 0, unroll=True)
    add_lines()
    one_field(count - 1, 0)
    for f in range(count):
        for copy in out_copies(f):
            copy.wait()
    for f, i in outer_rows:
        outer_copy(f, i, True).wait()


def finished(
    first, new_state, remapped, recv, odd, x_rims, y_rims, closing, rates, mix, factors, received
):
    count, cells_x, cells_y = recv.shape
    chan = 2 * count
    with_x = x_rims is not None
    anywhere = pl.BlockSpec(memory_space=pl.ANY)
    operands = [rates, mix, *received, factors, recv, *y_rims]
    if with_x:
        late_rims, base_early, late_done = closing
        operands += [*x_rims, *late_rims, base_early]
    operands.append(odd)
    specs = [pl.BlockSpec(memory_space=pltpu.VMEM)] * len(operands) + [anywhere]
    aliases = {len(operands): 0}
    operands.append(new_state)
    if remapped is not None:
        aliases[len(operands)] = 1
        operands += [remapped, late_done]
        specs += [anywhere, anywhere]
    return pl.pallas_call(
        functools.partial(finish_kernel, first, with_x),
        in_specs=specs,
        out_specs=[anywhere, anywhere, pl.BlockSpec(memory_space=pltpu.VMEM)],
        out_shape=[
            jax.ShapeDtypeStruct(new_state.shape, jnp.float32),
            jax.ShapeDtypeStruct((1, chan, cells_x, cells_y), jnp.float32),
            jax.ShapeDtypeStruct((8, LANES), jnp.float32),
        ],
        input_output_aliases=aliases,
        scratch_shapes=[
            pltpu.VMEM((count, cells_x, cells_y), jnp.float32),
            pltpu.VMEM((cells_x + 2 * STRIP, cells_y), jnp.float32),
            pltpu.VMEM((2 * count, cells_y), jnp.float32),
            pltpu.VMEM((2 * count, cells_x), jnp.float32),
            pltpu.VMEM((count, 2, STRIP, cells_y), jnp.float32),
            pltpu.SemaphoreType.DMA((count,)),
            pltpu.SemaphoreType.DMA((2, count)),
            pltpu.SemaphoreType.DMA((count, 2)),
        ],
        compiler_params=pltpu.CompilerParams(vmem_limit_bytes=12 * 1024 * 1024),
        cost_estimate=pl.CostEstimate(
            flops=20 * recv.size, bytes_accessed=20 * recv.size, transcendentals=0
        ),
        name="finish",
    )(*operands)


def body(state, coefs, land_sea, gamma, pair_src, pair_dev, pair_blk, weights):
    tx, ty = lax.axis_size("tx"), lax.axis_size("ty")
    tiles = tx * ty
    nfield, cells_x, cells_y = state.shape[1:]
    chan = gamma.shape[1]
    pairs, width = weights.shape[1], weights.shape[2]
    capacity = max(2, 2 * pairs // tiles)
    half = chan // 2
    early, late = contributions(
        state, pair_src, pair_dev, pair_blk, weights, tiles, capacity, chan
    )
    swap = [(0, 1), (1, 0)]

    def exchanged(rows):
        rows = rows.reshape(tiles, -1, half, width)
        return lax.all_to_all(rows, ("tx", "ty"), split_axis=0, concat_axis=0, tiled=True)

    def add_up(odd, ids, rows):
        return summed(odd, ids, rows, tiles, capacity, half, cells_x, cells_y, width)

    late_in = exchanged(late)
    early = lax.ppermute(early, "comp", swap)
    early_in = placed_rows(early, tiles, capacity, pairs, cells_x * cells_y // width)

    land_after, _ = lax.optimization_barrier((land_sea, late))
    is_atmos = lax.axis_index("comp") == 0
    mix = jnp.where(is_atmos, jnp.array([[0.0, 1.0]]), jnp.array([[0.5, 0.5]]))
    mix = mix.astype(jnp.float32)
    rates = jnp.concatenate([gamma, jnp.zeros((1, nfield - chan), jnp.float32)], axis=1)
    x_low, x_high, y_low, y_high = edges_of(state, coefs, land_after, mix)
    left = lax.ppermute(y_high, "ty", shift_pairs(ty, 1))
    right = lax.ppermute(y_low, "ty", shift_pairs(ty, -1))
    above = lax.ppermute(x_high, "tx", shift_pairs(tx, 1))
    below = lax.ppermute(x_low, "tx", shift_pairs(tx, -1))
    early_in, above, below, left, right = lax.optimization_barrier(
        (early_in, above, below, left, right)
    )
    received = (above, below, left, right)
    early_in = exchanged(early_in)

    ends = jnp.concatenate([above[:, cells_y - LANES :], below[:, cells_y - LANES :]], axis=0)
    starts = jnp.concatenate([above[:, :LANES], below[:, :LANES]], axis=0)
    corners_left = lax.ppermute(ends, "ty", shift_pairs(ty, 1))
    corners_right = lax.ppermute(starts, "ty", shift_pairs(ty, -1))
    base, base_early, factors = base_of(
        state, coefs, land_after, rates, mix, (x_low, x_high, y_low, y_high), received,
        (corners_left, corners_right), half,
    )

    ids_late = late_in[:, capacity, 0, :]
    ids_early = lax.ppermute(ids_late, "comp", swap)
    odd = jnp.stack([lax.axis_index("tx"), lax.axis_index("ty")]).astype(jnp.int32)[None] & 1
    odd_lanes = jnp.broadcast_to(odd.T.astype(jnp.float32), (2, LANES))
    recv_late, x_odd, x_even, y_odd, y_even = add_up(odd_lanes, ids_late, late_in)
    recv_late = lax.ppermute(recv_late, "comp", swap)
    late_x = (
        lax.ppermute(x_odd, ("comp", "tx"), crossed("tx", 1)),
        lax.ppermute(x_even, ("comp", "tx"), crossed("tx", 0)),
    )
    late_y = (
        lax.ppermute(y_odd, ("comp", "ty"), crossed("ty", 1)),
        lax.ppermute(y_even, ("comp", "ty"), crossed("ty", 0)),
    )
    lanes = lambda a: jnp.broadcast_to(a.T, (a.shape[1], LANES))
    rest = (lanes(rates), lanes(mix), factors, received)
    new_state, remapped, done = finished(
        half, base, None, recv_late, odd_lanes, None, late_y, None, *rest
    )
    early_in, done = lax.optimization_barrier((early_in, done))
    recv_early, x_odd, x_even, y_odd, y_even = add_up(odd_lanes, ids_early, early_in)
    early_x = (
        lax.ppermute(x_odd, "tx", neighbour_pairs(tx, 1)),
        lax.ppermute(x_even, "tx", neighbour_pairs(tx, 0)),
    )
    early_y = (
        lax.ppermute(y_odd, "ty", neighbour_pairs(ty, 1)),
        lax.ppermute(y_even, "ty", neighbour_pairs(ty, 0)),
    )
    new_state, remapped, _ = finished(
        0, new_state, remapped, recv_early, odd_lanes, early_x, early_y, (late_x, base_early, done), *rest
    )
    return new_state, remapped


def solution(mesh):
    placed = (
        P("comp", None, "tx", "ty"),
        P("comp", None, "tx", "ty"),
        P("tx", "ty"),
        P("comp", None),
        P("comp", ("tx", "ty")),
        P("comp", ("tx", "ty"), None),
        P("comp", ("tx", "ty")),
        P("comp", ("tx", "ty"), None, None),
    )
    return jax.shard_map(
        body,
        mesh=mesh,
        in_specs=placed,
        out_specs=(P("comp", None, "tx", "ty"), P("comp", None, "tx", "ty")),
        check_vma=False,
    )
```
